32 devices in a mesh: seq: 4 (over y, core), kv: 2 (over x), dp: 4 (over z).
Axes of the slice: x: 2, y: 2, z: 4, core: 2. Of those that a mesh axis runs over, the one named last changes fastest.
Arguments:
- queries: bfloat16 [4096, 2048], P(('dp', 'seq', 'kv')), parts along dimension 0, may hold values from -9 to 9
- keys: bfloat16 [4096, 512], P(('dp', 'seq', 'kv')), parts along dimension 0, may hold values from -4 to 4
- values: bfloat16 [4096, 512], P(('dp', 'seq', 'kv')), parts along dimension 0, may hold values from -6 to 6
- doc_ids: int32 [4096], P(('dp', 'seq', 'kv')), parts along dimension 0, may hold values from 0 to 7, never falling along the last dimension, each value on 1 to 256 neighbouring positions
- beta: float32 [16], replicated, may hold values from -2 to 2
- lin_gain: float32 [2048], replicated, may hold values from 0.1 to 1.9
Outputs:
- mixed: float32 [4096, 2048], P(('dp', 'seq', 'kv')), parts along dimension 0
The draws below stay inside these ranges and needn't reach their ends.
There are 4 independent parts, one for each index of `dp`. The reference program is written for one: setup_inputs(seed, part) draws one part's arguments, and reference() takes and returns one part's arrays. A program takes and returns all parts, laid end to end along the dimension named above; an argument that names none is the same for every part. Nothing has to cross between parts.
Inputs may be any that keep to these rules, and one draw needn't show every extreme that they name: `doc_ids`: document ids never fall along a packed sequence; each document holds 1 to 256 tokens.
All inputs are finite; a program needn't handle non-finite values.
Results may differ from the reference program's by a relative error of at most 0.0012.
Values may be sent and summed in bfloat16 or wider, within the bound.
No kernel may reach another device: no remote copies, remote signals or barrier semaphores. Data moves between devices by JAX's collectives and lax.ppermute only.
A program may use at most 64 MiB of HBM per device.

```python
import math
import jax
import jax.numpy as jnp
import numpy as np
from jax import lax

HEADS = 16
KV_HEADS = 4
HEAD_DIM = 128
DOCS = 8
SEG = 256
TOKENS = 1024
DOC_MOST = 256


def draw_keys(key, part):
    shape = (TOKENS, KV_HEADS * HEAD_DIM)
    base = jnp.clip(jax.random.normal(jax.random.fold_in(key, 3), shape, jnp.float32), -4.0, 4.0)
    return base.astype(jnp.bfloat16)


def draw_queries(key, part):
    shape = (TOKENS, HEADS * HEAD_DIM)
    base = jnp.clip(jax.random.normal(jax.random.fold_in(key, 5), shape, jnp.float32), -4.0, 4.0)
    return base.astype(jnp.bfloat16)


def shard_levels(own_key, shape, split, smallest, high):
    def one(position, blocks):
        heights = jax.random.uniform(jax.random.fold_in(jax.random.fold_in(own_key, 6), position), (blocks,), jnp.float32, smallest / len(split), high / len(split))
        return jnp.repeat(jnp.exp(heights), shape[position] // blocks).reshape((-1,) + (1,) * (len(shape) - position - 1))

    level = one(*split[0])
    for cut in split[1:]:
        level = level * one(*cut)
    return level


def length_profile(number_of, total, reach, skew):
    weights = [(1 << 20) // math.isqrt(rank ** skew) + 1 for rank in range(2, number_of + 1)]
    spare, given = total - reach - (number_of - 1), [1] * (number_of - 1)
    while spare > 0:
        movable = [i for i in range(number_of - 1) if given[i] < reach]
        whole, remaining = sum([weights[i] for i in movable]), spare
        for i in movable:
            more = min(reach - given[i], max(1, remaining * weights[i] // whole), spare)
            given[i] = given[i] + more
            spare = spare - more
    return np.array([reach] + given)


def ragged_sizes(rng, amount, total, bound, skew):
    if amount == 2:
        one = jax.random.randint(rng, (), max(1, total - bound), min(bound, total - 1) + 1)
        return jnp.stack([one, total - one])
    sizes = jnp.asarray(length_profile(amount, total, bound, skew), jnp.int32)
    pairs = (amount - 1) // 2
    giver, receiver = sizes[1:1 + 2 * pairs:2], sizes[2:2 + 2 * pairs:2]
    room = jnp.minimum(giver - 1, bound - receiver)
    moved = jax.random.randint(jax.random.fold_in(rng, 1), (pairs,), 0, 1 << 20) % (room + 1)
    sizes = sizes.at[1:1 + 2 * pairs:2].set(giver - moved).at[2:2 + 2 * pairs:2].set(receiver + moved)
    return sizes[jax.random.permutation(jax.random.fold_in(rng, 2), amount)]


def noise(key, shape, scale, bound, shards=(), held_as=jnp.bfloat16):
    result = scale * jax.random.normal(key, shape, jnp.float32)
    if shards:
        result = result * shard_levels(key, shape, shards, -0.22, 0.18)
    return jnp.clip(result, -bound, bound).astype(held_as)


def setup_inputs(seed: int = 0, part: int = 0) -> dict:
    arg_keys = jax.random.split(jax.random.key(seed), 7)
    own_keys = jax.random.split(jax.random.fold_in(arg_keys[6], part), 7)
    queries = draw_queries(jax.random.fold_in(jax.random.fold_in(arg_keys[6], part), 71), part)
    keys = draw_keys(jax.random.fold_in(jax.random.fold_in(arg_keys[6], part), 71), part)
    values = noise(own_keys[2], (TOKENS, KV_HEADS * HEAD_DIM), 1.0, 6.0, ((0, 8),))
    doc_ids = jnp.searchsorted(jnp.cumsum(ragged_sizes(own_keys[3], DOCS, TOKENS, DOC_MOST, 1)), jnp.arange(TOKENS), side="right").astype(jnp.int32)
    beta = jnp.clip(jax.random.uniform(arg_keys[4], (HEADS,), jnp.float32, -2.0, 2.0), -2.0, 2.0)
    lin_gain = jnp.clip(1.0 + 0.18 * jax.random.normal(arg_keys[5], (HEADS * HEAD_DIM,), jnp.float32), 0.1, 1.9)
    return dict(queries=queries, keys=keys, values=values, doc_ids=doc_ids, beta=beta, lin_gain=lin_gain)


def reference(queries, keys, values, doc_ids, beta, lin_gain):
    groups = HEADS // KV_HEADS
    segments = TOKENS // SEG
    query_heads = queries.reshape(segments, SEG, KV_HEADS, groups, HEAD_DIM)
    key_heads = keys.reshape(segments, SEG, KV_HEADS, HEAD_DIM)
    value_heads = values.reshape(segments, SEG, KV_HEADS, HEAD_DIM)
    seg_docs = doc_ids.reshape(segments, SEG)

    def memory_step(carry, item):
        state, last_doc = carry
        seg_queries, seg_keys, seg_values, docs_here = item
        live = (docs_here == last_doc).astype(jnp.float32)
        recalled = jnp.einsum('sgqd,gde->sgqe', seg_queries.astype(jnp.float32), state, precision=lax.Precision.HIGHEST)
        recalled = recalled * live[:, None, None, None]
        tail = (docs_here == docs_here[-1]).astype(jnp.float32)
        part_state = jnp.einsum('sgd,sge->gde', seg_keys.astype(jnp.float32) * tail[:, None, None], seg_values.astype(jnp.float32), precision=lax.Precision.HIGHEST)
        joined = (docs_here[0] == docs_here[-1]) & (last_doc == docs_here[-1])
        new_state = part_state + jnp.where(joined, state, jnp.zeros_like(state))
        return ((new_state, docs_here[-1]), recalled)
    initial = (jnp.zeros((KV_HEADS, HEAD_DIM, HEAD_DIM), jnp.float32), jnp.array(-1, jnp.int32))
    _, recalled = lax.scan(memory_step, initial, (query_heads, key_heads, value_heads, seg_docs))
    mean_square = lax.optimization_barrier(jnp.mean(recalled * recalled, axis=-1, keepdims=True))
    normed = recalled * lax.rsqrt(mean_square + 1e-06) * lin_gain.reshape(KV_HEADS, groups, HEAD_DIM)

    def attend(item):
        seg_queries, seg_keys, seg_values, docs_here = item
        scores = jnp.einsum('sgqd,tgd->gqst', seg_queries.astype(jnp.float32), seg_keys.astype(jnp.float32)) / jnp.sqrt(jnp.float32(HEAD_DIM))
        places = jnp.arange(SEG, dtype=jnp.int32)
        allowed = (places[None, :] <= places[:, None]) & (docs_here[None, :] == docs_here[:, None])
        masked = jnp.where(allowed, scores, jnp.float32(-1e+30))
        row_max = lax.optimization_barrier(jnp.max(masked, axis=-1, keepdims=True))
        expos = jnp.where(allowed, jnp.exp(masked - row_max), jnp.float32(0.0))
        total = lax.optimization_barrier(jnp.sum(expos, axis=-1))
        weights = expos.astype(jnp.bfloat16)
        summed = jnp.einsum('gqst,tge->sgqe', weights.astype(jnp.float32), seg_values.astype(jnp.float32))
        return summed / jnp.transpose(total, (2, 0, 1))[..., None]
    attended = lax.map(attend, (query_heads, key_heads, value_heads, seg_docs))
    mixing = jax.nn.sigmoid(beta).reshape(KV_HEADS, groups)[None, None, :, :, None]
    mixed = mixing * normed + (1.0 - mixing) * attended
    return mixed.reshape(TOKENS, HEADS * HEAD_DIM).astype(jnp.float32)
```

```python
import functools

import jax
import jax.numpy as jnp
from jax import lax
from jax.experimental import pallas as pl
from jax.experimental.pallas import tpu as pltpu
from jax.sharding import PartitionSpec as P

HEADS = 16
KV_HEADS = 4
HEAD_DIM = 128
GROUPS = HEADS // KV_HEADS
LONGEST = 4

NT = (((1,), (1,)), ((), ()))
TN = (((0,), (0,)), ((), ()))
NN = (((1,), (0,)), ((), ()))


def dot(a, b, dims):
    return lax.dot_general(a, b, dims, preferred_element_type=jnp.float32)


def column(row):
    n = row.shape[1]
    return jnp.transpose(jnp.broadcast_to(row, (HEAD_DIM, n)))


def mix_kernel(blocks, n_kv, place_ref, beta_ref, *refs):
    q_ref, gain_ref = refs[:2]
    key_refs = refs[2 : 2 + blocks]
    value_refs = refs[2 + blocks : 2 + 2 * blocks]
    doc_refs = refs[2 + 2 * blocks : 2 + 3 * blocks]
    out_ref = refs[2 + 3 * blocks]
    rows = q_ref.shape[0]
    segment, part = place_ref[0], place_ref[1]
    docs = [ref[...].astype(jnp.float32) for ref in doc_refs]
    own = docs[0]
    first = own[:, 0:1]
    for j in range(1, n_kv):
        first = jnp.where(part == j, docs[j][:, 0:1], first)
    first = jnp.broadcast_to(first, (1, rows))
    reads = jnp.where((own == first) & (segment > 0), 1.0, 0.0)

    place = lax.broadcasted_iota(jnp.int32, (rows, rows), 0)
    row = lax.broadcasted_iota(jnp.int32, (rows, rows), 1)
    allowed = [(place <= row) & (column(docs[0]) == own)]
    for j in range(1, n_kv):
        allowed.append((column(docs[j]) == own) & (j <= part))

    live = []
    for j in range(1, blocks):
        other = jnp.where((docs[j] == first) & (j > part), 0.0, 1.0)
        count = jnp.sum(other, axis=1, keepdims=True).astype(jnp.int32)
        live.append(lax.broadcasted_iota(jnp.int32, (rows, HEAD_DIM), 0) >= count)

    gain = gain_ref[...]
    scale = 1.0 / (float(HEAD_DIM) ** 0.5)
    for g in range(KV_HEADS):
        cols = slice(g * HEAD_DIM, (g + 1) * HEAD_DIM)
        heads = [
            q_ref[:, (g * GROUPS + i) * HEAD_DIM : (g * GROUPS + i + 1) * HEAD_DIM]
            for i in range(GROUPS)
        ]
        q = jnp.concatenate(heads, axis=0)
        state = jnp.zeros((HEAD_DIM, HEAD_DIM), jnp.float32)
        for j in range(1, blocks):
            k = key_refs[j][:, cols]
            k = jnp.where(live[j - 1], k.astype(jnp.float32), 0.0).astype(jnp.bfloat16)
            state = state + dot(value_refs[j][:, cols], k, TN)
        high = state.astype(jnp.bfloat16)
        low = (state - high.astype(jnp.float32)).astype(jnp.bfloat16)
        recalled = dot(high, q, NT) + dot(low, q, NT)
        scores = [dot(key_refs[j][:, cols], q, NT) for j in range(n_kv)]
        for i in range(GROUPS):
            h = g * GROUPS + i
            cut = slice(i * rows, (i + 1) * rows)
            masked = [
                jnp.where(allowed[j], scores[j][:, cut] * scale, -1e30) for j in range(n_kv)
            ]
            top = functools.reduce(
                jnp.maximum, [jnp.max(m, axis=0, keepdims=True) for m in masked]
            )
            weights = [jnp.exp(m - top) for m in masked]
            total = functools.reduce(
                jnp.add, [jnp.sum(w, axis=0, keepdims=True) for w in weights]
            )
            summed = functools.reduce(
                jnp.add,
                [
                    dot(value_refs[j][:, cols], weights[j].astype(jnp.bfloat16), TN)
                    for j in range(n_kv)
                ],
            )
            read = recalled[:, cut]
            square = jnp.sum(read * read, axis=0, keepdims=True) * (1.0 / HEAD_DIM)
            share = 1.0 / (1.0 + jnp.exp(-jnp.full((1, rows), beta_ref[h], jnp.float32)))
            read_scale = share * lax.rsqrt(square + 1e-06) * reads
            mixed = (
                column(gain[h : h + 1, :]) * (read * read_scale)
                + summed * ((1.0 - share) / total)
            )
            out_ref[:, h * HEAD_DIM : (h + 1) * HEAD_DIM] = jnp.transpose(mixed)


def near_device(n_seq, n_kv, queries, keys, values, doc_ids, beta, lin_gain):
    rows = queries.shape[0]
    devices = n_seq * n_kv
    blocks = 2 * n_kv
    doc_row = doc_ids.reshape(1, rows)
    key_list, value_list, doc_list = [keys], [values], [doc_row]
    for j in range(1, blocks):
        pairs = [
            (b - j, b) for b in range(j, devices) if j <= b % n_kv + n_kv
        ]
        send = functools.partial(lax.ppermute, axis_name=("seq", "kv"), perm=pairs)
        key_list.append(send(keys))
        value_list.append(send(values))
        doc_list.append(send(doc_row))
    place = jnp.stack([lax.axis_index("seq"), lax.axis_index("kv")]).astype(jnp.int32)
    vmem = pl.BlockSpec(memory_space=pltpu.VMEM)
    smem = pl.BlockSpec(memory_space=pltpu.SMEM)
    return pl.pallas_call(
        functools.partial(mix_kernel, blocks, n_kv),
        out_shape=jax.ShapeDtypeStruct((rows, HEADS * HEAD_DIM), jnp.float32),
        in_specs=[smem, smem] + [vmem] * (2 + 3 * blocks),
        out_specs=vmem,
        compiler_params=pltpu.CompilerParams(vmem_limit_bytes=32 * 1024 * 1024),
    )(
        place,
        beta,
        queries,
        lin_gain.reshape(HEADS, HEAD_DIM),
        *key_list,
        *value_list,
        *doc_list,
    )


def carried_in(part, axis, combine, identity):
    place = lax.axis_index(axis)
    gathered = jax.tree.map(lambda a: lax.all_gather(a, axis), part)
    state = jax.tree.map(lambda a, e: jnp.zeros_like(a) + jnp.asarray(e, a.dtype), part, identity)

    def one(step, state):
        return combine(
            state, jax.tree.map(lambda a: lax.dynamic_index_in_dim(a, step, 0, False), gathered)
        )

    return lax.fori_loop(0, place, one, state)


def join_states(earlier, later):
    state_early, first_early, last_early = earlier
    state_late, first_late, last_late = later
    empty_late = first_late < 0
    joined = (first_late == last_late) & (last_early == first_late)
    merged = state_late + jnp.where(joined, state_early, jnp.zeros_like(state_early))
    combined = jnp.where(empty_late, state_early, merged)
    first_doc = jnp.where(first_early < 0, first_late, first_early)
    last_doc = jnp.where(empty_late, last_early, last_late)
    return (combined, first_doc, last_doc)


def tail_merge(one_side, other_side):
    state_one, first_one, last_one = one_side
    state_other, first_other, last_other = other_side
    top_doc = jnp.maximum(last_one, last_other)
    state_sum = jnp.where(last_one == top_doc, state_one, jnp.zeros_like(state_one))
    state_sum = state_sum + jnp.where(
        last_other == top_doc, state_other, jnp.zeros_like(state_other)
    )
    return (state_sum, jnp.minimum(first_one, first_other), top_doc)


def tail_state(key_rows, value_rows, doc_rows, target_doc):
    count = key_rows.shape[0]
    key_heads = key_rows.reshape(count, KV_HEADS, HEAD_DIM)
    value_heads = value_rows.reshape(count, KV_HEADS, HEAD_DIM)
    live = doc_rows == target_doc
    masked = jnp.where(live[:, None, None], key_heads, jnp.zeros_like(key_heads))
    return jnp.einsum("rgd,rge->gde", masked, value_heads, preferred_element_type=jnp.float32)


def attend_block(
    carry, query_heads, query_pos, query_doc, key_rows, value_rows, key_doc, key_start
):
    running_max, running_sum, accumulated = carry
    key_count = key_rows.shape[0]
    key_heads = key_rows.reshape(key_count, KV_HEADS, HEAD_DIM)
    value_heads = value_rows.reshape(key_count, KV_HEADS, HEAD_DIM)
    scores = jnp.einsum(
        "rgqd,kgd->gqrk", query_heads, key_heads, preferred_element_type=jnp.float32
    )
    scores = scores / jnp.sqrt(jnp.float32(HEAD_DIM))
    key_pos = key_start + jnp.arange(key_count, dtype=jnp.int32)
    allowed = (key_pos[None, :] <= query_pos[:, None]) & (key_doc[None, :] == query_doc[:, None])
    masked = jnp.where(allowed, scores, jnp.float32(-1e30))
    new_max = jnp.maximum(running_max, jnp.max(masked, axis=-1))
    factor = jnp.exp(running_max - new_max)
    weights = jnp.where(allowed, jnp.exp(masked - new_max[..., None]), jnp.float32(0.0))
    new_sum = running_sum * factor + jnp.sum(weights, axis=-1)
    product = jnp.einsum(
        "gqrk,kge->gqre",
        weights.astype(jnp.bfloat16),
        value_heads,
        preferred_element_type=jnp.float32,
    )
    new_accum = accumulated * factor[..., None] + product
    return (new_max, new_sum, new_accum)


def far_device(queries, keys, values, doc_ids, beta, lin_gain):
    row_count = queries.shape[0]
    groups = HEADS // KV_HEADS
    query_heads = queries.reshape(row_count, KV_HEADS, groups, HEAD_DIM)
    position = lax.axis_index("kv") * row_count
    query_pos = position + jnp.arange(row_count, dtype=jnp.int32)
    last_query = position + row_count - 1
    initial = (
        jnp.full((KV_HEADS, groups, row_count), -1e30, jnp.float32),
        jnp.zeros((KV_HEADS, groups, row_count), jnp.float32),
        jnp.zeros((KV_HEADS, groups, row_count, HEAD_DIM), jnp.float32),
    )
    empty_tail = (
        jnp.zeros((KV_HEADS, HEAD_DIM, HEAD_DIM), jnp.float32),
        jnp.array(2**30, jnp.int32),
        jnp.array(-1, jnp.int32),
    )
    key_piece = lax.all_gather(keys, "kv", axis=0, tiled=True)
    value_piece = lax.all_gather(values, "kv", axis=0, tiled=True)
    doc_piece = lax.all_gather(doc_ids, "kv", axis=0, tiled=True)
    blocks = key_piece.shape[0] // row_count

    def one_block(state, item):
        soft_state, tail_now = state
        key_block, value_block, doc_block, number = item
        block_start = number * row_count
        soft_next = lax.cond(
            block_start <= last_query,
            lambda inner: attend_block(
                inner,
                query_heads,
                query_pos,
                doc_ids,
                key_block,
                value_block,
                doc_block,
                block_start,
            ),
            lambda inner: inner,
            soft_state,
        )
        block_tail = (
            tail_state(key_block, value_block, doc_block, doc_block[-1]),
            doc_block[0],
            doc_block[-1],
        )
        tail_now = tail_merge(tail_now, block_tail)
        return ((soft_next, tail_now), None)

    stacked = (
        key_piece.reshape(blocks, row_count, -1),
        value_piece.reshape(blocks, row_count, -1),
        doc_piece.reshape(blocks, row_count),
        jnp.arange(blocks, dtype=jnp.int32),
    )
    result, _ = lax.scan(one_block, (initial, empty_tail), stacked)
    running, segment_tail = result
    running_max, running_sum, accumulated = running
    soft_out = jnp.transpose(accumulated / running_sum[..., None], (2, 0, 1, 3))
    identity = (
        jnp.zeros((KV_HEADS, HEAD_DIM, HEAD_DIM), jnp.float32),
        jnp.array(-1, jnp.int32),
        jnp.array(-1, jnp.int32),
    )
    memory = carried_in(segment_tail, "seq", join_states, identity)
    memory_state, memory_first, memory_last = memory
    query_float = query_heads.astype(jnp.float32)
    recalled = jnp.einsum(
        "rgqd,gde->rgqe", query_float, memory_state, precision=lax.Precision.HIGHEST
    )
    recalled = jnp.where((doc_ids == memory_last)[:, None, None, None], recalled, jnp.float32(0.0))
    mean_square = jnp.mean(recalled * recalled, axis=-1, keepdims=True)
    normed = (
        recalled * lax.rsqrt(mean_square + 1e-06) * lin_gain.reshape(KV_HEADS, groups, HEAD_DIM)
    )
    mixing = jax.nn.sigmoid(beta).reshape(KV_HEADS, groups)[None, :, :, None]
    mixed = mixing * normed + (1.0 - mixing) * soft_out
    return mixed.reshape(row_count, HEADS * HEAD_DIM).astype(jnp.float32)


def solution(mesh):
    n_seq, n_kv = mesh.shape["seq"], mesh.shape["kv"]
    in_specs = (
        P(("dp", "seq", "kv"), None),
        P(("dp", "seq", "kv"), None),
        P(("dp", "seq", "kv"), None),
        P(("dp", "seq", "kv")),
        P(),
        P(),
    )
    out_specs = P(("dp", "seq", "kv"), None)
    if n_seq <= LONGEST:
        on_device = functools.partial(near_device, n_seq, n_kv)
    else:
        on_device = far_device
    return jax.shard_map(
        on_device, mesh=mesh, in_specs=in_specs, out_specs=out_specs, check_vma=False
    )
```

```python
import functools
import math

import jax
import jax.numpy as jnp
from jax import lax
from jax.experimental import pallas as pl
from jax.experimental.pallas import tpu as pltpu
from jax.sharding import PartitionSpec as P

HEADS = 16
KV_HEADS = 4
HEAD_DIM = 128
GROUPS = HEADS // KV_HEADS
LONGEST = 4
SCALE = math.log2(math.e) / math.sqrt(HEAD_DIM)
LOWEST = -1e30
DOC_ROWS = 16

NT = (((1,), (1,)), ((), ()))
TN = (((0,), (0,)), ((), ()))


def dot(a, b, dims):
    return lax.dot_general(a, b, dims, preferred_element_type=jnp.float32)


def column(row):
    return jnp.transpose(jnp.broadcast_to(row, (HEAD_DIM, row.shape[1])))


def group_cols(g):
    return slice(g * HEAD_DIM, (g + 1) * HEAD_DIM)


def head_cols(h):
    return slice(h * HEAD_DIM, (h + 1) * HEAD_DIM)


def group_queries(q_ref, g):
    return jnp.concatenate([q_ref[:, head_cols(g * GROUPS + i)] for i in range(GROUPS)], axis=0)


def pack_kernel(key_ref, value_ref, doc_ref, out_ref, doc_scratch, sems):
    rows = key_ref.shape[0]
    doc_copy = pltpu.make_async_copy(doc_ref, doc_scratch, sems.at[0])
    key_copy = pltpu.make_async_copy(key_ref, out_ref.at[0:rows], sems.at[1])
    value_copy = pltpu.make_async_copy(value_ref, out_ref.at[rows : 2 * rows], sems.at[2])
    doc_copy.start()
    key_copy.start()
    value_copy.start()
    doc_copy.wait()
    docs = jnp.broadcast_to(doc_scratch[...].astype(jnp.float32), (DOC_ROWS, rows))
    out_ref[2 * rows : 2 * rows + DOC_ROWS, 0:rows] = docs.astype(jnp.bfloat16)
    key_copy.wait()
    value_copy.wait()


def payload_docs(ref, rows):
    return ref[2 * rows : 2 * rows + DOC_ROWS, 0:rows].astype(jnp.float32)[0:1, :]


def own_kernel(beta_ref, q_ref, own_ref, gain_ref, summed_ref, stats_ref, gain_out_ref):
    rows = q_ref.shape[0]
    docs = payload_docs(own_ref, rows)
    place = lax.broadcasted_iota(jnp.int32, (rows, rows), 0)
    row = lax.broadcasted_iota(jnp.int32, (rows, rows), 1)
    allowed = (place <= row) & (column(docs) == docs)
    bias = jnp.where(allowed, 0.0, LOWEST)
    for g in range(KV_HEADS):
        scores = dot(own_ref[0:rows, group_cols(g)], group_queries(q_ref, g), NT)
        tops, totals, weights, rest = [], [], [], []
        for i in range(GROUPS):
            h = g * GROUPS + i
            masked = scores[:, i * rows : (i + 1) * rows] * SCALE + bias
            top = jnp.max(masked, axis=0, keepdims=True)
            weight = jnp.exp2(masked - top)
            tops.append(top)
            totals.append(jnp.sum(weight, axis=0, keepdims=True))
            weights.append(weight.astype(jnp.bfloat16))
            share = 1.0 / (1.0 + jnp.exp(-jnp.full((1, HEAD_DIM), beta_ref[h], jnp.float32)))
            rest.append(jnp.broadcast_to((1.0 - share)[:, 0:1], (1, rows)))
            gain_out_ref[head_cols(h), :] = column(gain_ref[h : h + 1, :] * share)
        summed_ref[group_cols(g), :] = dot(
            own_ref[rows : 2 * rows, group_cols(g)], jnp.concatenate(weights, axis=1), TN
        )
        stats_ref[g : g + 1, :] = jnp.concatenate(tops, axis=1)
        stats_ref[KV_HEADS + g : KV_HEADS + g + 1, :] = jnp.concatenate(totals, axis=1)
        stats_ref[2 * KV_HEADS + g : 2 * KV_HEADS + g + 1, :] = jnp.concatenate(rest, axis=1)


def join_kernel(
    q_ref, own_ref, one_ref, two_ref, summed_ref, stats_ref, gain_ref, out_ref, held, sems
):
    rows = q_ref.shape[0]
    part = lax.axis_index("kv")
    own = payload_docs(own_ref, rows)
    first = jnp.broadcast_to(own[:, 0:1], (1, rows))
    reads = jnp.where(own == first, 1.0, 0.0)

    def tail(ref):
        others = jnp.where(payload_docs(ref, rows) == first, 0.0, 1.0)
        count = jnp.sum(others, axis=1, keepdims=True)
        place = lax.broadcasted_iota(jnp.int32, (rows, HEAD_DIM), 0).astype(jnp.float32)
        return place >= count

    tail_one, tail_two = tail(one_ref), tail(two_ref)
    in_memory = tail_one & (part == 0)
    row_bias = jnp.where((own == first) & (part == 1), 0.0, LOWEST)
    bias = jnp.where(tail_one, row_bias, LOWEST)

    copies = []
    for g in range(KV_HEADS):
        cols = group_cols(g)
        q = group_queries(q_ref, g)
        key_one, value_one = one_ref[0:rows, cols], one_ref[rows : 2 * rows, cols]
        key_two, value_two = two_ref[0:rows, cols], two_ref[rows : 2 * rows, cols]
        memory_keys = jnp.concatenate(
            [
                jnp.where(in_memory, key_one.astype(jnp.float32), 0.0).astype(jnp.bfloat16),
                jnp.where(tail_two, key_two.astype(jnp.float32), 0.0).astype(jnp.bfloat16),
            ],
            axis=0,
        )
        state = dot(jnp.concatenate([value_one, value_two], axis=0), memory_keys, TN)
        high = state.astype(jnp.bfloat16)
        low = (state - high.astype(jnp.float32)).astype(jnp.bfloat16)
        recalled = dot(high, q, NT) + dot(low, q, NT)
        scores = dot(key_one, q, NT)
        weights, factors, totals = [], [], []
        for i in range(GROUPS):
            cut = slice(i * rows, (i + 1) * rows)
            masked = scores[:, cut] * SCALE + bias
            top_own = stats_ref[g : g + 1, cut]
            top = jnp.maximum(jnp.max(masked, axis=0, keepdims=True), top_own)
            weight = jnp.exp2(masked - top)
            factor = jnp.exp2(top_own - top)
            total = stats_ref[KV_HEADS + g : KV_HEADS + g + 1, cut] * factor
            totals.append(total + jnp.sum(weight, axis=0, keepdims=True))
            factors.append(factor)
            weights.append(weight.astype(jnp.bfloat16))
        added = dot(value_one, jnp.concatenate(weights, axis=1), TN)
        for i in range(GROUPS):
            h = g * GROUPS + i
            cut = slice(i * rows, (i + 1) * rows)
            read = recalled[:, cut]
            square = jnp.sum(read * read, axis=0, keepdims=True) * (1.0 / HEAD_DIM)
            read = read * (lax.rsqrt(square + 1e-06) * reads)
            summed = summed_ref[cols, cut] * factors[i] + added[:, cut]
            rest = stats_ref[2 * KV_HEADS + g : 2 * KV_HEADS + g + 1, cut]
            mixed = read * gain_ref[head_cols(h), :] + summed * (rest / totals[i])
            held[:, head_cols(h)] = jnp.transpose(mixed)
        wide = slice(g * GROUPS * HEAD_DIM, (g + 1) * GROUPS * HEAD_DIM)
        copy = pltpu.make_async_copy(held.at[:, wide], out_ref.at[:, wide], sems.at[g])
        copy.start()
        copies.append(copy)
    for copy in copies:
        copy.wait()


def near_device(n_seq, n_kv, queries, keys, values, doc_ids, beta, lin_gain):
    rows = queries.shape[0]
    devices = n_seq * n_kv
    vmem = pl.BlockSpec(memory_space=pltpu.VMEM)
    smem = pl.BlockSpec(memory_space=pltpu.SMEM)
    hbm = pl.BlockSpec(memory_space=pltpu.HBM)
    params = pltpu.CompilerParams(vmem_limit_bytes=32 * 1024 * 1024)
    width = KV_HEADS * HEAD_DIM
    deep = 2 * rows + DOC_ROWS
    own = pl.pallas_call(
        pack_kernel,
        out_shape=jax.ShapeDtypeStruct((deep, width), jnp.bfloat16),
        in_specs=[hbm] * 3,
        out_specs=vmem,
        scratch_shapes=[pltpu.VMEM((1, rows), jnp.int32), pltpu.SemaphoreType.DMA((3,))],
        compiler_params=params,
        cost_estimate=pl.CostEstimate(flops=0, bytes_accessed=4 * rows * width, transcendentals=0),
    )(keys, values, doc_ids.reshape(1, rows))

    def before(j):
        pairs = [(b - j, b) for b in range(j, devices)]
        return lax.ppermute(own, ("seq", "kv"), pairs)

    one, two = before(1), before(2)
    summed, stats, gains = pl.pallas_call(
        own_kernel,
        out_shape=[
            jax.ShapeDtypeStruct((KV_HEADS * HEAD_DIM, GROUPS * rows), jnp.float32),
            jax.ShapeDtypeStruct((4 * KV_HEADS, GROUPS * rows), jnp.float32),
            jax.ShapeDtypeStruct((HEADS * HEAD_DIM, rows), jnp.float32),
        ],
        in_specs=[smem, vmem, vmem, vmem],
        out_specs=[vmem] * 3,
        compiler_params=params,
        cost_estimate=pl.CostEstimate(
            flops=4 * HEADS * HEAD_DIM * rows * rows,
            bytes_accessed=4 * 1024 * 1024,
            transcendentals=HEADS * rows * rows,
        ),
    )(beta, queries, own, lin_gain.reshape(HEADS, HEAD_DIM))
    return pl.pallas_call(
        join_kernel,
        out_shape=jax.ShapeDtypeStruct((rows, HEADS * HEAD_DIM), jnp.float32),
        in_specs=[vmem] * 7,
        out_specs=hbm,
        scratch_shapes=[
            pltpu.VMEM((rows, HEADS * HEAD_DIM), jnp.float32),
            pltpu.SemaphoreType.DMA((KV_HEADS,)),
        ],
        compiler_params=params,
    )(queries, own, one, two, summed, stats, gains)


def carried_in(part, axis, combine, identity):
    place = lax.axis_index(axis)
    gathered = jax.tree.map(lambda a: lax.all_gather(a, axis), part)
    state = jax.tree.map(lambda a, e: jnp.zeros_like(a) + jnp.asarray(e, a.dtype), part, identity)

    def one(step, state):
        return combine(
            state, jax.tree.map(lambda a: lax.dynamic_index_in_dim(a, step, 0, False), gathered)
        )

    return lax.fori_loop(0, place, one, state)


def join_states(earlier, later):
    state_early, first_early, last_early = earlier
    state_late, first_late, last_late = later
    empty_late = first_late < 0
    joined = (first_late == last_late) & (last_early == first_late)
    merged = state_late + jnp.where(joined, state_early, jnp.zeros_like(state_early))
    combined = jnp.where(empty_late, state_early, merged)
    first_doc = jnp.where(first_early < 0, first_late, first_early)
    last_doc = jnp.where(empty_late, last_early, last_late)
    return (combined, first_doc, last_doc)


def tail_merge(one_side, other_side):
    state_one, first_one, last_one = one_side
    state_other, first_other, last_other = other_side
    top_doc = jnp.maximum(last_one, last_other)
    state_sum = jnp.where(last_one == top_doc, state_one, jnp.zeros_like(state_one))
    state_sum = state_sum + jnp.where(
        last_other == top_doc, state_other, jnp.zeros_like(state_other)
    )
    return (state_sum, jnp.minimum(first_one, first_other), top_doc)


def tail_state(key_rows, value_rows, doc_rows, target_doc):
    count = key_rows.shape[0]
    key_heads = key_rows.reshape(count, KV_HEADS, HEAD_DIM)
    value_heads = value_rows.reshape(count, KV_HEADS, HEAD_DIM)
    live = doc_rows == target_doc
    masked = jnp.where(live[:, None, None], key_heads, jnp.zeros_like(key_heads))
    return jnp.einsum("rgd,rge->gde", masked, value_heads, preferred_element_type=jnp.float32)


def attend_block(
    carry, query_heads, query_pos, query_doc, key_rows, value_rows, key_doc, key_start
):
    running_max, running_sum, accumulated = carry
    key_count = key_rows.shape[0]
    key_heads = key_rows.reshape(key_count, KV_HEADS, HEAD_DIM)
    value_heads = value_rows.reshape(key_count, KV_HEADS, HEAD_DIM)
    scores = jnp.einsum(
        "rgqd,kgd->gqrk", query_heads, key_heads, preferred_element_type=jnp.float32
    )
    scores = scores / jnp.sqrt(jnp.float32(HEAD_DIM))
    key_pos = key_start + jnp.arange(key_count, dtype=jnp.int32)
    allowed = (key_pos[None, :] <= query_pos[:, None]) & (key_doc[None, :] == query_doc[:, None])
    masked = jnp.where(allowed, scores, jnp.float32(-1e30))
    new_max = jnp.maximum(running_max, jnp.max(masked, axis=-1))
    factor = jnp.exp(running_max - new_max)
    weights = jnp.where(allowed, jnp.exp(masked - new_max[..., None]), jnp.float32(0.0))
    new_sum = running_sum * factor + jnp.sum(weights, axis=-1)
    product = jnp.einsum(
        "gqrk,kge->gqre",
        weights.astype(jnp.bfloat16),
        value_heads,
        preferred_element_type=jnp.float32,
    )
    new_accum = accumulated * factor[..., None] + product
    return (new_max, new_sum, new_accum)


def far_device(queries, keys, values, doc_ids, beta, lin_gain):
    row_count = queries.shape[0]
    groups = HEADS // KV_HEADS
    query_heads = queries.reshape(row_count, KV_HEADS, groups, HEAD_DIM)
    position = lax.axis_index("kv") * row_count
    query_pos = position + jnp.arange(row_count, dtype=jnp.int32)
    last_query = position + row_count - 1
    initial = (
        jnp.full((KV_HEADS, groups, row_count), -1e30, jnp.float32),
        jnp.zeros((KV_HEADS, groups, row_count), jnp.float32),
        jnp.zeros((KV_HEADS, groups, row_count, HEAD_DIM), jnp.float32),
    )
    empty_tail = (
        jnp.zeros((KV_HEADS, HEAD_DIM, HEAD_DIM), jnp.float32),
        jnp.array(2**30, jnp.int32),
        jnp.array(-1, jnp.int32),
    )
    key_piece = lax.all_gather(keys, "kv", axis=0, tiled=True)
    value_piece = lax.all_gather(values, "kv", axis=0, tiled=True)
    doc_piece = lax.all_gather(doc_ids, "kv", axis=0, tiled=True)
    blocks = key_piece.shape[0] // row_count

    def one_block(state, item):
        soft_state, tail_now = state
        key_block, value_block, doc_block, number = item
        block_start = number * row_count
        soft_next = lax.cond(
            block_start <= last_query,
            lambda inner: attend_block(
                inner,
                query_heads,
                query_pos,
                doc_ids,
                key_block,
                value_block,
                doc_block,
                block_start,
            ),
            lambda inner: inner,
            soft_state,
        )
        block_tail = (
            tail_state(key_block, value_block, doc_block, doc_block[-1]),
            doc_block[0],
            doc_block[-1],
        )
        tail_now = tail_merge(tail_now, block_tail)
        return ((soft_next, tail_now), None)

    stacked = (
        key_piece.reshape(blocks, row_count, -1),
        value_piece.reshape(blocks, row_count, -1),
        doc_piece.reshape(blocks, row_count),
        jnp.arange(blocks, dtype=jnp.int32),
    )
    result, _ = lax.scan(one_block, (initial, empty_tail), stacked)
    running, segment_tail = result
    running_max, running_sum, accumulated = running
    soft_out = jnp.transpose(accumulated / running_sum[..., None], (2, 0, 1, 3))
    identity = (
        jnp.zeros((KV_HEADS, HEAD_DIM, HEAD_DIM), jnp.float32),
        jnp.array(-1, jnp.int32),
        jnp.array(-1, jnp.int32),
    )
    memory = carried_in(segment_tail, "seq", join_states, identity)
    memory_state, memory_first, memory_last = memory
    query_float = query_heads.astype(jnp.float32)
    recalled = jnp.einsum(
        "rgqd,gde->rgqe", query_float, memory_state, precision=lax.Precision.HIGHEST
    )
    recalled = jnp.where((doc_ids == memory_last)[:, None, None, None], recalled, jnp.float32(0.0))
    mean_square = jnp.mean(recalled * recalled, axis=-1, keepdims=True)
    normed = (
        recalled * lax.rsqrt(mean_square + 1e-06) * lin_gain.reshape(KV_HEADS, groups, HEAD_DIM)
    )
    mixing = jax.nn.sigmoid(beta).reshape(KV_HEADS, groups)[None, :, :, None]
    mixed = mixing * normed + (1.0 - mixing) * soft_out
    return mixed.reshape(row_count, HEADS * HEAD_DIM).astype(jnp.float32)


def solution(mesh):
    n_seq, n_kv = mesh.shape["seq"], mesh.shape["kv"]
    in_specs = (
        P(("dp", "seq", "kv"), None),
        P(("dp", "seq", "kv"), None),
        P(("dp", "seq", "kv"), None),
        P(("dp", "seq", "kv")),
        P(),
        P(),
    )
    out_specs = P(("dp", "seq", "kv"), None)
    if n_kv == 2 and n_seq * n_kv <= 2 * LONGEST:
        on_device = functools.partial(near_device, n_seq, n_kv)
    else:
        on_device = far_device
    return jax.shard_map(
        on_device, mesh=mesh, in_specs=in_specs, out_specs=out_specs, check_vma=False
    )
```

```python
import functools
import math

import jax
import jax.numpy as jnp
from jax import lax
from jax.experimental import pallas as pl
from jax.experimental.pallas import tpu as pltpu
from jax.sharding import PartitionSpec as P

HEADS = 16
KV_HEADS = 4
HEAD_DIM = 128
GROUPS = HEADS // KV_HEADS
LONGEST = 4
SCALE = math.log2(math.e) / math.sqrt(HEAD_DIM)
LOWEST = -1e30
DOC_ROWS = 16

NT = (((1,), (1,)), ((), ()))
TN = (((0,), (0,)), ((), ()))


def dot(a, b, dims):
    return lax.dot_general(a, b, dims, preferred_element_type=jnp.float32)


def column(row):
    return jnp.transpose(jnp.broadcast_to(row, (HEAD_DIM, row.shape[1])))


def part_of(i, size):
    return slice(i * size, (i + 1) * size)


def group_queries(q_ref, g):
    heads = [q_ref[:, part_of(g * GROUPS + i, HEAD_DIM)] for i in range(GROUPS)]
    return jnp.concatenate(heads, axis=0)


def payload_keys(ref, g, rows):
    return ref[part_of(g, rows), :]


def payload_values(ref, g, rows):
    return ref[part_of(KV_HEADS + g, rows), :]


def payload_docs(ref, rows):
    start = 2 * KV_HEADS * rows
    return ref[start : start + DOC_ROWS, :].astype(jnp.float32)[0:1, :]


def pack_kernel(key_ref, value_ref, doc_ref, out_ref, doc_scratch, doc_rows, sems):
    rows = key_ref.shape[0]
    doc_copy = pltpu.make_async_copy(doc_ref, doc_scratch, sems.at[2 * KV_HEADS])
    doc_copy.start()
    copies = []
    for g in range(2 * KV_HEADS):
        source = key_ref if g < KV_HEADS else value_ref
        copy = pltpu.make_async_copy(
            source.at[:, part_of(g % KV_HEADS, HEAD_DIM)],
            out_ref.at[part_of(g, rows), :],
            sems.at[g],
        )
        copy.start()
        copies.append(copy)
    doc_copy.wait()
    docs = jnp.broadcast_to(doc_scratch[...].astype(jnp.float32), (DOC_ROWS, rows))
    doc_rows[...] = docs.astype(jnp.bfloat16)
    start = 2 * KV_HEADS * rows
    doc_copy = pltpu.make_async_copy(
        doc_rows, out_ref.at[start : start + DOC_ROWS, :], sems.at[2 * KV_HEADS + 1]
    )
    doc_copy.start()
    for copy in copies:
        copy.wait()
    doc_copy.wait()


def own_kernel(beta_ref, q_ref, own_ref, gain_ref, summed_ref, stats_ref, gain_out_ref):
    rows = q_ref.shape[0]
    docs = payload_docs(own_ref, rows)
    place = lax.broadcasted_iota(jnp.int32, (rows, rows), 0)
    row = lax.broadcasted_iota(jnp.int32, (rows, rows), 1)
    allowed = (place <= row) & (column(docs) == docs)
    bias = jnp.where(allowed, 0.0, LOWEST)
    for g in range(KV_HEADS):
        scores = dot(payload_keys(own_ref, g, rows), group_queries(q_ref, g), NT)
        tops, totals, weights, rest = [], [], [], []
        for i in range(GROUPS):
            h = g * GROUPS + i
            masked = scores[:, part_of(i, rows)] * SCALE + bias
            top = jnp.max(masked, axis=0, keepdims=True)
            weight = jnp.exp2(masked - top)
            tops.append(top)
            totals.append(jnp.sum(weight, axis=0, keepdims=True))
            weights.append(weight.astype(jnp.bfloat16))
            share = 1.0 / (1.0 + jnp.exp(-jnp.full((1, HEAD_DIM), beta_ref[h], jnp.float32)))
            rest.append(jnp.broadcast_to((1.0 - share)[:, 0:1], (1, rows)))
            gain_out_ref[part_of(h, HEAD_DIM), :] = column(gain_ref[h : h + 1, :] * share)
        summed_ref[part_of(g, HEAD_DIM), :] = dot(
            payload_values(own_ref, g, rows), jnp.concatenate(weights, axis=1), TN
        )
        stats_ref[g : g + 1, :] = jnp.concatenate(tops, axis=1)
        stats_ref[KV_HEADS + g : KV_HEADS + g + 1, :] = jnp.concatenate(totals, axis=1)
        stats_ref[2 * KV_HEADS + g : 2 * KV_HEADS + g + 1, :] = jnp.concatenate(rest, axis=1)


def first_document(own_ref, rows):
    own = payload_docs(own_ref, rows)
    first = jnp.broadcast_to(own[:, 0:1], (1, rows))
    return first, own == first


def tail(ref, first, rows):
    others = jnp.where(payload_docs(ref, rows) == first, 0.0, 1.0)
    count = jnp.sum(others, axis=1, keepdims=True)
    place = lax.broadcasted_iota(jnp.int32, (rows, HEAD_DIM), 0).astype(jnp.float32)
    return place >= count


def block_state(ref, live, g, rows):
    keys = payload_keys(ref, g, rows).astype(jnp.float32)
    keys = jnp.where(live, keys, 0.0).astype(jnp.bfloat16)
    return dot(payload_values(ref, g, rows), keys, TN)


def memory_read(state, q_ref, g, gain_ref, reads):
    rows = q_ref.shape[0]
    q = group_queries(q_ref, g)
    high = state.astype(jnp.bfloat16)
    low = (state - high.astype(jnp.float32)).astype(jnp.bfloat16)
    recalled = dot(high, q, NT) + dot(low, q, NT)
    heads = []
    for i in range(GROUPS):
        read = recalled[:, part_of(i, rows)]
        square = jnp.sum(read * read, axis=0, keepdims=True) * (1.0 / HEAD_DIM)
        read = read * (lax.rsqrt(square + 1e-06) * reads)
        heads.append(read * gain_ref[part_of(g * GROUPS + i, HEAD_DIM), :])
    return heads


def middle_kernel(
    q_ref, own_ref, two_ref, summed_ref, stats_ref, gain_ref, state_ref, ready_ref
):
    rows = q_ref.shape[0]
    part = lax.axis_index("kv")
    first, same = first_document(own_ref, rows)
    reads = jnp.where(same, 1.0, 0.0)
    live = tail(two_ref, first, rows)
    for g in range(KV_HEADS):
        state_ref[part_of(g, HEAD_DIM), :] = block_state(two_ref, live, g, rows)

    @pl.when(part == 0)
    def _():
        for g in range(KV_HEADS):
            rest = stats_ref[2 * KV_HEADS + g : 2 * KV_HEADS + g + 1, :]
            scaled = rest / stats_ref[KV_HEADS + g : KV_HEADS + g + 1, :]
            group = part_of(g, HEAD_DIM)
            ready_ref[group, :] = summed_ref[group, :] * scaled

    @pl.when(part == 1)
    def _():
        for g in range(KV_HEADS):
            state = state_ref[part_of(g, HEAD_DIM), :]
            heads = memory_read(state, q_ref, g, gain_ref, reads)
            ready_ref[part_of(g, HEAD_DIM), :] = jnp.concatenate(heads, axis=1)


def join_kernel(
    q_ref, own_ref, one_ref, summed_ref, stats_ref, gain_ref, state_ref, ready_ref,
    out_ref, held, sems,
):
    rows = q_ref.shape[0]
    part = lax.axis_index("kv")
    first, same = first_document(own_ref, rows)
    live = tail(one_ref, first, rows)

    def copy(g):
        wide = part_of(g, GROUPS * HEAD_DIM)
        return pltpu.make_async_copy(held.at[:, wide], out_ref.at[:, wide], sems.at[g])

    @pl.when(part == 0)
    def _():
        reads = jnp.where(same, 1.0, 0.0)
        for g in range(KV_HEADS):
            state = state_ref[part_of(g, HEAD_DIM), :] + block_state(one_ref, live, g, rows)
            heads = memory_read(state, q_ref, g, gain_ref, reads)
            for i in range(GROUPS):
                mixed = heads[i] + ready_ref[part_of(g, HEAD_DIM), part_of(i, rows)]
                held[:, part_of(g * GROUPS + i, HEAD_DIM)] = jnp.transpose(mixed)
            copy(g).start()

    @pl.when(part == 1)
    def _():
        bias = jnp.where(live & same, 0.0, LOWEST)
        for g in range(KV_HEADS):
            scores = dot(payload_keys(one_ref, g, rows), group_queries(q_ref, g), NT)
            weights, factors, scales = [], [], []
            for i in range(GROUPS):
                cut = part_of(i, rows)
                masked = scores[:, cut] * SCALE + bias
                top_own = stats_ref[g : g + 1, cut]
                top = jnp.maximum(jnp.max(masked, axis=0, keepdims=True), top_own)
                weight = jnp.exp2(masked - top)
                factor = jnp.exp2(top_own - top)
                total = stats_ref[KV_HEADS + g : KV_HEADS + g + 1, cut] * factor
                total = total + jnp.sum(weight, axis=0, keepdims=True)
                factors.append(factor)
                scales.append(stats_ref[2 * KV_HEADS + g : 2 * KV_HEADS + g + 1, cut] / total)
                weights.append(weight.astype(jnp.bfloat16))
            added = dot(payload_values(one_ref, g, rows), jnp.concatenate(weights, axis=1), TN)
            for i in range(GROUPS):
                cut, group = part_of(i, rows), part_of(g, HEAD_DIM)
                summed = summed_ref[group, cut] * factors[i] + added[:, cut]
                mixed = ready_ref[group, cut] + summed * scales[i]
                held[:, part_of(g * GROUPS + i, HEAD_DIM)] = jnp.transpose(mixed)
            copy(g).start()

    for g in range(KV_HEADS):
        copy(g).wait()


def near_device(n_seq, n_kv, queries, keys, values, doc_ids, beta, lin_gain):
    rows = queries.shape[0]
    devices = n_seq * n_kv
    vmem = pl.BlockSpec(memory_space=pltpu.VMEM)
    smem = pl.BlockSpec(memory_space=pltpu.SMEM)
    hbm = pl.BlockSpec(memory_space=pltpu.HBM)
    params = pltpu.CompilerParams(vmem_limit_bytes=32 * 1024 * 1024)
    wide = GROUPS * rows
    group_shape = jax.ShapeDtypeStruct((KV_HEADS * HEAD_DIM, wide), jnp.float32)
    deep = 2 * KV_HEADS * rows + DOC_ROWS
    own = pl.pallas_call(
        pack_kernel,
        out_shape=jax.ShapeDtypeStruct((deep, HEAD_DIM), jnp.bfloat16),
        in_specs=[hbm] * 3,
        out_specs=hbm,
        scratch_shapes=[
            pltpu.VMEM((1, rows), jnp.int32),
            pltpu.VMEM((DOC_ROWS, rows), jnp.bfloat16),
            pltpu.SemaphoreType.DMA((2 * KV_HEADS + 2,)),
        ],
        compiler_params=pltpu.CompilerParams(vmem_limit_bytes=60 * 1024 * 1024),
        cost_estimate=pl.CostEstimate(
            flops=0, bytes_accessed=4 * deep * HEAD_DIM, transcendentals=0
        ),
    )(keys, values, doc_ids.reshape(1, rows))

    def before(j):
        pairs = [(b - j, b) for b in range(j, devices)]
        return lax.ppermute(own, ("seq", "kv"), pairs)

    one, two = before(1), before(2)
    summed, stats, gains = pl.pallas_call(
        own_kernel,
        out_shape=[
            group_shape,
            jax.ShapeDtypeStruct((4 * KV_HEADS, wide), jnp.float32),
            jax.ShapeDtypeStruct((HEADS * HEAD_DIM, rows), jnp.float32),
        ],
        in_specs=[smem, vmem, vmem, vmem],
        out_specs=[vmem] * 3,
        compiler_params=params,
        cost_estimate=pl.CostEstimate(
            flops=4 * HEADS * HEAD_DIM * rows * rows,
            bytes_accessed=4 * 1024 * 1024,
            transcendentals=HEADS * rows * rows,
        ),
    )(beta, queries, own, lin_gain.reshape(HEADS, HEAD_DIM))
    state, ready = pl.pallas_call(
        middle_kernel,
        out_shape=[
            jax.ShapeDtypeStruct((KV_HEADS * HEAD_DIM, HEAD_DIM), jnp.float32),
            group_shape,
        ],
        in_specs=[vmem] * 6,
        out_specs=[vmem] * 2,
        compiler_params=params,
        cost_estimate=pl.CostEstimate(
            flops=4 * HEADS * HEAD_DIM * HEAD_DIM * rows,
            bytes_accessed=4 * 1024 * 1024,
            transcendentals=0,
        ),
    )(queries, own, two, summed, stats, gains)
    return pl.pallas_call(
        join_kernel,
        out_shape=jax.ShapeDtypeStruct((rows, HEADS * HEAD_DIM), jnp.float32),
        in_specs=[vmem] * 8,
        out_specs=hbm,
        scratch_shapes=[
            pltpu.VMEM((rows, HEADS * HEAD_DIM), jnp.float32),
            pltpu.SemaphoreType.DMA((KV_HEADS,)),
        ],
        compiler_params=params,
    )(queries, own, one, summed, stats, gains, state, ready)


def carried_in(part, axis, combine, identity):
    place = lax.axis_index(axis)
    gathered = jax.tree.map(lambda a: lax.all_gather(a, axis), part)
    state = jax.tree.map(lambda a, e: jnp.zeros_like(a) + jnp.asarray(e, a.dtype), part, identity)

    def one(step, state):
        return combine(
            state, jax.tree.map(lambda a: lax.dynamic_index_in_dim(a, step, 0, False), gathered)
        )

    return lax.fori_loop(0, place, one, state)


def join_states(earlier, later):
    state_early, first_early, last_early = earlier
    state_late, first_late, last_late = later
    empty_late = first_late < 0
    joined = (first_late == last_late) & (last_early == first_late)
    merged = state_late + jnp.where(joined, state_early, jnp.zeros_like(state_early))
    combined = jnp.where(empty_late, state_early, merged)
    first_doc = jnp.where(first_early < 0, first_late, first_early)
    last_doc = jnp.where(empty_late, last_early, last_late)
    return (combined, first_doc, last_doc)


def tail_merge(one_side, other_side):
    state_one, first_one, last_one = one_side
    state_other, first_other, last_other = other_side
    top_doc = jnp.maximum(last_one, last_other)
    state_sum = jnp.where(last_one == top_doc, state_one, jnp.zeros_like(state_one))
    state_sum = state_sum + jnp.where(
        last_other == top_doc, state_other, jnp.zeros_like(state_other)
    )
    return (state_sum, jnp.minimum(first_one, first_other), top_doc)


def tail_state(key_rows, value_rows, doc_rows, target_doc):
    count = key_rows.shape[0]
    key_heads = key_rows.reshape(count, KV_HEADS, HEAD_DIM)
    value_heads = value_rows.reshape(count, KV_HEADS, HEAD_DIM)
    live = doc_rows == target_doc
    masked = jnp.where(live[:, None, None], key_heads, jnp.zeros_like(key_heads))
    return jnp.einsum("rgd,rge->gde", masked, value_heads, preferred_element_type=jnp.float32)


def attend_block(
    carry, query_heads, query_pos, query_doc, key_rows, value_rows, key_doc, key_start
):
    running_max, running_sum, accumulated = carry
    key_count = key_rows.shape[0]
    key_heads = key_rows.reshape(key_count, KV_HEADS, HEAD_DIM)
    value_heads = value_rows.reshape(key_count, KV_HEADS, HEAD_DIM)
    scores = jnp.einsum(
        "rgqd,kgd->gqrk", query_heads, key_heads, preferred_element_type=jnp.float32
    )
    scores = scores / jnp.sqrt(jnp.float32(HEAD_DIM))
    key_pos = key_start + jnp.arange(key_count, dtype=jnp.int32)
    allowed = (key_pos[None, :] <= query_pos[:, None]) & (key_doc[None, :] == query_doc[:, None])
    masked = jnp.where(allowed, scores, jnp.float32(-1e30))
    new_max = jnp.maximum(running_max, jnp.max(masked, axis=-1))
    factor = jnp.exp(running_max - new_max)
    weights = jnp.where(allowed, jnp.exp(masked - new_max[..., None]), jnp.float32(0.0))
    new_sum = running_sum * factor + jnp.sum(weights, axis=-1)
    product = jnp.einsum(
        "gqrk,kge->gqre",
        weights.astype(jnp.bfloat16),
        value_heads,
        preferred_element_type=jnp.float32,
    )
    new_accum = accumulated * factor[..., None] + product
    return (new_max, new_sum, new_accum)


def far_device(queries, keys, values, doc_ids, beta, lin_gain):
    row_count = queries.shape[0]
    groups = HEADS // KV_HEADS
    query_heads = queries.reshape(row_count, KV_HEADS, groups, HEAD_DIM)
    position = lax.axis_index("kv") * row_count
    query_pos = position + jnp.arange(row_count, dtype=jnp.int32)
    last_query = position + row_count - 1
    initial = (
        jnp.full((KV_HEADS, groups, row_count), -1e30, jnp.float32),
        jnp.zeros((KV_HEADS, groups, row_count), jnp.float32),
        jnp.zeros((KV_HEADS, groups, row_count, HEAD_DIM), jnp.float32),
    )
    empty_tail = (
        jnp.zeros((KV_HEADS, HEAD_DIM, HEAD_DIM), jnp.float32),
        jnp.array(2**30, jnp.int32),
        jnp.array(-1, jnp.int32),
    )
    key_piece = lax.all_gather(keys, "kv", axis=0, tiled=True)
    value_piece = lax.all_gather(values, "kv", axis=0, tiled=True)
    doc_piece = lax.all_gather(doc_ids, "kv", axis=0, tiled=True)
    blocks = key_piece.shape[0] // row_count

    def one_block(state, item):
        soft_state, tail_now = state
        key_block, value_block, doc_block, number = item
        block_start = number * row_count
        soft_next = lax.cond(
            block_start <= last_query,
            lambda inner: attend_block(
                inner,
                query_heads,
                query_pos,
                doc_ids,
                key_block,
                value_block,
                doc_block,
                block_start,
            ),
            lambda inner: inner,
            soft_state,
        )
        block_tail = (
            tail_state(key_block, value_block, doc_block, doc_block[-1]),
            doc_block[0],
            doc_block[-1],
        )
        tail_now = tail_merge(tail_now, block_tail)
        return ((soft_next, tail_now), None)

    stacked = (
        key_piece.reshape(blocks, row_count, -1),
        value_piece.reshape(blocks, row_count, -1),
        doc_piece.reshape(blocks, row_count),
        jnp.arange(blocks, dtype=jnp.int32),
    )
    result, _ = lax.scan(one_block, (initial, empty_tail), stacked)
    running, segment_tail = result
    running_max, running_sum, accumulated = running
    soft_out = jnp.transpose(accumulated / running_sum[..., None], (2, 0, 1, 3))
    identity = (
        jnp.zeros((KV_HEADS, HEAD_DIM, HEAD_DIM), jnp.float32),
        jnp.array(-1, jnp.int32),
        jnp.array(-1, jnp.int32),
    )
    memory = carried_in(segment_tail, "seq", join_states, identity)
    memory_state, memory_first, memory_last = memory
    query_float = query_heads.astype(jnp.float32)
    recalled = jnp.einsum(
        "rgqd,gde->rgqe", query_float, memory_state, precision=lax.Precision.HIGHEST
    )
    recalled = jnp.where((doc_ids == memory_last)[:, None, None, None], recalled, jnp.float32(0.0))
    mean_square = jnp.mean(recalled * recalled, axis=-1, keepdims=True)
    normed = (
        recalled * lax.rsqrt(mean_square + 1e-06) * lin_gain.reshape(KV_HEADS, groups, HEAD_DIM)
    )
    mixing = jax.nn.sigmoid(beta).reshape(KV_HEADS, groups)[None, :, :, None]
    mixed = mixing * normed + (1.0 - mixing) * soft_out
    return mixed.reshape(row_count, HEADS * HEAD_DIM).astype(jnp.float32)


def solution(mesh):
    n_seq, n_kv = mesh.shape["seq"], mesh.shape["kv"]
    in_specs = (
        P(("dp", "seq", "kv"), None),
        P(("dp", "seq", "kv"), None),
        P(("dp", "seq", "kv"), None),
        P(("dp", "seq", "kv")),
        P(),
        P(),
    )
    out_specs = P(("dp", "seq", "kv"), None)
    if n_kv == 2 and n_seq * n_kv <= 2 * LONGEST:
        on_device = functools.partial(near_device, n_seq, n_kv)
    else:
        on_device = far_device
    return jax.shard_map(
        on_device, mesh=mesh, in_specs=in_specs, out_specs=out_specs, check_vma=False
    )
```

```python
import functools
import math

import jax
import jax.numpy as jnp
from jax import lax
from jax.experimental import pallas as pl
from jax.experimental.pallas import tpu as pltpu
from jax.sharding import PartitionSpec as P

HEADS = 16
KV_HEADS = 4
HEAD_DIM = 128
GROUPS = HEADS // KV_HEADS
LONGEST = 4
SCALE = math.log2(math.e) / math.sqrt(HEAD_DIM)
LOWEST = -1e30
DOC_ROWS = 16

NT = (((1,), (1,)), ((), ()))
TN = (((0,), (0,)), ((), ()))


def dot(a, b, dims):
    return lax.dot_general(a, b, dims, preferred_element_type=jnp.float32)


def column(row):
    return jnp.transpose(jnp.broadcast_to(row, (HEAD_DIM, row.shape[1])))


def part_of(i, size):
    return slice(i * size, (i + 1) * size)


def group_queries(q_ref, g):
    heads = [q_ref[:, part_of(g * GROUPS + i, HEAD_DIM)] for i in range(GROUPS)]
    return jnp.concatenate(heads, axis=0)


def payload_keys(ref, g, rows):
    return ref[part_of(g, rows), :]


def payload_values(ref, g, rows):
    return ref[part_of(KV_HEADS + g, rows), :]


def payload_docs(ref, rows):
    start = 2 * KV_HEADS * rows
    return ref[start : start + DOC_ROWS, :].astype(jnp.float32)[0:1, :]


def pack_kernel(key_ref, value_ref, doc_ref, out_ref, doc_scratch, sems):
    rows = key_ref.shape[0]
    doc_copy = pltpu.make_async_copy(doc_ref, doc_scratch, sems.at[2 * KV_HEADS])
    doc_copy.start()
    copies = []
    for g in range(2 * KV_HEADS):
        source = key_ref if g < KV_HEADS else value_ref
        copy = pltpu.make_async_copy(
            source.at[:, part_of(g % KV_HEADS, HEAD_DIM)],
            out_ref.at[part_of(g, rows), :],
            sems.at[g],
        )
        copy.start()
        copies.append(copy)
    doc_copy.wait()
    docs = jnp.broadcast_to(doc_scratch[...].astype(jnp.float32), (DOC_ROWS, rows))
    start = 2 * KV_HEADS * rows
    out_ref[start : start + DOC_ROWS, :] = docs.astype(jnp.bfloat16)
    for copy in copies:
        copy.wait()


def own_kernel(beta_ref, q_ref, own_ref, gain_ref, summed_ref, stats_ref, gain_out_ref):
    rows = q_ref.shape[0]
    docs = payload_docs(own_ref, rows)
    place = lax.broadcasted_iota(jnp.int32, (rows, rows), 0)
    row = lax.broadcasted_iota(jnp.int32, (rows, rows), 1)
    allowed = (place <= row) & (column(docs) == docs)
    bias = jnp.where(allowed, 0.0, LOWEST)
    for g in range(KV_HEADS):
        scores = dot(payload_keys(own_ref, g, rows), group_queries(q_ref, g), NT)
        tops, totals, weights, rest = [], [], [], []
        for i in range(GROUPS):
            h = g * GROUPS + i
            masked = scores[:, part_of(i, rows)] * SCALE + bias
            top = jnp.max(masked, axis=0, keepdims=True)
            weight = jnp.exp2(masked - top)
            tops.append(top)
            totals.append(jnp.sum(weight, axis=0, keepdims=True))
            weights.append(weight.astype(jnp.bfloat16))
            share = 1.0 / (1.0 + jnp.exp(-jnp.full((1, HEAD_DIM), beta_ref[h], jnp.float32)))
            rest.append(jnp.broadcast_to((1.0 - share)[:, 0:1], (1, rows)))
            gain_out_ref[part_of(h, HEAD_DIM), :] = column(gain_ref[h : h + 1, :] * share)
        summed_ref[part_of(g, HEAD_DIM), :] = dot(
            payload_values(own_ref, g, rows), jnp.concatenate(weights, axis=1), TN
        )
        stats_ref[g : g + 1, :] = jnp.concatenate(tops, axis=1)
        stats_ref[KV_HEADS + g : KV_HEADS + g + 1, :] = jnp.concatenate(totals, axis=1)
        stats_ref[2 * KV_HEADS + g : 2 * KV_HEADS + g + 1, :] = jnp.concatenate(rest, axis=1)


def first_document(own_ref, rows):
    own = payload_docs(own_ref, rows)
    first = jnp.broadcast_to(own[:, 0:1], (1, rows))
    return first, own == first


def tail(ref, first, rows):
    others = jnp.where(payload_docs(ref, rows) == first, 0.0, 1.0)
    count = jnp.sum(others, axis=1, keepdims=True)
    place = lax.broadcasted_iota(jnp.int32, (rows, HEAD_DIM), 0).astype(jnp.float32)
    return place >= count


def block_state(ref, live, g, rows):
    keys = payload_keys(ref, g, rows).astype(jnp.float32)
    keys = jnp.where(live, keys, 0.0).astype(jnp.bfloat16)
    return dot(payload_values(ref, g, rows), keys, TN)


def memory_read(state, q_ref, g, gain_ref, reads):
    rows = q_ref.shape[0]
    q = group_queries(q_ref, g)
    high = state.astype(jnp.bfloat16)
    low = (state - high.astype(jnp.float32)).astype(jnp.bfloat16)
    recalled = dot(high, q, NT) + dot(low, q, NT)
    heads = []
    for i in range(GROUPS):
        read = recalled[:, part_of(i, rows)]
        square = jnp.sum(read * read, axis=0, keepdims=True) * (1.0 / HEAD_DIM)
        read = read * (lax.rsqrt(square + 1e-06) * reads)
        heads.append(read * gain_ref[part_of(g * GROUPS + i, HEAD_DIM), :])
    return heads


def middle_kernel(
    q_ref, own_ref, two_ref, summed_ref, stats_ref, gain_ref, state_ref, ready_ref
):
    rows = q_ref.shape[0]
    part = lax.axis_index("kv")
    first, same = first_document(own_ref, rows)
    reads = jnp.where(same, 1.0, 0.0)
    live = tail(two_ref, first, rows)
    for g in range(KV_HEADS):
        state_ref[part_of(g, HEAD_DIM), :] = block_state(two_ref, live, g, rows)

    @pl.when(part == 0)
    def _():
        for g in range(KV_HEADS):
            rest = stats_ref[2 * KV_HEADS + g : 2 * KV_HEADS + g + 1, :]
            scaled = rest / stats_ref[KV_HEADS + g : KV_HEADS + g + 1, :]
            group = part_of(g, HEAD_DIM)
            ready_ref[group, :] = summed_ref[group, :] * scaled

    @pl.when(part == 1)
    def _():
        for g in range(KV_HEADS):
            state = state_ref[part_of(g, HEAD_DIM), :]
            heads = memory_read(state, q_ref, g, gain_ref, reads)
            ready_ref[part_of(g, HEAD_DIM), :] = jnp.concatenate(heads, axis=1)


def join_kernel(
    q_ref, own_ref, one_ref, summed_ref, stats_ref, gain_ref, state_ref, ready_ref,
    out_ref, held, sems,
):
    rows = q_ref.shape[0]
    part = lax.axis_index("kv")
    first, same = first_document(own_ref, rows)
    live = tail(one_ref, first, rows)

    def copy(g):
        wide = part_of(g, GROUPS * HEAD_DIM)
        return pltpu.make_async_copy(held.at[:, wide], out_ref.at[:, wide], sems.at[g])

    @pl.when(part == 0)
    def _():
        reads = jnp.where(same, 1.0, 0.0)
        for g in range(KV_HEADS):
            state = state_ref[part_of(g, HEAD_DIM), :] + block_state(one_ref, live, g, rows)
            heads = memory_read(state, q_ref, g, gain_ref, reads)
            for i in range(GROUPS):
                mixed = heads[i] + ready_ref[part_of(g, HEAD_DIM), part_of(i, rows)]
                held[:, part_of(g * GROUPS + i, HEAD_DIM)] = jnp.transpose(mixed)
            copy(g).start()

    @pl.when(part == 1)
    def _():
        bias = jnp.where(live & same, 0.0, LOWEST)
        for g in range(KV_HEADS):
            scores = dot(payload_keys(one_ref, g, rows), group_queries(q_ref, g), NT)
            weights, factors, scales = [], [], []
            for i in range(GROUPS):
                cut = part_of(i, rows)
                masked = scores[:, cut] * SCALE + bias
                top_own = stats_ref[g : g + 1, cut]
                top = jnp.maximum(jnp.max(masked, axis=0, keepdims=True), top_own)
                weight = jnp.exp2(masked - top)
                factor = jnp.exp2(top_own - top)
                total = stats_ref[KV_HEADS + g : KV_HEADS + g + 1, cut] * factor
                total = total + jnp.sum(weight, axis=0, keepdims=True)
                factors.append(factor)
                scales.append(stats_ref[2 * KV_HEADS + g : 2 * KV_HEADS + g + 1, cut] / total)
                weights.append(weight.astype(jnp.bfloat16))
            added = dot(payload_values(one_ref, g, rows), jnp.concatenate(weights, axis=1), TN)
            for i in range(GROUPS):
                cut, group = part_of(i, rows), part_of(g, HEAD_DIM)
                summed = summed_ref[group, cut] * factors[i] + added[:, cut]
                mixed = ready_ref[group, cut] + summed * scales[i]
                held[:, part_of(g * GROUPS + i, HEAD_DIM)] = jnp.transpose(mixed)
            copy(g).start()

    for g in range(KV_HEADS):
        copy(g).wait()


def near_device(n_seq, n_kv, queries, keys, values, doc_ids, beta, lin_gain):
    rows = queries.shape[0]
    devices = n_seq * n_kv
    vmem = pl.BlockSpec(memory_space=pltpu.VMEM)
    smem = pl.BlockSpec(memory_space=pltpu.SMEM)
    hbm = pl.BlockSpec(memory_space=pltpu.HBM)
    in_hbm = functools.partial(pltpu.with_memory_space_constraint, memory_space=pltpu.HBM)
    params = pltpu.CompilerParams(vmem_limit_bytes=32 * 1024 * 1024)
    wide = GROUPS * rows
    group_shape = jax.ShapeDtypeStruct((KV_HEADS * HEAD_DIM, wide), jnp.float32)
    deep = 2 * KV_HEADS * rows + DOC_ROWS
    own = pl.pallas_call(
        pack_kernel,
        out_shape=jax.ShapeDtypeStruct((deep, HEAD_DIM), jnp.bfloat16),
        in_specs=[hbm] * 3,
        out_specs=vmem,
        scratch_shapes=[
            pltpu.VMEM((1, rows), jnp.int32),
            pltpu.SemaphoreType.DMA((2 * KV_HEADS + 1,)),
        ],
        compiler_params=params,
        cost_estimate=pl.CostEstimate(
            flops=0, bytes_accessed=4 * deep * HEAD_DIM, transcendentals=0
        ),
    )(in_hbm(keys), in_hbm(values), in_hbm(doc_ids.reshape(1, rows)))

    def before(j):
        pairs = [(b - j, b) for b in range(j, devices)]
        return lax.ppermute(own, ("seq", "kv"), pairs)

    one, two = before(1), before(2)
    summed, stats, gains = pl.pallas_call(
        own_kernel,
        out_shape=[
            group_shape,
            jax.ShapeDtypeStruct((4 * KV_HEADS, wide), jnp.float32),
            jax.ShapeDtypeStruct((HEADS * HEAD_DIM, rows), jnp.float32),
        ],
        in_specs=[smem, vmem, vmem, vmem],
        out_specs=[vmem] * 3,
        compiler_params=params,
        cost_estimate=pl.CostEstimate(
            flops=4 * HEADS * HEAD_DIM * rows * rows,
            bytes_accessed=4 * 1024 * 1024,
            transcendentals=HEADS * rows * rows,
        ),
    )(beta, queries, own, lin_gain.reshape(HEADS, HEAD_DIM))
    state, ready = pl.pallas_call(
        middle_kernel,
        out_shape=[
            jax.ShapeDtypeStruct((KV_HEADS * HEAD_DIM, HEAD_DIM), jnp.float32),
            group_shape,
        ],
        in_specs=[vmem] * 6,
        out_specs=[vmem] * 2,
        compiler_params=params,
        cost_estimate=pl.CostEstimate(
            flops=4 * HEADS * HEAD_DIM * HEAD_DIM * rows,
            bytes_accessed=4 * 1024 * 1024,
            transcendentals=0,
        ),
    )(queries, own, two, summed, stats, gains)
    return pl.pallas_call(
        join_kernel,
        out_shape=jax.ShapeDtypeStruct((rows, HEADS * HEAD_DIM), jnp.float32),
        in_specs=[vmem] * 8,
        out_specs=hbm,
        scratch_shapes=[
            pltpu.VMEM((rows, HEADS * HEAD_DIM), jnp.float32),
            pltpu.SemaphoreType.DMA((KV_HEADS,)),
        ],
        compiler_params=params,
    )(queries, own, one, summed, stats, gains, state, ready)


def carried_in(part, axis, combine, identity):
    place = lax.axis_index(axis)
    gathered = jax.tree.map(lambda a: lax.all_gather(a, axis), part)
    state = jax.tree.map(lambda a, e: jnp.zeros_like(a) + jnp.asarray(e, a.dtype), part, identity)

    def one(step, state):
        return combine(
            state, jax.tree.map(lambda a: lax.dynamic_index_in_dim(a, step, 0, False), gathered)
        )

    return lax.fori_loop(0, place, one, state)


def join_states(earlier, later):
    state_early, first_early, last_early = earlier
    state_late, first_late, last_late = later
    empty_late = first_late < 0
    joined = (first_late == last_late) & (last_early == first_late)
    merged = state_late + jnp.where(joined, state_early, jnp.zeros_like(state_early))
    combined = jnp.where(empty_late, state_early, merged)
    first_doc = jnp.where(first_early < 0, first_late, first_early)
    last_doc = jnp.where(empty_late, last_early, last_late)
    return (combined, first_doc, last_doc)


def tail_merge(one_side, other_side):
    state_one, first_one, last_one = one_side
    state_other, first_other, last_other = other_side
    top_doc = jnp.maximum(last_one, last_other)
    state_sum = jnp.where(last_one == top_doc, state_one, jnp.zeros_like(state_one))
    state_sum = state_sum + jnp.where(
        last_other == top_doc, state_other, jnp.zeros_like(state_other)
    )
    return (state_sum, jnp.minimum(first_one, first_other), top_doc)


def tail_state(key_rows, value_rows, doc_rows, target_doc):
    count = key_rows.shape[0]
    key_heads = key_rows.reshape(count, KV_HEADS, HEAD_DIM)
    value_heads = value_rows.reshape(count, KV_HEADS, HEAD_DIM)
    live = doc_rows == target_doc
    masked = jnp.where(live[:, None, None], key_heads, jnp.zeros_like(key_heads))
    return jnp.einsum("rgd,rge->gde", masked, value_heads, preferred_element_type=jnp.float32)


def attend_block(
    carry, query_heads, query_pos, query_doc, key_rows, value_rows, key_doc, key_start
):
    running_max, running_sum, accumulated = carry
    key_count = key_rows.shape[0]
    key_heads = key_rows.reshape(key_count, KV_HEADS, HEAD_DIM)
    value_heads = value_rows.reshape(key_count, KV_HEADS, HEAD_DIM)
    scores = jnp.einsum(
        "rgqd,kgd->gqrk", query_heads, key_heads, preferred_element_type=jnp.float32
    )
    scores = scores / jnp.sqrt(jnp.float32(HEAD_DIM))
    key_pos = key_start + jnp.arange(key_count, dtype=jnp.int32)
    allowed = (key_pos[None, :] <= query_pos[:, None]) & (key_doc[None, :] == query_doc[:, None])
    masked = jnp.where(allowed, scores, jnp.float32(-1e30))
    new_max = jnp.maximum(running_max, jnp.max(masked, axis=-1))
    factor = jnp.exp(running_max - new_max)
    weights = jnp.where(allowed, jnp.exp(masked - new_max[..., None]), jnp.float32(0.0))
    new_sum = running_sum * factor + jnp.sum(weights, axis=-1)
    product = jnp.einsum(
        "gqrk,kge->gqre",
        weights.astype(jnp.bfloat16),
        value_heads,
        preferred_element_type=jnp.float32,
    )
    new_accum = accumulated * factor[..., None] + product
    return (new_max, new_sum, new_accum)


def far_device(queries, keys, values, doc_ids, beta, lin_gain):
    row_count = queries.shape[0]
    groups = HEADS // KV_HEADS
    query_heads = queries.reshape(row_count, KV_HEADS, groups, HEAD_DIM)
    position = lax.axis_index("kv") * row_count
    query_pos = position + jnp.arange(row_count, dtype=jnp.int32)
    last_query = position + row_count - 1
    initial = (
        jnp.full((KV_HEADS, groups, row_count), -1e30, jnp.float32),
        jnp.zeros((KV_HEADS, groups, row_count), jnp.float32),
        jnp.zeros((KV_HEADS, groups, row_count, HEAD_DIM), jnp.float32),
    )
    empty_tail = (
        jnp.zeros((KV_HEADS, HEAD_DIM, HEAD_DIM), jnp.float32),
        jnp.array(2**30, jnp.int32),
        jnp.array(-1, jnp.int32),
    )
    key_piece = lax.all_gather(keys, "kv", axis=0, tiled=True)
    value_piece = lax.all_gather(values, "kv", axis=0, tiled=True)
    doc_piece = lax.all_gather(doc_ids, "kv", axis=0, tiled=True)
    blocks = key_piece.shape[0] // row_count

    def one_block(state, item):
        soft_state, tail_now = state
        key_block, value_block, doc_block, number = item
        block_start = number * row_count
        soft_next = lax.cond(
            block_start <= last_query,
            lambda inner: attend_block(
                inner,
                query_heads,
                query_pos,
                doc_ids,
                key_block,
                value_block,
                doc_block,
                block_start,
            ),
            lambda inner: inner,
            soft_state,
        )
        block_tail = (
            tail_state(key_block, value_block, doc_block, doc_block[-1]),
            doc_block[0],
            doc_block[-1],
        )
        tail_now = tail_merge(tail_now, block_tail)
        return ((soft_next, tail_now), None)

    stacked = (
        key_piece.reshape(blocks, row_count, -1),
        value_piece.reshape(blocks, row_count, -1),
        doc_piece.reshape(blocks, row_count),
        jnp.arange(blocks, dtype=jnp.int32),
    )
    result, _ = lax.scan(one_block, (initial, empty_tail), stacked)
    running, segment_tail = result
    running_max, running_sum, accumulated = running
    soft_out = jnp.transpose(accumulated / running_sum[..., None], (2, 0, 1, 3))
    identity = (
        jnp.zeros((KV_HEADS, HEAD_DIM, HEAD_DIM), jnp.float32),
        jnp.array(-1, jnp.int32),
        jnp.array(-1, jnp.int32),
    )
    memory = carried_in(segment_tail, "seq", join_states, identity)
    memory_state, memory_first, memory_last = memory
    query_float = query_heads.astype(jnp.float32)
    recalled = jnp.einsum(
        "rgqd,gde->rgqe", query_float, memory_state, precision=lax.Precision.HIGHEST
    )
    recalled = jnp.where((doc_ids == memory_last)[:, None, None, None], recalled, jnp.float32(0.0))
    mean_square = jnp.mean(recalled * recalled, axis=-1, keepdims=True)
    normed = (
        recalled * lax.rsqrt(mean_square + 1e-06) * lin_gain.reshape(KV_HEADS, groups, HEAD_DIM)
    )
    mixing = jax.nn.sigmoid(beta).reshape(KV_HEADS, groups)[None, :, :, None]
    mixed = mixing * normed + (1.0 - mixing) * soft_out
    return mixed.reshape(row_count, HEADS * HEAD_DIM).astype(jnp.float32)


def solution(mesh):
    n_seq, n_kv = mesh.shape["seq"], mesh.shape["kv"]
    in_specs = (
        P(("dp", "seq", "kv"), None),
        P(("dp", "seq", "kv"), None),
        P(("dp", "seq", "kv"), None),
        P(("dp", "seq", "kv")),
        P(),
        P(),
    )
    out_specs = P(("dp", "seq", "kv"), None)
    if n_kv == 2 and n_seq * n_kv <= 2 * LONGEST:
        on_device = functools.partial(near_device, n_seq, n_kv)
    else:
        on_device = far_device
    return jax.shard_map(
        on_device, mesh=mesh, in_specs=in_specs, out_specs=out_specs, check_vma=False
    )
```

```python
import functools
import math

import jax
import jax.numpy as jnp
from jax import lax
from jax.experimental import pallas as pl
from jax.experimental.pallas import tpu as pltpu
from jax.sharding import PartitionSpec as P

HEADS = 16
KV_HEADS = 4
HEAD_DIM = 128
GROUPS = HEADS // KV_HEADS
LONGEST = 4
SCALE = math.log2(math.e) / math.sqrt(HEAD_DIM)
LOWEST = -1e30
DOC_ROWS = 16

NT = (((1,), (1,)), ((), ()))
TN = (((0,), (0,)), ((), ()))


def dot(a, b, dims):
    return lax.dot_general(a, b, dims, preferred_element_type=jnp.float32)


def column(row):
    return jnp.transpose(jnp.broadcast_to(row, (HEAD_DIM, row.shape[1])))


def part_of(i, size):
    return slice(i * size, (i + 1) * size)


def group_queries(q_ref, g):
    heads = [q_ref[:, part_of(g * GROUPS + i, HEAD_DIM)] for i in range(GROUPS)]
    return jnp.concatenate(heads, axis=0)


def payload_keys(ref, g, rows):
    return ref[part_of(g, rows), :]


def payload_values(ref, g, rows):
    return ref[part_of(KV_HEADS + g, rows), :]


def payload_docs(ref, rows):
    start = 2 * KV_HEADS * rows
    return ref[start : start + DOC_ROWS, :].astype(jnp.float32)[0:1, :]


def pack_kernel(key_ref, value_ref, doc_ref, next_ref, own_ref, doc_scratch, sems):
    rows = key_ref.shape[0]
    doc_copy = pltpu.make_async_copy(doc_ref, doc_scratch, sems.at[0])
    doc_copy.start()
    copies = []
    for out_ref in (next_ref, own_ref):
        for g in range(2 * KV_HEADS):
            source = key_ref if g < KV_HEADS else value_ref
            copy = pltpu.make_async_copy(
                source.at[:, part_of(g % KV_HEADS, HEAD_DIM)],
                out_ref.at[part_of(g, rows), :],
                sems.at[1 + len(copies)],
            )
            copy.start()
            copies.append(copy)
    doc_copy.wait()
    start = 2 * KV_HEADS * rows
    for out_ref in (next_ref, own_ref):
        count = out_ref.shape[0] - start
        docs = jnp.broadcast_to(doc_scratch[...].astype(jnp.float32), (count, rows))
        out_ref[start:, :] = docs.astype(jnp.bfloat16)
    for copy in copies:
        copy.wait()


def own_kernel(beta_ref, q_ref, own_ref, gain_ref, summed_ref, stats_ref, gain_out_ref):
    rows = q_ref.shape[0]
    docs = payload_docs(own_ref, rows)
    place = lax.broadcasted_iota(jnp.int32, (rows, rows), 0)
    row = lax.broadcasted_iota(jnp.int32, (rows, rows), 1)
    allowed = (place <= row) & (column(docs) == docs)
    bias = jnp.where(allowed, 0.0, LOWEST)
    for g in range(KV_HEADS):
        scores = dot(payload_keys(own_ref, g, rows), group_queries(q_ref, g), NT)
        tops, totals, weights, rest = [], [], [], []
        for i in range(GROUPS):
            h = g * GROUPS + i
            masked = scores[:, part_of(i, rows)] * SCALE + bias
            top = jnp.max(masked, axis=0, keepdims=True)
            weight = jnp.exp2(masked - top)
            tops.append(top)
            totals.append(jnp.sum(weight, axis=0, keepdims=True))
            weights.append(weight.astype(jnp.bfloat16))
            share = 1.0 / (1.0 + jnp.exp(-jnp.full((1, HEAD_DIM), beta_ref[h], jnp.float32)))
            rest.append(jnp.broadcast_to((1.0 - share)[:, 0:1], (1, rows)))
            gain_out_ref[part_of(h, HEAD_DIM), :] = column(gain_ref[h : h + 1, :] * share)
        summed_ref[part_of(g, HEAD_DIM), :] = dot(
            payload_values(own_ref, g, rows), jnp.concatenate(weights, axis=1), TN
        )
        stats_ref[g : g + 1, :] = jnp.concatenate(tops, axis=1)
        stats_ref[KV_HEADS + g : KV_HEADS + g + 1, :] = jnp.concatenate(totals, axis=1)
        stats_ref[2 * KV_HEADS + g : 2 * KV_HEADS + g + 1, :] = jnp.concatenate(rest, axis=1)


def first_document(own_ref, rows):
    own = payload_docs(own_ref, rows)
    first = jnp.broadcast_to(own[:, 0:1], (1, rows))
    return first, own == first


def tail(ref, first, rows):
    others = jnp.where(payload_docs(ref, rows) == first, 0.0, 1.0)
    count = jnp.sum(others, axis=1, keepdims=True)
    place = lax.broadcasted_iota(jnp.int32, (rows, HEAD_DIM), 0).astype(jnp.float32)
    return place >= count


def block_state(ref, live, g, rows):
    keys = payload_keys(ref, g, rows).astype(jnp.float32)
    keys = jnp.where(live, keys, 0.0).astype(jnp.bfloat16)
    return dot(payload_values(ref, g, rows), keys, TN)


def memory_read(state, q_ref, g, gain_ref, reads):
    rows = q_ref.shape[0]
    q = group_queries(q_ref, g)
    high = state.astype(jnp.bfloat16)
    low = (state - high.astype(jnp.float32)).astype(jnp.bfloat16)
    recalled = dot(high, q, NT) + dot(low, q, NT)
    heads = []
    for i in range(GROUPS):
        read = recalled[:, part_of(i, rows)]
        square = jnp.sum(read * read, axis=0, keepdims=True) * (1.0 / HEAD_DIM)
        read = read * (lax.rsqrt(square + 1e-06) * reads)
        heads.append(read * gain_ref[part_of(g * GROUPS + i, HEAD_DIM), :])
    return heads


def middle_kernel(
    q_ref, own_ref, two_ref, summed_ref, stats_ref, gain_ref, state_ref, ready_ref
):
    rows = q_ref.shape[0]
    part = lax.axis_index("kv")
    first, same = first_document(own_ref, rows)
    reads = jnp.where(same, 1.0, 0.0)
    live = tail(two_ref, first, rows)
    for g in range(KV_HEADS):
        state_ref[part_of(g, HEAD_DIM), :] = block_state(two_ref, live, g, rows)

    @pl.when(part == 0)
    def _():
        for g in range(KV_HEADS):
            rest = stats_ref[2 * KV_HEADS + g : 2 * KV_HEADS + g + 1, :]
            scaled = rest / stats_ref[KV_HEADS + g : KV_HEADS + g + 1, :]
            group = part_of(g, HEAD_DIM)
            ready_ref[group, :] = summed_ref[group, :] * scaled

    @pl.when(part == 1)
    def _():
        for g in range(KV_HEADS):
            state = state_ref[part_of(g, HEAD_DIM), :]
            heads = memory_read(state, q_ref, g, gain_ref, reads)
            ready_ref[part_of(g, HEAD_DIM), :] = jnp.concatenate(heads, axis=1)


def join_kernel(
    q_ref, own_ref, one_ref, summed_ref, stats_ref, gain_ref, state_ref, ready_ref,
    out_ref, held, sems,
):
    rows = q_ref.shape[0]
    part = lax.axis_index("kv")
    first, same = first_document(own_ref, rows)
    live = tail(one_ref, first, rows)

    def copy(g):
        wide = part_of(g, GROUPS * HEAD_DIM)
        return pltpu.make_async_copy(held.at[:, wide], out_ref.at[:, wide], sems.at[g])

    @pl.when(part == 0)
    def _():
        reads = jnp.where(same, 1.0, 0.0)
        for g in range(KV_HEADS):
            state = state_ref[part_of(g, HEAD_DIM), :] + block_state(one_ref, live, g, rows)
            heads = memory_read(state, q_ref, g, gain_ref, reads)
            for i in range(GROUPS):
                mixed = heads[i] + ready_ref[part_of(g, HEAD_DIM), part_of(i, rows)]
                held[:, part_of(g * GROUPS + i, HEAD_DIM)] = jnp.transpose(mixed)
            copy(g).start()

    @pl.when(part == 1)
    def _():
        bias = jnp.where(live & same, 0.0, LOWEST)
        for g in range(KV_HEADS):
            scores = dot(payload_keys(one_ref, g, rows), group_queries(q_ref, g), NT)
            weights, factors, scales = [], [], []
            for i in range(GROUPS):
                cut = part_of(i, rows)
                masked = scores[:, cut] * SCALE + bias
                top_own = stats_ref[g : g + 1, cut]
                top = jnp.maximum(jnp.max(masked, axis=0, keepdims=True), top_own)
                weight = jnp.exp2(masked - top)
                factor = jnp.exp2(top_own - top)
                total = stats_ref[KV_HEADS + g : KV_HEADS + g + 1, cut] * factor
                total = total + jnp.sum(weight, axis=0, keepdims=True)
                factors.append(factor)
                scales.append(stats_ref[2 * KV_HEADS + g : 2 * KV_HEADS + g + 1, cut] / total)
                weights.append(weight.astype(jnp.bfloat16))
            added = dot(payload_values(one_ref, g, rows), jnp.concatenate(weights, axis=1), TN)
            for i in range(GROUPS):
                cut, group = part_of(i, rows), part_of(g, HEAD_DIM)
                summed = summed_ref[group, cut] * factors[i] + added[:, cut]
                mixed = ready_ref[group, cut] + summed * scales[i]
                held[:, part_of(g * GROUPS + i, HEAD_DIM)] = jnp.transpose(mixed)
            copy(g).start()

    for g in range(KV_HEADS):
        copy(g).wait()


def near_device(n_seq, n_kv, queries, keys, values, doc_ids, beta, lin_gain):
    rows = queries.shape[0]
    devices = n_seq * n_kv
    vmem = pl.BlockSpec(memory_space=pltpu.VMEM)
    smem = pl.BlockSpec(memory_space=pltpu.SMEM)
    hbm = pl.BlockSpec(memory_space=pltpu.HBM)
    in_hbm = functools.partial(pltpu.with_memory_space_constraint, memory_space=pltpu.HBM)
    params = pltpu.CompilerParams(vmem_limit_bytes=32 * 1024 * 1024)
    wide = GROUPS * rows
    group_shape = jax.ShapeDtypeStruct((KV_HEADS * HEAD_DIM, wide), jnp.float32)
    deep = 2 * KV_HEADS * rows + DOC_ROWS
    ahead, own = pl.pallas_call(
        pack_kernel,
        out_shape=[
            jax.ShapeDtypeStruct((deep + DOC_ROWS, HEAD_DIM), jnp.bfloat16),
            jax.ShapeDtypeStruct((deep, HEAD_DIM), jnp.bfloat16),
        ],
        in_specs=[hbm] * 3,
        out_specs=[vmem] * 2,
        scratch_shapes=[
            pltpu.VMEM((1, rows), jnp.int32),
            pltpu.SemaphoreType.DMA((4 * KV_HEADS + 1,)),
        ],
        compiler_params=params,
        cost_estimate=pl.CostEstimate(
            flops=0, bytes_accessed=4 * deep * HEAD_DIM, transcendentals=0
        ),
    )(in_hbm(keys), in_hbm(values), in_hbm(doc_ids.reshape(1, rows)))

    def before(j, payload):
        pairs = [(b - j, b) for b in range(j, devices)]
        return lax.ppermute(payload, ("seq", "kv"), pairs)

    one, two = before(1, ahead), before(2, own)
    summed, stats, gains = pl.pallas_call(
        own_kernel,
        out_shape=[
            group_shape,
            jax.ShapeDtypeStruct((4 * KV_HEADS, wide), jnp.float32),
            jax.ShapeDtypeStruct((HEADS * HEAD_DIM, rows), jnp.float32),
        ],
        in_specs=[smem, vmem, vmem, vmem],
        out_specs=[vmem] * 3,
        compiler_params=params,
        cost_estimate=pl.CostEstimate(
            flops=4 * HEADS * HEAD_DIM * rows * rows,
            bytes_accessed=4 * 1024 * 1024,
            transcendentals=HEADS * rows * rows,
        ),
    )(beta, queries, own, lin_gain.reshape(HEADS, HEAD_DIM))
    state, ready = pl.pallas_call(
        middle_kernel,
        out_shape=[
            jax.ShapeDtypeStruct((KV_HEADS * HEAD_DIM, HEAD_DIM), jnp.float32),
            group_shape,
        ],
        in_specs=[vmem] * 6,
        out_specs=[vmem] * 2,
        compiler_params=params,
    )(queries, own, two, summed, stats, gains)
    return pl.pallas_call(
        join_kernel,
        out_shape=jax.ShapeDtypeStruct((rows, HEADS * HEAD_DIM), jnp.float32),
        in_specs=[vmem] * 8,
        out_specs=hbm,
        scratch_shapes=[
            pltpu.VMEM((rows, HEADS * HEAD_DIM), jnp.float32),
            pltpu.SemaphoreType.DMA((KV_HEADS,)),
        ],
        compiler_params=params,
    )(queries, own, one, summed, stats, gains, state, ready)


def carried_in(part, axis, combine, identity):
    place = lax.axis_index(axis)
    gathered = jax.tree.map(lambda a: lax.all_gather(a, axis), part)
    state = jax.tree.map(lambda a, e: jnp.zeros_like(a) + jnp.asarray(e, a.dtype), part, identity)

    def one(step, state):
        return combine(
            state, jax.tree.map(lambda a: lax.dynamic_index_in_dim(a, step, 0, False), gathered)
        )

    return lax.fori_loop(0, place, one, state)


def join_states(earlier, later):
    state_early, first_early, last_early = earlier
    state_late, first_late, last_late = later
    empty_late = first_late < 0
    joined = (first_late == last_late) & (last_early == first_late)
    merged = state_late + jnp.where(joined, state_early, jnp.zeros_like(state_early))
    combined = jnp.where(empty_late, state_early, merged)
    first_doc = jnp.where(first_early < 0, first_late, first_early)
    last_doc = jnp.where(empty_late, last_early, last_late)
    return (combined, first_doc, last_doc)


def tail_merge(one_side, other_side):
    state_one, first_one, last_one = one_side
    state_other, first_other, last_other = other_side
    top_doc = jnp.maximum(last_one, last_other)
    state_sum = jnp.where(last_one == top_doc, state_one, jnp.zeros_like(state_one))
    state_sum = state_sum + jnp.where(
        last_other == top_doc, state_other, jnp.zeros_like(state_other)
    )
    return (state_sum, jnp.minimum(first_one, first_other), top_doc)


def tail_state(key_rows, value_rows, doc_rows, target_doc):
    count = key_rows.shape[0]
    key_heads = key_rows.reshape(count, KV_HEADS, HEAD_DIM)
    value_heads = value_rows.reshape(count, KV_HEADS, HEAD_DIM)
    live = doc_rows == target_doc
    masked = jnp.where(live[:, None, None], key_heads, jnp.zeros_like(key_heads))
    return jnp.einsum("rgd,rge->gde", masked, value_heads, preferred_element_type=jnp.float32)


def attend_block(
    carry, query_heads, query_pos, query_doc, key_rows, value_rows, key_doc, key_start
):
    running_max, running_sum, accumulated = carry
    key_count = key_rows.shape[0]
    key_heads = key_rows.reshape(key_count, KV_HEADS, HEAD_DIM)
    value_heads = value_rows.reshape(key_count, KV_HEADS, HEAD_DIM)
    scores = jnp.einsum(
        "rgqd,kgd->gqrk", query_heads, key_heads, preferred_element_type=jnp.float32
    )
    scores = scores / jnp.sqrt(jnp.float32(HEAD_DIM))
    key_pos = key_start + jnp.arange(key_count, dtype=jnp.int32)
    allowed = (key_pos[None, :] <= query_pos[:, None]) & (key_doc[None, :] == query_doc[:, None])
    masked = jnp.where(allowed, scores, jnp.float32(-1e30))
    new_max = jnp.maximum(running_max, jnp.max(masked, axis=-1))
    factor = jnp.exp(running_max - new_max)
    weights = jnp.where(allowed, jnp.exp(masked - new_max[..., None]), jnp.float32(0.0))
    new_sum = running_sum * factor + jnp.sum(weights, axis=-1)
    product = jnp.einsum(
        "gqrk,kge->gqre",
        weights.astype(jnp.bfloat16),
        value_heads,
        preferred_element_type=jnp.float32,
    )
    new_accum = accumulated * factor[..., None] + product
    return (new_max, new_sum, new_accum)


def far_device(queries, keys, values, doc_ids, beta, lin_gain):
    row_count = queries.shape[0]
    groups = HEADS // KV_HEADS
    query_heads = queries.reshape(row_count, KV_HEADS, groups, HEAD_DIM)
    position = lax.axis_index("kv") * row_count
    query_pos = position + jnp.arange(row_count, dtype=jnp.int32)
    last_query = position + row_count - 1
    initial = (
        jnp.full((KV_HEADS, groups, row_count), -1e30, jnp.float32),
        jnp.zeros((KV_HEADS, groups, row_count), jnp.float32),
        jnp.zeros((KV_HEADS, groups, row_count, HEAD_DIM), jnp.float32),
    )
    empty_tail = (
        jnp.zeros((KV_HEADS, HEAD_DIM, HEAD_DIM), jnp.float32),
        jnp.array(2**30, jnp.int32),
        jnp.array(-1, jnp.int32),
    )
    key_piece = lax.all_gather(keys, "kv", axis=0, tiled=True)
    value_piece = lax.all_gather(values, "kv", axis=0, tiled=True)
    doc_piece = lax.all_gather(doc_ids, "kv", axis=0, tiled=True)
    blocks = key_piece.shape[0] // row_count

    def one_block(state, item):
        soft_state, tail_now = state
        key_block, value_block, doc_block, number = item
        block_start = number * row_count
        soft_next = lax.cond(
            block_start <= last_query,
            lambda inner: attend_block(
                inner,
                query_heads,
                query_pos,
                doc_ids,
                key_block,
                value_block,
                doc_block,
                block_start,
            ),
            lambda inner: inner,
            soft_state,
        )
        block_tail = (
            tail_state(key_block, value_block, doc_block, doc_block[-1]),
            doc_block[0],
            doc_block[-1],
        )
        tail_now = tail_merge(tail_now, block_tail)
        return ((soft_next, tail_now), None)

    stacked = (
        key_piece.reshape(blocks, row_count, -1),
        value_piece.reshape(blocks, row_count, -1),
        doc_piece.reshape(blocks, row_count),
        jnp.arange(blocks, dtype=jnp.int32),
    )
    result, _ = lax.scan(one_block, (initial, empty_tail), stacked)
    running, segment_tail = result
    running_max, running_sum, accumulated = running
    soft_out = jnp.transpose(accumulated / running_sum[..., None], (2, 0, 1, 3))
    identity = (
        jnp.zeros((KV_HEADS, HEAD_DIM, HEAD_DIM), jnp.float32),
        jnp.array(-1, jnp.int32),
        jnp.array(-1, jnp.int32),
    )
    memory = carried_in(segment_tail, "seq", join_states, identity)
    memory_state, memory_first, memory_last = memory
    query_float = query_heads.astype(jnp.float32)
    recalled = jnp.einsum(
        "rgqd,gde->rgqe", query_float, memory_state, precision=lax.Precision.HIGHEST
    )
    recalled = jnp.where((doc_ids == memory_last)[:, None, None, None], recalled, jnp.float32(0.0))
    mean_square = jnp.mean(recalled * recalled, axis=-1, keepdims=True)
    normed = (
        recalled * lax.rsqrt(mean_square + 1e-06) * lin_gain.reshape(KV_HEADS, groups, HEAD_DIM)
    )
    mixing = jax.nn.sigmoid(beta).reshape(KV_HEADS, groups)[None, :, :, None]
    mixed = mixing * normed + (1.0 - mixing) * soft_out
    return mixed.reshape(row_count, HEADS * HEAD_DIM).astype(jnp.float32)


def solution(mesh):
    n_seq, n_kv = mesh.shape["seq"], mesh.shape["kv"]
    in_specs = (
        P(("dp", "seq", "kv"), None),
        P(("dp", "seq", "kv"), None),
        P(("dp", "seq", "kv"), None),
        P(("dp", "seq", "kv")),
        P(),
        P(),
    )
    out_specs = P(("dp", "seq", "kv"), None)
    if n_kv == 2 and n_seq * n_kv <= 2 * LONGEST:
        on_device = functools.partial(near_device, n_seq, n_kv)
    else:
        on_device = far_device
    return jax.shard_map(
        on_device, mesh=mesh, in_specs=in_specs, out_specs=out_specs, check_vma=False
    )
```

```python
import functools
import math

import jax
import jax.numpy as jnp
from jax import lax
from jax.experimental import pallas as pl
from jax.experimental.pallas import tpu as pltpu
from jax.sharding import PartitionSpec as P

HEADS = 16
KV_HEADS = 4
HEAD_DIM = 128
GROUPS = HEADS // KV_HEADS
LONGEST = 4
SCALE = math.log2(math.e) / math.sqrt(HEAD_DIM)
LOWEST = -1e30
EXTRA = 16
STEPS = 14.0

NT = (((1,), (1,)), ((), ()))
TN = (((0,), (0,)), ((), ()))


def dot(a, b, dims):
    return lax.dot_general(a, b, dims, preferred_element_type=jnp.float32)


def column(row):
    return jnp.transpose(jnp.broadcast_to(row, (HEAD_DIM, row.shape[1])))


def part_of(i, size):
    return slice(i * size, (i + 1) * size)


def group_queries(q_ref, g):
    heads = [q_ref[:, part_of(g * GROUPS + i, HEAD_DIM)] for i in range(GROUPS)]
    return jnp.concatenate(heads, axis=0)


def share_of(beta_ref, h):
    return 1.0 / (1.0 + jnp.exp(-jnp.full((1, HEAD_DIM), beta_ref[h], jnp.float32)))


def scaled_gains(beta_ref, gain_ref, out_ref):
    for h in range(HEADS):
        scaled = gain_ref[h : h + 1, :] * share_of(beta_ref, h)
        out_ref[part_of(h, HEAD_DIM), :] = column(scaled)


def suffix(others):
    count = jnp.sum(others, axis=1, keepdims=True)
    shape = (others.shape[1], HEAD_DIM)
    return lax.broadcasted_iota(jnp.int32, shape, 0).astype(jnp.float32) >= count


def first_document(docs):
    first = jnp.broadcast_to(docs[:, 0:1], docs.shape)
    return first, docs == first


def load_block(key_ref, value_ref, doc_ref, out_ref, doc_scratch, sems):
    rows = key_ref.shape[0]
    doc_copy = pltpu.make_async_copy(doc_ref, doc_scratch, sems.at[0])
    doc_copy.start()
    copies = []
    for g in range(2 * KV_HEADS):
        source = key_ref if g < KV_HEADS else value_ref
        copy = pltpu.make_async_copy(
            source.at[:, part_of(g % KV_HEADS, HEAD_DIM)],
            out_ref.at[part_of(g, rows), :],
            sems.at[1 + g],
        )
        copy.start()
        copies.append(copy)
    doc_copy.wait()
    docs = jnp.broadcast_to(doc_scratch[...].astype(jnp.float32), (EXTRA, rows))
    start = 2 * KV_HEADS * rows
    out_ref[start : start + EXTRA, :] = docs.astype(jnp.bfloat16)
    for copy in copies:
        copy.wait()


def block_keys(ref, g):
    return ref[part_of(g, HEAD_DIM), :]


def block_values(ref, g):
    return ref[part_of(KV_HEADS + g, HEAD_DIM), :]


def block_docs(ref):
    start = 2 * KV_HEADS * HEAD_DIM
    return ref[start : start + EXTRA, :].astype(jnp.float32)[0:1, :]


def pack_kernel(key_ref, value_ref, doc_ref, out_ref, doc_scratch, sems):
    @pl.when(lax.axis_index("kv") == 0)
    def _():
        load_block(key_ref, value_ref, doc_ref, out_ref, doc_scratch, sems)


def attend_own(q_ref, block_ref, g, bias):
    rows = q_ref.shape[0]
    scores = dot(block_keys(block_ref, g), group_queries(q_ref, g), NT)
    tops, totals, weights = [], [], []
    for i in range(GROUPS):
        masked = scores[:, part_of(i, rows)] * SCALE + bias
        top = jnp.max(masked, axis=0, keepdims=True)
        weight = jnp.exp2(masked - top)
        tops.append(top)
        totals.append(jnp.sum(weight, axis=0, keepdims=True))
        weights.append(weight.astype(jnp.bfloat16))
    summed = dot(block_values(block_ref, g), jnp.concatenate(weights, axis=1), TN)
    return summed, jnp.concatenate(tops, axis=1), jnp.concatenate(totals, axis=1)


def own_bias(docs):
    rows = docs.shape[1]
    place = lax.broadcasted_iota(jnp.int32, (rows, rows), 0)
    row = lax.broadcasted_iota(jnp.int32, (rows, rows), 1)
    return jnp.where((place <= row) & (column(docs) == docs), 0.0, LOWEST)


def block_state(block_ref, state_ref):
    docs = block_docs(block_ref)
    rows = docs.shape[1]
    last = jnp.broadcast_to(docs[:, rows - 1 : rows], docs.shape)
    live = suffix(jnp.where(docs == last, 0.0, 1.0))
    extra = jnp.broadcast_to(last, (EXTRA, HEAD_DIM))
    line = lax.broadcasted_iota(jnp.int32, (EXTRA, HEAD_DIM), 0)
    for g in range(KV_HEADS):
        keys = jnp.where(live, block_keys(block_ref, g).astype(jnp.float32), 0.0)
        state = dot(block_values(block_ref, g), keys.astype(jnp.bfloat16), TN)
        largest = jnp.max(jnp.abs(state), axis=0, keepdims=True)
        power = jnp.ceil(jnp.log2(jnp.maximum(largest, 1e-30)))
        steps = jnp.round(state * jnp.exp2(STEPS - power))
        state_ref[part_of(g, HEAD_DIM), :] = steps.astype(jnp.int32).astype(jnp.int16)
        extra = jnp.where(line == g, power, extra)
    extra = jnp.where(line == KV_HEADS + 1, docs, extra)
    start = KV_HEADS * HEAD_DIM
    state_ref[start : start + EXTRA, :] = extra.astype(jnp.int32).astype(jnp.int16)


def state_extra(ref):
    start = KV_HEADS * HEAD_DIM
    return ref[start : start + EXTRA, :].astype(jnp.int32).astype(jnp.float32)


def state_docs(ref):
    return state_extra(ref)[KV_HEADS + 1 : KV_HEADS + 2, :]


def state_kernel(
    q_ref, gain_ref, packed_ref, beta_ref, key_ref, value_ref, doc_ref,
    state_ref, summed_ref, stats_ref, gains_ref,
    own_ref, doc_scratch, beta_scratch, sems,
):
    part = lax.axis_index("kv")

    @pl.when(part == 0)
    def _():
        block_state(packed_ref, state_ref)

    @pl.when(part == 1)
    def _():
        beta_copy = pltpu.make_async_copy(beta_ref, beta_scratch, sems.at[2 * KV_HEADS + 1])
        beta_copy.start()
        load_block(key_ref, value_ref, doc_ref, own_ref, doc_scratch, sems)
        beta_copy.wait()
        block_state(own_ref, state_ref)
        bias = own_bias(block_docs(own_ref))
        for g in range(KV_HEADS):
            summed, top, total = attend_own(q_ref, own_ref, g, bias)
            summed_ref[part_of(g, HEAD_DIM), :] = summed
            stats_ref[g : g + 1, :] = top
            stats_ref[KV_HEADS + g : KV_HEADS + g + 1, :] = total
            rest = [1.0 - share_of(beta_scratch, g * GROUPS + i) for i in range(GROUPS)]
            stats_ref[2 * KV_HEADS + g : 2 * KV_HEADS + g + 1, :] = jnp.concatenate(rest, axis=1)
        scaled_gains(beta_scratch, gain_ref, gains_ref)


def own_kernel(beta_ref, q_ref, packed_ref, gain_ref, ready_ref, gains_ref):
    @pl.when(lax.axis_index("kv") == 0)
    def _():
        bias = own_bias(block_docs(packed_ref))
        for g in range(KV_HEADS):
            summed, _, total = attend_own(q_ref, packed_ref, g, bias)
            rest = [1.0 - share_of(beta_ref, g * GROUPS + i) for i in range(GROUPS)]
            scale = jnp.concatenate(rest, axis=1) / total
            ready_ref[part_of(g, HEAD_DIM), :] = summed * scale
        scaled_gains(beta_ref, gain_ref, gains_ref)


def before_kernel(q_ref, state_ref, one_ref, summed_ref, stats_ref, ready_ref):
    @pl.when(lax.axis_index("kv") == 1)
    def _():
        docs = state_docs(state_ref)
        rows = docs.shape[1]
        first, same = first_document(docs)
        live = suffix(jnp.where(block_docs(one_ref) == first, 0.0, 1.0))
        bias = jnp.where(live & same, 0.0, LOWEST)
        for g in range(KV_HEADS):
            scores = dot(block_keys(one_ref, g), group_queries(q_ref, g), NT)
            weights, factors, scales = [], [], []
            for i in range(GROUPS):
                cut = part_of(i, rows)
                masked = scores[:, cut] * SCALE + bias
                top_own = stats_ref[g : g + 1, cut]
                top = jnp.maximum(jnp.max(masked, axis=0, keepdims=True), top_own)
                weight = jnp.exp2(masked - top)
                factor = jnp.exp2(top_own - top)
                total = stats_ref[KV_HEADS + g : KV_HEADS + g + 1, cut] * factor
                total = total + jnp.sum(weight, axis=0, keepdims=True)
                factors.append(factor)
                scales.append(stats_ref[2 * KV_HEADS + g : 2 * KV_HEADS + g + 1, cut] / total)
                weights.append(weight.astype(jnp.bfloat16))
            added = dot(block_values(one_ref, g), jnp.concatenate(weights, axis=1), TN)
            group = part_of(g, HEAD_DIM)
            summed = summed_ref[group, :] * jnp.concatenate(factors, axis=1) + added
            ready_ref[group, :] = summed * jnp.concatenate(scales, axis=1)


def join_kernel(
    q_ref, state_ref, one_ref, two_ref, ready_zero, gains_zero, ready_one, gains_one,
    out_ref, held, sems,
):
    docs = state_docs(state_ref)
    rows = docs.shape[1]
    first, same = first_document(docs)
    reads = jnp.where(same, 1.0, 0.0)
    extras = []
    for ref in (one_ref, two_ref):
        extra = state_extra(ref)
        valid = jnp.where(extra[KV_HEADS : KV_HEADS + 1, :] == first, 1.0, 0.0)
        extras.append(jnp.exp2(extra[0:KV_HEADS, :] - STEPS) * valid)

    def copy(g):
        wide = part_of(g, GROUPS * HEAD_DIM)
        return pltpu.make_async_copy(held.at[:, wide], out_ref.at[:, wide], sems.at[g])

    def finish(ready_ref, gains_ref):
        for g in range(KV_HEADS):
            group = part_of(g, HEAD_DIM)
            one = one_ref[group, :].astype(jnp.int32).astype(jnp.float32)
            two = two_ref[group, :].astype(jnp.int32).astype(jnp.float32)
            state = one * extras[0][g : g + 1, :] + two * extras[1][g : g + 1, :]
            q = group_queries(q_ref, g)
            high = state.astype(jnp.bfloat16)
            low = (state - high.astype(jnp.float32)).astype(jnp.bfloat16)
            recalled = dot(high, q, NT) + dot(low, q, NT)
            for i in range(GROUPS):
                h, cut = g * GROUPS + i, part_of(i, rows)
                read = recalled[:, cut]
                square = jnp.sum(read * read, axis=0, keepdims=True) * (1.0 / HEAD_DIM)
                read = read * (lax.rsqrt(square + 1e-06) * reads)
                mixed = read * gains_ref[part_of(h, HEAD_DIM), :] + ready_ref[group, cut]
                held[:, part_of(h, HEAD_DIM)] = jnp.transpose(mixed)
            copy(g).start()

    part = lax.axis_index("kv")

    @pl.when(part == 0)
    def _():
        finish(ready_zero, gains_zero)

    @pl.when(part == 1)
    def _():
        finish(ready_one, gains_one)

    for g in range(KV_HEADS):
        copy(g).wait()


def near_device(n_seq, queries, keys, values, doc_ids, beta, lin_gain):
    rows = queries.shape[0]
    devices = 2 * n_seq
    vmem = pl.BlockSpec(memory_space=pltpu.VMEM)
    smem = pl.BlockSpec(memory_space=pltpu.SMEM)
    hbm = pl.BlockSpec(memory_space=pltpu.HBM)
    in_hbm = functools.partial(pltpu.with_memory_space_constraint, memory_space=pltpu.HBM)
    params = pltpu.CompilerParams(vmem_limit_bytes=32 * 1024 * 1024)
    wide = GROUPS * rows
    group_shape = jax.ShapeDtypeStruct((KV_HEADS * HEAD_DIM, wide), jnp.float32)
    gains_shape = jax.ShapeDtypeStruct((HEADS * HEAD_DIM, HEAD_DIM), jnp.float32)
    docs = doc_ids.reshape(1, rows)
    gain = lin_gain.reshape(HEADS, HEAD_DIM)
    deep = 2 * KV_HEADS * rows + EXTRA

    def estimate(share):
        return pl.CostEstimate(
            flops=int(share * 4 * HEADS * HEAD_DIM * rows * rows),
            bytes_accessed=int(share * 4 * 1024 * 1024),
            transcendentals=int(share * HEADS * rows * rows),
        )

    def send(payload, pairs):
        return lax.ppermute(payload, ("seq", "kv"), pairs)

    packed = pl.pallas_call(
        pack_kernel,
        out_shape=jax.ShapeDtypeStruct((deep, HEAD_DIM), jnp.bfloat16),
        in_specs=[hbm] * 3,
        out_specs=vmem,
        scratch_shapes=[
            pltpu.VMEM((1, rows), jnp.int32),
            pltpu.SemaphoreType.DMA((2 * KV_HEADS + 1,)),
        ],
        compiler_params=params,
        cost_estimate=estimate(0.1),
    )(in_hbm(keys), in_hbm(values), in_hbm(docs))
    block = send(packed, [(b, b + 1) for b in range(0, devices, 2)])
    state, summed, stats, gains_one = pl.pallas_call(
        state_kernel,
        out_shape=[
            jax.ShapeDtypeStruct((KV_HEADS * HEAD_DIM + EXTRA, HEAD_DIM), jnp.int16),
            group_shape,
            jax.ShapeDtypeStruct((4 * KV_HEADS, wide), jnp.float32),
            gains_shape,
        ],
        in_specs=[vmem] * 3 + [hbm] * 4,
        out_specs=[vmem] * 4,
        scratch_shapes=[
            pltpu.VMEM((deep, HEAD_DIM), jnp.bfloat16),
            pltpu.VMEM((1, rows), jnp.int32),
            pltpu.SMEM((HEADS,), jnp.float32),
            pltpu.SemaphoreType.DMA((2 * KV_HEADS + 2,)),
        ],
        compiler_params=params,
        cost_estimate=estimate(1.0),
    )(queries, gain, packed, in_hbm(beta), in_hbm(keys), in_hbm(values), in_hbm(docs))
    one = send(state, [(b, b + 1) for b in range(1, devices - 1, 2)])
    two = send(state, [(b, b + 2) for b in range(devices - 2)])
    ready_zero, gains_zero = pl.pallas_call(
        own_kernel,
        out_shape=[group_shape, gains_shape],
        in_specs=[smem] + [vmem] * 3,
        out_specs=[vmem] * 2,
        compiler_params=params,
        cost_estimate=estimate(1.0),
    )(beta, queries, packed, gain)
    ready_one = pl.pallas_call(
        before_kernel,
        out_shape=group_shape,
        in_specs=[vmem] * 5,
        out_specs=vmem,
        compiler_params=params,
        cost_estimate=estimate(1.0),
    )(queries, state, block, summed, stats)
    return pl.pallas_call(
        join_kernel,
        out_shape=jax.ShapeDtypeStruct((rows, HEADS * HEAD_DIM), jnp.float32),
        in_specs=[vmem] * 8,
        out_specs=hbm,
        scratch_shapes=[
            pltpu.VMEM((rows, HEADS * HEAD_DIM), jnp.float32),
            pltpu.SemaphoreType.DMA((KV_HEADS,)),
        ],
        compiler_params=params,
    )(queries, state, one, two, ready_zero, gains_zero, ready_one, gains_one)


def carried_in(part, axis, combine, identity):
    place = lax.axis_index(axis)
    gathered = jax.tree.map(lambda a: lax.all_gather(a, axis), part)
    state = jax.tree.map(lambda a, e: jnp.zeros_like(a) + jnp.asarray(e, a.dtype), part, identity)

    def one(step, state):
        return combine(
            state, jax.tree.map(lambda a: lax.dynamic_index_in_dim(a, step, 0, False), gathered)
        )

    return lax.fori_loop(0, place, one, state)


def join_states(earlier, later):
    state_early, first_early, last_early = earlier
    state_late, first_late, last_late = later
    empty_late = first_late < 0
    joined = (first_late == last_late) & (last_early == first_late)
    merged = state_late + jnp.where(joined, state_early, jnp.zeros_like(state_early))
    combined = jnp.where(empty_late, state_early, merged)
    first_doc = jnp.where(first_early < 0, first_late, first_early)
    last_doc = jnp.where(empty_late, last_early, last_late)
    return (combined, first_doc, last_doc)


def tail_merge(one_side, other_side):
    state_one, first_one, last_one = one_side
    state_other, first_other, last_other = other_side
    top_doc = jnp.maximum(last_one, last_other)
    state_sum = jnp.where(last_one == top_doc, state_one, jnp.zeros_like(state_one))
    state_sum = state_sum + jnp.where(
        last_other == top_doc, state_other, jnp.zeros_like(state_other)
    )
    return (state_sum, jnp.minimum(first_one, first_other), top_doc)


def tail_state(key_rows, value_rows, doc_rows, target_doc):
    count = key_rows.shape[0]
    key_heads = key_rows.reshape(count, KV_HEADS, HEAD_DIM)
    value_heads = value_rows.reshape(count, KV_HEADS, HEAD_DIM)
    live = doc_rows == target_doc
    masked = jnp.where(live[:, None, None], key_heads, jnp.zeros_like(key_heads))
    return jnp.einsum("rgd,rge->gde", masked, value_heads, preferred_element_type=jnp.float32)


def attend_block(
    carry, query_heads, query_pos, query_doc, key_rows, value_rows, key_doc, key_start
):
    running_max, running_sum, accumulated = carry
    key_count = key_rows.shape[0]
    key_heads = key_rows.reshape(key_count, KV_HEADS, HEAD_DIM)
    value_heads = value_rows.reshape(key_count, KV_HEADS, HEAD_DIM)
    scores = jnp.einsum(
        "rgqd,kgd->gqrk", query_heads, key_heads, preferred_element_type=jnp.float32
    )
    scores = scores / jnp.sqrt(jnp.float32(HEAD_DIM))
    key_pos = key_start + jnp.arange(key_count, dtype=jnp.int32)
    allowed = (key_pos[None, :] <= query_pos[:, None]) & (key_doc[None, :] == query_doc[:, None])
    masked = jnp.where(allowed, scores, jnp.float32(-1e30))
    new_max = jnp.maximum(running_max, jnp.max(masked, axis=-1))
    factor = jnp.exp(running_max - new_max)
    weights = jnp.where(allowed, jnp.exp(masked - new_max[..., None]), jnp.float32(0.0))
    new_sum = running_sum * factor + jnp.sum(weights, axis=-1)
    product = jnp.einsum(
        "gqrk,kge->gqre",
        weights.astype(jnp.bfloat16),
        value_heads,
        preferred_element_type=jnp.float32,
    )
    new_accum = accumulated * factor[..., None] + product
    return (new_max, new_sum, new_accum)


def far_device(queries, keys, values, doc_ids, beta, lin_gain):
    row_count = queries.shape[0]
    groups = HEADS // KV_HEADS
    query_heads = queries.reshape(row_count, KV_HEADS, groups, HEAD_DIM)
    position = lax.axis_index("kv") * row_count
    query_pos = position + jnp.arange(row_count, dtype=jnp.int32)
    last_query = position + row_count - 1
    initial = (
        jnp.full((KV_HEADS, groups, row_count), -1e30, jnp.float32),
        jnp.zeros((KV_HEADS, groups, row_count), jnp.float32),
        jnp.zeros((KV_HEADS, groups, row_count, HEAD_DIM), jnp.float32),
    )
    empty_tail = (
        jnp.zeros((KV_HEADS, HEAD_DIM, HEAD_DIM), jnp.float32),
        jnp.array(2**30, jnp.int32),
        jnp.array(-1, jnp.int32),
    )
    key_piece = lax.all_gather(keys, "kv", axis=0, tiled=True)
    value_piece = lax.all_gather(values, "kv", axis=0, tiled=True)
    doc_piece = lax.all_gather(doc_ids, "kv", axis=0, tiled=True)
    blocks = key_piece.shape[0] // row_count

    def one_block(state, item):
        soft_state, tail_now = state
        key_block, value_block, doc_block, number = item
        block_start = number * row_count
        soft_next = lax.cond(
            block_start <= last_query,
            lambda inner: attend_block(
                inner,
                query_heads,
                query_pos,
                doc_ids,
                key_block,
                value_block,
                doc_block,
                block_start,
            ),
            lambda inner: inner,
            soft_state,
        )
        block_tail = (
            tail_state(key_block, value_block, doc_block, doc_block[-1]),
            doc_block[0],
            doc_block[-1],
        )
        tail_now = tail_merge(tail_now, block_tail)
        return ((soft_next, tail_now), None)

    stacked = (
        key_piece.reshape(blocks, row_count, -1),
        value_piece.reshape(blocks, row_count, -1),
        doc_piece.reshape(blocks, row_count),
        jnp.arange(blocks, dtype=jnp.int32),
    )
    result, _ = lax.scan(one_block, (initial, empty_tail), stacked)
    running, segment_tail = result
    running_max, running_sum, accumulated = running
    soft_out = jnp.transpose(accumulated / running_sum[..., None], (2, 0, 1, 3))
    identity = (
        jnp.zeros((KV_HEADS, HEAD_DIM, HEAD_DIM), jnp.float32),
        jnp.array(-1, jnp.int32),
        jnp.array(-1, jnp.int32),
    )
    memory = carried_in(segment_tail, "seq", join_states, identity)
    memory_state, memory_first, memory_last = memory
    query_float = query_heads.astype(jnp.float32)
    recalled = jnp.einsum(
        "rgqd,gde->rgqe", query_float, memory_state, precision=lax.Precision.HIGHEST
    )
    recalled = jnp.where((doc_ids == memory_last)[:, None, None, None], recalled, jnp.float32(0.0))
    mean_square = jnp.mean(recalled * recalled, axis=-1, keepdims=True)
    normed = (
        recalled * lax.rsqrt(mean_square + 1e-06) * lin_gain.reshape(KV_HEADS, groups, HEAD_DIM)
    )
    mixing = jax.nn.sigmoid(beta).reshape(KV_HEADS, groups)[None, :, :, None]
    mixed = mixing * normed + (1.0 - mixing) * soft_out
    return mixed.reshape(row_count, HEADS * HEAD_DIM).astype(jnp.float32)


def solution(mesh):
    n_seq, n_kv = mesh.shape["seq"], mesh.shape["kv"]
    in_specs = (
        P(("dp", "seq", "kv"), None),
        P(("dp", "seq", "kv"), None),
        P(("dp", "seq", "kv"), None),
        P(("dp", "seq", "kv")),
        P(),
        P(),
    )
    out_specs = P(("dp", "seq", "kv"), None)
    if n_kv == 2 and n_seq * n_kv <= 2 * LONGEST:
        on_device = functools.partial(near_device, n_seq)
    else:
        on_device = far_device
    return jax.shard_map(
        on_device, mesh=mesh, in_specs=in_specs, out_specs=out_specs, check_vma=False
    )
```

```python
import functools
import math

import jax
import jax.numpy as jnp
from jax import lax
from jax.experimental import pallas as pl
from jax.experimental.pallas import tpu as pltpu
from jax.sharding import PartitionSpec as P

HEADS = 16
KV_HEADS = 4
HEAD_DIM = 128
GROUPS = HEADS // KV_HEADS
LONGEST = 4
SCALE = math.log2(math.e) / math.sqrt(HEAD_DIM)
LOWEST = -1e30
EXTRA = 16

NT = (((1,), (1,)), ((), ()))
TN = (((0,), (0,)), ((), ()))


def dot(a, b, dims):
    return lax.dot_general(a, b, dims, preferred_element_type=jnp.float32)


def column(row):
    return jnp.transpose(jnp.broadcast_to(row, (HEAD_DIM, row.shape[1])))


def part_of(i, size):
    return slice(i * size, (i + 1) * size)


def group_queries(q_ref, g):
    heads = [q_ref[:, part_of(g * GROUPS + i, HEAD_DIM)] for i in range(GROUPS)]
    return jnp.concatenate(heads, axis=0)


def share_of(beta_ref, h):
    return 1.0 / (1.0 + jnp.exp(-jnp.full((1, HEAD_DIM), beta_ref[h], jnp.float32)))


def scaled_gains(beta_ref, gain_ref, out_ref):
    for h in range(HEADS):
        scaled = gain_ref[h : h + 1, :] * share_of(beta_ref, h)
        out_ref[part_of(h, HEAD_DIM), :] = column(scaled)


def suffix(others):
    count = jnp.sum(others, axis=1, keepdims=True)
    shape = (others.shape[1], HEAD_DIM)
    return lax.broadcasted_iota(jnp.int32, shape, 0).astype(jnp.float32) >= count


def first_document(docs):
    first = jnp.broadcast_to(docs[:, 0:1], docs.shape)
    return first, docs == first


def load_block(query_ref, key_ref, value_ref, doc_ref, q_ref, out_refs, doc_scratch, sems):
    rows = key_ref.shape[0]
    doc_copy = pltpu.make_async_copy(doc_ref, doc_scratch, sems.at[0])
    doc_copy.start()
    query_copy = pltpu.make_async_copy(query_ref, q_ref, sems.at[1])
    copies = []
    for out_ref in out_refs:
        for g in range(2 * KV_HEADS):
            source = key_ref if g < KV_HEADS else value_ref
            copy = pltpu.make_async_copy(
                source.at[:, part_of(g % KV_HEADS, HEAD_DIM)],
                out_ref.at[part_of(g, rows), :],
                sems.at[2 + len(copies)],
            )
            copy.start()
            copies.append(copy)
    query_copy.start()
    copies.append(query_copy)
    doc_copy.wait()
    docs = jnp.broadcast_to(doc_scratch[...].astype(jnp.float32), (EXTRA, rows))
    start = 2 * KV_HEADS * rows
    for out_ref in out_refs:
        out_ref[start : start + EXTRA, :] = docs.astype(jnp.bfloat16)
    for copy in copies:
        copy.wait()


def block_keys(ref, g):
    return ref[part_of(g, HEAD_DIM), :]


def block_values(ref, g):
    return ref[part_of(KV_HEADS + g, HEAD_DIM), :]


def block_docs(ref):
    start = 2 * KV_HEADS * HEAD_DIM
    return ref[start : start + EXTRA, :].astype(jnp.float32)[0:1, :]


class Plan:
    def __init__(self, n_seq):
        devices = 2 * n_seq
        near = [(b, b + 1) for b in range(devices - 1)]
        far = [(b, b + 2) for b in range(devices - 2)]
        crossing = [p for p in far if p[0] // 2 % 2 == 1]
        touched = {b for p in crossing for b in p}
        targets = {p[1] for p in crossing}
        early = [p for p in near if p[0] not in touched and p[1] not in targets]
        self.pairs = [
            crossing + early,
            [p for p in near if p not in early],
            [p for p in far if p not in crossing],
        ]
        self.senders = sorted({p[0] for p in self.pairs[0]})
        busy = {b for p in self.pairs[1] for b in p}
        self.idle = [b for b in range(devices) if b not in busy]
        self.attend_first = [p[1] for p in early if p[1] % 2 == 1]


def block_number():
    return 2 * lax.axis_index("seq") + lax.axis_index("kv")


def among(members):
    block = block_number()
    return functools.reduce(jnp.logical_or, [block == b for b in members])


def pack_kernel(
    plan, query_ref, key_ref, value_ref, doc_ref, first_ref, out_ref, q_ref, doc_scratch, sems
):
    @pl.when(among(plan.senders))
    def _():
        outs = (first_ref, out_ref)
        load_block(query_ref, key_ref, value_ref, doc_ref, q_ref, outs, doc_scratch, sems)


def attend_own(q_ref, block_ref, g, bias):
    rows = q_ref.shape[0]
    scores = dot(block_keys(block_ref, g), group_queries(q_ref, g), NT)
    tops, totals, weights = [], [], []
    for i in range(GROUPS):
        masked = scores[:, part_of(i, rows)] * SCALE + bias
        top = jnp.max(masked, axis=0, keepdims=True)
        weight = jnp.exp2(masked - top)
        tops.append(top)
        totals.append(jnp.sum(weight, axis=0, keepdims=True))
        weights.append(weight.astype(jnp.bfloat16))
    summed = dot(block_values(block_ref, g), jnp.concatenate(weights, axis=1), TN)
    return summed, jnp.concatenate(tops, axis=1), jnp.concatenate(totals, axis=1)


def own_bias(docs):
    rows = docs.shape[1]
    place = lax.broadcasted_iota(jnp.int32, (rows, rows), 0)
    row = lax.broadcasted_iota(jnp.int32, (rows, rows), 1)
    return jnp.where((place <= row) & (column(docs) == docs), 0.0, LOWEST)


def attend_itself(q_ref, block_ref, gain_ref, beta_ref, summed_ref, stats_ref, gains_ref, beta_copy):
    bias = own_bias(block_docs(block_ref))
    done = lax.axis_index("kv") == 0
    for g in range(KV_HEADS):
        summed, top, total = attend_own(q_ref, block_ref, g, bias)
        summed_ref[part_of(g, HEAD_DIM), :] = summed
        stats_ref[g : g + 1, :] = top
        stats_ref[KV_HEADS + g : KV_HEADS + g + 1, :] = total
    beta_copy.wait()
    for g in range(KV_HEADS):
        rest = [1.0 - share_of(beta_ref, g * GROUPS + i) for i in range(GROUPS)]
        rest = jnp.concatenate(rest, axis=1)
        stats_ref[2 * KV_HEADS + g : 2 * KV_HEADS + g + 1, :] = rest
        scale = rest / stats_ref[KV_HEADS + g : KV_HEADS + g + 1, :]
        group = part_of(g, HEAD_DIM)
        summed_ref[group, :] = summed_ref[group, :] * jnp.where(done, scale, 1.0)
    scaled_gains(beta_ref, gain_ref, gains_ref)


def settle_kernel(
    plan, gain_ref, packed_ref, q_in, beta_ref, query_ref, key_ref, value_ref, doc_ref,
    out_ref, q_ref, summed_ref, stats_ref, gains_ref, beta_scratch, doc_scratch, sems,
):
    beta_copy = pltpu.make_async_copy(beta_ref, beta_scratch, sems.at[2 * KV_HEADS + 2])

    @pl.when(among(plan.idle))
    def _():
        beta_copy.start()

    @pl.when(jnp.logical_not(among(plan.senders)))
    def _():
        outs = (out_ref,)
        load_block(query_ref, key_ref, value_ref, doc_ref, q_ref, outs, doc_scratch, sems)

    @pl.when(among(plan.idle))
    def _():
        attend_itself(
            q_ref, out_ref, gain_ref, beta_scratch, summed_ref, stats_ref, gains_ref, beta_copy
        )


def own_kernel(
    plan, q_ref, own_ref, gain_ref, beta_ref, summed_in, stats_in, gains_in,
    summed_ref, stats_ref, gains_ref, beta_scratch, sem,
):
    @pl.when(jnp.logical_not(among(plan.idle)))
    def _():
        beta_copy = pltpu.make_async_copy(beta_ref, beta_scratch, sem)
        beta_copy.start()
        attend_itself(
            q_ref, own_ref, gain_ref, beta_scratch, summed_ref, stats_ref, gains_ref, beta_copy
        )


def before_kernel(plan, q_ref, own_ref, one_ref, two_ref, stats_ref, summed_in, summed_ref):
    docs = block_docs(own_ref)
    rows = docs.shape[1]
    first, same = first_document(docs)

    def attend(ref):
        live = suffix(jnp.where(block_docs(ref) == first, 0.0, 1.0))
        bias = jnp.where(live & same, 0.0, LOWEST)
        for g in range(KV_HEADS):
            scores = dot(block_keys(ref, g), group_queries(q_ref, g), NT)
            weights, factors, scales = [], [], []
            for i in range(GROUPS):
                cut = part_of(i, rows)
                masked = scores[:, cut] * SCALE + bias
                top_own = stats_ref[g : g + 1, cut]
                top = jnp.maximum(jnp.max(masked, axis=0, keepdims=True), top_own)
                weight = jnp.exp2(masked - top)
                factor = jnp.exp2(top_own - top)
                total = stats_ref[KV_HEADS + g : KV_HEADS + g + 1, cut] * factor
                total = total + jnp.sum(weight, axis=0, keepdims=True)
                factors.append(factor)
                scales.append(stats_ref[2 * KV_HEADS + g : 2 * KV_HEADS + g + 1, cut] / total)
                weights.append(weight.astype(jnp.bfloat16))
            added = dot(block_values(ref, g), jnp.concatenate(weights, axis=1), TN)
            group = part_of(g, HEAD_DIM)
            summed = summed_ref[group, :] * jnp.concatenate(factors, axis=1) + added
            summed_ref[group, :] = summed * jnp.concatenate(scales, axis=1)

    attend_first = among(plan.attend_first)

    @pl.when(attend_first)
    def _():
        attend(one_ref)

    @pl.when((lax.axis_index("kv") == 1) & jnp.logical_not(attend_first))
    def _():
        attend(two_ref)


def join_kernel(
    plan, q_ref, own_ref, one_ref, two_ref, three_ref, ready_ref, gains_ref, out_ref, held, sems
):
    docs = block_docs(own_ref)
    rows = docs.shape[1]
    first, same = first_document(docs)
    reads = jnp.where(same, 1.0, 0.0)
    sources = (one_ref, two_ref, three_ref)
    attended = (among(plan.attend_first), lax.axis_index("kv") == 1, False)
    lives = []
    for ref, other in zip(sources, attended):
        others = jnp.where((block_docs(ref) == first) & jnp.logical_not(other), 0.0, 1.0)
        lives.append(suffix(others))

    def copy(g):
        wide = part_of(g, GROUPS * HEAD_DIM)
        return pltpu.make_async_copy(held.at[:, wide], out_ref.at[:, wide], sems.at[g])

    for g in range(KV_HEADS):
        keys, values = [], []
        for ref, live in zip(sources, lives):
            masked = jnp.where(live, block_keys(ref, g).astype(jnp.float32), 0.0)
            keys.append(masked.astype(jnp.bfloat16))
            values.append(block_values(ref, g))
        state = dot(jnp.concatenate(values, axis=0), jnp.concatenate(keys, axis=0), TN)
        q = group_queries(q_ref, g)
        high = state.astype(jnp.bfloat16)
        state = state - high.astype(jnp.float32)
        middle = state.astype(jnp.bfloat16)
        low = (state - middle.astype(jnp.float32)).astype(jnp.bfloat16)
        recalled = dot(high, q, NT) + (dot(middle, q, NT) + dot(low, q, NT))
        for i in range(GROUPS):
            h, cut = g * GROUPS + i, part_of(i, rows)
            read = recalled[:, cut]
            square = jnp.sum(read * read, axis=0, keepdims=True) * (1.0 / HEAD_DIM)
            read = read * (lax.rsqrt(square + 1e-06) * reads)
            mixed = read * gains_ref[part_of(h, HEAD_DIM), :]
            mixed = mixed + ready_ref[part_of(g, HEAD_DIM), cut]
            held[:, part_of(h, HEAD_DIM)] = jnp.transpose(mixed)
        copy(g).start()
    for g in range(KV_HEADS):
        copy(g).wait()


def near_device(n_seq, queries, keys, values, doc_ids, beta, lin_gain):
    rows = queries.shape[0]
    vmem = pl.BlockSpec(memory_space=pltpu.VMEM)
    hbm = pl.BlockSpec(memory_space=pltpu.HBM)
    in_hbm = functools.partial(pltpu.with_memory_space_constraint, memory_space=pltpu.HBM)
    params = pltpu.CompilerParams(vmem_limit_bytes=32 * 1024 * 1024)
    wide = GROUPS * rows
    group_shape = jax.ShapeDtypeStruct((KV_HEADS * HEAD_DIM, wide), jnp.float32)
    gains_shape = jax.ShapeDtypeStruct((HEADS * HEAD_DIM, HEAD_DIM), jnp.float32)
    docs = doc_ids.reshape(1, rows)
    gain = lin_gain.reshape(HEADS, HEAD_DIM)
    deep = 2 * KV_HEADS * rows + EXTRA

    def estimate(share):
        return pl.CostEstimate(
            flops=int(share * 4 * HEADS * HEAD_DIM * rows * rows),
            bytes_accessed=int(share * 4 * 1024 * 1024),
            transcendentals=int(share * HEADS * rows * rows),
        )

    def send(payload, pairs):
        return lax.ppermute(payload, ("seq", "kv"), pairs)

    plan = Plan(n_seq)
    block_shape = jax.ShapeDtypeStruct((deep, HEAD_DIM), jnp.bfloat16)
    stats_shape = jax.ShapeDtypeStruct((4 * KV_HEADS, wide), jnp.float32)
    doc_scratch = pltpu.VMEM((1, rows), jnp.int32)
    beta_scratch = pltpu.SMEM((HEADS,), jnp.float32)
    query_shape = jax.ShapeDtypeStruct(queries.shape, queries.dtype)
    block = (in_hbm(queries), in_hbm(keys), in_hbm(values), in_hbm(docs))
    first, packed, q = pl.pallas_call(
        functools.partial(pack_kernel, plan),
        out_shape=[block_shape] * 2 + [query_shape],
        in_specs=[hbm] * 4,
        out_specs=[vmem] * 3,
        scratch_shapes=[doc_scratch, pltpu.SemaphoreType.DMA((4 * KV_HEADS + 2,))],
        compiler_params=params,
        cost_estimate=estimate(0.1),
    )(*block)
    one = send(first, plan.pairs[0])
    own, q, summed, stats, gains = pl.pallas_call(
        functools.partial(settle_kernel, plan),
        out_shape=[block_shape, query_shape, group_shape, stats_shape, gains_shape],
        in_specs=[vmem] * 3 + [hbm] * 5,
        out_specs=[vmem] * 5,
        scratch_shapes=[
            beta_scratch,
            doc_scratch,
            pltpu.SemaphoreType.DMA((2 * KV_HEADS + 3,)),
        ],
        input_output_aliases={1: 0, 2: 1},
        compiler_params=params,
        cost_estimate=estimate(1.0),
    )(gain, packed, q, in_hbm(beta), *block)
    two = send(own, plan.pairs[1])
    three = send(own, plan.pairs[2])
    summed, stats, gains = pl.pallas_call(
        functools.partial(own_kernel, plan),
        out_shape=[group_shape, stats_shape, gains_shape],
        in_specs=[vmem] * 3 + [hbm] + [vmem] * 3,
        out_specs=[vmem] * 3,
        scratch_shapes=[beta_scratch, pltpu.SemaphoreType.DMA],
        input_output_aliases={4: 0, 5: 1, 6: 2},
        compiler_params=params,
        cost_estimate=estimate(1.0),
    )(q, own, gain, in_hbm(beta), summed, stats, gains)
    ready = pl.pallas_call(
        functools.partial(before_kernel, plan),
        out_shape=group_shape,
        in_specs=[vmem] * 6,
        out_specs=vmem,
        input_output_aliases={5: 0},
        compiler_params=params,
        cost_estimate=estimate(1.0),
    )(q, own, one, two, stats, summed)
    return pl.pallas_call(
        functools.partial(join_kernel, plan),
        out_shape=jax.ShapeDtypeStruct((rows, HEADS * HEAD_DIM), jnp.float32),
        in_specs=[vmem] * 7,
        out_specs=hbm,
        scratch_shapes=[
            pltpu.VMEM((rows, HEADS * HEAD_DIM), jnp.float32),
            pltpu.SemaphoreType.DMA((KV_HEADS,)),
        ],
        compiler_params=params,
    )(q, own, one, two, three, ready, gains)


def carried_in(part, axis, combine, identity):
    place = lax.axis_index(axis)
    gathered = jax.tree.map(lambda a: lax.all_gather(a, axis), part)
    state = jax.tree.map(lambda a, e: jnp.zeros_like(a) + jnp.asarray(e, a.dtype), part, identity)

    def one(step, state):
        return combine(
            state, jax.tree.map(lambda a: lax.dynamic_index_in_dim(a, step, 0, False), gathered)
        )

    return lax.fori_loop(0, place, one, state)


def join_states(earlier, later):
    state_early, first_early, last_early = earlier
    state_late, first_late, last_late = later
    empty_late = first_late < 0
    joined = (first_late == last_late) & (last_early == first_late)
    merged = state_late + jnp.where(joined, state_early, jnp.zeros_like(state_early))
    combined = jnp.where(empty_late, state_early, merged)
    first_doc = jnp.where(first_early < 0, first_late, first_early)
    last_doc = jnp.where(empty_late, last_early, last_late)
    return (combined, first_doc, last_doc)


def tail_merge(one_side, other_side):
    state_one, first_one, last_one = one_side
    state_other, first_other, last_other = other_side
    top_doc = jnp.maximum(last_one, last_other)
    state_sum = jnp.where(last_one == top_doc, state_one, jnp.zeros_like(state_one))
    state_sum = state_sum + jnp.where(
        last_other == top_doc, state_other, jnp.zeros_like(state_other)
    )
    return (state_sum, jnp.minimum(first_one, first_other), top_doc)


def tail_state(key_rows, value_rows, doc_rows, target_doc):
    count = key_rows.shape[0]
    key_heads = key_rows.reshape(count, KV_HEADS, HEAD_DIM)
    value_heads = value_rows.reshape(count, KV_HEADS, HEAD_DIM)
    live = doc_rows == target_doc
    masked = jnp.where(live[:, None, None], key_heads, jnp.zeros_like(key_heads))
    return jnp.einsum("rgd,rge->gde", masked, value_heads, preferred_element_type=jnp.float32)


def attend_block(
    carry, query_heads, query_pos, query_doc, key_rows, value_rows, key_doc, key_start
):
    running_max, running_sum, accumulated = carry
    key_count = key_rows.shape[0]
    key_heads = key_rows.reshape(key_count, KV_HEADS, HEAD_DIM)
    value_heads = value_rows.reshape(key_count, KV_HEADS, HEAD_DIM)
    scores = jnp.einsum(
        "rgqd,kgd->gqrk", query_heads, key_heads, preferred_element_type=jnp.float32
    )
    scores = scores / jnp.sqrt(jnp.float32(HEAD_DIM))
    key_pos = key_start + jnp.arange(key_count, dtype=jnp.int32)
    allowed = (key_pos[None, :] <= query_pos[:, None]) & (key_doc[None, :] == query_doc[:, None])
    masked = jnp.where(allowed, scores, jnp.float32(-1e30))
    new_max = jnp.maximum(running_max, jnp.max(masked, axis=-1))
    factor = jnp.exp(running_max - new_max)
    weights = jnp.where(allowed, jnp.exp(masked - new_max[..., None]), jnp.float32(0.0))
    new_sum = running_sum * factor + jnp.sum(weights, axis=-1)
    product = jnp.einsum(
        "gqrk,kge->gqre",
        weights.astype(jnp.bfloat16),
        value_heads,
        preferred_element_type=jnp.float32,
    )
    new_accum = accumulated * factor[..., None] + product
    return (new_max, new_sum, new_accum)


def far_device(queries, keys, values, doc_ids, beta, lin_gain):
    row_count = queries.shape[0]
    groups = HEADS // KV_HEADS
    query_heads = queries.reshape(row_count, KV_HEADS, groups, HEAD_DIM)
    position = lax.axis_index("kv") * row_count
    query_pos = position + jnp.arange(row_count, dtype=jnp.int32)
    last_query = position + row_count - 1
    initial = (
        jnp.full((KV_HEADS, groups, row_count), -1e30, jnp.float32),
        jnp.zeros((KV_HEADS, groups, row_count), jnp.float32),
        jnp.zeros((KV_HEADS, groups, row_count, HEAD_DIM), jnp.float32),
    )
    empty_tail = (
        jnp.zeros((KV_HEADS, HEAD_DIM, HEAD_DIM), jnp.float32),
        jnp.array(2**30, jnp.int32),
        jnp.array(-1, jnp.int32),
    )
    key_piece = lax.all_gather(keys, "kv", axis=0, tiled=True)
    value_piece = lax.all_gather(values, "kv", axis=0, tiled=True)
    doc_piece = lax.all_gather(doc_ids, "kv", axis=0, tiled=True)
    blocks = key_piece.shape[0] // row_count

    def one_block(state, item):
        soft_state, tail_now = state
        key_block, value_block, doc_block, number = item
        block_start = number * row_count
        soft_next = lax.cond(
            block_start <= last_query,
            lambda inner: attend_block(
                inner,
                query_heads,
                query_pos,
                doc_ids,
                key_block,
                value_block,
                doc_block,
                block_start,
            ),
            lambda inner: inner,
            soft_state,
        )
        block_tail = (
            tail_state(key_block, value_block, doc_block, doc_block[-1]),
            doc_block[0],
            doc_block[-1],
        )
        tail_now = tail_merge(tail_now, block_tail)
        return ((soft_next, tail_now), None)

    stacked = (
        key_piece.reshape(blocks, row_count, -1),
        value_piece.reshape(blocks, row_count, -1),
        doc_piece.reshape(blocks, row_count),
        jnp.arange(blocks, dtype=jnp.int32),
    )
    result, _ = lax.scan(one_block, (initial, empty_tail), stacked)
    running, segment_tail = result
    running_max, running_sum, accumulated = running
    soft_out = jnp.transpose(accumulated / running_sum[..., None], (2, 0, 1, 3))
    identity = (
        jnp.zeros((KV_HEADS, HEAD_DIM, HEAD_DIM), jnp.float32),
        jnp.array(-1, jnp.int32),
        jnp.array(-1, jnp.int32),
    )
    memory = carried_in(segment_tail, "seq", join_states, identity)
    memory_state, memory_first, memory_last = memory
    query_float = query_heads.astype(jnp.float32)
    recalled = jnp.einsum(
        "rgqd,gde->rgqe", query_float, memory_state, precision=lax.Precision.HIGHEST
    )
    recalled = jnp.where((doc_ids == memory_last)[:, None, None, None], recalled, jnp.float32(0.0))
    mean_square = jnp.mean(recalled * recalled, axis=-1, keepdims=True)
    normed = (
        recalled * lax.rsqrt(mean_square + 1e-06) * lin_gain.reshape(KV_HEADS, groups, HEAD_DIM)
    )
    mixing = jax.nn.sigmoid(beta).reshape(KV_HEADS, groups)[None, :, :, None]
    mixed = mixing * normed + (1.0 - mixing) * soft_out
    return mixed.reshape(row_count, HEADS * HEAD_DIM).astype(jnp.float32)


def solution(mesh):
    n_seq, n_kv = mesh.shape["seq"], mesh.shape["kv"]
    in_specs = (
        P(("dp", "seq", "kv"), None),
        P(("dp", "seq", "kv"), None),
        P(("dp", "seq", "kv"), None),
        P(("dp", "seq", "kv")),
        P(),
        P(),
    )
    out_specs = P(("dp", "seq", "kv"), None)
    if n_kv == 2 and n_seq * n_kv <= 2 * LONGEST:
        on_device = functools.partial(near_device, n_seq)
    else:
        on_device = far_device
    return jax.shard_map(
        on_device, mesh=mesh, in_specs=in_specs, out_specs=out_specs, check_vma=False
    )
```

```python
import functools
import math

import jax
import jax.numpy as jnp
from jax import lax
from jax.experimental import pallas as pl
from jax.experimental.pallas import tpu as pltpu
from jax.sharding import PartitionSpec as P

HEADS = 16
KV_HEADS = 4
HEAD_DIM = 128
GROUPS = HEADS // KV_HEADS
LONGEST = 4
SCALE = math.log2(math.e) / math.sqrt(HEAD_DIM)
LOWEST = -1e30
EXTRA = 16

NT = (((1,), (1,)), ((), ()))
TN = (((0,), (0,)), ((), ()))


def dot(a, b, dims):
    return lax.dot_general(a, b, dims, preferred_element_type=jnp.float32)


def column(row):
    return jnp.transpose(jnp.broadcast_to(row, (HEAD_DIM, row.shape[1])))


def part_of(i, size):
    return slice(i * size, (i + 1) * size)


def group_queries(q_ref, g):
    heads = [q_ref[:, part_of(g * GROUPS + i, HEAD_DIM)] for i in range(GROUPS)]
    return jnp.concatenate(heads, axis=0)


def share_of(beta_ref, h):
    return 1.0 / (1.0 + jnp.exp(-jnp.full((1, HEAD_DIM), beta_ref[h], jnp.float32)))


def scaled_gains(beta_ref, gain_ref, out_ref):
    for h in range(HEADS):
        scaled = gain_ref[h : h + 1, :] * share_of(beta_ref, h)
        out_ref[part_of(h, HEAD_DIM), :] = column(scaled)


def suffix(others):
    count = jnp.sum(others, axis=1, keepdims=True)
    shape = (others.shape[1], HEAD_DIM)
    return lax.broadcasted_iota(jnp.int32, shape, 0).astype(jnp.float32) >= count


def first_document(docs):
    first = jnp.broadcast_to(docs[:, 0:1], docs.shape)
    return first, docs == first


def load_block(key_ref, value_ref, doc_ref, out_ref, doc_scratch, sems):
    rows = key_ref.shape[0]
    doc_copy = pltpu.make_async_copy(doc_ref, doc_scratch, sems.at[0])
    doc_copy.start()
    copies = []
    for g in range(2 * KV_HEADS):
        source = key_ref if g < KV_HEADS else value_ref
        copy = pltpu.make_async_copy(
            source.at[:, part_of(g % KV_HEADS, HEAD_DIM)],
            out_ref.at[part_of(g, rows), :],
            sems.at[1 + g],
        )
        copy.start()
        copies.append(copy)
    doc_copy.wait()
    docs = jnp.broadcast_to(doc_scratch[...].astype(jnp.float32), (EXTRA, rows))
    start = 2 * KV_HEADS * rows
    out_ref[start : start + EXTRA, :] = docs.astype(jnp.bfloat16)
    for copy in copies:
        copy.wait()


def block_keys(ref, g):
    return ref[part_of(g, HEAD_DIM), :]


def block_values(ref, g):
    return ref[part_of(KV_HEADS + g, HEAD_DIM), :]


def block_docs(ref):
    start = 2 * KV_HEADS * HEAD_DIM
    return ref[start : start + EXTRA, :].astype(jnp.float32)[0:1, :]


class Plan:
    def __init__(self, n_seq):
        devices = 2 * n_seq
        near = [(b, b + 1) for b in range(devices - 1)]
        far = [(b, b + 2) for b in range(devices - 2)]
        first = [p for p in near if p[0] % 2 == 0 or p[0] // 2 % 2 == 1]
        last = [p for p in far if p[0] // 2 % 2 == 0]
        second = [p for p in near + far if p not in first + last]
        self.pairs = [first, second, last]
        self.senders = sorted({p[0] for p in first})
        busy = {b for p in second for b in p}
        self.idle = [b for b in range(devices) if b not in busy]


def among(members):
    block = 2 * lax.axis_index("seq") + lax.axis_index("kv")
    return functools.reduce(jnp.logical_or, [block == b for b in members])


def pack_kernel(plan, key_ref, value_ref, doc_ref, out_ref, doc_scratch, sems):
    @pl.when(among(plan.senders))
    def _():
        load_block(key_ref, value_ref, doc_ref, out_ref, doc_scratch, sems)


def attend_own(q_ref, block_ref, g, bias):
    rows = q_ref.shape[0]
    scores = dot(block_keys(block_ref, g), group_queries(q_ref, g), NT)
    tops, totals, weights = [], [], []
    for i in range(GROUPS):
        masked = scores[:, part_of(i, rows)] * SCALE + bias
        top = jnp.max(masked, axis=0, keepdims=True)
        weight = jnp.exp2(masked - top)
        tops.append(top)
        totals.append(jnp.sum(weight, axis=0, keepdims=True))
        weights.append(weight.astype(jnp.bfloat16))
    summed = dot(block_values(block_ref, g), jnp.concatenate(weights, axis=1), TN)
    return summed, jnp.concatenate(tops, axis=1), jnp.concatenate(totals, axis=1)


def own_bias(docs):
    rows = docs.shape[1]
    place = lax.broadcasted_iota(jnp.int32, (rows, rows), 0)
    row = lax.broadcasted_iota(jnp.int32, (rows, rows), 1)
    return jnp.where((place <= row) & (column(docs) == docs), 0.0, LOWEST)


def attend_itself(
    query_ref, block_ref, gain_ref, beta_ref, q_ref, summed_ref, stats_ref, gains_ref,
    beta_scratch, sems,
):
    copies = []
    for g in range(KV_HEADS):
        wide = part_of(g, GROUPS * HEAD_DIM)
        copies.append(
            pltpu.make_async_copy(query_ref.at[:, wide], q_ref.at[:, wide], sems.at[g])
        )
        copies[g].start()
    beta_copy = pltpu.make_async_copy(beta_ref, beta_scratch, sems.at[KV_HEADS])
    beta_copy.start()
    bias = own_bias(block_docs(block_ref))
    done = lax.axis_index("kv") == 0
    beta_copy.wait()
    scaled_gains(beta_scratch, gain_ref, gains_ref)
    for g in range(KV_HEADS):
        copies[g].wait()
        summed, top, total = attend_own(q_ref, block_ref, g, bias)
        rest = [1.0 - share_of(beta_scratch, g * GROUPS + i) for i in range(GROUPS)]
        rest = jnp.concatenate(rest, axis=1)
        summed_ref[part_of(g, HEAD_DIM), :] = summed * jnp.where(done, rest / total, 1.0)
        stats_ref[g : g + 1, :] = top
        stats_ref[KV_HEADS + g : KV_HEADS + g + 1, :] = total
        stats_ref[2 * KV_HEADS + g : 2 * KV_HEADS + g + 1, :] = rest


def settle_kernel(
    plan, gain_ref, packed_ref, query_ref, key_ref, value_ref, doc_ref, beta_ref,
    out_ref, q_ref, summed_ref, stats_ref, gains_ref, beta_scratch, doc_scratch, sems,
):
    sender = among(plan.senders)

    @pl.when(sender)
    def _():
        out_ref[...] = packed_ref[...]

    @pl.when(jnp.logical_not(sender))
    def _():
        load_block(key_ref, value_ref, doc_ref, out_ref, doc_scratch, sems)

    @pl.when(among(plan.idle))
    def _():
        attend_itself(
            query_ref, out_ref, gain_ref, beta_ref, q_ref, summed_ref, stats_ref, gains_ref,
            beta_scratch, sems,
        )


def own_kernel(
    plan, gain_ref, own_ref, query_ref, beta_ref, q_in, summed_in, stats_in, gains_in,
    q_ref, summed_ref, stats_ref, gains_ref, beta_scratch, sems,
):
    @pl.when(jnp.logical_not(among(plan.idle)))
    def _():
        attend_itself(
            query_ref, own_ref, gain_ref, beta_ref, q_ref, summed_ref, stats_ref, gains_ref,
            beta_scratch, sems,
        )


def before_kernel(q_ref, own_ref, one_ref, stats_ref, summed_in, summed_ref):
    @pl.when(lax.axis_index("kv") == 1)
    def _():
        docs = block_docs(own_ref)
        rows = docs.shape[1]
        first, same = first_document(docs)
        live = suffix(jnp.where(block_docs(one_ref) == first, 0.0, 1.0))
        bias = jnp.where(live & same, 0.0, LOWEST)
        for g in range(KV_HEADS):
            scores = dot(block_keys(one_ref, g), group_queries(q_ref, g), NT)
            weights, factors, scales = [], [], []
            for i in range(GROUPS):
                cut = part_of(i, rows)
                masked = scores[:, cut] * SCALE + bias
                top_own = stats_ref[g : g + 1, cut]
                top = jnp.maximum(jnp.max(masked, axis=0, keepdims=True), top_own)
                weight = jnp.exp2(masked - top)
                factor = jnp.exp2(top_own - top)
                total = stats_ref[KV_HEADS + g : KV_HEADS + g + 1, cut] * factor
                total = total + jnp.sum(weight, axis=0, keepdims=True)
                factors.append(factor)
                scales.append(stats_ref[2 * KV_HEADS + g : 2 * KV_HEADS + g + 1, cut] / total)
                weights.append(weight.astype(jnp.bfloat16))
            added = dot(block_values(one_ref, g), jnp.concatenate(weights, axis=1), TN)
            group = part_of(g, HEAD_DIM)
            summed = summed_ref[group, :] * jnp.concatenate(factors, axis=1) + added
            summed_ref[group, :] = summed * jnp.concatenate(scales, axis=1)


def join_kernel(
    q_ref, own_ref, one_ref, three_ref, two_ref, ready_ref, gains_ref, out_ref, held, sems
):
    docs = block_docs(own_ref)
    rows = docs.shape[1]
    first, same = first_document(docs)
    reads = jnp.where(same, 1.0, 0.0)
    sources = (one_ref, two_ref, three_ref)
    attended = (lax.axis_index("kv") == 1, False, False)
    lives = []
    for ref, other in zip(sources, attended):
        others = jnp.where((block_docs(ref) == first) & jnp.logical_not(other), 0.0, 1.0)
        lives.append(suffix(others))

    def copy(g):
        wide = part_of(g, GROUPS * HEAD_DIM)
        return pltpu.make_async_copy(held.at[:, wide], out_ref.at[:, wide], sems.at[g])

    for g in range(KV_HEADS):
        keys, values = [], []
        for ref, live in zip(sources, lives):
            masked = jnp.where(live, block_keys(ref, g).astype(jnp.float32), 0.0)
            keys.append(masked.astype(jnp.bfloat16))
            values.append(block_values(ref, g))
        state = dot(jnp.concatenate(values, axis=0), jnp.concatenate(keys, axis=0), TN)
        high = state.astype(jnp.bfloat16)
        state = state - high.astype(jnp.float32)
        middle = state.astype(jnp.bfloat16)
        low = (state - middle.astype(jnp.float32)).astype(jnp.bfloat16)
        pieces = dot(jnp.concatenate([high, middle, low], axis=0), group_queries(q_ref, g), NT)
        recalled = pieces[part_of(0, HEAD_DIM), :] + (
            pieces[part_of(1, HEAD_DIM), :] + pieces[part_of(2, HEAD_DIM), :]
        )
        for i in range(GROUPS):
            h, cut = g * GROUPS + i, part_of(i, rows)
            read = recalled[:, cut]
            square = jnp.sum(read * read, axis=0, keepdims=True) * (1.0 / HEAD_DIM)
            read = read * (lax.rsqrt(square + 1e-06) * reads)
            mixed = read * gains_ref[part_of(h, HEAD_DIM), :]
            mixed = mixed + ready_ref[part_of(g, HEAD_DIM), cut]
            held[:, part_of(h, HEAD_DIM)] = jnp.transpose(mixed)
        copy(g).start()
    for g in range(KV_HEADS):
        copy(g).wait()


def near_device(n_seq, queries, keys, values, doc_ids, beta, lin_gain):
    rows = queries.shape[0]
    vmem = pl.BlockSpec(memory_space=pltpu.VMEM)
    hbm = pl.BlockSpec(memory_space=pltpu.HBM)
    in_hbm = functools.partial(pltpu.with_memory_space_constraint, memory_space=pltpu.HBM)
    params = pltpu.CompilerParams(vmem_limit_bytes=32 * 1024 * 1024)
    wide = GROUPS * rows
    group_shape = jax.ShapeDtypeStruct((KV_HEADS * HEAD_DIM, wide), jnp.float32)
    gains_shape = jax.ShapeDtypeStruct((HEADS * HEAD_DIM, HEAD_DIM), jnp.float32)
    docs = doc_ids.reshape(1, rows)
    gain = lin_gain.reshape(HEADS, HEAD_DIM)
    deep = 2 * KV_HEADS * rows + EXTRA

    def estimate(share):
        return pl.CostEstimate(
            flops=int(share * 4 * HEADS * HEAD_DIM * rows * rows),
            bytes_accessed=int(share * 4 * 1024 * 1024),
            transcendentals=int(share * HEADS * rows * rows),
        )

    def send(payload, pairs):
        return lax.ppermute(payload, ("seq", "kv"), pairs)

    plan = Plan(n_seq)
    block_shape = jax.ShapeDtypeStruct((deep, HEAD_DIM), jnp.bfloat16)
    query_shape = jax.ShapeDtypeStruct(queries.shape, queries.dtype)
    stats_shape = jax.ShapeDtypeStruct((4 * KV_HEADS, wide), jnp.float32)
    results = [query_shape, group_shape, stats_shape, gains_shape]
    doc_scratch = pltpu.VMEM((1, rows), jnp.int32)
    beta_scratch = pltpu.SMEM((HEADS,), jnp.float32)
    sems = pltpu.SemaphoreType.DMA((2 * KV_HEADS + 1,))
    block = (in_hbm(keys), in_hbm(values), in_hbm(docs))
    queries, beta = in_hbm(queries), in_hbm(beta)
    packed = pl.pallas_call(
        functools.partial(pack_kernel, plan),
        out_shape=block_shape,
        in_specs=[hbm] * 3,
        out_specs=vmem,
        scratch_shapes=[doc_scratch, sems],
        compiler_params=params,
        cost_estimate=estimate(0.1),
    )(*block)
    one = send(packed, plan.pairs[0])
    own, q, summed, stats, gains = pl.pallas_call(
        functools.partial(settle_kernel, plan),
        out_shape=[block_shape] + results,
        in_specs=[vmem] * 2 + [hbm] * 5,
        out_specs=[vmem] * 5,
        scratch_shapes=[beta_scratch, doc_scratch, sems],
        compiler_params=params,
        cost_estimate=estimate(1.0),
    )(gain, packed, queries, *block, beta)
    two = send(own, plan.pairs[1])
    three = send(own, plan.pairs[2])
    q, summed, stats, gains = pl.pallas_call(
        functools.partial(own_kernel, plan),
        out_shape=results,
        in_specs=[vmem] * 2 + [hbm] * 2 + [vmem] * 4,
        out_specs=[vmem] * 4,
        scratch_shapes=[beta_scratch, sems],
        input_output_aliases={4: 0, 5: 1, 6: 2, 7: 3},
        compiler_params=params,
        cost_estimate=estimate(1.0),
    )(gain, own, queries, beta, q, summed, stats, gains)
    ready = pl.pallas_call(
        before_kernel,
        out_shape=group_shape,
        in_specs=[vmem] * 5,
        out_specs=vmem,
        input_output_aliases={4: 0},
        compiler_params=params,
        cost_estimate=estimate(1.0),
    )(q, own, one, stats, summed)
    return pl.pallas_call(
        join_kernel,
        out_shape=jax.ShapeDtypeStruct((rows, HEADS * HEAD_DIM), jnp.float32),
        in_specs=[vmem] * 7,
        out_specs=hbm,
        scratch_shapes=[
            pltpu.VMEM((rows, HEADS * HEAD_DIM), jnp.float32),
            pltpu.SemaphoreType.DMA((KV_HEADS,)),
        ],
        compiler_params=params,
    )(q, own, one, three, two, ready, gains)


def carried_in(part, axis, combine, identity):
    place = lax.axis_index(axis)
    gathered = jax.tree.map(lambda a: lax.all_gather(a, axis), part)
    state = jax.tree.map(lambda a, e: jnp.zeros_like(a) + jnp.asarray(e, a.dtype), part, identity)

    def one(step, state):
        return combine(
            state, jax.tree.map(lambda a: lax.dynamic_index_in_dim(a, step, 0, False), gathered)
        )

    return lax.fori_loop(0, place, one, state)


def join_states(earlier, later):
    state_early, first_early, last_early = earlier
    state_late, first_late, last_late = later
    empty_late = first_late < 0
    joined = (first_late == last_late) & (last_early == first_late)
    merged = state_late + jnp.where(joined, state_early, jnp.zeros_like(state_early))
    combined = jnp.where(empty_late, state_early, merged)
    first_doc = jnp.where(first_early < 0, first_late, first_early)
    last_doc = jnp.where(empty_late, last_early, last_late)
    return (combined, first_doc, last_doc)


def tail_merge(one_side, other_side):
    state_one, first_one, last_one = one_side
    state_other, first_other, last_other = other_side
    top_doc = jnp.maximum(last_one, last_other)
    state_sum = jnp.where(last_one == top_doc, state_one, jnp.zeros_like(state_one))
    state_sum = state_sum + jnp.where(
        last_other == top_doc, state_other, jnp.zeros_like(state_other)
    )
    return (state_sum, jnp.minimum(first_one, first_other), top_doc)


def tail_state(key_rows, value_rows, doc_rows, target_doc):
    count = key_rows.shape[0]
    key_heads = key_rows.reshape(count, KV_HEADS, HEAD_DIM)
    value_heads = value_rows.reshape(count, KV_HEADS, HEAD_DIM)
    live = doc_rows == target_doc
    masked = jnp.where(live[:, None, None], key_heads, jnp.zeros_like(key_heads))
    return jnp.einsum("rgd,rge->gde", masked, value_heads, preferred_element_type=jnp.float32)


def attend_block(
    carry, query_heads, query_pos, query_doc, key_rows, value_rows, key_doc, key_start
):
    running_max, running_sum, accumulated = carry
    key_count = key_rows.shape[0]
    key_heads = key_rows.reshape(key_count, KV_HEADS, HEAD_DIM)
    value_heads = value_rows.reshape(key_count, KV_HEADS, HEAD_DIM)
    scores = jnp.einsum(
        "rgqd,kgd->gqrk", query_heads, key_heads, preferred_element_type=jnp.float32
    )
    scores = scores / jnp.sqrt(jnp.float32(HEAD_DIM))
    key_pos = key_start + jnp.arange(key_count, dtype=jnp.int32)
    allowed = (key_pos[None, :] <= query_pos[:, None]) & (key_doc[None, :] == query_doc[:, None])
    masked = jnp.where(allowed, scores, jnp.float32(-1e30))
    new_max = jnp.maximum(running_max, jnp.max(masked, axis=-1))
    factor = jnp.exp(running_max - new_max)
    weights = jnp.where(allowed, jnp.exp(masked - new_max[..., None]), jnp.float32(0.0))
    new_sum = running_sum * factor + jnp.sum(weights, axis=-1)
    product = jnp.einsum(
        "gqrk,kge->gqre",
        weights.astype(jnp.bfloat16),
        value_heads,
        preferred_element_type=jnp.float32,
    )
    new_accum = accumulated * factor[..., None] + product
    return (new_max, new_sum, new_accum)


def far_device(queries, keys, values, doc_ids, beta, lin_gain):
    row_count = queries.shape[0]
    groups = HEADS // KV_HEADS
    query_heads = queries.reshape(row_count, KV_HEADS, groups, HEAD_DIM)
    position = lax.axis_index("kv") * row_count
    query_pos = position + jnp.arange(row_count, dtype=jnp.int32)
    last_query = position + row_count - 1
    initial = (
        jnp.full((KV_HEADS, groups, row_count), -1e30, jnp.float32),
        jnp.zeros((KV_HEADS, groups, row_count), jnp.float32),
        jnp.zeros((KV_HEADS, groups, row_count, HEAD_DIM), jnp.float32),
    )
    empty_tail = (
        jnp.zeros((KV_HEADS, HEAD_DIM, HEAD_DIM), jnp.float32),
        jnp.array(2**30, jnp.int32),
        jnp.array(-1, jnp.int32),
    )
    key_piece = lax.all_gather(keys, "kv", axis=0, tiled=True)
    value_piece = lax.all_gather(values, "kv", axis=0, tiled=True)
    doc_piece = lax.all_gather(doc_ids, "kv", axis=0, tiled=True)
    blocks = key_piece.shape[0] // row_count

    def one_block(state, item):
        soft_state, tail_now = state
        key_block, value_block, doc_block, number = item
        block_start = number * row_count
        soft_next = lax.cond(
            block_start <= last_query,
            lambda inner: attend_block(
                inner,
                query_heads,
                query_pos,
                doc_ids,
                key_block,
                value_block,
                doc_block,
                block_start,
            ),
            lambda inner: inner,
            soft_state,
        )
        block_tail = (
            tail_state(key_block, value_block, doc_block, doc_block[-1]),
            doc_block[0],
            doc_block[-1],
        )
        tail_now = tail_merge(tail_now, block_tail)
        return ((soft_next, tail_now), None)

    stacked = (
        key_piece.reshape(blocks, row_count, -1),
        value_piece.reshape(blocks, row_count, -1),
        doc_piece.reshape(blocks, row_count),
        jnp.arange(blocks, dtype=jnp.int32),
    )
    result, _ = lax.scan(one_block, (initial, empty_tail), stacked)
    running, segment_tail = result
    running_max, running_sum, accumulated = running
    soft_out = jnp.transpose(accumulated / running_sum[..., None], (2, 0, 1, 3))
    identity = (
        jnp.zeros((KV_HEADS, HEAD_DIM, HEAD_DIM), jnp.float32),
        jnp.array(-1, jnp.int32),
        jnp.array(-1, jnp.int32),
    )
    memory = carried_in(segment_tail, "seq", join_states, identity)
    memory_state, memory_first, memory_last = memory
    query_float = query_heads.astype(jnp.float32)
    recalled = jnp.einsum(
        "rgqd,gde->rgqe", query_float, memory_state, precision=lax.Precision.HIGHEST
    )
    recalled = jnp.where((doc_ids == memory_last)[:, None, None, None], recalled, jnp.float32(0.0))
    mean_square = jnp.mean(recalled * recalled, axis=-1, keepdims=True)
    normed = (
        recalled * lax.rsqrt(mean_square + 1e-06) * lin_gain.reshape(KV_HEADS, groups, HEAD_DIM)
    )
    mixing = jax.nn.sigmoid(beta).reshape(KV_HEADS, groups)[None, :, :, None]
    mixed = mixing * normed + (1.0 - mixing) * soft_out
    return mixed.reshape(row_count, HEADS * HEAD_DIM).astype(jnp.float32)


def solution(mesh):
    n_seq, n_kv = mesh.shape["seq"], mesh.shape["kv"]
    in_specs = (
        P(("dp", "seq", "kv"), None),
        P(("dp", "seq", "kv"), None),
        P(("dp", "seq", "kv"), None),
        P(("dp", "seq", "kv")),
        P(),
        P(),
    )
    out_specs = P(("dp", "seq", "kv"), None)
    if n_kv == 2 and n_seq * n_kv <= 2 * LONGEST:
        on_device = functools.partial(near_device, n_seq)
    else:
        on_device = far_device
    return jax.shard_map(
        on_device, mesh=mesh, in_specs=in_specs, out_specs=out_specs, check_vma=False
    )
```

```python
import functools
import math

import jax
import jax.numpy as jnp
from jax import lax
from jax.experimental import pallas as pl
from jax.experimental.pallas import tpu as pltpu
from jax.sharding import PartitionSpec as P

HEADS = 16
KV_HEADS = 4
HEAD_DIM = 128
GROUPS = HEADS // KV_HEADS
LONGEST = 4
SCALE = math.log2(math.e) / math.sqrt(HEAD_DIM)
LOWEST = -1e30
EXTRA = 16

NT = (((1,), (1,)), ((), ()))
TN = (((0,), (0,)), ((), ()))
NN = (((1,), (0,)), ((), ()))


def dot(a, b, dims):
    return lax.dot_general(a, b, dims, preferred_element_type=jnp.float32)


def column(row):
    return jnp.transpose(jnp.broadcast_to(row, (HEAD_DIM, row.shape[1])))


def part_of(i, size):
    return slice(i * size, (i + 1) * size)


def group_queries(q_ref, g):
    heads = [q_ref[:, part_of(g * GROUPS + i, HEAD_DIM)] for i in range(GROUPS)]
    return jnp.concatenate(heads, axis=0)


def share_of(beta_ref, h):
    return 1.0 / (1.0 + jnp.exp(-jnp.full((1, HEAD_DIM), beta_ref[h], jnp.float32)))


def suffix(others):
    count = jnp.sum(others, axis=1, keepdims=True)
    shape = (others.shape[1], HEAD_DIM)
    return lax.broadcasted_iota(jnp.int32, shape, 0).astype(jnp.float32) >= count


def first_document(docs):
    first = jnp.broadcast_to(docs[:, 0:1], docs.shape)
    return first, docs == first


def load_block(key_ref, value_ref, doc_ref, out_ref, doc_scratch, sems):
    rows = key_ref.shape[0]
    doc_copy = pltpu.make_async_copy(doc_ref, doc_scratch, sems.at[0])
    doc_copy.start()
    copies = []
    for g in range(2 * KV_HEADS):
        source = key_ref if g < KV_HEADS else value_ref
        copy = pltpu.make_async_copy(
            source.at[:, part_of(g % KV_HEADS, HEAD_DIM)],
            out_ref.at[part_of(g, rows), :],
            sems.at[1 + g],
        )
        copy.start()
        copies.append(copy)
    doc_copy.wait()
    docs = jnp.broadcast_to(doc_scratch[...].astype(jnp.float32), (EXTRA, rows))
    start = 2 * KV_HEADS * rows
    out_ref[start : start + EXTRA, :] = docs.astype(jnp.bfloat16)
    for copy in copies:
        copy.wait()


def block_keys(ref, g):
    return ref[part_of(g, HEAD_DIM), :]


def block_values(ref, g):
    return ref[part_of(KV_HEADS + g, HEAD_DIM), :]


def block_docs(ref):
    start = 2 * KV_HEADS * HEAD_DIM
    return ref[start : start + EXTRA, :].astype(jnp.float32)[0:1, :]


class Plan:
    def __init__(self, n_seq):
        devices = 2 * n_seq
        near = [(b, b + 1) for b in range(devices - 1)]
        far = [(b, b + 2) for b in range(devices - 2)]
        first = [p for p in near if p[0] % 2 == 0 or p[0] // 2 % 2 == 1]
        last = [p for p in far if p[0] // 2 % 2 == 0]
        second = [p for p in near + far if p not in first + last]
        self.pairs = [first, second, last]
        self.senders = sorted({p[0] for p in first})
        busy = {p[0] for p in second if p[0] in self.senders} | {p[1] for p in second}
        self.early = [b for b in range(devices) if b not in busy]


def among(members):
    block = 2 * lax.axis_index("seq") + lax.axis_index("kv")
    return functools.reduce(jnp.logical_or, [block == b for b in members])


def pack_kernel(plan, key_ref, value_ref, doc_ref, out_ref, doc_scratch, sems):
    @pl.when(among(plan.senders))
    def _():
        load_block(key_ref, value_ref, doc_ref, out_ref, doc_scratch, sems)


def attend_own(q_ref, block_ref, g, bias):
    rows = q_ref.shape[0]
    scores = dot(block_keys(block_ref, g), group_queries(q_ref, g), NT)
    tops, totals, weights = [], [], []
    for i in range(GROUPS):
        masked = scores[:, part_of(i, rows)] * SCALE + bias
        top = jnp.max(masked, axis=0, keepdims=True)
        weight = jnp.exp2(masked - top)
        tops.append(top)
        totals.append(jnp.sum(weight, axis=0, keepdims=True))
        weights.append(weight.astype(jnp.bfloat16))
    summed = dot(block_values(block_ref, g), jnp.concatenate(weights, axis=1), TN)
    return summed, jnp.concatenate(tops, axis=1), jnp.concatenate(totals, axis=1)


def own_bias(docs):
    rows = docs.shape[1]
    place = lax.broadcasted_iota(jnp.int32, (rows, rows), 0)
    row = lax.broadcasted_iota(jnp.int32, (rows, rows), 1)
    return jnp.where((place <= row) & (column(docs) == docs), 0.0, LOWEST)


def attend_itself(
    q_ref, block_ref, gain_ref, beta_ref, beta_copy, ready_ref, summed_ref, stats_ref, gains_ref
):
    bias = own_bias(block_docs(block_ref))
    rows = bias.shape[0]
    done = lax.axis_index("kv") == 0
    for g in range(KV_HEADS):
        summed, top, total = attend_own(q_ref, block_ref, g, bias)
        if g == 0:
            beta_copy.wait()
        shares = [share_of(beta_ref, g * GROUPS + i) for i in range(GROUPS)]
        rest = jnp.concatenate([1.0 - share for share in shares], axis=1)
        for i in range(GROUPS):
            h = g * GROUPS + i
            gains_ref[h : h + 1, :] = gain_ref[h : h + 1, :] * shares[i]

        @pl.when(done)
        def _():
            scaled = summed * (rest / total)
            for i in range(GROUPS):
                part = jnp.transpose(scaled[:, part_of(i, rows)])
                ready_ref[:, part_of(g * GROUPS + i, HEAD_DIM)] = part

        @pl.when(jnp.logical_not(done))
        def _():
            summed_ref[part_of(g, HEAD_DIM), :] = summed
            stats_ref[g : g + 1, :] = top
            stats_ref[KV_HEADS + g : KV_HEADS + g + 1, :] = total
            stats_ref[2 * KV_HEADS + g : 2 * KV_HEADS + g + 1, :] = rest


def settle_kernel(
    plan, gain_ref, packed_ref, query_ref, key_ref, value_ref, doc_ref, beta_ref,
    out_ref, ready_ref, summed_ref, stats_ref, gains_ref,
    q_scratch, beta_scratch, doc_scratch, sems, early_sems,
):
    sender, early = among(plan.senders), among(plan.early)
    query_copy = pltpu.make_async_copy(query_ref, q_scratch, early_sems.at[0])
    beta_copy = pltpu.make_async_copy(beta_ref, beta_scratch, early_sems.at[1])

    @pl.when(early)
    def _():
        query_copy.start()
        beta_copy.start()

    @pl.when(sender)
    def _():
        out_ref[...] = packed_ref[...]

    @pl.when(jnp.logical_not(sender))
    def _():
        load_block(key_ref, value_ref, doc_ref, out_ref, doc_scratch, sems)

    @pl.when(early)
    def _():
        query_copy.wait()
        attend_itself(
            q_scratch, out_ref, gain_ref, beta_scratch, beta_copy,
            ready_ref, summed_ref, stats_ref, gains_ref,
        )


def own_kernel(
    plan, q_ref, gain_ref, own_ref, beta_ref, ready_in, summed_in, stats_in, gains_in,
    ready_ref, summed_ref, stats_ref, gains_ref, beta_scratch, sem,
):
    @pl.when(jnp.logical_not(among(plan.early)))
    def _():
        beta_copy = pltpu.make_async_copy(beta_ref, beta_scratch, sem)
        beta_copy.start()
        attend_itself(
            q_ref, own_ref, gain_ref, beta_scratch, beta_copy,
            ready_ref, summed_ref, stats_ref, gains_ref,
        )


def before_kernel(q_ref, own_ref, one_ref, stats_ref, summed_ref, ready_in, ready_ref):
    @pl.when(lax.axis_index("kv") == 1)
    def _():
        docs = block_docs(own_ref)
        rows = docs.shape[1]
        first, same = first_document(docs)
        live = suffix(jnp.where(block_docs(one_ref) == first, 0.0, 1.0))
        bias = jnp.where(live & same, 0.0, LOWEST)
        for g in range(KV_HEADS):
            scores = dot(block_keys(one_ref, g), group_queries(q_ref, g), NT)
            weights, factors, scales = [], [], []
            for i in range(GROUPS):
                cut = part_of(i, rows)
                masked = scores[:, cut] * SCALE + bias
                top_own = stats_ref[g : g + 1, cut]
                top = jnp.maximum(jnp.max(masked, axis=0, keepdims=True), top_own)
                weight = jnp.exp2(masked - top)
                factor = jnp.exp2(top_own - top)
                total = stats_ref[KV_HEADS + g : KV_HEADS + g + 1, cut] * factor
                total = total + jnp.sum(weight, axis=0, keepdims=True)
                factors.append(factor)
                scales.append(stats_ref[2 * KV_HEADS + g : 2 * KV_HEADS + g + 1, cut] / total)
                weights.append(weight.astype(jnp.bfloat16))
            added = dot(block_values(one_ref, g), jnp.concatenate(weights, axis=1), TN)
            group = part_of(g, HEAD_DIM)
            summed = summed_ref[group, :] * jnp.concatenate(factors, axis=1) + added
            summed = summed * jnp.concatenate(scales, axis=1)
            for i in range(GROUPS):
                part = jnp.transpose(summed[:, part_of(i, rows)])
                ready_ref[:, part_of(g * GROUPS + i, HEAD_DIM)] = part


def join_kernel(
    q_ref, own_ref, one_ref, three_ref, two_ref, ready_ref, gains_ref, out_ref, held, sems
):
    docs = block_docs(own_ref)
    rows = docs.shape[1]
    first, same = first_document(docs)
    reads = column(jnp.where(same, 1.0, 0.0))
    ones = jnp.full((2 * HEAD_DIM, HEAD_DIM), 1.0 / HEAD_DIM, jnp.bfloat16)
    sources = (one_ref, two_ref, three_ref)
    attended = (lax.axis_index("kv") == 1, False, False)
    lives = []
    for ref, other in zip(sources, attended):
        others = jnp.where((block_docs(ref) == first) & jnp.logical_not(other), 0.0, 1.0)
        lives.append(suffix(others))

    def copy(g):
        wide = part_of(g, GROUPS * HEAD_DIM)
        return pltpu.make_async_copy(held.at[:, wide], out_ref.at[:, wide], sems.at[g])

    for g in range(KV_HEADS):
        keys, values = [], []
        for ref, live in zip(sources, lives):
            masked = jnp.where(live, block_keys(ref, g).astype(jnp.float32), 0.0)
            keys.append(masked.astype(jnp.bfloat16))
            values.append(block_values(ref, g))
        state = dot(jnp.concatenate(keys, axis=0), jnp.concatenate(values, axis=0), TN)
        high = state.astype(jnp.bfloat16)
        state = state - high.astype(jnp.float32)
        middle = state.astype(jnp.bfloat16)
        low = (state - middle.astype(jnp.float32)).astype(jnp.bfloat16)
        pieces = dot(group_queries(q_ref, g), jnp.concatenate([high, middle, low], axis=1), NN)
        recalled = pieces[:, part_of(0, HEAD_DIM)] + (
            pieces[:, part_of(1, HEAD_DIM)] + pieces[:, part_of(2, HEAD_DIM)]
        )
        square = recalled * recalled
        high = square.astype(jnp.bfloat16)
        low = (square - high.astype(jnp.float32)).astype(jnp.bfloat16)
        mean = dot(jnp.concatenate([high, low], axis=1), ones, NN)
        for i in range(GROUPS):
            h, cut = g * GROUPS + i, part_of(i, rows)
            wide = part_of(h, HEAD_DIM)
            read = recalled[cut, :] * (lax.rsqrt(mean[cut, :] + 1e-06) * reads)
            held[:, wide] = read * gains_ref[h : h + 1, :] + ready_ref[:, wide]
        copy(g).start()
    for g in range(KV_HEADS):
        copy(g).wait()


def near_device(n_seq, queries, keys, values, doc_ids, beta, lin_gain):
    rows = queries.shape[0]
    vmem = pl.BlockSpec(memory_space=pltpu.VMEM)
    hbm = pl.BlockSpec(memory_space=pltpu.HBM)
    in_hbm = functools.partial(pltpu.with_memory_space_constraint, memory_space=pltpu.HBM)
    params = pltpu.CompilerParams(vmem_limit_bytes=32 * 1024 * 1024)
    wide = GROUPS * rows
    group_shape = jax.ShapeDtypeStruct((KV_HEADS * HEAD_DIM, wide), jnp.float32)
    docs = doc_ids.reshape(1, rows)
    gain = lin_gain.reshape(HEADS, HEAD_DIM)
    deep = 2 * KV_HEADS * rows + EXTRA

    def estimate(share):
        return pl.CostEstimate(
            flops=int(share * 4 * HEADS * HEAD_DIM * rows * rows),
            bytes_accessed=int(share * 4 * 1024 * 1024),
            transcendentals=int(share * HEADS * rows * rows),
        )

    def send(payload, pairs):
        return lax.ppermute(payload, ("seq", "kv"), pairs)

    plan = Plan(n_seq)
    block_shape = jax.ShapeDtypeStruct((deep, HEAD_DIM), jnp.bfloat16)
    stats_shape = jax.ShapeDtypeStruct((4 * KV_HEADS, wide), jnp.float32)
    out_shape = jax.ShapeDtypeStruct((rows, HEADS * HEAD_DIM), jnp.float32)
    gains_shape = jax.ShapeDtypeStruct((HEADS, HEAD_DIM), jnp.float32)
    results = [out_shape, group_shape, stats_shape, gains_shape]
    doc_scratch = pltpu.VMEM((1, rows), jnp.int32)
    beta_scratch = pltpu.SMEM((HEADS,), jnp.float32)
    sems = pltpu.SemaphoreType.DMA((2 * KV_HEADS + 1,))
    block = (in_hbm(keys), in_hbm(values), in_hbm(docs))
    beta = in_hbm(beta)
    packed = pl.pallas_call(
        functools.partial(pack_kernel, plan),
        out_shape=block_shape,
        in_specs=[hbm] * 3,
        out_specs=vmem,
        scratch_shapes=[doc_scratch, sems],
        compiler_params=params,
        cost_estimate=estimate(0.1),
    )(*block)
    one = send(packed, plan.pairs[0])
    own, ready, summed, stats, gains = pl.pallas_call(
        functools.partial(settle_kernel, plan),
        out_shape=[block_shape] + results,
        in_specs=[vmem] * 2 + [hbm] * 5,
        out_specs=[vmem] * 5,
        scratch_shapes=[
            pltpu.VMEM(queries.shape, queries.dtype),
            beta_scratch,
            doc_scratch,
            sems,
            pltpu.SemaphoreType.DMA((2,)),
        ],
        compiler_params=params,
        cost_estimate=estimate(1.0),
    )(gain, packed, in_hbm(queries), *block, beta)
    two = send(own, plan.pairs[1])
    three = send(own, plan.pairs[2])
    ready, summed, stats, gains = pl.pallas_call(
        functools.partial(own_kernel, plan),
        out_shape=results,
        in_specs=[vmem] * 3 + [hbm] + [vmem] * 4,
        out_specs=[vmem] * 4,
        scratch_shapes=[beta_scratch, pltpu.SemaphoreType.DMA],
        input_output_aliases={4: 0, 5: 1, 6: 2, 7: 3},
        compiler_params=params,
        cost_estimate=estimate(1.0),
    )(queries, gain, own, beta, ready, summed, stats, gains)
    ready = pl.pallas_call(
        before_kernel,
        out_shape=out_shape,
        in_specs=[vmem] * 6,
        out_specs=vmem,
        input_output_aliases={5: 0},
        compiler_params=params,
        cost_estimate=estimate(1.0),
    )(queries, own, one, stats, summed, ready)
    return pl.pallas_call(
        join_kernel,
        out_shape=out_shape,
        in_specs=[vmem] * 7,
        out_specs=hbm,
        scratch_shapes=[
            pltpu.VMEM((rows, HEADS * HEAD_DIM), jnp.float32),
            pltpu.SemaphoreType.DMA((KV_HEADS,)),
        ],
        compiler_params=params,
    )(queries, own, one, three, two, ready, gains)


def carried_in(part, axis, combine, identity):
    place = lax.axis_index(axis)
    gathered = jax.tree.map(lambda a: lax.all_gather(a, axis), part)
    state = jax.tree.map(lambda a, e: jnp.zeros_like(a) + jnp.asarray(e, a.dtype), part, identity)

    def one(step, state):
        return combine(
            state, jax.tree.map(lambda a: lax.dynamic_index_in_dim(a, step, 0, False), gathered)
        )

    return lax.fori_loop(0, place, one, state)


def join_states(earlier, later):
    state_early, first_early, last_early = earlier
    state_late, first_late, last_late = later
    empty_late = first_late < 0
    joined = (first_late == last_late) & (last_early == first_late)
    merged = state_late + jnp.where(joined, state_early, jnp.zeros_like(state_early))
    combined = jnp.where(empty_late, state_early, merged)
    first_doc = jnp.where(first_early < 0, first_late, first_early)
    last_doc = jnp.where(empty_late, last_early, last_late)
    return (combined, first_doc, last_doc)


def tail_merge(one_side, other_side):
    state_one, first_one, last_one = one_side
    state_other, first_other, last_other = other_side
    top_doc = jnp.maximum(last_one, last_other)
    state_sum = jnp.where(last_one == top_doc, state_one, jnp.zeros_like(state_one))
    state_sum = state_sum + jnp.where(
        last_other == top_doc, state_other, jnp.zeros_like(state_other)
    )
    return (state_sum, jnp.minimum(first_one, first_other), top_doc)


def tail_state(key_rows, value_rows, doc_rows, target_doc):
    count = key_rows.shape[0]
    key_heads = key_rows.reshape(count, KV_HEADS, HEAD_DIM)
    value_heads = value_rows.reshape(count, KV_HEADS, HEAD_DIM)
    live = doc_rows == target_doc
    masked = jnp.where(live[:, None, None], key_heads, jnp.zeros_like(key_heads))
    return jnp.einsum("rgd,rge->gde", masked, value_heads, preferred_element_type=jnp.float32)


def attend_block(
    carry, query_heads, query_pos, query_doc, key_rows, value_rows, key_doc, key_start
):
    running_max, running_sum, accumulated = carry
    key_count = key_rows.shape[0]
    key_heads = key_rows.reshape(key_count, KV_HEADS, HEAD_DIM)
    value_heads = value_rows.reshape(key_count, KV_HEADS, HEAD_DIM)
    scores = jnp.einsum(
        "rgqd,kgd->gqrk", query_heads, key_heads, preferred_element_type=jnp.float32
    )
    scores = scores / jnp.sqrt(jnp.float32(HEAD_DIM))
    key_pos = key_start + jnp.arange(key_count, dtype=jnp.int32)
    allowed = (key_pos[None, :] <= query_pos[:, None]) & (key_doc[None, :] == query_doc[:, None])
    masked = jnp.where(allowed, scores, jnp.float32(-1e30))
    new_max = jnp.maximum(running_max, jnp.max(masked, axis=-1))
    factor = jnp.exp(running_max - new_max)
    weights = jnp.where(allowed, jnp.exp(masked - new_max[..., None]), jnp.float32(0.0))
    new_sum = running_sum * factor + jnp.sum(weights, axis=-1)
    product = jnp.einsum(
        "gqrk,kge->gqre",
        weights.astype(jnp.bfloat16),
        value_heads,
        preferred_element_type=jnp.float32,
    )
    new_accum = accumulated * factor[..., None] + product
    return (new_max, new_sum, new_accum)


def far_device(queries, keys, values, doc_ids, beta, lin_gain):
    row_count = queries.shape[0]
    groups = HEADS // KV_HEADS
    query_heads = queries.reshape(row_count, KV_HEADS, groups, HEAD_DIM)
    position = lax.axis_index("kv") * row_count
    query_pos = position + jnp.arange(row_count, dtype=jnp.int32)
    last_query = position + row_count - 1
    initial = (
        jnp.full((KV_HEADS, groups, row_count), -1e30, jnp.float32),
        jnp.zeros((KV_HEADS, groups, row_count), jnp.float32),
        jnp.zeros((KV_HEADS, groups, row_count, HEAD_DIM), jnp.float32),
    )
    empty_tail = (
        jnp.zeros((KV_HEADS, HEAD_DIM, HEAD_DIM), jnp.float32),
        jnp.array(2**30, jnp.int32),
        jnp.array(-1, jnp.int32),
    )
    key_piece = lax.all_gather(keys, "kv", axis=0, tiled=True)
    value_piece = lax.all_gather(values, "kv", axis=0, tiled=True)
    doc_piece = lax.all_gather(doc_ids, "kv", axis=0, tiled=True)
    blocks = key_piece.shape[0] // row_count

    def one_block(state, item):
        soft_state, tail_now = state
        key_block, value_block, doc_block, number = item
        block_start = number * row_count
        soft_next = lax.cond(
            block_start <= last_query,
            lambda inner: attend_block(
                inner,
                query_heads,
                query_pos,
                doc_ids,
                key_block,
                value_block,
                doc_block,
                block_start,
            ),
            lambda inner: inner,
            soft_state,
        )
        block_tail = (
            tail_state(key_block, value_block, doc_block, doc_block[-1]),
            doc_block[0],
            doc_block[-1],
        )
        tail_now = tail_merge(tail_now, block_tail)
        return ((soft_next, tail_now), None)

    stacked = (
        key_piece.reshape(blocks, row_count, -1),
        value_piece.reshape(blocks, row_count, -1),
        doc_piece.reshape(blocks, row_count),
        jnp.arange(blocks, dtype=jnp.int32),
    )
    result, _ = lax.scan(one_block, (initial, empty_tail), stacked)
    running, segment_tail = result
    running_max, running_sum, accumulated = running
    soft_out = jnp.transpose(accumulated / running_sum[..., None], (2, 0, 1, 3))
    identity = (
        jnp.zeros((KV_HEADS, HEAD_DIM, HEAD_DIM), jnp.float32),
        jnp.array(-1, jnp.int32),
        jnp.array(-1, jnp.int32),
    )
    memory = carried_in(segment_tail, "seq", join_states, identity)
    memory_state, memory_first, memory_last = memory
    query_float = query_heads.astype(jnp.float32)
    recalled = jnp.einsum(
        "rgqd,gde->rgqe", query_float, memory_state, precision=lax.Precision.HIGHEST
    )
    recalled = jnp.where((doc_ids == memory_last)[:, None, None, None], recalled, jnp.float32(0.0))
    mean_square = jnp.mean(recalled * recalled, axis=-1, keepdims=True)
    normed = (
        recalled * lax.rsqrt(mean_square + 1e-06) * lin_gain.reshape(KV_HEADS, groups, HEAD_DIM)
    )
    mixing = jax.nn.sigmoid(beta).reshape(KV_HEADS, groups)[None, :, :, None]
    mixed = mixing * normed + (1.0 - mixing) * soft_out
    return mixed.reshape(row_count, HEADS * HEAD_DIM).astype(jnp.float32)


def solution(mesh):
    n_seq, n_kv = mesh.shape["seq"], mesh.shape["kv"]
    in_specs = (
        P(("dp", "seq", "kv"), None),
        P(("dp", "seq", "kv"), None),
        P(("dp", "seq", "kv"), None),
        P(("dp", "seq", "kv")),
        P(),
        P(),
    )
    out_specs = P(("dp", "seq", "kv"), None)
    if n_kv == 2 and n_seq * n_kv <= 2 * LONGEST:
        on_device = functools.partial(near_device, n_seq)
    else:
        on_device = far_device
    return jax.shard_map(
        on_device, mesh=mesh, in_specs=in_specs, out_specs=out_specs, check_vma=False
    )
```

```python
import functools
import math

import jax
import jax.numpy as jnp
from jax import lax
from jax.experimental import pallas as pl
from jax.experimental.pallas import tpu as pltpu
from jax.sharding import PartitionSpec as P

HEADS = 16
KV_HEADS = 4
HEAD_DIM = 128
GROUPS = HEADS // KV_HEADS
LONGEST = 4
SCALE = math.log2(math.e) / math.sqrt(HEAD_DIM)
LOWEST = -1e30
EXTRA = 16

NT = (((1,), (1,)), ((), ()))
TN = (((0,), (0,)), ((), ()))


def dot(a, b, dims):
    return lax.dot_general(a, b, dims, preferred_element_type=jnp.float32)


def column(row):
    return jnp.transpose(jnp.broadcast_to(row, (HEAD_DIM, row.shape[1])))


def part_of(i, size):
    return slice(i * size, (i + 1) * size)


def group_queries(q_ref, g):
    heads = [q_ref[:, part_of(g * GROUPS + i, HEAD_DIM)] for i in range(GROUPS)]
    return jnp.concatenate(heads, axis=0)


def share_of(beta_ref, h):
    return 1.0 / (1.0 + jnp.exp(-jnp.full((1, HEAD_DIM), beta_ref[h], jnp.float32)))


def scaled_gains(beta_ref, gain_ref, out_ref):
    for h in range(HEADS):
        scaled = gain_ref[h : h + 1, :] * share_of(beta_ref, h)
        out_ref[part_of(h, HEAD_DIM), :] = column(scaled)


def suffix(others):
    count = jnp.sum(others, axis=1, keepdims=True)
    shape = (others.shape[1], HEAD_DIM)
    return lax.broadcasted_iota(jnp.int32, shape, 0).astype(jnp.float32) >= count


def first_document(docs):
    first = jnp.broadcast_to(docs[:, 0:1], docs.shape)
    return first, docs == first


def load_block(key_ref, value_ref, doc_ref, out_ref, doc_scratch, sems):
    rows = key_ref.shape[0]
    doc_copy = pltpu.make_async_copy(doc_ref, doc_scratch, sems.at[0])
    doc_copy.start()
    copies = []
    for g in range(2 * KV_HEADS):
        source = key_ref if g < KV_HEADS else value_ref
        copy = pltpu.make_async_copy(
            source.at[:, part_of(g % KV_HEADS, HEAD_DIM)],
            out_ref.at[part_of(g, rows), :],
            sems.at[1 + g],
        )
        copy.start()
        copies.append(copy)
    doc_copy.wait()
    start = 2 * KV_HEADS * rows
    docs = doc_scratch[...].astype(jnp.float32)
    docs = jnp.broadcast_to(docs, (out_ref.shape[0] - start, rows))
    out_ref[start:, :] = docs.astype(jnp.bfloat16)
    for copy in copies:
        copy.wait()


def block_keys(ref, g):
    return ref[part_of(g, HEAD_DIM), :]


def block_values(ref, g):
    return ref[part_of(KV_HEADS + g, HEAD_DIM), :]


def block_docs(ref):
    start = 2 * KV_HEADS * HEAD_DIM
    return ref[start : start + EXTRA, :].astype(jnp.float32)[0:1, :]


class Plan:
    def __init__(self, n_seq):
        devices = 2 * n_seq
        near = [(b, b + 1) for b in range(devices - 1)]
        far = [(b, b + 2) for b in range(devices - 2)]
        first = [p for p in near if p[0] % 2 == 0 or p[0] // 2 % 2 == 1]
        last = [p for p in far if p[0] // 2 % 2 == 0]
        second = [p for p in near + far if p not in first + last]
        self.pairs = [first, second, last]
        self.senders = sorted({p[0] for p in first})
        busy = {p[0] for p in second if p[0] in self.senders} | {p[1] for p in second}
        self.early = [b for b in range(devices) if b not in busy]


def among(members):
    block = 2 * lax.axis_index("seq") + lax.axis_index("kv")
    return functools.reduce(jnp.logical_or, [block == b for b in members])


def pack_kernel(plan, key_ref, value_ref, doc_ref, out_ref, doc_scratch, sems):
    @pl.when(among(plan.senders))
    def _():
        load_block(key_ref, value_ref, doc_ref, out_ref, doc_scratch, sems)


def attend_own(q_ref, block_ref, g, bias):
    rows = q_ref.shape[0]
    scores = dot(block_keys(block_ref, g), group_queries(q_ref, g), NT)
    tops, totals, weights = [], [], []
    for i in range(GROUPS):
        masked = scores[:, part_of(i, rows)] * SCALE + bias
        top = jnp.max(masked, axis=0, keepdims=True)
        weight = jnp.exp2(masked - top)
        tops.append(top)
        totals.append(jnp.sum(weight, axis=0, keepdims=True))
        weights.append(weight.astype(jnp.bfloat16))
    summed = dot(block_values(block_ref, g), jnp.concatenate(weights, axis=1), TN)
    return summed, jnp.concatenate(tops, axis=1), jnp.concatenate(totals, axis=1)


def own_bias(docs):
    rows = docs.shape[1]
    place = lax.broadcasted_iota(jnp.int32, (rows, rows), 0)
    row = lax.broadcasted_iota(jnp.int32, (rows, rows), 1)
    return jnp.where((place <= row) & (column(docs) == docs), 0.0, LOWEST)


def attend_itself(
    q_ref, block_ref, gain_ref, beta_ref, beta_copy, summed_ref, stats_ref, gains_ref
):
    bias = own_bias(block_docs(block_ref))
    results = [attend_own(q_ref, block_ref, g, bias) for g in range(KV_HEADS)]
    beta_copy.wait()
    scaled_gains(beta_ref, gain_ref, gains_ref)
    done = lax.axis_index("kv") == 0
    for g, (summed, top, total) in enumerate(results):
        rest = [1.0 - share_of(beta_ref, g * GROUPS + i) for i in range(GROUPS)]
        rest = jnp.concatenate(rest, axis=1)
        summed_ref[part_of(g, HEAD_DIM), :] = summed * jnp.where(done, rest / total, 1.0)
        stats_ref[g : g + 1, :] = top
        stats_ref[KV_HEADS + g : KV_HEADS + g + 1, :] = total
        stats_ref[2 * KV_HEADS + g : 2 * KV_HEADS + g + 1, :] = rest


def settle_kernel(
    plan, gain_ref, packed_ref, query_ref, key_ref, value_ref, doc_ref, beta_ref,
    second_ref, own_ref, summed_ref, stats_ref, gains_ref,
    q_scratch, beta_scratch, doc_scratch, sems, early_sems,
):
    sender, early = among(plan.senders), among(plan.early)
    query_copy = pltpu.make_async_copy(query_ref, q_scratch, early_sems.at[0])
    beta_copy = pltpu.make_async_copy(beta_ref, beta_scratch, early_sems.at[1])
    deep = own_ref.shape[0]

    @pl.when(early)
    def _():
        query_copy.start()
        beta_copy.start()

    @pl.when(sender)
    def _():
        own_ref[...] = packed_ref[0:deep, :]

    @pl.when(jnp.logical_not(sender))
    def _():
        load_block(key_ref, value_ref, doc_ref, own_ref, doc_scratch, sems)

    second_ref[0:deep, :] = own_ref[...]
    second_ref[deep:, :] = jnp.zeros((EXTRA, HEAD_DIM), jnp.bfloat16)

    @pl.when(early)
    def _():
        query_copy.wait()
        attend_itself(
            q_scratch, own_ref, gain_ref, beta_scratch, beta_copy,
            summed_ref, stats_ref, gains_ref,
        )


def own_kernel(
    plan, q_ref, gain_ref, own_ref, beta_ref, summed_in, stats_in, gains_in,
    summed_ref, stats_ref, gains_ref, beta_scratch, sem,
):
    @pl.when(jnp.logical_not(among(plan.early)))
    def _():
        beta_copy = pltpu.make_async_copy(beta_ref, beta_scratch, sem)
        beta_copy.start()
        attend_itself(
            q_ref, own_ref, gain_ref, beta_scratch, beta_copy, summed_ref, stats_ref, gains_ref
        )


def memory_state(ref, first, g):
    live = suffix(jnp.where(block_docs(ref) == first, 0.0, 1.0))
    keys = jnp.where(live, block_keys(ref, g).astype(jnp.float32), 0.0).astype(jnp.bfloat16)
    return dot(block_values(ref, g), keys, TN)


def before_kernel(
    q_ref, own_ref, one_ref, three_ref, stats_ref, summed_in, state_ref, summed_ref
):
    docs = block_docs(own_ref)
    rows = docs.shape[1]
    first, same = first_document(docs)

    @pl.when(lax.axis_index("kv") == 0)
    def _():
        for g in range(KV_HEADS):
            state = memory_state(one_ref, first, g) + memory_state(three_ref, first, g)
            state_ref[part_of(g, HEAD_DIM), :] = state

    @pl.when(lax.axis_index("kv") == 1)
    def _():
        live = suffix(jnp.where(block_docs(one_ref) == first, 0.0, 1.0))
        bias = jnp.where(live & same, 0.0, LOWEST)
        for g in range(KV_HEADS):
            scores = dot(block_keys(one_ref, g), group_queries(q_ref, g), NT)
            weights, factors, scales = [], [], []
            for i in range(GROUPS):
                cut = part_of(i, rows)
                masked = scores[:, cut] * SCALE + bias
                top_own = stats_ref[g : g + 1, cut]
                top = jnp.maximum(jnp.max(masked, axis=0, keepdims=True), top_own)
                weight = jnp.exp2(masked - top)
                factor = jnp.exp2(top_own - top)
                total = stats_ref[KV_HEADS + g : KV_HEADS + g + 1, cut] * factor
                total = total + jnp.sum(weight, axis=0, keepdims=True)
                factors.append(factor)
                scales.append(stats_ref[2 * KV_HEADS + g : 2 * KV_HEADS + g + 1, cut] / total)
                weights.append(weight.astype(jnp.bfloat16))
            added = dot(block_values(one_ref, g), jnp.concatenate(weights, axis=1), TN)
            group = part_of(g, HEAD_DIM)
            summed = summed_ref[group, :] * jnp.concatenate(factors, axis=1) + added
            summed_ref[group, :] = summed * jnp.concatenate(scales, axis=1)
            state_ref[group, :] = memory_state(three_ref, first, g)


def join_kernel(
    q_ref, own_ref, two_ref, state_ref, ready_ref, gains_ref, out_ref, held, sems
):
    docs = block_docs(own_ref)
    rows = docs.shape[1]
    first, same = first_document(docs)
    reads = jnp.where(same, 1.0, 0.0)
    groups = range(KV_HEADS)
    states = [state_ref[part_of(g, HEAD_DIM), :] + memory_state(two_ref, first, g) for g in groups]
    pieces = []
    for state in states:
        high = state.astype(jnp.bfloat16)
        state = state - high.astype(jnp.float32)
        middle = state.astype(jnp.bfloat16)
        low = (state - middle.astype(jnp.float32)).astype(jnp.bfloat16)
        pieces.append(jnp.concatenate([high, middle, low], axis=0))
    products = [dot(pieces[g], group_queries(q_ref, g), NT) for g in groups]

    copies = []
    for g in groups:
        recalled = products[g][part_of(0, HEAD_DIM), :] + (
            products[g][part_of(1, HEAD_DIM), :] + products[g][part_of(2, HEAD_DIM), :]
        )
        for i in range(GROUPS):
            h, cut = g * GROUPS + i, part_of(i, rows)
            read = recalled[:, cut]
            square = jnp.sum(read * read, axis=0, keepdims=True) * (1.0 / HEAD_DIM)
            read = read * (lax.rsqrt(square + 1e-06) * reads)
            mixed = read * gains_ref[part_of(h, HEAD_DIM), :]
            mixed = mixed + ready_ref[part_of(g, HEAD_DIM), cut]
            held[:, part_of(h, HEAD_DIM)] = jnp.transpose(mixed)
        wide = part_of(g, GROUPS * HEAD_DIM)
        copies.append(
            pltpu.make_async_copy(held.at[:, wide], out_ref.at[:, wide], sems.at[g])
        )
        copies[g].start()
    for copy in copies:
        copy.wait()


def near_device(n_seq, queries, keys, values, doc_ids, beta, lin_gain):
    rows = queries.shape[0]
    vmem = pl.BlockSpec(memory_space=pltpu.VMEM)
    hbm = pl.BlockSpec(memory_space=pltpu.HBM)
    in_hbm = functools.partial(pltpu.with_memory_space_constraint, memory_space=pltpu.HBM)
    params = pltpu.CompilerParams(vmem_limit_bytes=32 * 1024 * 1024)
    wide = GROUPS * rows
    group_shape = jax.ShapeDtypeStruct((KV_HEADS * HEAD_DIM, wide), jnp.float32)
    gains_shape = jax.ShapeDtypeStruct((HEADS * HEAD_DIM, HEAD_DIM), jnp.float32)
    docs = doc_ids.reshape(1, rows)
    gain = lin_gain.reshape(HEADS, HEAD_DIM)
    deep = 2 * KV_HEADS * rows + EXTRA

    def estimate(share):
        return pl.CostEstimate(
            flops=int(share * 4 * HEADS * HEAD_DIM * rows * rows),
            bytes_accessed=int(share * 4 * 1024 * 1024),
            transcendentals=int(share * HEADS * rows * rows),
        )

    def send(payload, pairs):
        return lax.ppermute(payload, ("seq", "kv"), pairs)

    plan = Plan(n_seq)
    block_shape = jax.ShapeDtypeStruct((deep, HEAD_DIM), jnp.bfloat16)
    longer_shape = jax.ShapeDtypeStruct((deep + EXTRA, HEAD_DIM), jnp.bfloat16)
    stats_shape = jax.ShapeDtypeStruct((4 * KV_HEADS, wide), jnp.float32)
    state_shape = jax.ShapeDtypeStruct((KV_HEADS * HEAD_DIM, HEAD_DIM), jnp.float32)
    results = [group_shape, stats_shape, gains_shape]
    doc_scratch = pltpu.VMEM((1, rows), jnp.int32)
    beta_scratch = pltpu.SMEM((HEADS,), jnp.float32)
    sems = pltpu.SemaphoreType.DMA((2 * KV_HEADS + 1,))
    block = (in_hbm(keys), in_hbm(values), in_hbm(docs))
    beta = in_hbm(beta)
    packed = pl.pallas_call(
        functools.partial(pack_kernel, plan),
        out_shape=longer_shape,
        in_specs=[hbm] * 3,
        out_specs=vmem,
        scratch_shapes=[doc_scratch, sems],
        compiler_params=params,
        cost_estimate=estimate(0.1),
    )(*block)
    one = send(packed, plan.pairs[0])
    second, own, summed, stats, gains = pl.pallas_call(
        functools.partial(settle_kernel, plan),
        out_shape=[longer_shape, block_shape] + results,
        in_specs=[vmem] * 2 + [hbm] * 5,
        out_specs=[vmem] * 5,
        scratch_shapes=[
            pltpu.VMEM(queries.shape, queries.dtype),
            beta_scratch,
            doc_scratch,
            sems,
            pltpu.SemaphoreType.DMA((2,)),
        ],
        compiler_params=params,
        cost_estimate=estimate(1.0),
    )(gain, packed, in_hbm(queries), *block, beta)
    two = send(second, plan.pairs[1])
    three = send(own, plan.pairs[2])
    summed, stats, gains = pl.pallas_call(
        functools.partial(own_kernel, plan),
        out_shape=results,
        in_specs=[vmem] * 3 + [hbm] + [vmem] * 3,
        out_specs=[vmem] * 3,
        scratch_shapes=[beta_scratch, pltpu.SemaphoreType.DMA],
        input_output_aliases={4: 0, 5: 1, 6: 2},
        compiler_params=params,
        cost_estimate=estimate(1.0),
    )(queries, gain, own, beta, summed, stats, gains)
    state, ready = pl.pallas_call(
        before_kernel,
        out_shape=[state_shape, group_shape],
        in_specs=[vmem] * 6,
        out_specs=[vmem] * 2,
        input_output_aliases={5: 1},
        compiler_params=params,
    )(queries, own, one, three, stats, summed)
    return pl.pallas_call(
        join_kernel,
        out_shape=jax.ShapeDtypeStruct((rows, HEADS * HEAD_DIM), jnp.float32),
        in_specs=[vmem] * 6,
        out_specs=hbm,
        scratch_shapes=[
            pltpu.VMEM((rows, HEADS * HEAD_DIM), jnp.float32),
            pltpu.SemaphoreType.DMA((KV_HEADS,)),
        ],
        compiler_params=params,
    )(queries, own, two, state, ready, gains)


def carried_in(part, axis, combine, identity):
    place = lax.axis_index(axis)
    gathered = jax.tree.map(lambda a: lax.all_gather(a, axis), part)
    state = jax.tree.map(lambda a, e: jnp.zeros_like(a) + jnp.asarray(e, a.dtype), part, identity)

    def one(step, state):
        return combine(
            state, jax.tree.map(lambda a: lax.dynamic_index_in_dim(a, step, 0, False), gathered)
        )

    return lax.fori_loop(0, place, one, state)


def join_states(earlier, later):
    state_early, first_early, last_early = earlier
    state_late, first_late, last_late = later
    empty_late = first_late < 0
    joined = (first_late == last_late) & (last_early == first_late)
    merged = state_late + jnp.where(joined, state_early, jnp.zeros_like(state_early))
    combined = jnp.where(empty_late, state_early, merged)
    first_doc = jnp.where(first_early < 0, first_late, first_early)
    last_doc = jnp.where(empty_late, last_early, last_late)
    return (combined, first_doc, last_doc)


def tail_merge(one_side, other_side):
    state_one, first_one, last_one = one_side
    state_other, first_other, last_other = other_side
    top_doc = jnp.maximum(last_one, last_other)
    state_sum = jnp.where(last_one == top_doc, state_one, jnp.zeros_like(state_one))
    state_sum = state_sum + jnp.where(
        last_other == top_doc, state_other, jnp.zeros_like(state_other)
    )
    return (state_sum, jnp.minimum(first_one, first_other), top_doc)


def tail_state(key_rows, value_rows, doc_rows, target_doc):
    count = key_rows.shape[0]
    key_heads = key_rows.reshape(count, KV_HEADS, HEAD_DIM)
    value_heads = value_rows.reshape(count, KV_HEADS, HEAD_DIM)
    live = doc_rows == target_doc
    masked = jnp.where(live[:, None, None], key_heads, jnp.zeros_like(key_heads))
    return jnp.einsum("rgd,rge->gde", masked, value_heads, preferred_element_type=jnp.float32)


def attend_block(
    carry, query_heads, query_pos, query_doc, key_rows, value_rows, key_doc, key_start
):
    running_max, running_sum, accumulated = carry
    key_count = key_rows.shape[0]
    key_heads = key_rows.reshape(key_count, KV_HEADS, HEAD_DIM)
    value_heads = value_rows.reshape(key_count, KV_HEADS, HEAD_DIM)
    scores = jnp.einsum(
        "rgqd,kgd->gqrk", query_heads, key_heads, preferred_element_type=jnp.float32
    )
    scores = scores / jnp.sqrt(jnp.float32(HEAD_DIM))
    key_pos = key_start + jnp.arange(key_count, dtype=jnp.int32)
    allowed = (key_pos[None, :] <= query_pos[:, None]) & (key_doc[None, :] == query_doc[:, None])
    masked = jnp.where(allowed, scores, jnp.float32(-1e30))
    new_max = jnp.maximum(running_max, jnp.max(masked, axis=-1))
    factor = jnp.exp(running_max - new_max)
    weights = jnp.where(allowed, jnp.exp(masked - new_max[..., None]), jnp.float32(0.0))
    new_sum = running_sum * factor + jnp.sum(weights, axis=-1)
    product = jnp.einsum(
        "gqrk,kge->gqre",
        weights.astype(jnp.bfloat16),
        value_heads,
        preferred_element_type=jnp.float32,
    )
    new_accum = accumulated * factor[..., None] + product
    return (new_max, new_sum, new_accum)


def far_device(queries, keys, values, doc_ids, beta, lin_gain):
    row_count = queries.shape[0]
    groups = HEADS // KV_HEADS
    query_heads = queries.reshape(row_count, KV_HEADS, groups, HEAD_DIM)
    position = lax.axis_index("kv") * row_count
    query_pos = position + jnp.arange(row_count, dtype=jnp.int32)
    last_query = position + row_count - 1
    initial = (
        jnp.full((KV_HEADS, groups, row_count), -1e30, jnp.float32),
        jnp.zeros((KV_HEADS, groups, row_count), jnp.float32),
        jnp.zeros((KV_HEADS, groups, row_count, HEAD_DIM), jnp.float32),
    )
    empty_tail = (
        jnp.zeros((KV_HEADS, HEAD_DIM, HEAD_DIM), jnp.float32),
        jnp.array(2**30, jnp.int32),
        jnp.array(-1, jnp.int32),
    )
    key_piece = lax.all_gather(keys, "kv", axis=0, tiled=True)
    value_piece = lax.all_gather(values, "kv", axis=0, tiled=True)
    doc_piece = lax.all_gather(doc_ids, "kv", axis=0, tiled=True)
    blocks = key_piece.shape[0] // row_count

    def one_block(state, item):
        soft_state, tail_now = state
        key_block, value_block, doc_block, number = item
        block_start = number * row_count
        soft_next = lax.cond(
            block_start <= last_query,
            lambda inner: attend_block(
                inner,
                query_heads,
                query_pos,
                doc_ids,
                key_block,
                value_block,
                doc_block,
                block_start,
            ),
            lambda inner: inner,
            soft_state,
        )
        block_tail = (
            tail_state(key_block, value_block, doc_block, doc_block[-1]),
            doc_block[0],
            doc_block[-1],
        )
        tail_now = tail_merge(tail_now, block_tail)
        return ((soft_next, tail_now), None)

    stacked = (
        key_piece.reshape(blocks, row_count, -1),
        value_piece.reshape(blocks, row_count, -1),
        doc_piece.reshape(blocks, row_count),
        jnp.arange(blocks, dtype=jnp.int32),
    )
    result, _ = lax.scan(one_block, (initial, empty_tail), stacked)
    running, segment_tail = result
    running_max, running_sum, accumulated = running
    soft_out = jnp.transpose(accumulated / running_sum[..., None], (2, 0, 1, 3))
    identity = (
        jnp.zeros((KV_HEADS, HEAD_DIM, HEAD_DIM), jnp.float32),
        jnp.array(-1, jnp.int32),
        jnp.array(-1, jnp.int32),
    )
    memory = carried_in(segment_tail, "seq", join_states, identity)
    memory_state, memory_first, memory_last = memory
    query_float = query_heads.astype(jnp.float32)
    recalled = jnp.einsum(
        "rgqd,gde->rgqe", query_float, memory_state, precision=lax.Precision.HIGHEST
    )
    recalled = jnp.where((doc_ids == memory_last)[:, None, None, None], recalled, jnp.float32(0.0))
    mean_square = jnp.mean(recalled * recalled, axis=-1, keepdims=True)
    normed = (
        recalled * lax.rsqrt(mean_square + 1e-06) * lin_gain.reshape(KV_HEADS, groups, HEAD_DIM)
    )
    mixing = jax.nn.sigmoid(beta).reshape(KV_HEADS, groups)[None, :, :, None]
    mixed = mixing * normed + (1.0 - mixing) * soft_out
    return mixed.reshape(row_count, HEADS * HEAD_DIM).astype(jnp.float32)


def solution(mesh):
    n_seq, n_kv = mesh.shape["seq"], mesh.shape["kv"]
    in_specs = (
        P(("dp", "seq", "kv"), None),
        P(("dp", "seq", "kv"), None),
        P(("dp", "seq", "kv"), None),
        P(("dp", "seq", "kv")),
        P(),
        P(),
    )
    out_specs = P(("dp", "seq", "kv"), None)
    if n_kv == 2 and n_seq * n_kv <= 2 * LONGEST:
        on_device = functools.partial(near_device, n_seq)
    else:
        on_device = far_device
    return jax.shard_map(
        on_device, mesh=mesh, in_specs=in_specs, out_specs=out_specs, check_vma=False
    )
```

```python
import functools
import math

import jax
import jax.numpy as jnp
from jax import lax
from jax.experimental import pallas as pl
from jax.experimental.pallas import tpu as pltpu
from jax.sharding import PartitionSpec as P

HEADS = 16
KV_HEADS = 4
HEAD_DIM = 128
GROUPS = HEADS // KV_HEADS
LONGEST = 4
SCALE = math.log2(math.e) / math.sqrt(HEAD_DIM)
LOWEST = -1e30
EXTRA = 16

NT = (((1,), (1,)), ((), ()))
TN = (((0,), (0,)), ((), ()))


def dot(a, b, dims):
    return lax.dot_general(a, b, dims, preferred_element_type=jnp.float32)


def column(row):
    return jnp.transpose(jnp.broadcast_to(row, (HEAD_DIM, row.shape[1])))


def part_of(i, size):
    return slice(i * size, (i + 1) * size)


def group_queries(q_ref, g):
    heads = [q_ref[:, part_of(g * GROUPS + i, HEAD_DIM)] for i in range(GROUPS)]
    return jnp.concatenate(heads, axis=0)


def share_of(beta_ref, h):
    return 1.0 / (1.0 + jnp.exp(-jnp.full((1, HEAD_DIM), beta_ref[h], jnp.float32)))


def scaled_gains(beta_ref, gain_ref, out_ref):
    for h in range(HEADS):
        scaled = gain_ref[h : h + 1, :] * share_of(beta_ref, h)
        out_ref[part_of(h, HEAD_DIM), :] = column(scaled)


def suffix(others):
    count = jnp.sum(others, axis=1, keepdims=True)
    shape = (others.shape[1], HEAD_DIM)
    return lax.broadcasted_iota(jnp.int32, shape, 0).astype(jnp.float32) >= count


def first_document(docs):
    first = jnp.broadcast_to(docs[:, 0:1], docs.shape)
    return first, docs == first


def load_block(key_ref, value_ref, doc_ref, out_ref, doc_scratch, sems):
    rows = key_ref.shape[0]
    doc_copy = pltpu.make_async_copy(doc_ref, doc_scratch, sems.at[0])
    doc_copy.start()
    copies = []
    for g in range(2 * KV_HEADS):
        source = key_ref if g < KV_HEADS else value_ref
        copy = pltpu.make_async_copy(
            source.at[:, part_of(g % KV_HEADS, HEAD_DIM)],
            out_ref.at[part_of(g, rows), :],
            sems.at[1 + g],
        )
        copy.start()
        copies.append(copy)
    doc_copy.wait()
    start = 2 * KV_HEADS * rows
    docs = doc_scratch[...].astype(jnp.float32)
    docs = jnp.broadcast_to(docs, (out_ref.shape[0] - start, rows))
    out_ref[start:, :] = docs.astype(jnp.bfloat16)
    for copy in copies:
        copy.wait()


def block_keys(ref, g):
    return ref[part_of(g, HEAD_DIM), :]


def block_values(ref, g):
    return ref[part_of(KV_HEADS + g, HEAD_DIM), :]


def block_docs(ref):
    start = 2 * KV_HEADS * HEAD_DIM
    return ref[start : start + EXTRA, :].astype(jnp.float32)[0:1, :]


class Plan:
    def __init__(self, n_seq):
        devices = 2 * n_seq
        near = [(b, b + 1) for b in range(devices - 1)]
        far = [(b, b + 2) for b in range(devices - 2)]
        first = [p for p in near if p[0] % 2 == 0 or p[0] // 2 % 2 == 1 or p[0] == 1]
        last = [p for p in far if p[0] // 2 % 2 == 0]
        second = [p for p in near + far if p not in first + last]
        self.pairs = [first, second, last]
        self.senders = sorted({p[0] for p in first})
        busy = {b for p in second for b in p}
        self.early = [b for b in range(devices) if b not in busy]
        self.late = sorted({p[1] for p in second})


def among(members):
    block = 2 * lax.axis_index("seq") + lax.axis_index("kv")
    return functools.reduce(jnp.logical_or, [block == b for b in members])


def pack_kernel(plan, key_ref, value_ref, doc_ref, out_ref, doc_scratch, sems):
    @pl.when(among(plan.senders))
    def _():
        load_block(key_ref, value_ref, doc_ref, out_ref, doc_scratch, sems)


def attend_own(q_ref, block_ref, g, bias):
    rows = q_ref.shape[0]
    scores = dot(block_keys(block_ref, g), group_queries(q_ref, g), NT)
    tops, totals, weights = [], [], []
    for i in range(GROUPS):
        masked = scores[:, part_of(i, rows)] * SCALE + bias
        top = jnp.max(masked, axis=0, keepdims=True)
        weight = jnp.exp2(masked - top)
        tops.append(top)
        totals.append(jnp.sum(weight, axis=0, keepdims=True))
        weights.append(weight.astype(jnp.bfloat16))
    summed = dot(block_values(block_ref, g), jnp.concatenate(weights, axis=1), TN)
    return summed, jnp.concatenate(tops, axis=1), jnp.concatenate(totals, axis=1)


def own_bias(docs):
    rows = docs.shape[1]
    place = lax.broadcasted_iota(jnp.int32, (rows, rows), 0)
    row = lax.broadcasted_iota(jnp.int32, (rows, rows), 1)
    return jnp.where((place <= row) & (column(docs) == docs), 0.0, LOWEST)


def attend_itself(
    q_ref, block_ref, gain_ref, beta_ref, beta_copy, summed_ref, stats_ref, gains_ref
):
    bias = own_bias(block_docs(block_ref))
    results = [attend_own(q_ref, block_ref, g, bias) for g in range(KV_HEADS)]
    beta_copy.wait()
    scaled_gains(beta_ref, gain_ref, gains_ref)
    done = lax.axis_index("kv") == 0
    for g, (summed, top, total) in enumerate(results):
        rest = [1.0 - share_of(beta_ref, g * GROUPS + i) for i in range(GROUPS)]
        rest = jnp.concatenate(rest, axis=1)
        summed_ref[part_of(g, HEAD_DIM), :] = summed * jnp.where(done, rest / total, 1.0)
        stats_ref[g : g + 1, :] = top
        stats_ref[KV_HEADS + g : KV_HEADS + g + 1, :] = total
        stats_ref[2 * KV_HEADS + g : 2 * KV_HEADS + g + 1, :] = rest


def settle_kernel(
    plan, gain_ref, packed_ref, query_ref, key_ref, value_ref, doc_ref, beta_ref,
    second_ref, own_ref, summed_ref, stats_ref, gains_ref,
    q_scratch, beta_scratch, doc_scratch, sems, early_sems,
):
    sender, early = among(plan.senders), among(plan.early)
    query_copy = pltpu.make_async_copy(query_ref, q_scratch, early_sems.at[0])
    beta_copy = pltpu.make_async_copy(beta_ref, beta_scratch, early_sems.at[1])
    deep = own_ref.shape[0]

    @pl.when(early)
    def _():
        query_copy.start()
        beta_copy.start()

    @pl.when(sender)
    def _():
        own_ref[...] = packed_ref[0:deep, :]

    @pl.when(jnp.logical_not(sender))
    def _():
        load_block(key_ref, value_ref, doc_ref, own_ref, doc_scratch, sems)

    second_ref[0:deep, :] = own_ref[...]
    second_ref[deep:, :] = jnp.zeros((EXTRA, HEAD_DIM), jnp.bfloat16)

    @pl.when(early)
    def _():
        query_copy.wait()
        attend_itself(
            q_scratch, own_ref, gain_ref, beta_scratch, beta_copy,
            summed_ref, stats_ref, gains_ref,
        )


def own_kernel(
    plan, q_ref, gain_ref, own_ref, beta_ref, summed_in, stats_in, gains_in,
    summed_ref, stats_ref, gains_ref, beta_scratch, sem,
):
    @pl.when(jnp.logical_not(among(plan.early)))
    def _():
        beta_copy = pltpu.make_async_copy(beta_ref, beta_scratch, sem)
        beta_copy.start()
        attend_itself(
            q_ref, own_ref, gain_ref, beta_scratch, beta_copy, summed_ref, stats_ref, gains_ref
        )


def memory_state(ref, first, g):
    live = suffix(jnp.where(block_docs(ref) == first, 0.0, 1.0))
    keys = jnp.where(live, block_keys(ref, g).astype(jnp.float32), 0.0).astype(jnp.bfloat16)
    return dot(block_values(ref, g), keys, TN)


def memory_states(refs, first):
    return [
        functools.reduce(jnp.add, [memory_state(ref, first, g) for ref in refs])
        for g in range(KV_HEADS)
    ]


def read_memory(states, q_ref, gains_ref, reads):
    pieces = []
    for state in states:
        high = state.astype(jnp.bfloat16)
        state = state - high.astype(jnp.float32)
        middle = state.astype(jnp.bfloat16)
        low = (state - middle.astype(jnp.float32)).astype(jnp.bfloat16)
        pieces.append(jnp.concatenate([high, middle, low], axis=0))
    products = [dot(pieces[g], group_queries(q_ref, g), NT) for g in range(KV_HEADS)]
    rows = q_ref.shape[0]
    heads = []
    for g in range(KV_HEADS):
        recalled = products[g][part_of(0, HEAD_DIM), :] + (
            products[g][part_of(1, HEAD_DIM), :] + products[g][part_of(2, HEAD_DIM), :]
        )
        for i in range(GROUPS):
            read = recalled[:, part_of(i, rows)]
            square = jnp.sum(read * read, axis=0, keepdims=True) * (1.0 / HEAD_DIM)
            read = read * (lax.rsqrt(square + 1e-06) * reads)
            heads.append(read * gains_ref[part_of(g * GROUPS + i, HEAD_DIM), :])
    return heads


def attend_before(q_ref, one_ref, stats_ref, summed_ref, first, same):
    rows = q_ref.shape[0]
    live = suffix(jnp.where(block_docs(one_ref) == first, 0.0, 1.0))
    bias = jnp.where(live & same, 0.0, LOWEST)
    results = []
    for g in range(KV_HEADS):
        scores = dot(block_keys(one_ref, g), group_queries(q_ref, g), NT)
        weights, factors, scales = [], [], []
        for i in range(GROUPS):
            cut = part_of(i, rows)
            masked = scores[:, cut] * SCALE + bias
            top_own = stats_ref[g : g + 1, cut]
            top = jnp.maximum(jnp.max(masked, axis=0, keepdims=True), top_own)
            weight = jnp.exp2(masked - top)
            factor = jnp.exp2(top_own - top)
            total = stats_ref[KV_HEADS + g : KV_HEADS + g + 1, cut] * factor
            total = total + jnp.sum(weight, axis=0, keepdims=True)
            factors.append(factor)
            scales.append(stats_ref[2 * KV_HEADS + g : 2 * KV_HEADS + g + 1, cut] / total)
            weights.append(weight.astype(jnp.bfloat16))
        added = dot(block_values(one_ref, g), jnp.concatenate(weights, axis=1), TN)
        summed = summed_ref[part_of(g, HEAD_DIM), :] * jnp.concatenate(factors, axis=1) + added
        results.append(summed * jnp.concatenate(scales, axis=1))
    return results


def store_heads(mixed, out_ref, held, sems):
    copies = []
    for g in range(KV_HEADS):
        for i in range(GROUPS):
            h = g * GROUPS + i
            held[:, part_of(h, HEAD_DIM)] = jnp.transpose(mixed(g, i))
        wide = part_of(g, GROUPS * HEAD_DIM)
        copies.append(pltpu.make_async_copy(held.at[:, wide], out_ref.at[:, wide], sems.at[g]))
        copies[g].start()
    for copy in copies:
        copy.wait()


def read_kernel(plan, q_ref, own_ref, three_ref, gains_ref, read_ref):
    kv = lax.axis_index("kv")

    @pl.when((kv == 1) & jnp.logical_not(among(plan.late)))
    def _():
        first, same = first_document(block_docs(own_ref))
        states = memory_states([three_ref], first)
        heads = read_memory(states, q_ref, gains_ref, jnp.where(same, 1.0, 0.0))
        for h, head in enumerate(heads):
            read_ref[part_of(h, HEAD_DIM), :] = head


def early_kernel(
    plan, q_ref, own_ref, one_ref, three_ref, stats_ref, gains_ref, read_ref, summed_in,
    summed_ref, state_ref, out_ref, held, sems,
):
    first, same = first_document(block_docs(own_ref))
    rows = q_ref.shape[0]
    kv = lax.axis_index("kv")
    late = among(plan.late)

    def summed_part(g, i):
        return summed_ref[part_of(g, HEAD_DIM), part_of(i, rows)]

    @pl.when((kv == 0) & jnp.logical_not(late))
    def _():
        states = memory_states([one_ref, three_ref], first)
        heads = read_memory(states, q_ref, gains_ref, jnp.where(same, 1.0, 0.0))
        store_heads(lambda g, i: heads[g * GROUPS + i] + summed_part(g, i), out_ref, held, sems)

    @pl.when((kv == 1) & jnp.logical_not(late))
    def _():
        results = attend_before(q_ref, one_ref, stats_ref, summed_ref, first, same)

        def mixed(g, i):
            read = read_ref[part_of(g * GROUPS + i, HEAD_DIM), :]
            return read + results[g][:, part_of(i, rows)]

        store_heads(mixed, out_ref, held, sems)

    @pl.when((kv == 0) & late)
    def _():
        for g, state in enumerate(memory_states([one_ref, three_ref], first)):
            state_ref[part_of(g, HEAD_DIM), :] = state

    @pl.when((kv == 1) & late)
    def _():
        for g, state in enumerate(memory_states([three_ref], first)):
            state_ref[part_of(g, HEAD_DIM), :] = state
        results = attend_before(q_ref, one_ref, stats_ref, summed_ref, first, same)
        for g in range(KV_HEADS):
            summed_ref[part_of(g, HEAD_DIM), :] = results[g]


def late_kernel(
    plan, q_ref, own_ref, two_ref, state_ref, summed_ref, gains_ref, out_in, out_ref, held, sems
):
    @pl.when(among(plan.late))
    def _():
        first, same = first_document(block_docs(own_ref))
        rows = q_ref.shape[0]
        states = [
            state_ref[part_of(g, HEAD_DIM), :] + memory_state(two_ref, first, g)
            for g in range(KV_HEADS)
        ]
        heads = read_memory(states, q_ref, gains_ref, jnp.where(same, 1.0, 0.0))

        def mixed(g, i):
            summed = summed_ref[part_of(g, HEAD_DIM), part_of(i, rows)]
            return heads[g * GROUPS + i] + summed

        store_heads(mixed, out_ref, held, sems)


def near_device(n_seq, queries, keys, values, doc_ids, beta, lin_gain):
    rows = queries.shape[0]
    vmem = pl.BlockSpec(memory_space=pltpu.VMEM)
    hbm = pl.BlockSpec(memory_space=pltpu.HBM)
    in_hbm = functools.partial(pltpu.with_memory_space_constraint, memory_space=pltpu.HBM)
    params = pltpu.CompilerParams(vmem_limit_bytes=32 * 1024 * 1024)
    wide = GROUPS * rows
    group_shape = jax.ShapeDtypeStruct((KV_HEADS * HEAD_DIM, wide), jnp.float32)
    gains_shape = jax.ShapeDtypeStruct((HEADS * HEAD_DIM, HEAD_DIM), jnp.float32)
    docs = doc_ids.reshape(1, rows)
    gain = lin_gain.reshape(HEADS, HEAD_DIM)
    deep = 2 * KV_HEADS * rows + EXTRA

    def estimate(share):
        return pl.CostEstimate(
            flops=int(share * 4 * HEADS * HEAD_DIM * rows * rows),
            bytes_accessed=int(share * 4 * 1024 * 1024),
            transcendentals=int(share * HEADS * rows * rows),
        )

    def send(payload, pairs):
        return lax.ppermute(payload, ("seq", "kv"), pairs)

    plan = Plan(n_seq)
    block_shape = jax.ShapeDtypeStruct((deep, HEAD_DIM), jnp.bfloat16)
    longer_shape = jax.ShapeDtypeStruct((deep + EXTRA, HEAD_DIM), jnp.bfloat16)
    stats_shape = jax.ShapeDtypeStruct((4 * KV_HEADS, wide), jnp.float32)
    state_shape = jax.ShapeDtypeStruct((KV_HEADS * HEAD_DIM, HEAD_DIM), jnp.float32)
    results = [group_shape, stats_shape, gains_shape]
    doc_scratch = pltpu.VMEM((1, rows), jnp.int32)
    beta_scratch = pltpu.SMEM((HEADS,), jnp.float32)
    sems = pltpu.SemaphoreType.DMA((2 * KV_HEADS + 1,))
    block = (in_hbm(keys), in_hbm(values), in_hbm(docs))
    beta = in_hbm(beta)
    packed = pl.pallas_call(
        functools.partial(pack_kernel, plan),
        out_shape=longer_shape,
        in_specs=[hbm] * 3,
        out_specs=vmem,
        scratch_shapes=[doc_scratch, sems],
        compiler_params=params,
        cost_estimate=estimate(0.1),
    )(*block)
    one = send(packed, plan.pairs[0])
    second, own, summed, stats, gains = pl.pallas_call(
        functools.partial(settle_kernel, plan),
        out_shape=[longer_shape, block_shape] + results,
        in_specs=[vmem] * 2 + [hbm] * 5,
        out_specs=[vmem] * 5,
        scratch_shapes=[
            pltpu.VMEM(queries.shape, queries.dtype),
            beta_scratch,
            doc_scratch,
            sems,
            pltpu.SemaphoreType.DMA((2,)),
        ],
        compiler_params=params,
        cost_estimate=estimate(1.0),
    )(gain, packed, in_hbm(queries), *block, beta)
    two = send(second, plan.pairs[1])
    three = send(own, plan.pairs[2])
    summed, stats, gains = pl.pallas_call(
        functools.partial(own_kernel, plan),
        out_shape=results,
        in_specs=[vmem] * 3 + [hbm] + [vmem] * 3,
        out_specs=[vmem] * 3,
        scratch_shapes=[beta_scratch, pltpu.SemaphoreType.DMA],
        input_output_aliases={4: 0, 5: 1, 6: 2},
        compiler_params=params,
        cost_estimate=estimate(1.0),
    )(queries, gain, own, beta, summed, stats, gains)
    read = pl.pallas_call(
        functools.partial(read_kernel, plan),
        out_shape=gains_shape,
        in_specs=[vmem] * 4,
        out_specs=vmem,
        compiler_params=params,
    )(queries, own, three, gains)
    out_shape = jax.ShapeDtypeStruct((rows, HEADS * HEAD_DIM), jnp.float32)
    store_scratch = [
        pltpu.VMEM((rows, HEADS * HEAD_DIM), jnp.float32),
        pltpu.SemaphoreType.DMA((KV_HEADS,)),
    ]
    summed, state, out = pl.pallas_call(
        functools.partial(early_kernel, plan),
        out_shape=[group_shape, state_shape, out_shape],
        in_specs=[vmem] * 8,
        out_specs=[vmem] * 2 + [hbm],
        scratch_shapes=store_scratch,
        input_output_aliases={7: 0},
        compiler_params=params,
    )(queries, own, one, three, stats, gains, read, summed)
    return pl.pallas_call(
        functools.partial(late_kernel, plan),
        out_shape=out_shape,
        in_specs=[vmem] * 6 + [hbm],
        out_specs=hbm,
        scratch_shapes=store_scratch,
        input_output_aliases={6: 0},
        compiler_params=params,
    )(queries, own, two, state, summed, gains, out)


def carried_in(part, axis, combine, identity):
    place = lax.axis_index(axis)
    gathered = jax.tree.map(lambda a: lax.all_gather(a, axis), part)
    state = jax.tree.map(lambda a, e: jnp.zeros_like(a) + jnp.asarray(e, a.dtype), part, identity)

    def one(step, state):
        return combine(
            state, jax.tree.map(lambda a: lax.dynamic_index_in_dim(a, step, 0, False), gathered)
        )

    return lax.fori_loop(0, place, one, state)


def join_states(earlier, later):
    state_early, first_early, last_early = earlier
    state_late, first_late, last_late = later
    empty_late = first_late < 0
    joined = (first_late == last_late) & (last_early == first_late)
    merged = state_late + jnp.where(joined, state_early, jnp.zeros_like(state_early))
    combined = jnp.where(empty_late, state_early, merged)
    first_doc = jnp.where(first_early < 0, first_late, first_early)
    last_doc = jnp.where(empty_late, last_early, last_late)
    return (combined, first_doc, last_doc)


def tail_merge(one_side, other_side):
    state_one, first_one, last_one = one_side
    state_other, first_other, last_other = other_side
    top_doc = jnp.maximum(last_one, last_other)
    state_sum = jnp.where(last_one == top_doc, state_one, jnp.zeros_like(state_one))
    state_sum = state_sum + jnp.where(
        last_other == top_doc, state_other, jnp.zeros_like(state_other)
    )
    return (state_sum, jnp.minimum(first_one, first_other), top_doc)


def tail_state(key_rows, value_rows, doc_rows, target_doc):
    count = key_rows.shape[0]
    key_heads = key_rows.reshape(count, KV_HEADS, HEAD_DIM)
    value_heads = value_rows.reshape(count, KV_HEADS, HEAD_DIM)
    live = doc_rows == target_doc
    masked = jnp.where(live[:, None, None], key_heads, jnp.zeros_like(key_heads))
    return jnp.einsum("rgd,rge->gde", masked, value_heads, preferred_element_type=jnp.float32)


def attend_block(
    carry, query_heads, query_pos, query_doc, key_rows, value_rows, key_doc, key_start
):
    running_max, running_sum, accumulated = carry
    key_count = key_rows.shape[0]
    key_heads = key_rows.reshape(key_count, KV_HEADS, HEAD_DIM)
    value_heads = value_rows.reshape(key_count, KV_HEADS, HEAD_DIM)
    scores = jnp.einsum(
        "rgqd,kgd->gqrk", query_heads, key_heads, preferred_element_type=jnp.float32
    )
    scores = scores / jnp.sqrt(jnp.float32(HEAD_DIM))
    key_pos = key_start + jnp.arange(key_count, dtype=jnp.int32)
    allowed = (key_pos[None, :] <= query_pos[:, None]) & (key_doc[None, :] == query_doc[:, None])
    masked = jnp.where(allowed, scores, jnp.float32(-1e30))
    new_max = jnp.maximum(running_max, jnp.max(masked, axis=-1))
    factor = jnp.exp(running_max - new_max)
    weights = jnp.where(allowed, jnp.exp(masked - new_max[..., None]), jnp.float32(0.0))
    new_sum = running_sum * factor + jnp.sum(weights, axis=-1)
    product = jnp.einsum(
        "gqrk,kge->gqre",
        weights.astype(jnp.bfloat16),
        value_heads,
        preferred_element_type=jnp.float32,
    )
    new_accum = accumulated * factor[..., None] + product
    return (new_max, new_sum, new_accum)


def far_device(queries, keys, values, doc_ids, beta, lin_gain):
    row_count = queries.shape[0]
    groups = HEADS // KV_HEADS
    query_heads = queries.reshape(row_count, KV_HEADS, groups, HEAD_DIM)
    position = lax.axis_index("kv") * row_count
    query_pos = position + jnp.arange(row_count, dtype=jnp.int32)
    last_query = position + row_count - 1
    initial = (
        jnp.full((KV_HEADS, groups, row_count), -1e30, jnp.float32),
        jnp.zeros((KV_HEADS, groups, row_count), jnp.float32),
        jnp.zeros((KV_HEADS, groups, row_count, HEAD_DIM), jnp.float32),
    )
    empty_tail = (
        jnp.zeros((KV_HEADS, HEAD_DIM, HEAD_DIM), jnp.float32),
        jnp.array(2**30, jnp.int32),
        jnp.array(-1, jnp.int32),
    )
    key_piece = lax.all_gather(keys, "kv", axis=0, tiled=True)
    value_piece = lax.all_gather(values, "kv", axis=0, tiled=True)
    doc_piece = lax.all_gather(doc_ids, "kv", axis=0, tiled=True)
    blocks = key_piece.shape[0] // row_count

    def one_block(state, item):
        soft_state, tail_now = state
        key_block, value_block, doc_block, number = item
        block_start = number * row_count
        soft_next = lax.cond(
            block_start <= last_query,
            lambda inner: attend_block(
                inner,
                query_heads,
                query_pos,
                doc_ids,
                key_block,
                value_block,
                doc_block,
                block_start,
            ),
            lambda inner: inner,
            soft_state,
        )
        block_tail = (
            tail_state(key_block, value_block, doc_block, doc_block[-1]),
            doc_block[0],
            doc_block[-1],
        )
        tail_now = tail_merge(tail_now, block_tail)
        return ((soft_next, tail_now), None)

    stacked = (
        key_piece.reshape(blocks, row_count, -1),
        value_piece.reshape(blocks, row_count, -1),
        doc_piece.reshape(blocks, row_count),
        jnp.arange(blocks, dtype=jnp.int32),
    )
    result, _ = lax.scan(one_block, (initial, empty_tail), stacked)
    running, segment_tail = result
    running_max, running_sum, accumulated = running
    soft_out = jnp.transpose(accumulated / running_sum[..., None], (2, 0, 1, 3))
    identity = (
        jnp.zeros((KV_HEADS, HEAD_DIM, HEAD_DIM), jnp.float32),
        jnp.array(-1, jnp.int32),
        jnp.array(-1, jnp.int32),
    )
    memory = carried_in(segment_tail, "seq", join_states, identity)
    memory_state, memory_first, memory_last = memory
    query_float = query_heads.astype(jnp.float32)
    recalled = jnp.einsum(
        "rgqd,gde->rgqe", query_float, memory_state, precision=lax.Precision.HIGHEST
    )
    recalled = jnp.where((doc_ids == memory_last)[:, None, None, None], recalled, jnp.float32(0.0))
    mean_square = jnp.mean(recalled * recalled, axis=-1, keepdims=True)
    normed = (
        recalled * lax.rsqrt(mean_square + 1e-06) * lin_gain.reshape(KV_HEADS, groups, HEAD_DIM)
    )
    mixing = jax.nn.sigmoid(beta).reshape(KV_HEADS, groups)[None, :, :, None]
    mixed = mixing * normed + (1.0 - mixing) * soft_out
    return mixed.reshape(row_count, HEADS * HEAD_DIM).astype(jnp.float32)


def solution(mesh):
    n_seq, n_kv = mesh.shape["seq"], mesh.shape["kv"]
    in_specs = (
        P(("dp", "seq", "kv"), None),
        P(("dp", "seq", "kv"), None),
        P(("dp", "seq", "kv"), None),
        P(("dp", "seq", "kv")),
        P(),
        P(),
    )
    out_specs = P(("dp", "seq", "kv"), None)
    if n_kv == 2 and n_seq * n_kv <= 2 * LONGEST:
        on_device = functools.partial(near_device, n_seq)
    else:
        on_device = far_device
    return jax.shard_map(
        on_device, mesh=mesh, in_specs=in_specs, out_specs=out_specs, check_vma=False
    )
```

```python
import functools
import math

import jax
import jax.numpy as jnp
from jax import lax
from jax.experimental import pallas as pl
from jax.experimental.pallas import tpu as pltpu
from jax.sharding import PartitionSpec as P

HEADS = 16
KV_HEADS = 4
HEAD_DIM = 128
GROUPS = HEADS // KV_HEADS
LONGEST = 4
SCALE = math.log2(math.e) / math.sqrt(HEAD_DIM)
LOWEST = -1e30
EXTRA = 16

NT = (((1,), (1,)), ((), ()))
TN = (((0,), (0,)), ((), ()))


def dot(a, b, dims):
    return lax.dot_general(a, b, dims, preferred_element_type=jnp.float32)


def column(row):
    return jnp.transpose(jnp.broadcast_to(row, (HEAD_DIM, row.shape[1])))


def part_of(i, size):
    return slice(i * size, (i + 1) * size)


def group_queries(q_ref, g):
    heads = [q_ref[:, part_of(g * GROUPS + i, HEAD_DIM)] for i in range(GROUPS)]
    return jnp.concatenate(heads, axis=0)


def share_of(beta_ref, h):
    return 1.0 / (1.0 + jnp.exp(-jnp.full((1, HEAD_DIM), beta_ref[h], jnp.float32)))


def scaled_gains(beta_ref, gain_ref, out_ref):
    for h in range(HEADS):
        scaled = gain_ref[h : h + 1, :] * share_of(beta_ref, h)
        out_ref[part_of(h, HEAD_DIM), :] = column(scaled)


def suffix(others):
    count = jnp.sum(others, axis=1, keepdims=True)
    shape = (others.shape[1], HEAD_DIM)
    return lax.broadcasted_iota(jnp.int32, shape, 0).astype(jnp.float32) >= count


def first_document(docs):
    first = jnp.broadcast_to(docs[:, 0:1], docs.shape)
    return first, docs == first


def load_block(key_ref, value_ref, doc_ref, out_ref, doc_scratch, sems):
    rows = key_ref.shape[0]
    doc_copy = pltpu.make_async_copy(doc_ref, doc_scratch, sems.at[0])
    doc_copy.start()
    copies = []
    for g in range(2 * KV_HEADS):
        source = key_ref if g < KV_HEADS else value_ref
        copy = pltpu.make_async_copy(
            source.at[:, part_of(g % KV_HEADS, HEAD_DIM)],
            out_ref.at[part_of(g, rows), :],
            sems.at[1 + g],
        )
        copy.start()
        copies.append(copy)
    doc_copy.wait()
    start = 2 * KV_HEADS * rows
    docs = doc_scratch[...].astype(jnp.float32)
    docs = jnp.broadcast_to(docs, (out_ref.shape[0] - start, rows))
    out_ref[start:, :] = docs.astype(jnp.bfloat16)
    for copy in copies:
        copy.wait()


def block_keys(ref, g):
    return ref[part_of(g, HEAD_DIM), :]


def block_values(ref, g):
    return ref[part_of(KV_HEADS + g, HEAD_DIM), :]


def block_docs(ref):
    start = 2 * KV_HEADS * HEAD_DIM
    return ref[start : start + EXTRA, :].astype(jnp.float32)[0:1, :]


class Plan:
    def __init__(self, n_seq):
        devices = 2 * n_seq
        near = [(b, b + 1) for b in range(devices - 1)]
        far = [(b, b + 2) for b in range(devices - 2)]
        first = [p for p in near if p[0] % 2 == 0 or p[0] // 2 % 2 == 1 or p[0] == 1]
        first = [p for p in first if p[0] > 0]
        last = [p for p in far if p[0] // 2 % 2 == 0]
        second = [p for p in near + far if p not in first + last]
        self.pairs = [first, second, last]
        self.senders = sorted({p[0] for p in first})
        busy = {b for p in first for b in p} & {b for p in second for b in p}
        self.early = [b for b in range(devices) if b not in busy]
        self.late = sorted({p[1] for p in second})
        self.attend_late = [b for a, b in second if a + 1 == b and b % 2 == 1]


def among(members):
    block = 2 * lax.axis_index("seq") + lax.axis_index("kv")
    return functools.reduce(jnp.logical_or, [block == b for b in members])


def pack_kernel(plan, key_ref, value_ref, doc_ref, out_ref, doc_scratch, sems):
    @pl.when(among(plan.senders))
    def _():
        load_block(key_ref, value_ref, doc_ref, out_ref, doc_scratch, sems)


def attend_own(q_ref, block_ref, g, bias):
    rows = q_ref.shape[0]
    scores = dot(block_keys(block_ref, g), group_queries(q_ref, g), NT)
    tops, totals, weights = [], [], []
    for i in range(GROUPS):
        masked = scores[:, part_of(i, rows)] * SCALE + bias
        top = jnp.max(masked, axis=0, keepdims=True)
        weight = jnp.exp2(masked - top)
        tops.append(top)
        totals.append(jnp.sum(weight, axis=0, keepdims=True))
        weights.append(weight.astype(jnp.bfloat16))
    summed = dot(block_values(block_ref, g), jnp.concatenate(weights, axis=1), TN)
    return summed, jnp.concatenate(tops, axis=1), jnp.concatenate(totals, axis=1)


def own_bias(docs):
    rows = docs.shape[1]
    place = lax.broadcasted_iota(jnp.int32, (rows, rows), 0)
    row = lax.broadcasted_iota(jnp.int32, (rows, rows), 1)
    return jnp.where((place <= row) & (column(docs) == docs), 0.0, LOWEST)


def attend_itself(
    q_ref, block_ref, gain_ref, beta_ref, beta_copy, summed_ref, stats_ref, gains_ref
):
    bias = own_bias(block_docs(block_ref))
    results = [attend_own(q_ref, block_ref, g, bias) for g in range(KV_HEADS)]
    beta_copy.wait()
    scaled_gains(beta_ref, gain_ref, gains_ref)
    done = lax.axis_index("kv") == 0
    for g, (summed, top, total) in enumerate(results):
        rest = [1.0 - share_of(beta_ref, g * GROUPS + i) for i in range(GROUPS)]
        rest = jnp.concatenate(rest, axis=1)
        summed_ref[part_of(g, HEAD_DIM), :] = summed * jnp.where(done, rest / total, 1.0)
        stats_ref[g : g + 1, :] = top
        stats_ref[KV_HEADS + g : KV_HEADS + g + 1, :] = total
        stats_ref[2 * KV_HEADS + g : 2 * KV_HEADS + g + 1, :] = rest


def settle_kernel(
    plan, gain_ref, packed_ref, query_ref, key_ref, value_ref, doc_ref, beta_ref,
    second_ref, own_ref, summed_ref, stats_ref, gains_ref,
    q_scratch, beta_scratch, doc_scratch, sems, early_sems,
):
    sender, early = among(plan.senders), among(plan.early)
    query_copy = pltpu.make_async_copy(query_ref, q_scratch, early_sems.at[0])
    beta_copy = pltpu.make_async_copy(beta_ref, beta_scratch, early_sems.at[1])
    deep = own_ref.shape[0]

    @pl.when(early)
    def _():
        query_copy.start()
        beta_copy.start()

    @pl.when(sender)
    def _():
        own_ref[...] = packed_ref[0:deep, :]

    @pl.when(jnp.logical_not(sender))
    def _():
        load_block(key_ref, value_ref, doc_ref, own_ref, doc_scratch, sems)

    second_ref[0:deep, :] = own_ref[...]
    second_ref[deep:, :] = jnp.zeros((EXTRA, HEAD_DIM), jnp.bfloat16)

    @pl.when(early)
    def _():
        query_copy.wait()
        attend_itself(
            q_scratch, own_ref, gain_ref, beta_scratch, beta_copy,
            summed_ref, stats_ref, gains_ref,
        )


def own_kernel(
    plan, q_ref, gain_ref, own_ref, beta_ref, summed_in, stats_in, gains_in,
    summed_ref, stats_ref, gains_ref, beta_scratch, sem,
):
    @pl.when(jnp.logical_not(among(plan.early)))
    def _():
        beta_copy = pltpu.make_async_copy(beta_ref, beta_scratch, sem)
        beta_copy.start()
        attend_itself(
            q_ref, own_ref, gain_ref, beta_scratch, beta_copy, summed_ref, stats_ref, gains_ref
        )


def memory_state(ref, first, g):
    live = suffix(jnp.where(block_docs(ref) == first, 0.0, 1.0))
    keys = jnp.where(live, block_keys(ref, g).astype(jnp.float32), 0.0).astype(jnp.bfloat16)
    return dot(block_values(ref, g), keys, TN)


def memory_states(refs, first):
    return [
        functools.reduce(jnp.add, [memory_state(ref, first, g) for ref in refs])
        for g in range(KV_HEADS)
    ]


def read_memory(states, q_ref, gains_ref, reads):
    pieces = []
    for state in states:
        high = state.astype(jnp.bfloat16)
        state = state - high.astype(jnp.float32)
        middle = state.astype(jnp.bfloat16)
        low = (state - middle.astype(jnp.float32)).astype(jnp.bfloat16)
        pieces.append(jnp.concatenate([high, middle, low], axis=0))
    products = [dot(pieces[g], group_queries(q_ref, g), NT) for g in range(KV_HEADS)]
    rows = q_ref.shape[0]
    heads = []
    for g in range(KV_HEADS):
        recalled = products[g][part_of(0, HEAD_DIM), :] + (
            products[g][part_of(1, HEAD_DIM), :] + products[g][part_of(2, HEAD_DIM), :]
        )
        for i in range(GROUPS):
            read = recalled[:, part_of(i, rows)]
            square = jnp.sum(read * read, axis=0, keepdims=True) * (1.0 / HEAD_DIM)
            read = read * (lax.rsqrt(square + 1e-06) * reads)
            heads.append(read * gains_ref[part_of(g * GROUPS + i, HEAD_DIM), :])
    return heads


def attend_before(q_ref, one_ref, stats_ref, summed_ref, first, same):
    rows = q_ref.shape[0]
    live = suffix(jnp.where(block_docs(one_ref) == first, 0.0, 1.0))
    bias = jnp.where(live & same, 0.0, LOWEST)
    results = []
    for g in range(KV_HEADS):
        scores = dot(block_keys(one_ref, g), group_queries(q_ref, g), NT)
        weights, factors, scales = [], [], []
        for i in range(GROUPS):
            cut = part_of(i, rows)
            masked = scores[:, cut] * SCALE + bias
            top_own = stats_ref[g : g + 1, cut]
            top = jnp.maximum(jnp.max(masked, axis=0, keepdims=True), top_own)
            weight = jnp.exp2(masked - top)
            factor = jnp.exp2(top_own - top)
            total = stats_ref[KV_HEADS + g : KV_HEADS + g + 1, cut] * factor
            total = total + jnp.sum(weight, axis=0, keepdims=True)
            factors.append(factor)
            scales.append(stats_ref[2 * KV_HEADS + g : 2 * KV_HEADS + g + 1, cut] / total)
            weights.append(weight.astype(jnp.bfloat16))
        added = dot(block_values(one_ref, g), jnp.concatenate(weights, axis=1), TN)
        summed = summed_ref[part_of(g, HEAD_DIM), :] * jnp.concatenate(factors, axis=1) + added
        results.append(summed * jnp.concatenate(scales, axis=1))
    return results


def store_heads(mixed, out_ref, held, sems):
    copies = []
    for g in range(KV_HEADS):
        for i in range(GROUPS):
            h = g * GROUPS + i
            held[:, part_of(h, HEAD_DIM)] = jnp.transpose(mixed(g, i))
        wide = part_of(g, GROUPS * HEAD_DIM)
        copies.append(pltpu.make_async_copy(held.at[:, wide], out_ref.at[:, wide], sems.at[g]))
        copies[g].start()
    for copy in copies:
        copy.wait()


def read_kernel(plan, q_ref, own_ref, three_ref, gains_ref, read_ref):
    ready = jnp.logical_not(among(plan.late)) | among(plan.attend_late)

    @pl.when((lax.axis_index("kv") == 1) & ready)
    def _():
        first, same = first_document(block_docs(own_ref))
        states = memory_states([three_ref], first)
        heads = read_memory(states, q_ref, gains_ref, jnp.where(same, 1.0, 0.0))
        for h, head in enumerate(heads):
            read_ref[part_of(h, HEAD_DIM), :] = head


def early_kernel(
    plan, q_ref, own_ref, one_ref, three_ref, stats_ref, gains_ref, read_ref, summed_in,
    summed_ref, state_ref, out_ref, held, sems,
):
    first, same = first_document(block_docs(own_ref))
    rows = q_ref.shape[0]
    kv = lax.axis_index("kv")
    late = among(plan.late)

    def summed_part(g, i):
        return summed_ref[part_of(g, HEAD_DIM), part_of(i, rows)]

    @pl.when((kv == 0) & jnp.logical_not(late))
    def _():
        states = memory_states([one_ref, three_ref], first)
        heads = read_memory(states, q_ref, gains_ref, jnp.where(same, 1.0, 0.0))
        store_heads(lambda g, i: heads[g * GROUPS + i] + summed_part(g, i), out_ref, held, sems)

    @pl.when((kv == 1) & jnp.logical_not(late))
    def _():
        results = attend_before(q_ref, one_ref, stats_ref, summed_ref, first, same)

        def mixed(g, i):
            read = read_ref[part_of(g * GROUPS + i, HEAD_DIM), :]
            return read + results[g][:, part_of(i, rows)]

        store_heads(mixed, out_ref, held, sems)

    @pl.when((kv == 0) & late)
    def _():
        for g, state in enumerate(memory_states([one_ref, three_ref], first)):
            state_ref[part_of(g, HEAD_DIM), :] = state

    @pl.when((kv == 1) & late & jnp.logical_not(among(plan.attend_late)))
    def _():
        for g, state in enumerate(memory_states([three_ref], first)):
            state_ref[part_of(g, HEAD_DIM), :] = state
        results = attend_before(q_ref, one_ref, stats_ref, summed_ref, first, same)
        for g in range(KV_HEADS):
            summed_ref[part_of(g, HEAD_DIM), :] = results[g]


def late_kernel(
    plan, q_ref, own_ref, two_ref, state_ref, summed_ref, stats_ref, gains_ref, read_ref, out_in,
    out_ref, held, sems,
):
    first, same = first_document(block_docs(own_ref))
    rows = q_ref.shape[0]
    attend_late = among(plan.attend_late)

    @pl.when(attend_late)
    def _():
        results = attend_before(q_ref, two_ref, stats_ref, summed_ref, first, same)

        def mixed(g, i):
            read = read_ref[part_of(g * GROUPS + i, HEAD_DIM), :]
            return read + results[g][:, part_of(i, rows)]

        store_heads(mixed, out_ref, held, sems)

    @pl.when(among(plan.late) & jnp.logical_not(attend_late))
    def _():
        states = [
            state_ref[part_of(g, HEAD_DIM), :] + memory_state(two_ref, first, g)
            for g in range(KV_HEADS)
        ]
        heads = read_memory(states, q_ref, gains_ref, jnp.where(same, 1.0, 0.0))

        def mixed(g, i):
            summed = summed_ref[part_of(g, HEAD_DIM), part_of(i, rows)]
            return heads[g * GROUPS + i] + summed

        store_heads(mixed, out_ref, held, sems)


def near_device(n_seq, queries, keys, values, doc_ids, beta, lin_gain):
    rows = queries.shape[0]
    vmem = pl.BlockSpec(memory_space=pltpu.VMEM)
    hbm = pl.BlockSpec(memory_space=pltpu.HBM)
    in_hbm = functools.partial(pltpu.with_memory_space_constraint, memory_space=pltpu.HBM)
    params = pltpu.CompilerParams(vmem_limit_bytes=32 * 1024 * 1024)
    wide = GROUPS * rows
    group_shape = jax.ShapeDtypeStruct((KV_HEADS * HEAD_DIM, wide), jnp.float32)
    gains_shape = jax.ShapeDtypeStruct((HEADS * HEAD_DIM, HEAD_DIM), jnp.float32)
    docs = doc_ids.reshape(1, rows)
    gain = lin_gain.reshape(HEADS, HEAD_DIM)
    deep = 2 * KV_HEADS * rows + EXTRA

    def estimate(share):
        return pl.CostEstimate(
            flops=int(share * 4 * HEADS * HEAD_DIM * rows * rows),
            bytes_accessed=int(share * 4 * 1024 * 1024),
            transcendentals=int(share * HEADS * rows * rows),
        )

    def send(payload, pairs):
        return lax.ppermute(payload, ("seq", "kv"), pairs)

    plan = Plan(n_seq)
    block_shape = jax.ShapeDtypeStruct((deep, HEAD_DIM), jnp.bfloat16)
    longer_shape = jax.ShapeDtypeStruct((deep + EXTRA, HEAD_DIM), jnp.bfloat16)
    stats_shape = jax.ShapeDtypeStruct((4 * KV_HEADS, wide), jnp.float32)
    state_shape = jax.ShapeDtypeStruct((KV_HEADS * HEAD_DIM, HEAD_DIM), jnp.float32)
    results = [group_shape, stats_shape, gains_shape]
    doc_scratch = pltpu.VMEM((1, rows), jnp.int32)
    beta_scratch = pltpu.SMEM((HEADS,), jnp.float32)
    sems = pltpu.SemaphoreType.DMA((2 * KV_HEADS + 1,))
    block = (in_hbm(keys), in_hbm(values), in_hbm(docs))
    beta = in_hbm(beta)
    packed = pl.pallas_call(
        functools.partial(pack_kernel, plan),
        out_shape=longer_shape,
        in_specs=[hbm] * 3,
        out_specs=vmem,
        scratch_shapes=[doc_scratch, sems],
        compiler_params=params,
        cost_estimate=estimate(0.1),
    )(*block)
    one = send(packed, plan.pairs[0])
    second, own, summed, stats, gains = pl.pallas_call(
        functools.partial(settle_kernel, plan),
        out_shape=[longer_shape, block_shape] + results,
        in_specs=[vmem] * 2 + [hbm] * 5,
        out_specs=[vmem] * 5,
        scratch_shapes=[
            pltpu.VMEM(queries.shape, queries.dtype),
            beta_scratch,
            doc_scratch,
            sems,
            pltpu.SemaphoreType.DMA((2,)),
        ],
        compiler_params=params,
        cost_estimate=estimate(1.0),
    )(gain, packed, in_hbm(queries), *block, beta)
    two = send(second, plan.pairs[1])
    three = send(own, plan.pairs[2])
    summed, stats, gains = pl.pallas_call(
        functools.partial(own_kernel, plan),
        out_shape=results,
        in_specs=[vmem] * 3 + [hbm] + [vmem] * 3,
        out_specs=[vmem] * 3,
        scratch_shapes=[beta_scratch, pltpu.SemaphoreType.DMA],
        input_output_aliases={4: 0, 5: 1, 6: 2},
        compiler_params=params,
        cost_estimate=estimate(1.0),
    )(queries, gain, own, beta, summed, stats, gains)
    read = pl.pallas_call(
        functools.partial(read_kernel, plan),
        out_shape=gains_shape,
        in_specs=[vmem] * 4,
        out_specs=vmem,
        compiler_params=params,
    )(queries, own, three, gains)
    out_shape = jax.ShapeDtypeStruct((rows, HEADS * HEAD_DIM), jnp.float32)
    store_scratch = [
        pltpu.VMEM((rows, HEADS * HEAD_DIM), jnp.float32),
        pltpu.SemaphoreType.DMA((KV_HEADS,)),
    ]
    summed, state, out = pl.pallas_call(
        functools.partial(early_kernel, plan),
        out_shape=[group_shape, state_shape, out_shape],
        in_specs=[vmem] * 8,
        out_specs=[vmem] * 2 + [hbm],
        scratch_shapes=store_scratch,
        input_output_aliases={7: 0},
        compiler_params=params,
    )(queries, own, one, three, stats, gains, read, summed)
    return pl.pallas_call(
        functools.partial(late_kernel, plan),
        out_shape=out_shape,
        in_specs=[vmem] * 8 + [hbm],
        out_specs=hbm,
        scratch_shapes=store_scratch,
        input_output_aliases={8: 0},
        compiler_params=params,
    )(queries, own, two, state, summed, stats, gains, read, out)


def carried_in(part, axis, combine, identity):
    place = lax.axis_index(axis)
    gathered = jax.tree.map(lambda a: lax.all_gather(a, axis), part)
    state = jax.tree.map(lambda a, e: jnp.zeros_like(a) + jnp.asarray(e, a.dtype), part, identity)

    def one(step, state):
        return combine(
            state, jax.tree.map(lambda a: lax.dynamic_index_in_dim(a, step, 0, False), gathered)
        )

    return lax.fori_loop(0, place, one, state)


def join_states(earlier, later):
    state_early, first_early, last_early = earlier
    state_late, first_late, last_late = later
    empty_late = first_late < 0
    joined = (first_late == last_late) & (last_early == first_late)
    merged = state_late + jnp.where(joined, state_early, jnp.zeros_like(state_early))
    combined = jnp.where(empty_late, state_early, merged)
    first_doc = jnp.where(first_early < 0, first_late, first_early)
    last_doc = jnp.where(empty_late, last_early, last_late)
    return (combined, first_doc, last_doc)


def tail_merge(one_side, other_side):
    state_one, first_one, last_one = one_side
    state_other, first_other, last_other = other_side
    top_doc = jnp.maximum(last_one, last_other)
    state_sum = jnp.where(last_one == top_doc, state_one, jnp.zeros_like(state_one))
    state_sum = state_sum + jnp.where(
        last_other == top_doc, state_other, jnp.zeros_like(state_other)
    )
    return (state_sum, jnp.minimum(first_one, first_other), top_doc)


def tail_state(key_rows, value_rows, doc_rows, target_doc):
    count = key_rows.shape[0]
    key_heads = key_rows.reshape(count, KV_HEADS, HEAD_DIM)
    value_heads = value_rows.reshape(count, KV_HEADS, HEAD_DIM)
    live = doc_rows == target_doc
    masked = jnp.where(live[:, None, None], key_heads, jnp.zeros_like(key_heads))
    return jnp.einsum("rgd,rge->gde", masked, value_heads, preferred_element_type=jnp.float32)


def attend_block(
    carry, query_heads, query_pos, query_doc, key_rows, value_rows, key_doc, key_start
):
    running_max, running_sum, accumulated = carry
    key_count = key_rows.shape[0]
    key_heads = key_rows.reshape(key_count, KV_HEADS, HEAD_DIM)
    value_heads = value_rows.reshape(key_count, KV_HEADS, HEAD_DIM)
    scores = jnp.einsum(
        "rgqd,kgd->gqrk", query_heads, key_heads, preferred_element_type=jnp.float32
    )
    scores = scores / jnp.sqrt(jnp.float32(HEAD_DIM))
    key_pos = key_start + jnp.arange(key_count, dtype=jnp.int32)
    allowed = (key_pos[None, :] <= query_pos[:, None]) & (key_doc[None, :] == query_doc[:, None])
    masked = jnp.where(allowed, scores, jnp.float32(-1e30))
    new_max = jnp.maximum(running_max, jnp.max(masked, axis=-1))
    factor = jnp.exp(running_max - new_max)
    weights = jnp.where(allowed, jnp.exp(masked - new_max[..., None]), jnp.float32(0.0))
    new_sum = running_sum * factor + jnp.sum(weights, axis=-1)
    product = jnp.einsum(
        "gqrk,kge->gqre",
        weights.astype(jnp.bfloat16),
        value_heads,
        preferred_element_type=jnp.float32,
    )
    new_accum = accumulated * factor[..., None] + product
    return (new_max, new_sum, new_accum)


def far_device(queries, keys, values, doc_ids, beta, lin_gain):
    row_count = queries.shape[0]
    groups = HEADS // KV_HEADS
    query_heads = queries.reshape(row_count, KV_HEADS, groups, HEAD_DIM)
    position = lax.axis_index("kv") * row_count
    query_pos = position + jnp.arange(row_count, dtype=jnp.int32)
    last_query = position + row_count - 1
    initial = (
        jnp.full((KV_HEADS, groups, row_count), -1e30, jnp.float32),
        jnp.zeros((KV_HEADS, groups, row_count), jnp.float32),
        jnp.zeros((KV_HEADS, groups, row_count, HEAD_DIM), jnp.float32),
    )
    empty_tail = (
        jnp.zeros((KV_HEADS, HEAD_DIM, HEAD_DIM), jnp.float32),
        jnp.array(2**30, jnp.int32),
        jnp.array(-1, jnp.int32),
    )
    key_piece = lax.all_gather(keys, "kv", axis=0, tiled=True)
    value_piece = lax.all_gather(values, "kv", axis=0, tiled=True)
    doc_piece = lax.all_gather(doc_ids, "kv", axis=0, tiled=True)
    blocks = key_piece.shape[0] // row_count

    def one_block(state, item):
        soft_state, tail_now = state
        key_block, value_block, doc_block, number = item
        block_start = number * row_count
        soft_next = lax.cond(
            block_start <= last_query,
            lambda inner: attend_block(
                inner,
                query_heads,
                query_pos,
                doc_ids,
                key_block,
                value_block,
                doc_block,
                block_start,
            ),
            lambda inner: inner,
            soft_state,
        )
        block_tail = (
            tail_state(key_block, value_block, doc_block, doc_block[-1]),
            doc_block[0],
            doc_block[-1],
        )
        tail_now = tail_merge(tail_now, block_tail)
        return ((soft_next, tail_now), None)

    stacked = (
        key_piece.reshape(blocks, row_count, -1),
        value_piece.reshape(blocks, row_count, -1),
        doc_piece.reshape(blocks, row_count),
        jnp.arange(blocks, dtype=jnp.int32),
    )
    result, _ = lax.scan(one_block, (initial, empty_tail), stacked)
    running, segment_tail = result
    running_max, running_sum, accumulated = running
    soft_out = jnp.transpose(accumulated / running_sum[..., None], (2, 0, 1, 3))
    identity = (
        jnp.zeros((KV_HEADS, HEAD_DIM, HEAD_DIM), jnp.float32),
        jnp.array(-1, jnp.int32),
        jnp.array(-1, jnp.int32),
    )
    memory = carried_in(segment_tail, "seq", join_states, identity)
    memory_state, memory_first, memory_last = memory
    query_float = query_heads.astype(jnp.float32)
    recalled = jnp.einsum(
        "rgqd,gde->rgqe", query_float, memory_state, precision=lax.Precision.HIGHEST
    )
    recalled = jnp.where((doc_ids == memory_last)[:, None, None, None], recalled, jnp.float32(0.0))
    mean_square = jnp.mean(recalled * recalled, axis=-1, keepdims=True)
    normed = (
        recalled * lax.rsqrt(mean_square + 1e-06) * lin_gain.reshape(KV_HEADS, groups, HEAD_DIM)
    )
    mixing = jax.nn.sigmoid(beta).reshape(KV_HEADS, groups)[None, :, :, None]
    mixed = mixing * normed + (1.0 - mixing) * soft_out
    return mixed.reshape(row_count, HEADS * HEAD_DIM).astype(jnp.float32)


def solution(mesh):
    n_seq, n_kv = mesh.shape["seq"], mesh.shape["kv"]
    in_specs = (
        P(("dp", "seq", "kv"), None),
        P(("dp", "seq", "kv"), None),
        P(("dp", "seq", "kv"), None),
        P(("dp", "seq", "kv")),
        P(),
        P(),
    )
    out_specs = P(("dp", "seq", "kv"), None)
    if n_kv == 2 and n_seq * n_kv <= 2 * LONGEST:
        on_device = functools.partial(near_device, n_seq)
    else:
        on_device = far_device
    return jax.shard_map(
        on_device, mesh=mesh, in_specs=in_specs, out_specs=out_specs, check_vma=False
    )
```

```python
import functools
import math

import jax
import jax.numpy as jnp
from jax import lax
from jax.experimental import pallas as pl
from jax.experimental.pallas import tpu as pltpu
from jax.sharding import PartitionSpec as P

HEADS = 16
KV_HEADS = 4
HEAD_DIM = 128
GROUPS = HEADS // KV_HEADS
LONGEST = 4
SCALE = math.log2(math.e) / math.sqrt(HEAD_DIM)
LOWEST = -1e30
EXTRA = 16

NT = (((1,), (1,)), ((), ()))
TN = (((0,), (0,)), ((), ()))


def dot(a, b, dims):
    return lax.dot_general(a, b, dims, preferred_element_type=jnp.float32)


def column(row):
    return jnp.transpose(jnp.broadcast_to(row, (HEAD_DIM, row.shape[1])))


def part_of(i, size):
    return slice(i * size, (i + 1) * size)


def group_queries(q_ref, g):
    heads = [q_ref[:, part_of(g * GROUPS + i, HEAD_DIM)] for i in range(GROUPS)]
    return jnp.concatenate(heads, axis=0)


def share_of(beta_ref, h):
    return 1.0 / (1.0 + jnp.exp(-jnp.full((1, HEAD_DIM), beta_ref[h], jnp.float32)))


def scaled_gains(beta_ref, gain_ref, out_ref):
    for h in range(HEADS):
        scaled = gain_ref[h : h + 1, :] * share_of(beta_ref, h)
        out_ref[part_of(h, HEAD_DIM), :] = column(scaled)


def suffix(others):
    count = jnp.sum(others, axis=1, keepdims=True)
    shape = (others.shape[1], HEAD_DIM)
    return lax.broadcasted_iota(jnp.int32, shape, 0).astype(jnp.float32) >= count


def first_document(docs):
    first = jnp.broadcast_to(docs[:, 0:1], docs.shape)
    return first, docs == first


def load_block(key_ref, value_ref, doc_ref, out_ref, doc_scratch, sems):
    rows = key_ref.shape[0]
    doc_copy = pltpu.make_async_copy(doc_ref, doc_scratch, sems.at[0])
    doc_copy.start()
    copies = []
    for g in range(2 * KV_HEADS):
        source = key_ref if g < KV_HEADS else value_ref
        copy = pltpu.make_async_copy(
            source.at[:, part_of(g % KV_HEADS, HEAD_DIM)],
            out_ref.at[part_of(g, rows), :],
            sems.at[1 + g],
        )
        copy.start()
        copies.append(copy)
    doc_copy.wait()
    start = 2 * KV_HEADS * rows
    docs = doc_scratch[...].astype(jnp.float32)
    docs = jnp.broadcast_to(docs, (out_ref.shape[0] - start, rows))
    out_ref[start:, :] = docs.astype(jnp.bfloat16)
    for copy in copies:
        copy.wait()


def block_keys(ref, g):
    return ref[part_of(g, HEAD_DIM), :]


def block_values(ref, g):
    return ref[part_of(KV_HEADS + g, HEAD_DIM), :]


def block_docs(ref):
    start = 2 * KV_HEADS * HEAD_DIM
    return ref[start : start + EXTRA, :].astype(jnp.float32)[0:1, :]


class Plan:
    def __init__(self, n_seq):
        devices = 2 * n_seq
        near = [(b, b + 1) for b in range(devices - 1)]
        far = [(b, b + 2) for b in range(devices - 2)]
        crossing = [p for p in far if p[0] // 2 % 2 == 1]
        touched = {b for p in crossing for b in p}
        targets = {p[1] for p in crossing}
        first = crossing + [p for p in near if p[0] not in touched and p[1] not in targets]
        second = [p for p in near if p not in first]
        last = [p for p in far if p not in first]
        self.pairs = [first, second, last]
        self.senders = sorted({p[0] for p in first})
        busy = {b for p in first for b in p} & {b for p in second for b in p}
        self.early = [b for b in range(devices) if b not in busy]
        self.late = sorted({p[1] for p in second})
        self.memory_first = [p[1] for p in crossing if p[1] % 2 == 1]


def among(members):
    block = 2 * lax.axis_index("seq") + lax.axis_index("kv")
    return functools.reduce(jnp.logical_or, [block == b for b in members])


def pack_kernel(plan, key_ref, value_ref, doc_ref, out_ref, doc_scratch, sems):
    @pl.when(among(plan.senders))
    def _():
        load_block(key_ref, value_ref, doc_ref, out_ref, doc_scratch, sems)


def attend_own(q_ref, block_ref, g, bias):
    rows = q_ref.shape[0]
    scores = dot(block_keys(block_ref, g), group_queries(q_ref, g), NT)
    tops, totals, weights = [], [], []
    for i in range(GROUPS):
        masked = scores[:, part_of(i, rows)] * SCALE + bias
        top = jnp.max(masked, axis=0, keepdims=True)
        weight = jnp.exp2(masked - top)
        tops.append(top)
        totals.append(jnp.sum(weight, axis=0, keepdims=True))
        weights.append(weight.astype(jnp.bfloat16))
    summed = dot(block_values(block_ref, g), jnp.concatenate(weights, axis=1), TN)
    return summed, jnp.concatenate(tops, axis=1), jnp.concatenate(totals, axis=1)


def own_bias(docs):
    rows = docs.shape[1]
    place = lax.broadcasted_iota(jnp.int32, (rows, rows), 0)
    row = lax.broadcasted_iota(jnp.int32, (rows, rows), 1)
    return jnp.where((place <= row) & (column(docs) == docs), 0.0, LOWEST)


def attend_itself(
    q_ref, block_ref, gain_ref, beta_ref, beta_copy, summed_ref, stats_ref, gains_ref
):
    bias = own_bias(block_docs(block_ref))
    results = [attend_own(q_ref, block_ref, g, bias) for g in range(KV_HEADS)]
    beta_copy.wait()
    scaled_gains(beta_ref, gain_ref, gains_ref)
    done = lax.axis_index("kv") == 0
    for g, (summed, top, total) in enumerate(results):
        rest = [1.0 - share_of(beta_ref, g * GROUPS + i) for i in range(GROUPS)]
        rest = jnp.concatenate(rest, axis=1)
        summed_ref[part_of(g, HEAD_DIM), :] = summed * jnp.where(done, rest / total, 1.0)
        stats_ref[g : g + 1, :] = top
        stats_ref[KV_HEADS + g : KV_HEADS + g + 1, :] = total
        stats_ref[2 * KV_HEADS + g : 2 * KV_HEADS + g + 1, :] = rest


def settle_kernel(
    plan, gain_ref, packed_ref, query_ref, key_ref, value_ref, doc_ref, beta_ref,
    second_ref, own_ref, summed_ref, stats_ref, gains_ref,
    q_scratch, beta_scratch, doc_scratch, sems, early_sems,
):
    sender, early = among(plan.senders), among(plan.early)
    query_copy = pltpu.make_async_copy(query_ref, q_scratch, early_sems.at[0])
    beta_copy = pltpu.make_async_copy(beta_ref, beta_scratch, early_sems.at[1])
    deep = own_ref.shape[0]

    @pl.when(early)
    def _():
        query_copy.start()
        beta_copy.start()

    @pl.when(sender)
    def _():
        own_ref[...] = packed_ref[0:deep, :]

    @pl.when(jnp.logical_not(sender))
    def _():
        load_block(key_ref, value_ref, doc_ref, own_ref, doc_scratch, sems)

    second_ref[0:deep, :] = own_ref[...]
    second_ref[deep:, :] = jnp.zeros((EXTRA, HEAD_DIM), jnp.bfloat16)

    @pl.when(early)
    def _():
        query_copy.wait()
        attend_itself(
            q_scratch, own_ref, gain_ref, beta_scratch, beta_copy,
            summed_ref, stats_ref, gains_ref,
        )


def own_kernel(
    plan, q_ref, gain_ref, own_ref, beta_ref, summed_in, stats_in, gains_in,
    summed_ref, stats_ref, gains_ref, beta_scratch, sem,
):
    @pl.when(jnp.logical_not(among(plan.early)))
    def _():
        beta_copy = pltpu.make_async_copy(beta_ref, beta_scratch, sem)
        beta_copy.start()
        attend_itself(
            q_ref, own_ref, gain_ref, beta_scratch, beta_copy, summed_ref, stats_ref, gains_ref
        )


def memory_state(ref, first, g):
    live = suffix(jnp.where(block_docs(ref) == first, 0.0, 1.0))
    keys = jnp.where(live, block_keys(ref, g).astype(jnp.float32), 0.0).astype(jnp.bfloat16)
    return dot(block_values(ref, g), keys, TN)


def memory_states(refs, first):
    return [
        functools.reduce(jnp.add, [memory_state(ref, first, g) for ref in refs])
        for g in range(KV_HEADS)
    ]


def read_memory(states, q_ref, gains_ref, reads):
    pieces = []
    for state in states:
        high = state.astype(jnp.bfloat16)
        state = state - high.astype(jnp.float32)
        middle = state.astype(jnp.bfloat16)
        low = (state - middle.astype(jnp.float32)).astype(jnp.bfloat16)
        pieces.append(jnp.concatenate([high, middle, low], axis=0))
    products = [dot(pieces[g], group_queries(q_ref, g), NT) for g in range(KV_HEADS)]
    rows = q_ref.shape[0]
    heads = []
    for g in range(KV_HEADS):
        recalled = products[g][part_of(0, HEAD_DIM), :] + (
            products[g][part_of(1, HEAD_DIM), :] + products[g][part_of(2, HEAD_DIM), :]
        )
        for i in range(GROUPS):
            read = recalled[:, part_of(i, rows)]
            square = jnp.sum(read * read, axis=0, keepdims=True) * (1.0 / HEAD_DIM)
            read = read * (lax.rsqrt(square + 1e-06) * reads)
            heads.append(read * gains_ref[part_of(g * GROUPS + i, HEAD_DIM), :])
    return heads


def attend_before(q_ref, one_ref, stats_ref, summed_ref, first, same):
    rows = q_ref.shape[0]
    live = suffix(jnp.where(block_docs(one_ref) == first, 0.0, 1.0))
    bias = jnp.where(live & same, 0.0, LOWEST)
    results = []
    for g in range(KV_HEADS):
        scores = dot(block_keys(one_ref, g), group_queries(q_ref, g), NT)
        weights, factors, scales = [], [], []
        for i in range(GROUPS):
            cut = part_of(i, rows)
            masked = scores[:, cut] * SCALE + bias
            top_own = stats_ref[g : g + 1, cut]
            top = jnp.maximum(jnp.max(masked, axis=0, keepdims=True), top_own)
            weight = jnp.exp2(masked - top)
            factor = jnp.exp2(top_own - top)
            total = stats_ref[KV_HEADS + g : KV_HEADS + g + 1, cut] * factor
            total = total + jnp.sum(weight, axis=0, keepdims=True)
            factors.append(factor)
            scales.append(stats_ref[2 * KV_HEADS + g : 2 * KV_HEADS + g + 1, cut] / total)
            weights.append(weight.astype(jnp.bfloat16))
        added = dot(block_values(one_ref, g), jnp.concatenate(weights, axis=1), TN)
        summed = summed_ref[part_of(g, HEAD_DIM), :] * jnp.concatenate(factors, axis=1) + added
        results.append(summed * jnp.concatenate(scales, axis=1))
    return results


def store_heads(mixed, out_ref, held, sems):
    copies = []
    for g in range(KV_HEADS):
        for i in range(GROUPS):
            h = g * GROUPS + i
            held[:, part_of(h, HEAD_DIM)] = jnp.transpose(mixed(g, i))
        wide = part_of(g, GROUPS * HEAD_DIM)
        copies.append(pltpu.make_async_copy(held.at[:, wide], out_ref.at[:, wide], sems.at[g]))
        copies[g].start()
    for copy in copies:
        copy.wait()


def read_into(read_ref, refs, q_ref, own_ref, gains_ref):
    first, same = first_document(block_docs(own_ref))
    heads = read_memory(
        memory_states(refs, first), q_ref, gains_ref, jnp.where(same, 1.0, 0.0)
    )
    for h, head in enumerate(heads):
        read_ref[part_of(h, HEAD_DIM), :] = head


def read_kernel(plan, q_ref, own_ref, three_ref, gains_ref, read_ref):
    @pl.when((lax.axis_index("kv") == 1) & jnp.logical_not(among(plan.memory_first)))
    def _():
        read_into(read_ref, [three_ref], q_ref, own_ref, gains_ref)


def attend_and_store(
    q_ref, own_ref, earlier_ref, stats_ref, summed_ref, read_ref, out_ref, held, sems
):
    first, same = first_document(block_docs(own_ref))
    results = attend_before(q_ref, earlier_ref, stats_ref, summed_ref, first, same)
    rows = q_ref.shape[0]

    def mixed(g, i):
        read = read_ref[part_of(g * GROUPS + i, HEAD_DIM), :]
        return read + results[g][:, part_of(i, rows)]

    store_heads(mixed, out_ref, held, sems)


def read_and_store(states, q_ref, gains_ref, same, summed_ref, out_ref, held, sems):
    rows = q_ref.shape[0]
    heads = read_memory(states, q_ref, gains_ref, jnp.where(same, 1.0, 0.0))

    def mixed(g, i):
        summed = summed_ref[part_of(g, HEAD_DIM), part_of(i, rows)]
        return heads[g * GROUPS + i] + summed

    store_heads(mixed, out_ref, held, sems)


def early_kernel(
    plan, q_ref, own_ref, one_ref, three_ref, stats_ref, gains_ref, summed_ref, read_in,
    read_ref, state_ref, out_ref, held, sems,
):
    kv = lax.axis_index("kv")
    late = among(plan.late)

    @pl.when((kv == 0) & jnp.logical_not(late))
    def _():
        first, same = first_document(block_docs(own_ref))
        states = memory_states([one_ref, three_ref], first)
        read_and_store(states, q_ref, gains_ref, same, summed_ref, out_ref, held, sems)

    @pl.when((kv == 1) & jnp.logical_not(late))
    def _():
        attend_and_store(
            q_ref, own_ref, one_ref, stats_ref, summed_ref, read_ref, out_ref, held, sems
        )

    @pl.when((kv == 0) & late)
    def _():
        first, _ = first_document(block_docs(own_ref))
        for g, state in enumerate(memory_states([one_ref, three_ref], first)):
            state_ref[part_of(g, HEAD_DIM), :] = state

    @pl.when((kv == 1) & among(plan.memory_first))
    def _():
        read_into(read_ref, [one_ref, three_ref], q_ref, own_ref, gains_ref)


def late_kernel(
    plan, q_ref, own_ref, two_ref, state_ref, summed_ref, stats_ref, gains_ref, read_ref, out_in,
    out_ref, held, sems,
):
    kv = lax.axis_index("kv")
    late = among(plan.late)

    @pl.when((kv == 1) & late)
    def _():
        attend_and_store(
            q_ref, own_ref, two_ref, stats_ref, summed_ref, read_ref, out_ref, held, sems
        )

    @pl.when((kv == 0) & late)
    def _():
        first, same = first_document(block_docs(own_ref))
        states = [
            state_ref[part_of(g, HEAD_DIM), :] + memory_state(two_ref, first, g)
            for g in range(KV_HEADS)
        ]
        read_and_store(states, q_ref, gains_ref, same, summed_ref, out_ref, held, sems)


def near_device(n_seq, queries, keys, values, doc_ids, beta, lin_gain):
    rows = queries.shape[0]
    vmem = pl.BlockSpec(memory_space=pltpu.VMEM)
    hbm = pl.BlockSpec(memory_space=pltpu.HBM)
    in_hbm = functools.partial(pltpu.with_memory_space_constraint, memory_space=pltpu.HBM)
    params = pltpu.CompilerParams(vmem_limit_bytes=32 * 1024 * 1024)
    wide = GROUPS * rows
    group_shape = jax.ShapeDtypeStruct((KV_HEADS * HEAD_DIM, wide), jnp.float32)
    gains_shape = jax.ShapeDtypeStruct((HEADS * HEAD_DIM, HEAD_DIM), jnp.float32)
    docs = doc_ids.reshape(1, rows)
    gain = lin_gain.reshape(HEADS, HEAD_DIM)
    deep = 2 * KV_HEADS * rows + EXTRA

    def estimate(share):
        return pl.CostEstimate(
            flops=int(share * 4 * HEADS * HEAD_DIM * rows * rows),
            bytes_accessed=int(share * 4 * 1024 * 1024),
            transcendentals=int(share * HEADS * rows * rows),
        )

    def send(payload, pairs):
        return lax.ppermute(payload, ("seq", "kv"), pairs)

    plan = Plan(n_seq)
    block_shape = jax.ShapeDtypeStruct((deep, HEAD_DIM), jnp.bfloat16)
    longer_shape = jax.ShapeDtypeStruct((deep + EXTRA, HEAD_DIM), jnp.bfloat16)
    stats_shape = jax.ShapeDtypeStruct((4 * KV_HEADS, wide), jnp.float32)
    state_shape = jax.ShapeDtypeStruct((KV_HEADS * HEAD_DIM, HEAD_DIM), jnp.float32)
    results = [group_shape, stats_shape, gains_shape]
    doc_scratch = pltpu.VMEM((1, rows), jnp.int32)
    beta_scratch = pltpu.SMEM((HEADS,), jnp.float32)
    sems = pltpu.SemaphoreType.DMA((2 * KV_HEADS + 1,))
    block = (in_hbm(keys), in_hbm(values), in_hbm(docs))
    beta = in_hbm(beta)
    packed = pl.pallas_call(
        functools.partial(pack_kernel, plan),
        out_shape=longer_shape,
        in_specs=[hbm] * 3,
        out_specs=vmem,
        scratch_shapes=[doc_scratch, sems],
        compiler_params=params,
        cost_estimate=estimate(0.1),
    )(*block)
    one = send(packed, plan.pairs[0])
    second, own, summed, stats, gains = pl.pallas_call(
        functools.partial(settle_kernel, plan),
        out_shape=[longer_shape, block_shape] + results,
        in_specs=[vmem] * 2 + [hbm] * 5,
        out_specs=[vmem] * 5,
        scratch_shapes=[
            pltpu.VMEM(queries.shape, queries.dtype),
            beta_scratch,
            doc_scratch,
            sems,
            pltpu.SemaphoreType.DMA((2,)),
        ],
        compiler_params=params,
        cost_estimate=estimate(1.0),
    )(gain, packed, in_hbm(queries), *block, beta)
    two = send(second, plan.pairs[1])
    three = send(own, plan.pairs[2])
    summed, stats, gains = pl.pallas_call(
        functools.partial(own_kernel, plan),
        out_shape=results,
        in_specs=[vmem] * 3 + [hbm] + [vmem] * 3,
        out_specs=[vmem] * 3,
        scratch_shapes=[beta_scratch, pltpu.SemaphoreType.DMA],
        input_output_aliases={4: 0, 5: 1, 6: 2},
        compiler_params=params,
        cost_estimate=estimate(1.0),
    )(queries, gain, own, beta, summed, stats, gains)
    read = pl.pallas_call(
        functools.partial(read_kernel, plan),
        out_shape=gains_shape,
        in_specs=[vmem] * 4,
        out_specs=vmem,
        compiler_params=params,
    )(queries, own, three, gains)
    out_shape = jax.ShapeDtypeStruct((rows, HEADS * HEAD_DIM), jnp.float32)
    store_scratch = [
        pltpu.VMEM((rows, HEADS * HEAD_DIM), jnp.float32),
        pltpu.SemaphoreType.DMA((KV_HEADS,)),
    ]
    read, state, out = pl.pallas_call(
        functools.partial(early_kernel, plan),
        out_shape=[gains_shape, state_shape, out_shape],
        in_specs=[vmem] * 8,
        out_specs=[vmem] * 2 + [hbm],
        scratch_shapes=store_scratch,
        input_output_aliases={7: 0},
        compiler_params=params,
    )(queries, own, one, three, stats, gains, summed, read)
    return pl.pallas_call(
        functools.partial(late_kernel, plan),
        out_shape=out_shape,
        in_specs=[vmem] * 8 + [hbm],
        out_specs=hbm,
        scratch_shapes=store_scratch,
        input_output_aliases={8: 0},
        compiler_params=params,
    )(queries, own, two, state, summed, stats, gains, read, out)


def carried_in(part, axis, combine, identity):
    place = lax.axis_index(axis)
    gathered = jax.tree.map(lambda a: lax.all_gather(a, axis), part)
    state = jax.tree.map(lambda a, e: jnp.zeros_like(a) + jnp.asarray(e, a.dtype), part, identity)

    def one(step, state):
        return combine(
            state, jax.tree.map(lambda a: lax.dynamic_index_in_dim(a, step, 0, False), gathered)
        )

    return lax.fori_loop(0, place, one, state)


def join_states(earlier, later):
    state_early, first_early, last_early = earlier
    state_late, first_late, last_late = later
    empty_late = first_late < 0
    joined = (first_late == last_late) & (last_early == first_late)
    merged = state_late + jnp.where(joined, state_early, jnp.zeros_like(state_early))
    combined = jnp.where(empty_late, state_early, merged)
    first_doc = jnp.where(first_early < 0, first_late, first_early)
    last_doc = jnp.where(empty_late, last_early, last_late)
    return (combined, first_doc, last_doc)


def tail_merge(one_side, other_side):
    state_one, first_one, last_one = one_side
    state_other, first_other, last_other = other_side
    top_doc = jnp.maximum(last_one, last_other)
    state_sum = jnp.where(last_one == top_doc, state_one, jnp.zeros_like(state_one))
    state_sum = state_sum + jnp.where(
        last_other == top_doc, state_other, jnp.zeros_like(state_other)
    )
    return (state_sum, jnp.minimum(first_one, first_other), top_doc)


def tail_state(key_rows, value_rows, doc_rows, target_doc):
    count = key_rows.shape[0]
    key_heads = key_rows.reshape(count, KV_HEADS, HEAD_DIM)
    value_heads = value_rows.reshape(count, KV_HEADS, HEAD_DIM)
    live = doc_rows == target_doc
    masked = jnp.where(live[:, None, None], key_heads, jnp.zeros_like(key_heads))
    return jnp.einsum("rgd,rge->gde", masked, value_heads, preferred_element_type=jnp.float32)


def attend_block(
    carry, query_heads, query_pos, query_doc, key_rows, value_rows, key_doc, key_start
):
    running_max, running_sum, accumulated = carry
    key_count = key_rows.shape[0]
    key_heads = key_rows.reshape(key_count, KV_HEADS, HEAD_DIM)
    value_heads = value_rows.reshape(key_count, KV_HEADS, HEAD_DIM)
    scores = jnp.einsum(
        "rgqd,kgd->gqrk", query_heads, key_heads, preferred_element_type=jnp.float32
    )
    scores = scores / jnp.sqrt(jnp.float32(HEAD_DIM))
    key_pos = key_start + jnp.arange(key_count, dtype=jnp.int32)
    allowed = (key_pos[None, :] <= query_pos[:, None]) & (key_doc[None, :] == query_doc[:, None])
    masked = jnp.where(allowed, scores, jnp.float32(-1e30))
    new_max = jnp.maximum(running_max, jnp.max(masked, axis=-1))
    factor = jnp.exp(running_max - new_max)
    weights = jnp.where(allowed, jnp.exp(masked - new_max[..., None]), jnp.float32(0.0))
    new_sum = running_sum * factor + jnp.sum(weights, axis=-1)
    product = jnp.einsum(
        "gqrk,kge->gqre",
        weights.astype(jnp.bfloat16),
        value_heads,
        preferred_element_type=jnp.float32,
    )
    new_accum = accumulated * factor[..., None] + product
    return (new_max, new_sum, new_accum)


def far_device(queries, keys, values, doc_ids, beta, lin_gain):
    row_count = queries.shape[0]
    groups = HEADS // KV_HEADS
    query_heads = queries.reshape(row_count, KV_HEADS, groups, HEAD_DIM)
    position = lax.axis_index("kv") * row_count
    query_pos = position + jnp.arange(row_count, dtype=jnp.int32)
    last_query = position + row_count - 1
    initial = (
        jnp.full((KV_HEADS, groups, row_count), -1e30, jnp.float32),
        jnp.zeros((KV_HEADS, groups, row_count), jnp.float32),
        jnp.zeros((KV_HEADS, groups, row_count, HEAD_DIM), jnp.float32),
    )
    empty_tail = (
        jnp.zeros((KV_HEADS, HEAD_DIM, HEAD_DIM), jnp.float32),
        jnp.array(2**30, jnp.int32),
        jnp.array(-1, jnp.int32),
    )
    key_piece = lax.all_gather(keys, "kv", axis=0, tiled=True)
    value_piece = lax.all_gather(values, "kv", axis=0, tiled=True)
    doc_piece = lax.all_gather(doc_ids, "kv", axis=0, tiled=True)
    blocks = key_piece.shape[0] // row_count

    def one_block(state, item):
        soft_state, tail_now = state
        key_block, value_block, doc_block, number = item
        block_start = number * row_count
        soft_next = lax.cond(
            block_start <= last_query,
            lambda inner: attend_block(
                inner,
                query_heads,
                query_pos,
                doc_ids,
                key_block,
                value_block,
                doc_block,
                block_start,
            ),
            lambda inner: inner,
            soft_state,
        )
        block_tail = (
            tail_state(key_block, value_block, doc_block, doc_block[-1]),
            doc_block[0],
            doc_block[-1],
        )
        tail_now = tail_merge(tail_now, block_tail)
        return ((soft_next, tail_now), None)

    stacked = (
        key_piece.reshape(blocks, row_count, -1),
        value_piece.reshape(blocks, row_count, -1),
        doc_piece.reshape(blocks, row_count),
        jnp.arange(blocks, dtype=jnp.int32),
    )
    result, _ = lax.scan(one_block, (initial, empty_tail), stacked)
    running, segment_tail = result
    running_max, running_sum, accumulated = running
    soft_out = jnp.transpose(accumulated / running_sum[..., None], (2, 0, 1, 3))
    identity = (
        jnp.zeros((KV_HEADS, HEAD_DIM, HEAD_DIM), jnp.float32),
        jnp.array(-1, jnp.int32),
        jnp.array(-1, jnp.int32),
    )
    memory = carried_in(segment_tail, "seq", join_states, identity)
    memory_state, memory_first, memory_last = memory
    query_float = query_heads.astype(jnp.float32)
    recalled = jnp.einsum(
        "rgqd,gde->rgqe", query_float, memory_state, precision=lax.Precision.HIGHEST
    )
    recalled = jnp.where((doc_ids == memory_last)[:, None, None, None], recalled, jnp.float32(0.0))
    mean_square = jnp.mean(recalled * recalled, axis=-1, keepdims=True)
    normed = (
        recalled * lax.rsqrt(mean_square + 1e-06) * lin_gain.reshape(KV_HEADS, groups, HEAD_DIM)
    )
    mixing = jax.nn.sigmoid(beta).reshape(KV_HEADS, groups)[None, :, :, None]
    mixed = mixing * normed + (1.0 - mixing) * soft_out
    return mixed.reshape(row_count, HEADS * HEAD_DIM).astype(jnp.float32)


def solution(mesh):
    n_seq, n_kv = mesh.shape["seq"], mesh.shape["kv"]
    in_specs = (
        P(("dp", "seq", "kv"), None),
        P(("dp", "seq", "kv"), None),
        P(("dp", "seq", "kv"), None),
        P(("dp", "seq", "kv")),
        P(),
        P(),
    )
    out_specs = P(("dp", "seq", "kv"), None)
    if n_kv == 2 and n_seq * n_kv <= 2 * LONGEST:
        on_device = functools.partial(near_device, n_seq)
    else:
        on_device = far_device
    return jax.shard_map(
        on_device, mesh=mesh, in_specs=in_specs, out_specs=out_specs, check_vma=False
    )
```

```python
import functools
import math

import jax
import jax.numpy as jnp
from jax import lax
from jax.experimental import pallas as pl
from jax.experimental.pallas import tpu as pltpu
from jax.sharding import PartitionSpec as P

HEADS = 16
KV_HEADS = 4
HEAD_DIM = 128
GROUPS = HEADS // KV_HEADS
LONGEST = 4
SCALE = math.log2(math.e) / math.sqrt(HEAD_DIM)
LOWEST = -1e30
EXTRA = 16

NT = (((1,), (1,)), ((), ()))
TN = (((0,), (0,)), ((), ()))


def dot(a, b, dims):
    return lax.dot_general(a, b, dims, preferred_element_type=jnp.float32)


def column(row):
    return jnp.transpose(jnp.broadcast_to(row, (HEAD_DIM, row.shape[1])))


def part_of(i, size):
    return slice(i * size, (i + 1) * size)


def group_queries(q_ref, g):
    heads = [q_ref[:, part_of(g * GROUPS + i, HEAD_DIM)] for i in range(GROUPS)]
    return jnp.concatenate(heads, axis=0)


def share_of(beta_ref, h):
    return 1.0 / (1.0 + jnp.exp(-jnp.full((1, HEAD_DIM), beta_ref[h], jnp.float32)))


def scaled_gains(beta_ref, gain_ref, out_ref):
    for h in range(HEADS):
        scaled = gain_ref[h : h + 1, :] * share_of(beta_ref, h)
        out_ref[part_of(h, HEAD_DIM), :] = column(scaled)


def suffix(others):
    count = jnp.sum(others, axis=1, keepdims=True)
    shape = (others.shape[1], HEAD_DIM)
    return lax.broadcasted_iota(jnp.int32, shape, 0).astype(jnp.float32) >= count


def first_document(docs):
    first = jnp.broadcast_to(docs[:, 0:1], docs.shape)
    return first, docs == first


def load_block(key_ref, value_ref, doc_ref, out_ref, doc_scratch, sems):
    rows = key_ref.shape[0]
    doc_copy = pltpu.make_async_copy(doc_ref, doc_scratch, sems.at[0])
    doc_copy.start()
    copies = []
    for g in range(2 * KV_HEADS):
        source = key_ref if g < KV_HEADS else value_ref
        copy = pltpu.make_async_copy(
            source.at[:, part_of(g % KV_HEADS, HEAD_DIM)],
            out_ref.at[part_of(g, rows), :],
            sems.at[1 + g],
        )
        copy.start()
        copies.append(copy)
    doc_copy.wait()
    start = 2 * KV_HEADS * rows
    docs = doc_scratch[...].astype(jnp.float32)
    docs = jnp.broadcast_to(docs, (out_ref.shape[0] - start, rows))
    out_ref[start:, :] = docs.astype(jnp.bfloat16)
    for copy in copies:
        copy.wait()


def block_keys(ref, g):
    return ref[part_of(g, HEAD_DIM), :]


def block_values(ref, g):
    return ref[part_of(KV_HEADS + g, HEAD_DIM), :]


def block_docs(ref):
    start = 2 * KV_HEADS * HEAD_DIM
    return ref[start : start + EXTRA, :].astype(jnp.float32)[0:1, :]


class Plan:
    def __init__(self, n_seq):
        devices = 2 * n_seq
        near = [(b, b + 1) for b in range(devices - 1)]
        far = [(b, b + 2) for b in range(devices - 2)]
        crossing = [p for p in far if p[0] // 2 % 2 == 1]
        touched = {b for p in crossing for b in p}
        targets = {p[1] for p in crossing}
        first = crossing + [p for p in near if p[0] not in touched and p[1] not in targets]
        second = [p for p in near if p not in first]
        last = [p for p in far if p not in first]
        self.pairs = [first, second, last]
        self.senders = sorted({p[0] for p in first})
        busy = {b for p in first for b in p} & {b for p in second for b in p}
        self.early = [b for b in range(devices) if b not in busy]
        self.late = sorted({p[1] for p in second})
        self.memory_first = [p[1] for p in crossing if p[1] % 2 == 1]


def among(members):
    block = 2 * lax.axis_index("seq") + lax.axis_index("kv")
    return functools.reduce(jnp.logical_or, [block == b for b in members])


def pack_kernel(plan, key_ref, value_ref, doc_ref, out_ref, doc_scratch, sems):
    @pl.when(among(plan.senders))
    def _():
        load_block(key_ref, value_ref, doc_ref, out_ref, doc_scratch, sems)


def attend_own(q_ref, block_ref, g, bias):
    rows = q_ref.shape[0]
    scores = dot(block_keys(block_ref, g), group_queries(q_ref, g), NT)
    tops, totals, weights = [], [], []
    for i in range(GROUPS):
        masked = scores[:, part_of(i, rows)] * SCALE + bias
        top = jnp.max(masked, axis=0, keepdims=True)
        weight = jnp.exp2(masked - top)
        tops.append(top)
        totals.append(jnp.sum(weight, axis=0, keepdims=True))
        weights.append(weight.astype(jnp.bfloat16))
    summed = dot(block_values(block_ref, g), jnp.concatenate(weights, axis=1), TN)
    return summed, jnp.concatenate(tops, axis=1), jnp.concatenate(totals, axis=1)


def own_bias(docs):
    rows = docs.shape[1]
    place = lax.broadcasted_iota(jnp.int32, (rows, rows), 0)
    row = lax.broadcasted_iota(jnp.int32, (rows, rows), 1)
    return jnp.where((place <= row) & (column(docs) == docs), 0.0, LOWEST)


def attend_itself(
    q_ref, block_ref, gain_ref, beta_ref, beta_copy, summed_ref, stats_ref, gains_ref
):
    bias = own_bias(block_docs(block_ref))
    results = [attend_own(q_ref, block_ref, g, bias) for g in range(KV_HEADS)]
    beta_copy.wait()
    scaled_gains(beta_ref, gain_ref, gains_ref)
    done = lax.axis_index("kv") == 0
    for g, (summed, top, total) in enumerate(results):
        rest = [1.0 - share_of(beta_ref, g * GROUPS + i) for i in range(GROUPS)]
        rest = jnp.concatenate(rest, axis=1)
        summed_ref[part_of(g, HEAD_DIM), :] = summed * jnp.where(done, rest / total, 1.0)
        stats_ref[g : g + 1, :] = top
        stats_ref[KV_HEADS + g : KV_HEADS + g + 1, :] = total
        stats_ref[2 * KV_HEADS + g : 2 * KV_HEADS + g + 1, :] = rest


def settle_kernel(
    plan, gain_ref, packed_ref, query_ref, key_ref, value_ref, doc_ref, beta_ref,
    second_ref, own_ref, summed_ref, stats_ref, gains_ref,
    q_scratch, beta_scratch, doc_scratch, sems, early_sems,
):
    sender, early = among(plan.senders), among(plan.early)
    query_copy = pltpu.make_async_copy(query_ref, q_scratch, early_sems.at[0])
    beta_copy = pltpu.make_async_copy(beta_ref, beta_scratch, early_sems.at[1])
    deep = own_ref.shape[0]

    @pl.when(early)
    def _():
        query_copy.start()
        beta_copy.start()

    @pl.when(sender)
    def _():
        own_ref[...] = packed_ref[0:deep, :]

    @pl.when(jnp.logical_not(sender))
    def _():
        load_block(key_ref, value_ref, doc_ref, own_ref, doc_scratch, sems)

    second_ref[0:deep, :] = own_ref[...]
    second_ref[deep:, :] = jnp.zeros((EXTRA, HEAD_DIM), jnp.bfloat16)

    @pl.when(early)
    def _():
        query_copy.wait()
        attend_itself(
            q_scratch, own_ref, gain_ref, beta_scratch, beta_copy,
            summed_ref, stats_ref, gains_ref,
        )


def own_kernel(
    plan, q_ref, gain_ref, own_ref, beta_ref, summed_in, stats_in, gains_in,
    summed_ref, stats_ref, gains_ref, beta_scratch, sem,
):
    @pl.when(jnp.logical_not(among(plan.early)))
    def _():
        beta_copy = pltpu.make_async_copy(beta_ref, beta_scratch, sem)
        beta_copy.start()
        attend_itself(
            q_ref, own_ref, gain_ref, beta_scratch, beta_copy, summed_ref, stats_ref, gains_ref
        )


def memory_state(ref, first, g):
    live = suffix(jnp.where(block_docs(ref) == first, 0.0, 1.0))
    keys = jnp.where(live, block_keys(ref, g).astype(jnp.float32), 0.0).astype(jnp.bfloat16)
    return dot(block_values(ref, g), keys, TN)


def memory_states(refs, first):
    return [
        functools.reduce(jnp.add, [memory_state(ref, first, g) for ref in refs])
        for g in range(KV_HEADS)
    ]


def read_memory(states, q_ref, gains_ref, reads):
    pieces = []
    for state in states:
        high = state.astype(jnp.bfloat16)
        state = state - high.astype(jnp.float32)
        middle = state.astype(jnp.bfloat16)
        low = (state - middle.astype(jnp.float32)).astype(jnp.bfloat16)
        pieces.append(jnp.concatenate([high, middle, low], axis=0))
    products = [dot(pieces[g], group_queries(q_ref, g), NT) for g in range(KV_HEADS)]
    rows = q_ref.shape[0]
    heads = []
    for g in range(KV_HEADS):
        recalled = products[g][part_of(0, HEAD_DIM), :] + (
            products[g][part_of(1, HEAD_DIM), :] + products[g][part_of(2, HEAD_DIM), :]
        )
        for i in range(GROUPS):
            read = recalled[:, part_of(i, rows)]
            square = jnp.sum(read * read, axis=0, keepdims=True) * (1.0 / HEAD_DIM)
            read = read * (lax.rsqrt(square + 1e-06) * reads)
            heads.append(read * gains_ref[part_of(g * GROUPS + i, HEAD_DIM), :])
    return heads


def attend_before(q_ref, one_ref, stats_ref, summed_ref, first, same):
    rows = q_ref.shape[0]
    live = suffix(jnp.where(block_docs(one_ref) == first, 0.0, 1.0))
    bias = jnp.where(live & same, 0.0, LOWEST)
    results = []
    for g in range(KV_HEADS):
        scores = dot(block_keys(one_ref, g), group_queries(q_ref, g), NT)
        weights, factors, scales = [], [], []
        for i in range(GROUPS):
            cut = part_of(i, rows)
            masked = scores[:, cut] * SCALE + bias
            top_own = stats_ref[g : g + 1, cut]
            top = jnp.maximum(jnp.max(masked, axis=0, keepdims=True), top_own)
            weight = jnp.exp2(masked - top)
            factor = jnp.exp2(top_own - top)
            total = stats_ref[KV_HEADS + g : KV_HEADS + g + 1, cut] * factor
            total = total + jnp.sum(weight, axis=0, keepdims=True)
            factors.append(factor)
            scales.append(stats_ref[2 * KV_HEADS + g : 2 * KV_HEADS + g + 1, cut] / total)
            weights.append(weight.astype(jnp.bfloat16))
        added = dot(block_values(one_ref, g), jnp.concatenate(weights, axis=1), TN)
        summed = summed_ref[part_of(g, HEAD_DIM), :] * jnp.concatenate(factors, axis=1) + added
        results.append(summed * jnp.concatenate(scales, axis=1))
    return results


def store_heads(mixed, out_ref, held, sems):
    rows = held.shape[0]
    line = lax.broadcasted_iota(jnp.int32, (rows, 2 * rows), 0)
    place = lax.broadcasted_iota(jnp.int32, (rows, 2 * rows), 1)
    same = (place == line) | (place == line + rows)
    identity = jnp.where(same, 1.0, 0.0).astype(jnp.bfloat16)
    copies = []
    for g in range(KV_HEADS):
        heads = jnp.concatenate([mixed(g, i) for i in range(GROUPS)], axis=0)
        high = heads.astype(jnp.bfloat16)
        low = (heads - high.astype(jnp.float32)).astype(jnp.bfloat16)
        wide = part_of(g, GROUPS * HEAD_DIM)
        held[:, wide] = dot(identity, jnp.concatenate([high, low], axis=1), NT)
        copies.append(pltpu.make_async_copy(held.at[:, wide], out_ref.at[:, wide], sems.at[g]))
        copies[g].start()
    for copy in copies:
        copy.wait()


def read_into(read_ref, refs, q_ref, own_ref, gains_ref):
    first, same = first_document(block_docs(own_ref))
    heads = read_memory(
        memory_states(refs, first), q_ref, gains_ref, jnp.where(same, 1.0, 0.0)
    )
    for h, head in enumerate(heads):
        read_ref[part_of(h, HEAD_DIM), :] = head


def read_kernel(plan, q_ref, own_ref, three_ref, gains_ref, read_ref):
    @pl.when((lax.axis_index("kv") == 1) & jnp.logical_not(among(plan.memory_first)))
    def _():
        read_into(read_ref, [three_ref], q_ref, own_ref, gains_ref)


def attend_and_store(
    q_ref, own_ref, earlier_ref, stats_ref, summed_ref, read_ref, out_ref, held, sems
):
    first, same = first_document(block_docs(own_ref))
    results = attend_before(q_ref, earlier_ref, stats_ref, summed_ref, first, same)
    rows = q_ref.shape[0]

    def mixed(g, i):
        read = read_ref[part_of(g * GROUPS + i, HEAD_DIM), :]
        return read + results[g][:, part_of(i, rows)]

    store_heads(mixed, out_ref, held, sems)


def read_and_store(states, q_ref, gains_ref, same, summed_ref, out_ref, held, sems):
    rows = q_ref.shape[0]
    heads = read_memory(states, q_ref, gains_ref, jnp.where(same, 1.0, 0.0))

    def mixed(g, i):
        summed = summed_ref[part_of(g, HEAD_DIM), part_of(i, rows)]
        return heads[g * GROUPS + i] + summed

    store_heads(mixed, out_ref, held, sems)


def early_kernel(
    plan, q_ref, own_ref, one_ref, three_ref, stats_ref, gains_ref, summed_ref, read_in,
    read_ref, state_ref, out_ref, held, sems,
):
    kv = lax.axis_index("kv")
    late = among(plan.late)

    @pl.when((kv == 0) & jnp.logical_not(late))
    def _():
        first, same = first_document(block_docs(own_ref))
        states = memory_states([one_ref, three_ref], first)
        read_and_store(states, q_ref, gains_ref, same, summed_ref, out_ref, held, sems)

    @pl.when((kv == 1) & jnp.logical_not(late))
    def _():
        attend_and_store(
            q_ref, own_ref, one_ref, stats_ref, summed_ref, read_ref, out_ref, held, sems
        )

    @pl.when((kv == 0) & late)
    def _():
        first, _ = first_document(block_docs(own_ref))
        for g, state in enumerate(memory_states([one_ref, three_ref], first)):
            state_ref[part_of(g, HEAD_DIM), :] = state

    @pl.when((kv == 1) & among(plan.memory_first))
    def _():
        read_into(read_ref, [one_ref, three_ref], q_ref, own_ref, gains_ref)


def late_kernel(
    plan, q_ref, own_ref, two_ref, state_ref, summed_ref, stats_ref, gains_ref, read_ref, out_in,
    out_ref, held, sems,
):
    kv = lax.axis_index("kv")
    late = among(plan.late)

    @pl.when((kv == 1) & late)
    def _():
        attend_and_store(
            q_ref, own_ref, two_ref, stats_ref, summed_ref, read_ref, out_ref, held, sems
        )

    @pl.when((kv == 0) & late)
    def _():
        first, same = first_document(block_docs(own_ref))
        states = [
            state_ref[part_of(g, HEAD_DIM), :] + memory_state(two_ref, first, g)
            for g in range(KV_HEADS)
        ]
        read_and_store(states, q_ref, gains_ref, same, summed_ref, out_ref, held, sems)


def near_device(n_seq, queries, keys, values, doc_ids, beta, lin_gain):
    rows = queries.shape[0]
    vmem = pl.BlockSpec(memory_space=pltpu.VMEM)
    hbm = pl.BlockSpec(memory_space=pltpu.HBM)
    in_hbm = functools.partial(pltpu.with_memory_space_constraint, memory_space=pltpu.HBM)
    params = pltpu.CompilerParams(vmem_limit_bytes=32 * 1024 * 1024)
    wide = GROUPS * rows
    group_shape = jax.ShapeDtypeStruct((KV_HEADS * HEAD_DIM, wide), jnp.float32)
    gains_shape = jax.ShapeDtypeStruct((HEADS * HEAD_DIM, HEAD_DIM), jnp.float32)
    docs = doc_ids.reshape(1, rows)
    gain = lin_gain.reshape(HEADS, HEAD_DIM)
    deep = 2 * KV_HEADS * rows + EXTRA

    def estimate(share):
        return pl.CostEstimate(
            flops=int(share * 4 * HEADS * HEAD_DIM * rows * rows),
            bytes_accessed=int(share * 4 * 1024 * 1024),
            transcendentals=int(share * HEADS * rows * rows),
        )

    def send(payload, pairs):
        return lax.ppermute(payload, ("seq", "kv"), pairs)

    plan = Plan(n_seq)
    block_shape = jax.ShapeDtypeStruct((deep, HEAD_DIM), jnp.bfloat16)
    longer_shape = jax.ShapeDtypeStruct((deep + EXTRA, HEAD_DIM), jnp.bfloat16)
    stats_shape = jax.ShapeDtypeStruct((4 * KV_HEADS, wide), jnp.float32)
    state_shape = jax.ShapeDtypeStruct((KV_HEADS * HEAD_DIM, HEAD_DIM), jnp.float32)
    results = [group_shape, stats_shape, gains_shape]
    doc_scratch = pltpu.VMEM((1, rows), jnp.int32)
    beta_scratch = pltpu.SMEM((HEADS,), jnp.float32)
    sems = pltpu.SemaphoreType.DMA((2 * KV_HEADS + 1,))
    block = (in_hbm(keys), in_hbm(values), in_hbm(docs))
    beta = in_hbm(beta)
    packed = pl.pallas_call(
        functools.partial(pack_kernel, plan),
        out_shape=longer_shape,
        in_specs=[hbm] * 3,
        out_specs=vmem,
        scratch_shapes=[doc_scratch, sems],
        compiler_params=params,
        cost_estimate=estimate(0.1),
    )(*block)
    one = send(packed, plan.pairs[0])
    second, own, summed, stats, gains = pl.pallas_call(
        functools.partial(settle_kernel, plan),
        out_shape=[longer_shape, block_shape] + results,
        in_specs=[vmem] * 2 + [hbm] * 5,
        out_specs=[vmem] * 5,
        scratch_shapes=[
            pltpu.VMEM(queries.shape, queries.dtype),
            beta_scratch,
            doc_scratch,
            sems,
            pltpu.SemaphoreType.DMA((2,)),
        ],
        compiler_params=params,
        cost_estimate=estimate(1.0),
    )(gain, packed, in_hbm(queries), *block, beta)
    two = send(second, plan.pairs[1])
    three = send(own, plan.pairs[2])
    summed, stats, gains = pl.pallas_call(
        functools.partial(own_kernel, plan),
        out_shape=results,
        in_specs=[vmem] * 3 + [hbm] + [vmem] * 3,
        out_specs=[vmem] * 3,
        scratch_shapes=[beta_scratch, pltpu.SemaphoreType.DMA],
        input_output_aliases={4: 0, 5: 1, 6: 2},
        compiler_params=params,
        cost_estimate=estimate(1.0),
    )(queries, gain, own, beta, summed, stats, gains)
    read = pl.pallas_call(
        functools.partial(read_kernel, plan),
        out_shape=gains_shape,
        in_specs=[vmem] * 4,
        out_specs=vmem,
        compiler_params=params,
    )(queries, own, three, gains)
    out_shape = jax.ShapeDtypeStruct((rows, HEADS * HEAD_DIM), jnp.float32)
    store_scratch = [
        pltpu.VMEM((rows, HEADS * HEAD_DIM), jnp.float32),
        pltpu.SemaphoreType.DMA((KV_HEADS,)),
    ]
    read, state, out = pl.pallas_call(
        functools.partial(early_kernel, plan),
        out_shape=[gains_shape, state_shape, out_shape],
        in_specs=[vmem] * 8,
        out_specs=[vmem] * 2 + [hbm],
        scratch_shapes=store_scratch,
        input_output_aliases={7: 0},
        compiler_params=params,
    )(queries, own, one, three, stats, gains, summed, read)
    return pl.pallas_call(
        functools.partial(late_kernel, plan),
        out_shape=out_shape,
        in_specs=[vmem] * 8 + [hbm],
        out_specs=hbm,
        scratch_shapes=store_scratch,
        input_output_aliases={8: 0},
        compiler_params=params,
    )(queries, own, two, state, summed, stats, gains, read, out)


def carried_in(part, axis, combine, identity):
    place = lax.axis_index(axis)
    gathered = jax.tree.map(lambda a: lax.all_gather(a, axis), part)
    state = jax.tree.map(lambda a, e: jnp.zeros_like(a) + jnp.asarray(e, a.dtype), part, identity)

    def one(step, state):
        return combine(
            state, jax.tree.map(lambda a: lax.dynamic_index_in_dim(a, step, 0, False), gathered)
        )

    return lax.fori_loop(0, place, one, state)


def join_states(earlier, later):
    state_early, first_early, last_early = earlier
    state_late, first_late, last_late = later
    empty_late = first_late < 0
    joined = (first_late == last_late) & (last_early == first_late)
    merged = state_late + jnp.where(joined, state_early, jnp.zeros_like(state_early))
    combined = jnp.where(empty_late, state_early, merged)
    first_doc = jnp.where(first_early < 0, first_late, first_early)
    last_doc = jnp.where(empty_late, last_early, last_late)
    return (combined, first_doc, last_doc)


def tail_merge(one_side, other_side):
    state_one, first_one, last_one = one_side
    state_other, first_other, last_other = other_side
    top_doc = jnp.maximum(last_one, last_other)
    state_sum = jnp.where(last_one == top_doc, state_one, jnp.zeros_like(state_one))
    state_sum = state_sum + jnp.where(
        last_other == top_doc, state_other, jnp.zeros_like(state_other)
    )
    return (state_sum, jnp.minimum(first_one, first_other), top_doc)


def tail_state(key_rows, value_rows, doc_rows, target_doc):
    count = key_rows.shape[0]
    key_heads = key_rows.reshape(count, KV_HEADS, HEAD_DIM)
    value_heads = value_rows.reshape(count, KV_HEADS, HEAD_DIM)
    live = doc_rows == target_doc
    masked = jnp.where(live[:, None, None], key_heads, jnp.zeros_like(key_heads))
    return jnp.einsum("rgd,rge->gde", masked, value_heads, preferred_element_type=jnp.float32)


def attend_block(
    carry, query_heads, query_pos, query_doc, key_rows, value_rows, key_doc, key_start
):
    running_max, running_sum, accumulated = carry
    key_count = key_rows.shape[0]
    key_heads = key_rows.reshape(key_count, KV_HEADS, HEAD_DIM)
    value_heads = value_rows.reshape(key_count, KV_HEADS, HEAD_DIM)
    scores = jnp.einsum(
        "rgqd,kgd->gqrk", query_heads, key_heads, preferred_element_type=jnp.float32
    )
    scores = scores / jnp.sqrt(jnp.float32(HEAD_DIM))
    key_pos = key_start + jnp.arange(key_count, dtype=jnp.int32)
    allowed = (key_pos[None, :] <= query_pos[:, None]) & (key_doc[None, :] == query_doc[:, None])
    masked = jnp.where(allowed, scores, jnp.float32(-1e30))
    new_max = jnp.maximum(running_max, jnp.max(masked, axis=-1))
    factor = jnp.exp(running_max - new_max)
    weights = jnp.where(allowed, jnp.exp(masked - new_max[..., None]), jnp.float32(0.0))
    new_sum = running_sum * factor + jnp.sum(weights, axis=-1)
    product = jnp.einsum(
        "gqrk,kge->gqre",
        weights.astype(jnp.bfloat16),
        value_heads,
        preferred_element_type=jnp.float32,
    )
    new_accum = accumulated * factor[..., None] + product
    return (new_max, new_sum, new_accum)


def far_device(queries, keys, values, doc_ids, beta, lin_gain):
    row_count = queries.shape[0]
    groups = HEADS // KV_HEADS
    query_heads = queries.reshape(row_count, KV_HEADS, groups, HEAD_DIM)
    position = lax.axis_index("kv") * row_count
    query_pos = position + jnp.arange(row_count, dtype=jnp.int32)
    last_query = position + row_count - 1
    initial = (
        jnp.full((KV_HEADS, groups, row_count), -1e30, jnp.float32),
        jnp.zeros((KV_HEADS, groups, row_count), jnp.float32),
        jnp.zeros((KV_HEADS, groups, row_count, HEAD_DIM), jnp.float32),
    )
    empty_tail = (
        jnp.zeros((KV_HEADS, HEAD_DIM, HEAD_DIM), jnp.float32),
        jnp.array(2**30, jnp.int32),
        jnp.array(-1, jnp.int32),
    )
    key_piece = lax.all_gather(keys, "kv", axis=0, tiled=True)
    value_piece = lax.all_gather(values, "kv", axis=0, tiled=True)
    doc_piece = lax.all_gather(doc_ids, "kv", axis=0, tiled=True)
    blocks = key_piece.shape[0] // row_count

    def one_block(state, item):
        soft_state, tail_now = state
        key_block, value_block, doc_block, number = item
        block_start = number * row_count
        soft_next = lax.cond(
            block_start <= last_query,
            lambda inner: attend_block(
                inner,
                query_heads,
                query_pos,
                doc_ids,
                key_block,
                value_block,
                doc_block,
                block_start,
            ),
            lambda inner: inner,
            soft_state,
        )
        block_tail = (
            tail_state(key_block, value_block, doc_block, doc_block[-1]),
            doc_block[0],
            doc_block[-1],
        )
        tail_now = tail_merge(tail_now, block_tail)
        return ((soft_next, tail_now), None)

    stacked = (
        key_piece.reshape(blocks, row_count, -1),
        value_piece.reshape(blocks, row_count, -1),
        doc_piece.reshape(blocks, row_count),
        jnp.arange(blocks, dtype=jnp.int32),
    )
    result, _ = lax.scan(one_block, (initial, empty_tail), stacked)
    running, segment_tail = result
    running_max, running_sum, accumulated = running
    soft_out = jnp.transpose(accumulated / running_sum[..., None], (2, 0, 1, 3))
    identity = (
        jnp.zeros((KV_HEADS, HEAD_DIM, HEAD_DIM), jnp.float32),
        jnp.array(-1, jnp.int32),
        jnp.array(-1, jnp.int32),
    )
    memory = carried_in(segment_tail, "seq", join_states, identity)
    memory_state, memory_first, memory_last = memory
    query_float = query_heads.astype(jnp.float32)
    recalled = jnp.einsum(
        "rgqd,gde->rgqe", query_float, memory_state, precision=lax.Precision.HIGHEST
    )
    recalled = jnp.where((doc_ids == memory_last)[:, None, None, None], recalled, jnp.float32(0.0))
    mean_square = jnp.mean(recalled * recalled, axis=-1, keepdims=True)
    normed = (
        recalled * lax.rsqrt(mean_square + 1e-06) * lin_gain.reshape(KV_HEADS, groups, HEAD_DIM)
    )
    mixing = jax.nn.sigmoid(beta).reshape(KV_HEADS, groups)[None, :, :, None]
    mixed = mixing * normed + (1.0 - mixing) * soft_out
    return mixed.reshape(row_count, HEADS * HEAD_DIM).astype(jnp.float32)


def solution(mesh):
    n_seq, n_kv = mesh.shape["seq"], mesh.shape["kv"]
    in_specs = (
        P(("dp", "seq", "kv"), None),
        P(("dp", "seq", "kv"), None),
        P(("dp", "seq", "kv"), None),
        P(("dp", "seq", "kv")),
        P(),
        P(),
    )
    out_specs = P(("dp", "seq", "kv"), None)
    if n_kv == 2 and n_seq * n_kv <= 2 * LONGEST:
        on_device = functools.partial(near_device, n_seq)
    else:
        on_device = far_device
    return jax.shard_map(
        on_device, mesh=mesh, in_specs=in_specs, out_specs=out_specs, check_vma=False
    )
```

```python
import functools
import math

import jax
import jax.numpy as jnp
from jax import lax
from jax.experimental import pallas as pl
from jax.experimental.pallas import tpu as pltpu
from jax.sharding import PartitionSpec as P

HEADS = 16
KV_HEADS = 4
HEAD_DIM = 128
GROUPS = HEADS // KV_HEADS
LONGEST = 4
SCALE = math.log2(math.e) / math.sqrt(HEAD_DIM)
LOWEST = -1e30
EXTRA = 16

NT = (((1,), (1,)), ((), ()))
TN = (((0,), (0,)), ((), ()))


def dot(a, b, dims):
    return lax.dot_general(a, b, dims, preferred_element_type=jnp.float32)


def column(row):
    return jnp.transpose(jnp.broadcast_to(row, (HEAD_DIM, row.shape[1])))


def part_of(i, size):
    return slice(i * size, (i + 1) * size)


def group_queries(q_ref, g):
    heads = [q_ref[:, part_of(g * GROUPS + i, HEAD_DIM)] for i in range(GROUPS)]
    return jnp.concatenate(heads, axis=0)


def share_of(beta_ref, h):
    return 1.0 / (1.0 + jnp.exp(-jnp.full((1, HEAD_DIM), beta_ref[h], jnp.float32)))


def scaled_gains(beta_ref, gain_ref, out_ref):
    for h in range(HEADS):
        scaled = gain_ref[h : h + 1, :] * share_of(beta_ref, h)
        out_ref[part_of(h, HEAD_DIM), :] = column(scaled)


def suffix(others, least=0.0):
    count = jnp.maximum(jnp.sum(others, axis=1, keepdims=True), least)
    shape = (others.shape[1], HEAD_DIM)
    return lax.broadcasted_iota(jnp.int32, shape, 0).astype(jnp.float32) >= count


def first_document(docs):
    first = jnp.broadcast_to(docs[:, 0:1], docs.shape)
    return first, docs == first


def load_block(key_ref, value_ref, doc_ref, out_ref, doc_scratch, sems):
    rows = key_ref.shape[0]
    doc_copy = pltpu.make_async_copy(doc_ref, doc_scratch, sems.at[0])
    doc_copy.start()
    copies = []
    for g in range(2 * KV_HEADS):
        source = key_ref if g < KV_HEADS else value_ref
        copy = pltpu.make_async_copy(
            source.at[:, part_of(g % KV_HEADS, HEAD_DIM)],
            out_ref.at[part_of(g, rows), :],
            sems.at[1 + g],
        )
        copy.start()
        copies.append(copy)
    doc_copy.wait()
    start = 2 * KV_HEADS * rows
    docs = doc_scratch[...].astype(jnp.float32)
    docs = jnp.broadcast_to(docs, (out_ref.shape[0] - start, rows))
    out_ref[start:, :] = docs.astype(jnp.bfloat16)
    for copy in copies:
        copy.wait()


def block_keys(ref, g):
    return ref[part_of(g, HEAD_DIM), :]


def block_values(ref, g):
    return ref[part_of(KV_HEADS + g, HEAD_DIM), :]


def block_docs(ref):
    start = 2 * KV_HEADS * HEAD_DIM
    return ref[start : start + EXTRA, :].astype(jnp.float32)[0:1, :]


class Plan:
    def __init__(self, n_seq):
        devices = 2 * n_seq
        near = [(b, b + 1) for b in range(devices - 1)]
        far = [(b, b + 2) for b in range(devices - 2)]
        crossing = [p for p in far if p[0] // 2 % 2 == 1]
        touched = {b for p in crossing for b in p}
        targets = {p[1] for p in crossing}
        first = crossing + [p for p in near if p[0] not in touched and p[1] not in targets]
        second = [p for p in near if p not in first]
        last = [p for p in far if p not in first]
        self.pairs = [first, second, last]
        self.senders = sorted({p[0] for p in first})
        busy = {b for p in first for b in p} & {b for p in second for b in p}
        self.early = [b for b in range(devices) if b not in busy]
        self.late = sorted({p[1] for p in second})
        self.memory_first = [p[1] for p in crossing if p[1] % 2 == 1]


def among(members):
    block = 2 * lax.axis_index("seq") + lax.axis_index("kv")
    return functools.reduce(jnp.logical_or, [block == b for b in members])


def pack_kernel(plan, key_ref, value_ref, doc_ref, out_ref, doc_scratch, sems):
    @pl.when(among(plan.senders))
    def _():
        load_block(key_ref, value_ref, doc_ref, out_ref, doc_scratch, sems)


def attend_own(q_ref, block_ref, g, bias):
    rows = q_ref.shape[0]
    scores = dot(block_keys(block_ref, g), group_queries(q_ref, g), NT)
    tops, totals, weights = [], [], []
    for i in range(GROUPS):
        masked = scores[:, part_of(i, rows)] * SCALE + bias
        top = jnp.max(masked, axis=0, keepdims=True)
        weight = jnp.exp2(masked - top)
        tops.append(top)
        totals.append(jnp.sum(weight, axis=0, keepdims=True))
        weights.append(weight.astype(jnp.bfloat16))
    summed = dot(block_values(block_ref, g), jnp.concatenate(weights, axis=1), TN)
    return summed, jnp.concatenate(tops, axis=1), jnp.concatenate(totals, axis=1)


def own_bias(docs):
    rows = docs.shape[1]
    place = lax.broadcasted_iota(jnp.int32, (rows, rows), 0)
    row = lax.broadcasted_iota(jnp.int32, (rows, rows), 1)
    return jnp.where((place <= row) & (column(docs) == docs), 0.0, LOWEST)


def attend_itself(
    q_ref, block_ref, gain_ref, beta_ref, beta_copy, summed_ref, stats_ref, gains_ref
):
    bias = own_bias(block_docs(block_ref))
    results = [attend_own(q_ref, block_ref, g, bias) for g in range(KV_HEADS)]
    beta_copy.wait()
    scaled_gains(beta_ref, gain_ref, gains_ref)
    done = lax.axis_index("kv") == 0
    for g, (summed, top, total) in enumerate(results):
        rest = [1.0 - share_of(beta_ref, g * GROUPS + i) for i in range(GROUPS)]
        rest = jnp.concatenate(rest, axis=1)
        summed_ref[part_of(g, HEAD_DIM), :] = summed * jnp.where(done, rest / total, 1.0)
        stats_ref[g : g + 1, :] = top
        stats_ref[KV_HEADS + g : KV_HEADS + g + 1, :] = total
        stats_ref[2 * KV_HEADS + g : 2 * KV_HEADS + g + 1, :] = rest


def settle_kernel(
    plan, gain_ref, packed_ref, query_ref, key_ref, value_ref, doc_ref, beta_ref,
    own_ref, short_ref, summed_ref, stats_ref, gains_ref,
    q_scratch, beta_scratch, doc_scratch, sems, early_sems,
):
    sender, early = among(plan.senders), among(plan.early)
    query_copy = pltpu.make_async_copy(query_ref, q_scratch, early_sems.at[0])
    beta_copy = pltpu.make_async_copy(beta_ref, beta_scratch, early_sems.at[1])

    @pl.when(early)
    def _():
        query_copy.start()
        beta_copy.start()

    @pl.when(sender)
    def _():
        own_ref[...] = packed_ref[...]

    @pl.when(jnp.logical_not(sender))
    def _():
        load_block(key_ref, value_ref, doc_ref, own_ref, doc_scratch, sems)

    short_ref[...] = own_ref[0 : short_ref.shape[0], :]
    line = lax.broadcasted_iota(jnp.int32, (EXTRA, HEAD_DIM), 0)
    keys = own_ref[0:EXTRA, :].astype(jnp.float32)
    keys = jnp.where(line == 0, block_docs(own_ref), keys)
    short_ref[0:EXTRA, :] = keys.astype(jnp.bfloat16)

    @pl.when(early)
    def _():
        query_copy.wait()
        attend_itself(
            q_scratch, own_ref, gain_ref, beta_scratch, beta_copy,
            summed_ref, stats_ref, gains_ref,
        )


def own_kernel(
    plan, q_ref, gain_ref, own_ref, beta_ref, summed_in, stats_in, gains_in,
    summed_ref, stats_ref, gains_ref, beta_scratch, sem,
):
    @pl.when(jnp.logical_not(among(plan.early)))
    def _():
        beta_copy = pltpu.make_async_copy(beta_ref, beta_scratch, sem)
        beta_copy.start()
        attend_itself(
            q_ref, own_ref, gain_ref, beta_scratch, beta_copy, summed_ref, stats_ref, gains_ref
        )


def memory_state(ref, first, g):
    short = ref.shape[0] == 2 * KV_HEADS * HEAD_DIM
    docs = ref[0:EXTRA, :].astype(jnp.float32)[0:1, :] if short else block_docs(ref)
    live = suffix(jnp.where(docs == first, 0.0, 1.0), 1.0 if short else 0.0)
    keys = jnp.where(live, block_keys(ref, g).astype(jnp.float32), 0.0).astype(jnp.bfloat16)
    return dot(block_values(ref, g), keys, TN)


def memory_states(refs, first):
    return [
        functools.reduce(jnp.add, [memory_state(ref, first, g) for ref in refs])
        for g in range(KV_HEADS)
    ]


def read_memory(states, q_ref, gains_ref, reads):
    pieces = []
    for state in states:
        high = state.astype(jnp.bfloat16)
        state = state - high.astype(jnp.float32)
        middle = state.astype(jnp.bfloat16)
        low = (state - middle.astype(jnp.float32)).astype(jnp.bfloat16)
        pieces.append(jnp.concatenate([high, middle, low], axis=0))
    products = [dot(pieces[g], group_queries(q_ref, g), NT) for g in range(KV_HEADS)]
    rows = q_ref.shape[0]
    heads = []
    for g in range(KV_HEADS):
        recalled = products[g][part_of(0, HEAD_DIM), :] + (
            products[g][part_of(1, HEAD_DIM), :] + products[g][part_of(2, HEAD_DIM), :]
        )
        for i in range(GROUPS):
            read = recalled[:, part_of(i, rows)]
            square = jnp.sum(read * read, axis=0, keepdims=True) * (1.0 / HEAD_DIM)
            read = read * (lax.rsqrt(square + 1e-06) * reads)
            heads.append(read * gains_ref[part_of(g * GROUPS + i, HEAD_DIM), :])
    return heads


def attend_before(q_ref, one_ref, stats_ref, summed_ref, first, same):
    rows = q_ref.shape[0]
    live = suffix(jnp.where(block_docs(one_ref) == first, 0.0, 1.0))
    bias = jnp.where(live & same, 0.0, LOWEST)
    scores = [
        dot(block_keys(one_ref, g), group_queries(q_ref, g), NT) for g in range(KV_HEADS)
    ]

    def attend(g):
        weights, factors, scales = [], [], []
        for i in range(GROUPS):
            cut = part_of(i, rows)
            masked = scores[g][:, cut] * SCALE + bias
            top_own = stats_ref[g : g + 1, cut]
            top = jnp.maximum(jnp.max(masked, axis=0, keepdims=True), top_own)
            weight = jnp.exp2(masked - top)
            factor = jnp.exp2(top_own - top)
            total = stats_ref[KV_HEADS + g : KV_HEADS + g + 1, cut] * factor
            total = total + jnp.sum(weight, axis=0, keepdims=True)
            factors.append(factor)
            scales.append(stats_ref[2 * KV_HEADS + g : 2 * KV_HEADS + g + 1, cut] / total)
            weights.append(weight.astype(jnp.bfloat16))
        added = dot(block_values(one_ref, g), jnp.concatenate(weights, axis=1), TN)
        summed = summed_ref[part_of(g, HEAD_DIM), :] * jnp.concatenate(factors, axis=1) + added
        return summed * jnp.concatenate(scales, axis=1)

    return attend


def store_heads(mixed, out_ref, held, sems):
    copies = []
    for g in range(KV_HEADS):
        for i, head in enumerate(mixed(g)):
            held[:, part_of(g * GROUPS + i, HEAD_DIM)] = jnp.transpose(head)
        wide = part_of(g, GROUPS * HEAD_DIM)
        copies.append(pltpu.make_async_copy(held.at[:, wide], out_ref.at[:, wide], sems.at[g]))
        copies[g].start()
    for copy in copies:
        copy.wait()


def read_into(read_ref, refs, q_ref, own_ref, gains_ref):
    first, same = first_document(block_docs(own_ref))
    heads = read_memory(
        memory_states(refs, first), q_ref, gains_ref, jnp.where(same, 1.0, 0.0)
    )
    for h, head in enumerate(heads):
        read_ref[part_of(h, HEAD_DIM), :] = head


def read_kernel(plan, q_ref, own_ref, three_ref, gains_ref, read_ref):
    @pl.when((lax.axis_index("kv") == 1) & jnp.logical_not(among(plan.memory_first)))
    def _():
        read_into(read_ref, [three_ref], q_ref, own_ref, gains_ref)


def attend_and_store(
    q_ref, own_ref, earlier_ref, stats_ref, summed_ref, read_ref, out_ref, held, sems
):
    first, same = first_document(block_docs(own_ref))
    attend = attend_before(q_ref, earlier_ref, stats_ref, summed_ref, first, same)
    rows = q_ref.shape[0]

    def mixed(g):
        attended = attend(g)
        return [
            read_ref[part_of(g * GROUPS + i, HEAD_DIM), :] + attended[:, part_of(i, rows)]
            for i in range(GROUPS)
        ]

    store_heads(mixed, out_ref, held, sems)


def read_and_store(states, q_ref, gains_ref, same, summed_ref, out_ref, held, sems):
    rows = q_ref.shape[0]
    heads = read_memory(states, q_ref, gains_ref, jnp.where(same, 1.0, 0.0))

    def mixed(g):
        return [
            heads[g * GROUPS + i] + summed_ref[part_of(g, HEAD_DIM), part_of(i, rows)]
            for i in range(GROUPS)
        ]

    store_heads(mixed, out_ref, held, sems)


def early_kernel(
    plan, q_ref, own_ref, one_ref, three_ref, stats_ref, gains_ref, summed_ref, read_in,
    read_ref, state_ref, out_ref, held, sems,
):
    kv = lax.axis_index("kv")
    late = among(plan.late)

    @pl.when((kv == 0) & jnp.logical_not(late))
    def _():
        first, same = first_document(block_docs(own_ref))
        states = memory_states([one_ref, three_ref], first)
        read_and_store(states, q_ref, gains_ref, same, summed_ref, out_ref, held, sems)

    @pl.when((kv == 1) & jnp.logical_not(late))
    def _():
        attend_and_store(
            q_ref, own_ref, one_ref, stats_ref, summed_ref, read_ref, out_ref, held, sems
        )

    @pl.when((kv == 0) & late)
    def _():
        first, _ = first_document(block_docs(own_ref))
        for g, state in enumerate(memory_states([one_ref, three_ref], first)):
            state_ref[part_of(g, HEAD_DIM), :] = state

    @pl.when((kv == 1) & among(plan.memory_first))
    def _():
        read_into(read_ref, [one_ref, three_ref], q_ref, own_ref, gains_ref)


def late_kernel(
    plan, q_ref, own_ref, two_ref, state_ref, summed_ref, stats_ref, gains_ref, read_ref, out_in,
    out_ref, held, sems,
):
    kv = lax.axis_index("kv")
    late = among(plan.late)

    @pl.when((kv == 1) & late)
    def _():
        attend_and_store(
            q_ref, own_ref, two_ref, stats_ref, summed_ref, read_ref, out_ref, held, sems
        )

    @pl.when((kv == 0) & late)
    def _():
        first, same = first_document(block_docs(own_ref))
        states = [
            state_ref[part_of(g, HEAD_DIM), :] + memory_state(two_ref, first, g)
            for g in range(KV_HEADS)
        ]
        read_and_store(states, q_ref, gains_ref, same, summed_ref, out_ref, held, sems)


def near_device(n_seq, queries, keys, values, doc_ids, beta, lin_gain):
    rows = queries.shape[0]
    vmem = pl.BlockSpec(memory_space=pltpu.VMEM)
    hbm = pl.BlockSpec(memory_space=pltpu.HBM)
    in_hbm = functools.partial(pltpu.with_memory_space_constraint, memory_space=pltpu.HBM)
    params = pltpu.CompilerParams(vmem_limit_bytes=32 * 1024 * 1024)
    wide = GROUPS * rows
    group_shape = jax.ShapeDtypeStruct((KV_HEADS * HEAD_DIM, wide), jnp.float32)
    gains_shape = jax.ShapeDtypeStruct((HEADS * HEAD_DIM, HEAD_DIM), jnp.float32)
    docs = doc_ids.reshape(1, rows)
    gain = lin_gain.reshape(HEADS, HEAD_DIM)
    deep = 2 * KV_HEADS * rows + EXTRA

    def estimate(share):
        return pl.CostEstimate(
            flops=int(share * 4 * HEADS * HEAD_DIM * rows * rows),
            bytes_accessed=int(share * 4 * 1024 * 1024),
            transcendentals=int(share * HEADS * rows * rows),
        )

    def send(payload, pairs):
        return lax.ppermute(payload, ("seq", "kv"), pairs)

    plan = Plan(n_seq)
    block_shape = jax.ShapeDtypeStruct((deep, HEAD_DIM), jnp.bfloat16)
    short_shape = jax.ShapeDtypeStruct((deep - EXTRA, HEAD_DIM), jnp.bfloat16)
    stats_shape = jax.ShapeDtypeStruct((4 * KV_HEADS, wide), jnp.float32)
    state_shape = jax.ShapeDtypeStruct((KV_HEADS * HEAD_DIM, HEAD_DIM), jnp.float32)
    results = [group_shape, stats_shape, gains_shape]
    doc_scratch = pltpu.VMEM((1, rows), jnp.int32)
    beta_scratch = pltpu.SMEM((HEADS,), jnp.float32)
    sems = pltpu.SemaphoreType.DMA((2 * KV_HEADS + 1,))
    block = (in_hbm(keys), in_hbm(values), in_hbm(docs))
    beta = in_hbm(beta)
    packed = pl.pallas_call(
        functools.partial(pack_kernel, plan),
        out_shape=block_shape,
        in_specs=[hbm] * 3,
        out_specs=vmem,
        scratch_shapes=[doc_scratch, sems],
        compiler_params=params,
        cost_estimate=estimate(0.1),
    )(*block)
    one = send(packed, plan.pairs[0])
    own, short, summed, stats, gains = pl.pallas_call(
        functools.partial(settle_kernel, plan),
        out_shape=[block_shape, short_shape] + results,
        in_specs=[vmem] * 2 + [hbm] * 5,
        out_specs=[vmem] * 5,
        scratch_shapes=[
            pltpu.VMEM(queries.shape, queries.dtype),
            beta_scratch,
            doc_scratch,
            sems,
            pltpu.SemaphoreType.DMA((2,)),
        ],
        compiler_params=params,
        cost_estimate=estimate(1.0),
    )(gain, packed, in_hbm(queries), *block, beta)
    two = send(own, plan.pairs[1])
    three = send(short, plan.pairs[2])
    summed, stats, gains = pl.pallas_call(
        functools.partial(own_kernel, plan),
        out_shape=results,
        in_specs=[vmem] * 3 + [hbm] + [vmem] * 3,
        out_specs=[vmem] * 3,
        scratch_shapes=[beta_scratch, pltpu.SemaphoreType.DMA],
        input_output_aliases={4: 0, 5: 1, 6: 2},
        compiler_params=params,
        cost_estimate=estimate(1.0),
    )(queries, gain, own, beta, summed, stats, gains)
    read = pl.pallas_call(
        functools.partial(read_kernel, plan),
        out_shape=gains_shape,
        in_specs=[vmem] * 4,
        out_specs=vmem,
        compiler_params=params,
    )(queries, own, three, gains)
    out_shape = jax.ShapeDtypeStruct((rows, HEADS * HEAD_DIM), jnp.float32)
    store_scratch = [
        pltpu.VMEM((rows, HEADS * HEAD_DIM), jnp.float32),
        pltpu.SemaphoreType.DMA((KV_HEADS,)),
    ]
    read, state, out = pl.pallas_call(
        functools.partial(early_kernel, plan),
        out_shape=[gains_shape, state_shape, out_shape],
        in_specs=[vmem] * 8,
        out_specs=[vmem] * 2 + [hbm],
        scratch_shapes=store_scratch,
        input_output_aliases={7: 0},
        compiler_params=params,
    )(queries, own, one, three, stats, gains, summed, read)
    return pl.pallas_call(
        functools.partial(late_kernel, plan),
        out_shape=out_shape,
        in_specs=[vmem] * 8 + [hbm],
        out_specs=hbm,
        scratch_shapes=store_scratch,
        input_output_aliases={8: 0},
        compiler_params=params,
    )(queries, own, two, state, summed, stats, gains, read, out)


def carried_in(part, axis, combine, identity):
    place = lax.axis_index(axis)
    gathered = jax.tree.map(lambda a: lax.all_gather(a, axis), part)
    state = jax.tree.map(lambda a, e: jnp.zeros_like(a) + jnp.asarray(e, a.dtype), part, identity)

    def one(step, state):
        return combine(
            state, jax.tree.map(lambda a: lax.dynamic_index_in_dim(a, step, 0, False), gathered)
        )

    return lax.fori_loop(0, place, one, state)


def join_states(earlier, later):
    state_early, first_early, last_early = earlier
    state_late, first_late, last_late = later
    empty_late = first_late < 0
    joined = (first_late == last_late) & (last_early == first_late)
    merged = state_late + jnp.where(joined, state_early, jnp.zeros_like(state_early))
    combined = jnp.where(empty_late, state_early, merged)
    first_doc = jnp.where(first_early < 0, first_late, first_early)
    last_doc = jnp.where(empty_late, last_early, last_late)
    return (combined, first_doc, last_doc)


def tail_merge(one_side, other_side):
    state_one, first_one, last_one = one_side
    state_other, first_other, last_other = other_side
    top_doc = jnp.maximum(last_one, last_other)
    state_sum = jnp.where(last_one == top_doc, state_one, jnp.zeros_like(state_one))
    state_sum = state_sum + jnp.where(
        last_other == top_doc, state_other, jnp.zeros_like(state_other)
    )
    return (state_sum, jnp.minimum(first_one, first_other), top_doc)


def tail_state(key_rows, value_rows, doc_rows, target_doc):
    count = key_rows.shape[0]
    key_heads = key_rows.reshape(count, KV_HEADS, HEAD_DIM)
    value_heads = value_rows.reshape(count, KV_HEADS, HEAD_DIM)
    live = doc_rows == target_doc
    masked = jnp.where(live[:, None, None], key_heads, jnp.zeros_like(key_heads))
    return jnp.einsum("rgd,rge->gde", masked, value_heads, preferred_element_type=jnp.float32)


def attend_block(
    carry, query_heads, query_pos, query_doc, key_rows, value_rows, key_doc, key_start
):
    running_max, running_sum, accumulated = carry
    key_count = key_rows.shape[0]
    key_heads = key_rows.reshape(key_count, KV_HEADS, HEAD_DIM)
    value_heads = value_rows.reshape(key_count, KV_HEADS, HEAD_DIM)
    scores = jnp.einsum(
        "rgqd,kgd->gqrk", query_heads, key_heads, preferred_element_type=jnp.float32
    )
    scores = scores / jnp.sqrt(jnp.float32(HEAD_DIM))
    key_pos = key_start + jnp.arange(key_count, dtype=jnp.int32)
    allowed = (key_pos[None, :] <= query_pos[:, None]) & (key_doc[None, :] == query_doc[:, None])
    masked = jnp.where(allowed, scores, jnp.float32(-1e30))
    new_max = jnp.maximum(running_max, jnp.max(masked, axis=-1))
    factor = jnp.exp(running_max - new_max)
    weights = jnp.where(allowed, jnp.exp(masked - new_max[..., None]), jnp.float32(0.0))
    new_sum = running_sum * factor + jnp.sum(weights, axis=-1)
    product = jnp.einsum(
        "gqrk,kge->gqre",
        weights.astype(jnp.bfloat16),
        value_heads,
        preferred_element_type=jnp.float32,
    )
    new_accum = accumulated * factor[..., None] + product
    return (new_max, new_sum, new_accum)


def far_device(queries, keys, values, doc_ids, beta, lin_gain):
    row_count = queries.shape[0]
    groups = HEADS // KV_HEADS
    query_heads = queries.reshape(row_count, KV_HEADS, groups, HEAD_DIM)
    position = lax.axis_index("kv") * row_count
    query_pos = position + jnp.arange(row_count, dtype=jnp.int32)
    last_query = position + row_count - 1
    initial = (
        jnp.full((KV_HEADS, groups, row_count), -1e30, jnp.float32),
        jnp.zeros((KV_HEADS, groups, row_count), jnp.float32),
        jnp.zeros((KV_HEADS, groups, row_count, HEAD_DIM), jnp.float32),
    )
    empty_tail = (
        jnp.zeros((KV_HEADS, HEAD_DIM, HEAD_DIM), jnp.float32),
        jnp.array(2**30, jnp.int32),
        jnp.array(-1, jnp.int32),
    )
    key_piece = lax.all_gather(keys, "kv", axis=0, tiled=True)
    value_piece = lax.all_gather(values, "kv", axis=0, tiled=True)
    doc_piece = lax.all_gather(doc_ids, "kv", axis=0, tiled=True)
    blocks = key_piece.shape[0] // row_count

    def one_block(state, item):
        soft_state, tail_now = state
        key_block, value_block, doc_block, number = item
        block_start = number * row_count
        soft_next = lax.cond(
            block_start <= last_query,
            lambda inner: attend_block(
                inner,
                query_heads,
                query_pos,
                doc_ids,
                key_block,
                value_block,
                doc_block,
                block_start,
            ),
            lambda inner: inner,
            soft_state,
        )
        block_tail = (
            tail_state(key_block, value_block, doc_block, doc_block[-1]),
            doc_block[0],
            doc_block[-1],
        )
        tail_now = tail_merge(tail_now, block_tail)
        return ((soft_next, tail_now), None)

    stacked = (
        key_piece.reshape(blocks, row_count, -1),
        value_piece.reshape(blocks, row_count, -1),
        doc_piece.reshape(blocks, row_count),
        jnp.arange(blocks, dtype=jnp.int32),
    )
    result, _ = lax.scan(one_block, (initial, empty_tail), stacked)
    running, segment_tail = result
    running_max, running_sum, accumulated = running
    soft_out = jnp.transpose(accumulated / running_sum[..., None], (2, 0, 1, 3))
    identity = (
        jnp.zeros((KV_HEADS, HEAD_DIM, HEAD_DIM), jnp.float32),
        jnp.array(-1, jnp.int32),
        jnp.array(-1, jnp.int32),
    )
    memory = carried_in(segment_tail, "seq", join_states, identity)
    memory_state, memory_first, memory_last = memory
    query_float = query_heads.astype(jnp.float32)
    recalled = jnp.einsum(
        "rgqd,gde->rgqe", query_float, memory_state, precision=lax.Precision.HIGHEST
    )
    recalled = jnp.where((doc_ids == memory_last)[:, None, None, None], recalled, jnp.float32(0.0))
    mean_square = jnp.mean(recalled * recalled, axis=-1, keepdims=True)
    normed = (
        recalled * lax.rsqrt(mean_square + 1e-06) * lin_gain.reshape(KV_HEADS, groups, HEAD_DIM)
    )
    mixing = jax.nn.sigmoid(beta).reshape(KV_HEADS, groups)[None, :, :, None]
    mixed = mixing * normed + (1.0 - mixing) * soft_out
    return mixed.reshape(row_count, HEADS * HEAD_DIM).astype(jnp.float32)


def solution(mesh):
    n_seq, n_kv = mesh.shape["seq"], mesh.shape["kv"]
    in_specs = (
        P(("dp", "seq", "kv"), None),
        P(("dp", "seq", "kv"), None),
        P(("dp", "seq", "kv"), None),
        P(("dp", "seq", "kv")),
        P(),
        P(),
    )
    out_specs = P(("dp", "seq", "kv"), None)
    if n_kv == 2 and n_seq * n_kv <= 2 * LONGEST:
        on_device = functools.partial(near_device, n_seq)
    else:
        on_device = far_device
    return jax.shard_map(
        on_device, mesh=mesh, in_specs=in_specs, out_specs=out_specs, check_vma=False
    )
```

```python
import functools
import math

import jax
import jax.numpy as jnp
from jax import lax
from jax.experimental import pallas as pl
from jax.experimental.pallas import tpu as pltpu
from jax.sharding import PartitionSpec as P

HEADS = 16
KV_HEADS = 4
HEAD_DIM = 128
GROUPS = HEADS // KV_HEADS
LONGEST = 4
SCALE = math.log2(math.e) / math.sqrt(HEAD_DIM)
LOWEST = -1e30
EXTRA = 16

NT = (((1,), (1,)), ((), ()))
TN = (((0,), (0,)), ((), ()))


def dot(a, b, dims):
    return lax.dot_general(a, b, dims, preferred_element_type=jnp.float32)


def column(row):
    return jnp.transpose(jnp.broadcast_to(row, (HEAD_DIM, row.shape[1])))


def part_of(i, size):
    return slice(i * size, (i + 1) * size)


def group_queries(q_ref, g):
    heads = [q_ref[:, part_of(g * GROUPS + i, HEAD_DIM)] for i in range(GROUPS)]
    return jnp.concatenate(heads, axis=0)


def share_of(beta_ref, h):
    return 1.0 / (1.0 + jnp.exp(-jnp.full((1, HEAD_DIM), beta_ref[h], jnp.float32)))


def scaled_gains(beta_ref, gain_ref, out_ref):
    for h in range(HEADS):
        scaled = gain_ref[h : h + 1, :] * share_of(beta_ref, h)
        out_ref[part_of(h, HEAD_DIM), :] = column(scaled)


def suffix(others, least=0.0):
    count = jnp.maximum(jnp.sum(others, axis=1, keepdims=True), least)
    shape = (others.shape[1], HEAD_DIM)
    return lax.broadcasted_iota(jnp.int32, shape, 0).astype(jnp.float32) >= count


def first_document(docs):
    first = jnp.broadcast_to(docs[:, 0:1], docs.shape)
    return first, docs == first


def load_block(key_ref, value_ref, doc_ref, out_ref, doc_scratch, sems):
    rows = key_ref.shape[0]
    doc_copy = pltpu.make_async_copy(doc_ref, doc_scratch, sems.at[0])
    doc_copy.start()
    copies = []
    for g in range(2 * KV_HEADS):
        source = key_ref if g < KV_HEADS else value_ref
        copy = pltpu.make_async_copy(
            source.at[:, part_of(g % KV_HEADS, HEAD_DIM)],
            out_ref.at[part_of(g, rows), :],
            sems.at[1 + g],
        )
        copy.start()
        copies.append(copy)
    doc_copy.wait()
    start = 2 * KV_HEADS * rows
    docs = doc_scratch[...].astype(jnp.float32)
    docs = jnp.broadcast_to(docs, (out_ref.shape[0] - start, rows))
    out_ref[start:, :] = docs.astype(jnp.bfloat16)
    for copy in copies:
        copy.wait()


def block_keys(ref, g):
    return ref[part_of(g, HEAD_DIM), :]


def block_values(ref, g):
    return ref[part_of(KV_HEADS + g, HEAD_DIM), :]


def block_docs(ref):
    start = 2 * KV_HEADS * HEAD_DIM
    return ref[start : start + EXTRA, :].astype(jnp.float32)[0:1, :]


class Plan:
    def __init__(self, n_seq):
        devices = 2 * n_seq
        near = [(b, b + 1) for b in range(devices - 1)]
        far = [(b, b + 2) for b in range(devices - 2)]
        crossing = [p for p in far if p[0] // 2 % 2 == 1]
        touched = {b for p in crossing for b in p}
        targets = {p[1] for p in crossing}
        first = crossing + [p for p in near if p[0] not in touched and p[1] not in targets]
        second = [p for p in near if p not in first]
        last = [p for p in far if p not in first]
        self.pairs = [first, second, last]
        self.senders = sorted({p[0] for p in first})
        busy = {b for p in first for b in p} & {b for p in second for b in p}
        self.early = [b for b in range(devices) if b not in busy]
        self.late = sorted({p[1] for p in second})
        received = {p[1] for pairs in self.pairs for p in pairs}
        self.alone = [b for b in range(devices) if b not in received]
        self.memory_first = [p[1] for p in crossing if p[1] % 2 == 1]


def among(members):
    block = 2 * lax.axis_index("seq") + lax.axis_index("kv")
    return functools.reduce(jnp.logical_or, [block == b for b in members])


def pack_kernel(plan, key_ref, value_ref, doc_ref, out_ref, doc_scratch, sems):
    @pl.when(among(plan.senders))
    def _():
        load_block(key_ref, value_ref, doc_ref, out_ref, doc_scratch, sems)


def attend_own(q_ref, block_ref, g, bias):
    rows = q_ref.shape[0]
    scores = dot(block_keys(block_ref, g), group_queries(q_ref, g), NT)
    tops, totals, weights = [], [], []
    for i in range(GROUPS):
        masked = scores[:, part_of(i, rows)] * SCALE + bias
        top = jnp.max(masked, axis=0, keepdims=True)
        weight = jnp.exp2(masked - top)
        tops.append(top)
        totals.append(jnp.sum(weight, axis=0, keepdims=True))
        weights.append(weight.astype(jnp.bfloat16))
    summed = dot(block_values(block_ref, g), jnp.concatenate(weights, axis=1), TN)
    return summed, jnp.concatenate(tops, axis=1), jnp.concatenate(totals, axis=1)


def own_bias(docs):
    rows = docs.shape[1]
    place = lax.broadcasted_iota(jnp.int32, (rows, rows), 0)
    row = lax.broadcasted_iota(jnp.int32, (rows, rows), 1)
    return jnp.where((place <= row) & (column(docs) == docs), 0.0, LOWEST)


def attend_itself(
    q_ref, block_ref, gain_ref, beta_ref, beta_copy, summed_ref, stats_ref, gains_ref
):
    bias = own_bias(block_docs(block_ref))
    results = [attend_own(q_ref, block_ref, g, bias) for g in range(KV_HEADS)]
    beta_copy.wait()
    scaled_gains(beta_ref, gain_ref, gains_ref)
    done = lax.axis_index("kv") == 0
    for g, (summed, top, total) in enumerate(results):
        rest = [1.0 - share_of(beta_ref, g * GROUPS + i) for i in range(GROUPS)]
        rest = jnp.concatenate(rest, axis=1)
        summed_ref[part_of(g, HEAD_DIM), :] = summed * jnp.where(done, rest / total, 1.0)
        stats_ref[g : g + 1, :] = top
        stats_ref[KV_HEADS + g : KV_HEADS + g + 1, :] = total
        stats_ref[2 * KV_HEADS + g : 2 * KV_HEADS + g + 1, :] = rest


def settle_kernel(
    plan, gain_ref, packed_ref, query_ref, key_ref, value_ref, doc_ref, beta_ref,
    own_ref, short_ref, summed_ref, stats_ref, gains_ref,
    q_scratch, beta_scratch, doc_scratch, sems, early_sems,
):
    sender, early = among(plan.senders), among(plan.early)
    query_copy = pltpu.make_async_copy(query_ref, q_scratch, early_sems.at[0])
    beta_copy = pltpu.make_async_copy(beta_ref, beta_scratch, early_sems.at[1])

    @pl.when(early)
    def _():
        query_copy.start()
        beta_copy.start()

    @pl.when(sender)
    def _():
        own_ref[...] = packed_ref[...]

    @pl.when(jnp.logical_not(sender))
    def _():
        load_block(key_ref, value_ref, doc_ref, own_ref, doc_scratch, sems)

    short_ref[...] = own_ref[0 : short_ref.shape[0], :]
    line = lax.broadcasted_iota(jnp.int32, (EXTRA, HEAD_DIM), 0)
    keys = own_ref[0:EXTRA, :].astype(jnp.float32)
    keys = jnp.where(line == 0, block_docs(own_ref), keys)
    short_ref[0:EXTRA, :] = keys.astype(jnp.bfloat16)

    @pl.when(early)
    def _():
        query_copy.wait()
        attend_itself(
            q_scratch, own_ref, gain_ref, beta_scratch, beta_copy,
            summed_ref, stats_ref, gains_ref,
        )


def own_kernel(
    plan, q_ref, gain_ref, own_ref, beta_ref, summed_in, stats_in, gains_in,
    summed_ref, stats_ref, gains_ref, out_ref, beta_scratch, sem, held, sems,
):
    @pl.when(among(plan.alone))
    def _():
        _, same = first_document(block_docs(own_ref))
        states = [jnp.zeros((HEAD_DIM, HEAD_DIM), jnp.float32)] * KV_HEADS
        read_and_store(states, q_ref, gains_ref, same, summed_ref, out_ref, held, sems)

    @pl.when(jnp.logical_not(among(plan.early)))
    def _():
        beta_copy = pltpu.make_async_copy(beta_ref, beta_scratch, sem)
        beta_copy.start()
        attend_itself(
            q_ref, own_ref, gain_ref, beta_scratch, beta_copy, summed_ref, stats_ref, gains_ref
        )


def memory_state(ref, first, g):
    short = ref.shape[0] == 2 * KV_HEADS * HEAD_DIM
    docs = ref[0:EXTRA, :].astype(jnp.float32)[0:1, :] if short else block_docs(ref)
    live = suffix(jnp.where(docs == first, 0.0, 1.0), 1.0 if short else 0.0)
    keys = jnp.where(live, block_keys(ref, g).astype(jnp.float32), 0.0).astype(jnp.bfloat16)
    return dot(block_values(ref, g), keys, TN)


def memory_states(refs, first):
    return [
        functools.reduce(jnp.add, [memory_state(ref, first, g) for ref in refs])
        for g in range(KV_HEADS)
    ]


def read_memory(states, q_ref, gains_ref, reads):
    rows = q_ref.shape[0]
    ahead = {}

    def product(g):
        if g < KV_HEADS and g not in ahead:
            state = states[g]
            high = state.astype(jnp.bfloat16)
            state = state - high.astype(jnp.float32)
            middle = state.astype(jnp.bfloat16)
            low = (state - middle.astype(jnp.float32)).astype(jnp.bfloat16)
            pieces = jnp.concatenate([high, middle, low], axis=0)
            ahead[g] = dot(pieces, group_queries(q_ref, g), NT)

    def read(g):
        product(g)
        product(g + 1)
        recalled = ahead[g][part_of(0, HEAD_DIM), :] + (
            ahead[g][part_of(1, HEAD_DIM), :] + ahead[g][part_of(2, HEAD_DIM), :]
        )
        heads = []
        for i in range(GROUPS):
            head = recalled[:, part_of(i, rows)]
            square = jnp.sum(head * head, axis=0, keepdims=True) * (1.0 / HEAD_DIM)
            head = head * (lax.rsqrt(square + 1e-06) * reads)
            heads.append(head * gains_ref[part_of(g * GROUPS + i, HEAD_DIM), :])
        return heads

    return read


def attend_before(q_ref, one_ref, stats_ref, summed_ref, first, same):
    rows = q_ref.shape[0]
    live = suffix(jnp.where(block_docs(one_ref) == first, 0.0, 1.0))
    bias = jnp.where(live & same, 0.0, LOWEST)
    ahead = {}

    def score(g):
        if g < KV_HEADS and g not in ahead:
            ahead[g] = dot(block_keys(one_ref, g), group_queries(q_ref, g), NT)

    def attend(g):
        score(g)
        score(g + 1)
        weights, factors, scales = [], [], []
        for i in range(GROUPS):
            cut = part_of(i, rows)
            masked = ahead[g][:, cut] * SCALE + bias
            top_own = stats_ref[g : g + 1, cut]
            top = jnp.maximum(jnp.max(masked, axis=0, keepdims=True), top_own)
            weight = jnp.exp2(masked - top)
            factor = jnp.exp2(top_own - top)
            total = stats_ref[KV_HEADS + g : KV_HEADS + g + 1, cut] * factor
            total = total + jnp.sum(weight, axis=0, keepdims=True)
            factors.append(factor)
            scales.append(stats_ref[2 * KV_HEADS + g : 2 * KV_HEADS + g + 1, cut] / total)
            weights.append(weight.astype(jnp.bfloat16))
        added = dot(block_values(one_ref, g), jnp.concatenate(weights, axis=1), TN)
        summed = summed_ref[part_of(g, HEAD_DIM), :] * jnp.concatenate(factors, axis=1) + added
        return summed * jnp.concatenate(scales, axis=1)

    return attend


def store_heads(mixed, out_ref, held, sems):
    copies = []
    for g in range(KV_HEADS):
        for i, head in enumerate(mixed(g)):
            h = g * GROUPS + i
            held[:, part_of(h, HEAD_DIM)] = jnp.transpose(head)
            if h % 2 == 1:
                wide = part_of(h // 2, 2 * HEAD_DIM)
                copy = pltpu.make_async_copy(
                    held.at[:, wide], out_ref.at[:, wide], sems.at[h // 2]
                )
                copy.start()
                copies.append(copy)
    for copy in copies:
        copy.wait()


def read_into(read_ref, refs, q_ref, own_ref, gains_ref):
    first, same = first_document(block_docs(own_ref))
    read = read_memory(
        memory_states(refs, first), q_ref, gains_ref, jnp.where(same, 1.0, 0.0)
    )
    for g in range(KV_HEADS):
        for i, head in enumerate(read(g)):
            read_ref[part_of(g * GROUPS + i, HEAD_DIM), :] = head


def read_kernel(plan, q_ref, own_ref, three_ref, gains_ref, read_ref):
    @pl.when((lax.axis_index("kv") == 1) & jnp.logical_not(among(plan.memory_first)))
    def _():
        read_into(read_ref, [three_ref], q_ref, own_ref, gains_ref)


def attend_and_store(
    q_ref, own_ref, earlier_ref, stats_ref, summed_ref, read_ref, out_ref, held, sems
):
    first, same = first_document(block_docs(own_ref))
    attend = attend_before(q_ref, earlier_ref, stats_ref, summed_ref, first, same)
    rows = q_ref.shape[0]

    def mixed(g):
        attended = attend(g)
        return [
            read_ref[part_of(g * GROUPS + i, HEAD_DIM), :] + attended[:, part_of(i, rows)]
            for i in range(GROUPS)
        ]

    store_heads(mixed, out_ref, held, sems)


def read_and_store(states, q_ref, gains_ref, same, summed_ref, out_ref, held, sems):
    rows = q_ref.shape[0]
    read = read_memory(states, q_ref, gains_ref, jnp.where(same, 1.0, 0.0))

    def mixed(g):
        return [
            head + summed_ref[part_of(g, HEAD_DIM), part_of(i, rows)]
            for i, head in enumerate(read(g))
        ]

    store_heads(mixed, out_ref, held, sems)


def early_kernel(
    plan, q_ref, own_ref, one_ref, three_ref, stats_ref, gains_ref, summed_ref, read_in, out_in,
    read_ref, state_ref, out_ref, held, sems,
):
    kv = lax.axis_index("kv")
    late = among(plan.late)

    @pl.when((kv == 0) & jnp.logical_not(late | among(plan.alone)))
    def _():
        first, same = first_document(block_docs(own_ref))
        states = memory_states([one_ref, three_ref], first)
        read_and_store(states, q_ref, gains_ref, same, summed_ref, out_ref, held, sems)

    @pl.when((kv == 1) & jnp.logical_not(late))
    def _():
        attend_and_store(
            q_ref, own_ref, one_ref, stats_ref, summed_ref, read_ref, out_ref, held, sems
        )

    @pl.when((kv == 0) & late)
    def _():
        first, _ = first_document(block_docs(own_ref))
        for g, state in enumerate(memory_states([one_ref, three_ref], first)):
            state_ref[part_of(g, HEAD_DIM), :] = state

    @pl.when((kv == 1) & among(plan.memory_first))
    def _():
        read_into(read_ref, [one_ref, three_ref], q_ref, own_ref, gains_ref)


def late_kernel(
    plan, q_ref, own_ref, two_ref, state_ref, summed_ref, stats_ref, gains_ref, read_ref, out_in,
    out_ref, held, sems,
):
    kv = lax.axis_index("kv")
    late = among(plan.late)

    @pl.when((kv == 1) & late)
    def _():
        attend_and_store(
            q_ref, own_ref, two_ref, stats_ref, summed_ref, read_ref, out_ref, held, sems
        )

    @pl.when((kv == 0) & late)
    def _():
        first, same = first_document(block_docs(own_ref))
        states = [
            state_ref[part_of(g, HEAD_DIM), :] + memory_state(two_ref, first, g)
            for g in range(KV_HEADS)
        ]
        read_and_store(states, q_ref, gains_ref, same, summed_ref, out_ref, held, sems)


def near_device(n_seq, queries, keys, values, doc_ids, beta, lin_gain):
    rows = queries.shape[0]
    vmem = pl.BlockSpec(memory_space=pltpu.VMEM)
    hbm = pl.BlockSpec(memory_space=pltpu.HBM)
    in_hbm = functools.partial(pltpu.with_memory_space_constraint, memory_space=pltpu.HBM)
    params = pltpu.CompilerParams(vmem_limit_bytes=32 * 1024 * 1024)
    wide = GROUPS * rows
    group_shape = jax.ShapeDtypeStruct((KV_HEADS * HEAD_DIM, wide), jnp.float32)
    gains_shape = jax.ShapeDtypeStruct((HEADS * HEAD_DIM, HEAD_DIM), jnp.float32)
    docs = doc_ids.reshape(1, rows)
    gain = lin_gain.reshape(HEADS, HEAD_DIM)
    deep = 2 * KV_HEADS * rows + EXTRA

    def estimate(share):
        return pl.CostEstimate(
            flops=int(share * 4 * HEADS * HEAD_DIM * rows * rows),
            bytes_accessed=int(share * 4 * 1024 * 1024),
            transcendentals=int(share * HEADS * rows * rows),
        )

    def send(payload, pairs):
        return lax.ppermute(payload, ("seq", "kv"), pairs)

    plan = Plan(n_seq)
    block_shape = jax.ShapeDtypeStruct((deep, HEAD_DIM), jnp.bfloat16)
    short_shape = jax.ShapeDtypeStruct((deep - EXTRA, HEAD_DIM), jnp.bfloat16)
    stats_shape = jax.ShapeDtypeStruct((4 * KV_HEADS, wide), jnp.float32)
    state_shape = jax.ShapeDtypeStruct((KV_HEADS * HEAD_DIM, HEAD_DIM), jnp.float32)
    results = [group_shape, stats_shape, gains_shape]
    doc_scratch = pltpu.VMEM((1, rows), jnp.int32)
    beta_scratch = pltpu.SMEM((HEADS,), jnp.float32)
    sems = pltpu.SemaphoreType.DMA((2 * KV_HEADS + 1,))
    block = (in_hbm(keys), in_hbm(values), in_hbm(docs))
    beta = in_hbm(beta)
    packed = pl.pallas_call(
        functools.partial(pack_kernel, plan),
        out_shape=block_shape,
        in_specs=[hbm] * 3,
        out_specs=vmem,
        scratch_shapes=[doc_scratch, sems],
        compiler_params=params,
        cost_estimate=estimate(0.1),
    )(*block)
    one = send(packed, plan.pairs[0])
    own, short, summed, stats, gains = pl.pallas_call(
        functools.partial(settle_kernel, plan),
        out_shape=[block_shape, short_shape] + results,
        in_specs=[vmem] * 2 + [hbm] * 5,
        out_specs=[vmem] * 5,
        scratch_shapes=[
            pltpu.VMEM(queries.shape, queries.dtype),
            beta_scratch,
            doc_scratch,
            sems,
            pltpu.SemaphoreType.DMA((2,)),
        ],
        compiler_params=params,
        cost_estimate=estimate(1.0),
    )(gain, packed, in_hbm(queries), *block, beta)
    two = send(own, plan.pairs[1])
    three = send(short, plan.pairs[2])
    out_shape = jax.ShapeDtypeStruct((rows, HEADS * HEAD_DIM), jnp.float32)
    store_scratch = [
        pltpu.VMEM((rows, HEADS * HEAD_DIM), jnp.float32),
        pltpu.SemaphoreType.DMA((HEADS // 2,)),
    ]
    summed, stats, gains, out = pl.pallas_call(
        functools.partial(own_kernel, plan),
        out_shape=results + [out_shape],
        in_specs=[vmem] * 3 + [hbm] + [vmem] * 3,
        out_specs=[vmem] * 3 + [hbm],
        scratch_shapes=[beta_scratch, pltpu.SemaphoreType.DMA] + store_scratch,
        input_output_aliases={4: 0, 5: 1, 6: 2},
        compiler_params=params,
        cost_estimate=estimate(1.0),
    )(queries, gain, own, beta, summed, stats, gains)
    read = pl.pallas_call(
        functools.partial(read_kernel, plan),
        out_shape=gains_shape,
        in_specs=[vmem] * 4,
        out_specs=vmem,
        compiler_params=params,
    )(queries, own, three, gains)
    read, state, out = pl.pallas_call(
        functools.partial(early_kernel, plan),
        out_shape=[gains_shape, state_shape, out_shape],
        in_specs=[vmem] * 8 + [hbm],
        out_specs=[vmem] * 2 + [hbm],
        scratch_shapes=store_scratch,
        input_output_aliases={7: 0, 8: 2},
        compiler_params=params,
    )(queries, own, one, three, stats, gains, summed, read, out)
    return pl.pallas_call(
        functools.partial(late_kernel, plan),
        out_shape=out_shape,
        in_specs=[vmem] * 8 + [hbm],
        out_specs=hbm,
        scratch_shapes=store_scratch,
        input_output_aliases={8: 0},
        compiler_params=params,
    )(queries, own, two, state, summed, stats, gains, read, out)


def carried_in(part, axis, combine, identity):
    place = lax.axis_index(axis)
    gathered = jax.tree.map(lambda a: lax.all_gather(a, axis), part)
    state = jax.tree.map(lambda a, e: jnp.zeros_like(a) + jnp.asarray(e, a.dtype), part, identity)

    def one(step, state):
        return combine(
            state, jax.tree.map(lambda a: lax.dynamic_index_in_dim(a, step, 0, False), gathered)
        )

    return lax.fori_loop(0, place, one, state)


def join_states(earlier, later):
    state_early, first_early, last_early = earlier
    state_late, first_late, last_late = later
    empty_late = first_late < 0
    joined = (first_late == last_late) & (last_early == first_late)
    merged = state_late + jnp.where(joined, state_early, jnp.zeros_like(state_early))
    combined = jnp.where(empty_late, state_early, merged)
    first_doc = jnp.where(first_early < 0, first_late, first_early)
    last_doc = jnp.where(empty_late, last_early, last_late)
    return (combined, first_doc, last_doc)


def tail_merge(one_side, other_side):
    state_one, first_one, last_one = one_side
    state_other, first_other, last_other = other_side
    top_doc = jnp.maximum(last_one, last_other)
    state_sum = jnp.where(last_one == top_doc, state_one, jnp.zeros_like(state_one))
    state_sum = state_sum + jnp.where(
        last_other == top_doc, state_other, jnp.zeros_like(state_other)
    )
    return (state_sum, jnp.minimum(first_one, first_other), top_doc)


def tail_state(key_rows, value_rows, doc_rows, target_doc):
    count = key_rows.shape[0]
    key_heads = key_rows.reshape(count, KV_HEADS, HEAD_DIM)
    value_heads = value_rows.reshape(count, KV_HEADS, HEAD_DIM)
    live = doc_rows == target_doc
    masked = jnp.where(live[:, None, None], key_heads, jnp.zeros_like(key_heads))
    return jnp.einsum("rgd,rge->gde", masked, value_heads, preferred_element_type=jnp.float32)


def attend_block(
    carry, query_heads, query_pos, query_doc, key_rows, value_rows, key_doc, key_start
):
    running_max, running_sum, accumulated = carry
    key_count = key_rows.shape[0]
    key_heads = key_rows.reshape(key_count, KV_HEADS, HEAD_DIM)
    value_heads = value_rows.reshape(key_count, KV_HEADS, HEAD_DIM)
    scores = jnp.einsum(
        "rgqd,kgd->gqrk", query_heads, key_heads, preferred_element_type=jnp.float32
    )
    scores = scores / jnp.sqrt(jnp.float32(HEAD_DIM))
    key_pos = key_start + jnp.arange(key_count, dtype=jnp.int32)
    allowed = (key_pos[None, :] <= query_pos[:, None]) & (key_doc[None, :] == query_doc[:, None])
    masked = jnp.where(allowed, scores, jnp.float32(-1e30))
    new_max = jnp.maximum(running_max, jnp.max(masked, axis=-1))
    factor = jnp.exp(running_max - new_max)
    weights = jnp.where(allowed, jnp.exp(masked - new_max[..., None]), jnp.float32(0.0))
    new_sum = running_sum * factor + jnp.sum(weights, axis=-1)
    product = jnp.einsum(
        "gqrk,kge->gqre",
        weights.astype(jnp.bfloat16),
        value_heads,
        preferred_element_type=jnp.float32,
    )
    new_accum = accumulated * factor[..., None] + product
    return (new_max, new_sum, new_accum)


def far_device(queries, keys, values, doc_ids, beta, lin_gain):
    row_count = queries.shape[0]
    groups = HEADS // KV_HEADS
    query_heads = queries.reshape(row_count, KV_HEADS, groups, HEAD_DIM)
    position = lax.axis_index("kv") * row_count
    query_pos = position + jnp.arange(row_count, dtype=jnp.int32)
    last_query = position + row_count - 1
    initial = (
        jnp.full((KV_HEADS, groups, row_count), -1e30, jnp.float32),
        jnp.zeros((KV_HEADS, groups, row_count), jnp.float32),
        jnp.zeros((KV_HEADS, groups, row_count, HEAD_DIM), jnp.float32),
    )
    empty_tail = (
        jnp.zeros((KV_HEADS, HEAD_DIM, HEAD_DIM), jnp.float32),
        jnp.array(2**30, jnp.int32),
        jnp.array(-1, jnp.int32),
    )
    key_piece = lax.all_gather(keys, "kv", axis=0, tiled=True)
    value_piece = lax.all_gather(values, "kv", axis=0, tiled=True)
    doc_piece = lax.all_gather(doc_ids, "kv", axis=0, tiled=True)
    blocks = key_piece.shape[0] // row_count

    def one_block(state, item):
        soft_state, tail_now = state
        key_block, value_block, doc_block, number = item
        block_start = number * row_count
        soft_next = lax.cond(
            block_start <= last_query,
            lambda inner: attend_block(
                inner,
                query_heads,
                query_pos,
                doc_ids,
                key_block,
                value_block,
                doc_block,
                block_start,
            ),
            lambda inner: inner,
            soft_state,
        )
        block_tail = (
            tail_state(key_block, value_block, doc_block, doc_block[-1]),
            doc_block[0],
            doc_block[-1],
        )
        tail_now = tail_merge(tail_now, block_tail)
        return ((soft_next, tail_now), None)

    stacked = (
        key_piece.reshape(blocks, row_count, -1),
        value_piece.reshape(blocks, row_count, -1),
        doc_piece.reshape(blocks, row_count),
        jnp.arange(blocks, dtype=jnp.int32),
    )
    result, _ = lax.scan(one_block, (initial, empty_tail), stacked)
    running, segment_tail = result
    running_max, running_sum, accumulated = running
    soft_out = jnp.transpose(accumulated / running_sum[..., None], (2, 0, 1, 3))
    identity = (
        jnp.zeros((KV_HEADS, HEAD_DIM, HEAD_DIM), jnp.float32),
        jnp.array(-1, jnp.int32),
        jnp.array(-1, jnp.int32),
    )
    memory = carried_in(segment_tail, "seq", join_states, identity)
    memory_state, memory_first, memory_last = memory
    query_float = query_heads.astype(jnp.float32)
    recalled = jnp.einsum(
        "rgqd,gde->rgqe", query_float, memory_state, precision=lax.Precision.HIGHEST
    )
    recalled = jnp.where((doc_ids == memory_last)[:, None, None, None], recalled, jnp.float32(0.0))
    mean_square = jnp.mean(recalled * recalled, axis=-1, keepdims=True)
    normed = (
        recalled * lax.rsqrt(mean_square + 1e-06) * lin_gain.reshape(KV_HEADS, groups, HEAD_DIM)
    )
    mixing = jax.nn.sigmoid(beta).reshape(KV_HEADS, groups)[None, :, :, None]
    mixed = mixing * normed + (1.0 - mixing) * soft_out
    return mixed.reshape(row_count, HEADS * HEAD_DIM).astype(jnp.float32)


def solution(mesh):
    n_seq, n_kv = mesh.shape["seq"], mesh.shape["kv"]
    in_specs = (
        P(("dp", "seq", "kv"), None),
        P(("dp", "seq", "kv"), None),
        P(("dp", "seq", "kv"), None),
        P(("dp", "seq", "kv")),
        P(),
        P(),
    )
    out_specs = P(("dp", "seq", "kv"), None)
    if n_kv == 2 and n_seq * n_kv <= 2 * LONGEST:
        on_device = functools.partial(near_device, n_seq)
    else:
        on_device = far_device
    return jax.shard_map(
        on_device, mesh=mesh, in_specs=in_specs, out_specs=out_specs, check_vma=False
    )
```

```python
import functools
import math

import jax
import jax.numpy as jnp
from jax import lax
from jax.experimental import pallas as pl
from jax.experimental.pallas import tpu as pltpu
from jax.sharding import PartitionSpec as P

HEADS = 16
KV_HEADS = 4
HEAD_DIM = 128
GROUPS = HEADS // KV_HEADS
LONGEST = 4
SCALE = math.log2(math.e) / math.sqrt(HEAD_DIM)
LOWEST = -1e30
EXTRA = 16

NT = (((1,), (1,)), ((), ()))
TN = (((0,), (0,)), ((), ()))
NN = (((1,), (0,)), ((), ()))


def dot(a, b, dims):
    return lax.dot_general(a, b, dims, preferred_element_type=jnp.float32)


def column(row):
    return jnp.transpose(jnp.broadcast_to(row, (HEAD_DIM, row.shape[1])))


def part_of(i, size):
    return slice(i * size, (i + 1) * size)


def group_queries(q_ref, g):
    heads = [q_ref[:, part_of(g * GROUPS + i, HEAD_DIM)] for i in range(GROUPS)]
    return jnp.concatenate(heads, axis=0)


def share_of(beta_ref, h):
    return 1.0 / (1.0 + jnp.exp(-jnp.full((1, HEAD_DIM), beta_ref[h], jnp.float32)))


def scaled_gains(beta_ref, gain_ref, out_ref):
    for h in range(HEADS):
        scaled = gain_ref[h : h + 1, :] * share_of(beta_ref, h)
        out_ref[part_of(h, HEAD_DIM), :] = column(scaled)


def suffix(others, least=0.0):
    count = jnp.maximum(jnp.sum(others, axis=1, keepdims=True), least)
    shape = (others.shape[1], HEAD_DIM)
    return lax.broadcasted_iota(jnp.int32, shape, 0).astype(jnp.float32) >= count


def first_document(docs):
    first = jnp.broadcast_to(docs[:, 0:1], docs.shape)
    return first, docs == first


def load_block(key_ref, value_ref, doc_ref, out_ref, doc_scratch, sems):
    rows = key_ref.shape[0]
    doc_copy = pltpu.make_async_copy(doc_ref, doc_scratch, sems.at[0])
    doc_copy.start()
    copies = []
    for g in range(2 * KV_HEADS):
        source = key_ref if g < KV_HEADS else value_ref
        copy = pltpu.make_async_copy(
            source.at[:, part_of(g % KV_HEADS, HEAD_DIM)],
            out_ref.at[part_of(g, rows), :],
            sems.at[1 + g],
        )
        copy.start()
        copies.append(copy)
    doc_copy.wait()
    start = 2 * KV_HEADS * rows
    docs = doc_scratch[...].astype(jnp.float32)
    docs = jnp.broadcast_to(docs, (out_ref.shape[0] - start, rows))
    out_ref[start:, :] = docs.astype(jnp.bfloat16)
    for copy in copies:
        copy.wait()


def block_keys(ref, g):
    return ref[part_of(g, HEAD_DIM), :]


def block_values(ref, g):
    return ref[part_of(KV_HEADS + g, HEAD_DIM), :]


def block_docs(ref):
    start = 2 * KV_HEADS * HEAD_DIM
    return ref[start : start + EXTRA, :].astype(jnp.float32)[0:1, :]


class Plan:
    def __init__(self, n_seq):
        devices = 2 * n_seq
        near = [(b, b + 1) for b in range(devices - 1)]
        far = [(b, b + 2) for b in range(devices - 2)]
        crossing = [p for p in far if p[0] // 2 % 2 == 1]
        touched = {b for p in crossing for b in p}
        targets = {p[1] for p in crossing}
        first = crossing + [p for p in near if p[0] not in touched and p[1] not in targets]
        second = [p for p in near if p not in first]
        last = [p for p in far if p not in first]
        self.pairs = [first, second, last]
        self.senders = sorted({p[0] for p in first})
        busy = {b for p in first for b in p} & {b for p in second for b in p}
        self.early = [b for b in range(devices) if b not in busy]
        self.late = sorted({p[1] for p in second})
        received = {p[1] for pairs in self.pairs for p in pairs}
        self.alone = [b for b in range(devices) if b not in received]
        self.memory_first = [p[1] for p in crossing if p[1] % 2 == 1]


def among(members):
    block = 2 * lax.axis_index("seq") + lax.axis_index("kv")
    return functools.reduce(jnp.logical_or, [block == b for b in members])


def pack_kernel(plan, key_ref, value_ref, doc_ref, out_ref, doc_scratch, sems):
    @pl.when(among(plan.senders))
    def _():
        load_block(key_ref, value_ref, doc_ref, out_ref, doc_scratch, sems)


def attend_own(q_ref, block_ref, g, bias):
    rows = q_ref.shape[0]
    scores = dot(block_keys(block_ref, g), group_queries(q_ref, g), NT)
    tops, totals, weights = [], [], []
    for i in range(GROUPS):
        masked = scores[:, part_of(i, rows)] * SCALE + bias
        top = jnp.max(masked, axis=0, keepdims=True)
        weight = jnp.exp2(masked - top)
        tops.append(top)
        totals.append(jnp.sum(weight, axis=0, keepdims=True))
        weights.append(weight.astype(jnp.bfloat16))
    summed = dot(block_values(block_ref, g), jnp.concatenate(weights, axis=1), TN)
    return summed, jnp.concatenate(tops, axis=1), jnp.concatenate(totals, axis=1)


def own_bias(docs):
    rows = docs.shape[1]
    place = lax.broadcasted_iota(jnp.int32, (rows, rows), 0)
    row = lax.broadcasted_iota(jnp.int32, (rows, rows), 1)
    return jnp.where((place <= row) & (column(docs) == docs), 0.0, LOWEST)


def attend_itself(
    q_ref, block_ref, gain_ref, beta_ref, beta_copy, summed_ref, stats_ref, gains_ref
):
    bias = own_bias(block_docs(block_ref))
    results = [attend_own(q_ref, block_ref, g, bias) for g in range(KV_HEADS)]
    beta_copy.wait()
    scaled_gains(beta_ref, gain_ref, gains_ref)
    done = lax.axis_index("kv") == 0
    for g, (summed, top, total) in enumerate(results):
        rest = [1.0 - share_of(beta_ref, g * GROUPS + i) for i in range(GROUPS)]
        rest = jnp.concatenate(rest, axis=1)
        summed_ref[part_of(g, HEAD_DIM), :] = summed * jnp.where(done, rest / total, 1.0)
        stats_ref[g : g + 1, :] = top
        stats_ref[KV_HEADS + g : KV_HEADS + g + 1, :] = total
        stats_ref[2 * KV_HEADS + g : 2 * KV_HEADS + g + 1, :] = rest


def settle_kernel(
    plan, gain_ref, packed_ref, query_ref, key_ref, value_ref, doc_ref, beta_ref,
    own_ref, short_ref, summed_ref, stats_ref, gains_ref,
    q_scratch, beta_scratch, doc_scratch, sems, early_sems,
):
    sender, early = among(plan.senders), among(plan.early)
    query_copy = pltpu.make_async_copy(query_ref, q_scratch, early_sems.at[0])
    beta_copy = pltpu.make_async_copy(beta_ref, beta_scratch, early_sems.at[1])

    @pl.when(early)
    def _():
        query_copy.start()
        beta_copy.start()

    @pl.when(sender)
    def _():
        own_ref[...] = packed_ref[...]

    @pl.when(jnp.logical_not(sender))
    def _():
        load_block(key_ref, value_ref, doc_ref, own_ref, doc_scratch, sems)

    short_ref[...] = own_ref[0 : short_ref.shape[0], :]
    line = lax.broadcasted_iota(jnp.int32, (EXTRA, HEAD_DIM), 0)
    keys = own_ref[0:EXTRA, :].astype(jnp.float32)
    keys = jnp.where(line == 0, block_docs(own_ref), keys)
    short_ref[0:EXTRA, :] = keys.astype(jnp.bfloat16)

    @pl.when(early)
    def _():
        query_copy.wait()
        attend_itself(
            q_scratch, own_ref, gain_ref, beta_scratch, beta_copy,
            summed_ref, stats_ref, gains_ref,
        )


def own_kernel(
    plan, q_ref, gain_ref, own_ref, beta_ref, summed_in, stats_in, gains_in,
    summed_ref, stats_ref, gains_ref, out_ref, turned_ref, beta_scratch, sem, held, sems,
):
    rows = q_ref.shape[0]
    for g in range(KV_HEADS):
        for i in range(GROUPS):
            head = q_ref[:, part_of(g * GROUPS + i, HEAD_DIM)]
            turned_ref[part_of(g, HEAD_DIM), part_of(i, rows)] = jnp.transpose(head)

    @pl.when(among(plan.alone))
    def _():
        _, same = first_document(block_docs(own_ref))
        states = [jnp.zeros((HEAD_DIM, HEAD_DIM), jnp.float32)] * KV_HEADS
        read_and_store(states, turned_ref, gains_ref, same, summed_ref, out_ref, held, sems)

    @pl.when(jnp.logical_not(among(plan.early)))
    def _():
        beta_copy = pltpu.make_async_copy(beta_ref, beta_scratch, sem)
        beta_copy.start()
        attend_itself(
            q_ref, own_ref, gain_ref, beta_scratch, beta_copy, summed_ref, stats_ref, gains_ref
        )


def memory_states(refs, first):
    lives = []
    for ref in refs:
        short = ref.shape[0] == 2 * KV_HEADS * HEAD_DIM
        docs = ref[0:EXTRA, :].astype(jnp.float32)[0:1, :] if short else block_docs(ref)
        live = suffix(jnp.where(docs == first, 0.0, 1.0), 1.0 if short else 0.0)
        lives.append(jnp.where(live, 1.0, 0.0).astype(jnp.bfloat16))
    return [
        functools.reduce(
            jnp.add,
            [
                dot(block_values(ref, g), block_keys(ref, g) * live, TN)
                for ref, live in zip(refs, lives)
            ],
        )
        for g in range(KV_HEADS)
    ]


def read_memory(states, turned_ref, gains_ref, reads):
    rows = (turned_ref.shape[1] // GROUPS)
    ahead = {}

    def product(g):
        if g < KV_HEADS and g not in ahead:
            state = states[g]
            high = state.astype(jnp.bfloat16)
            state = state - high.astype(jnp.float32)
            middle = state.astype(jnp.bfloat16)
            low = (state - middle.astype(jnp.float32)).astype(jnp.bfloat16)
            pieces = jnp.concatenate([high, middle, low], axis=0)
            ahead[g] = dot(pieces, turned_ref[part_of(g, HEAD_DIM), :], NN)

    def read(g):
        product(g)
        product(g + 1)
        recalled = ahead[g][part_of(0, HEAD_DIM), :] + (
            ahead[g][part_of(1, HEAD_DIM), :] + ahead[g][part_of(2, HEAD_DIM), :]
        )
        heads = []
        for i in range(GROUPS):
            head = recalled[:, part_of(i, rows)]
            square = jnp.sum(head * head, axis=0, keepdims=True) * (1.0 / HEAD_DIM)
            head = head * (lax.rsqrt(square + 1e-06) * reads)
            heads.append(head * gains_ref[part_of(g * GROUPS + i, HEAD_DIM), :])
        return heads

    return read


def attend_before(turned_ref, one_ref, stats_ref, summed_ref, first, same):
    rows = (turned_ref.shape[1] // GROUPS)
    live = suffix(jnp.where(block_docs(one_ref) == first, 0.0, 1.0))
    bias = jnp.where(live & same, 0.0, LOWEST)
    ahead = {}

    def score(g):
        if g < KV_HEADS and g not in ahead:
            ahead[g] = dot(block_keys(one_ref, g), turned_ref[part_of(g, HEAD_DIM), :], NN)

    def attend(g):
        score(g)
        score(g + 1)
        weights, factors, scales = [], [], []
        for i in range(GROUPS):
            cut = part_of(i, rows)
            masked = ahead[g][:, cut] * SCALE + bias
            top_own = stats_ref[g : g + 1, cut]
            top = jnp.maximum(jnp.max(masked, axis=0, keepdims=True), top_own)
            weight = jnp.exp2(masked - top)
            factor = jnp.exp2(top_own - top)
            total = stats_ref[KV_HEADS + g : KV_HEADS + g + 1, cut] * factor
            total = total + jnp.sum(weight, axis=0, keepdims=True)
            factors.append(factor)
            scales.append(stats_ref[2 * KV_HEADS + g : 2 * KV_HEADS + g + 1, cut] / total)
            weights.append(weight.astype(jnp.bfloat16))
        added = dot(block_values(one_ref, g), jnp.concatenate(weights, axis=1), TN)
        summed = summed_ref[part_of(g, HEAD_DIM), :] * jnp.concatenate(factors, axis=1) + added
        return summed * jnp.concatenate(scales, axis=1)

    return attend


def store_heads(mixed, out_ref, held, sems):
    copies = []
    for g in range(KV_HEADS):
        for i, head in enumerate(mixed(g)):
            h = g * GROUPS + i
            held[:, part_of(h, HEAD_DIM)] = jnp.transpose(head)
            if h % 2 == 1:
                wide = part_of(h // 2, 2 * HEAD_DIM)
                copy = pltpu.make_async_copy(
                    held.at[:, wide], out_ref.at[:, wide], sems.at[h // 2]
                )
                copy.start()
                copies.append(copy)
    for copy in copies:
        copy.wait()


def read_into(read_ref, refs, turned_ref, own_ref, gains_ref):
    first, same = first_document(block_docs(own_ref))
    read = read_memory(
        memory_states(refs, first), turned_ref, gains_ref, jnp.where(same, 1.0, 0.0)
    )
    for g in range(KV_HEADS):
        for i, head in enumerate(read(g)):
            read_ref[part_of(g * GROUPS + i, HEAD_DIM), :] = head


def read_kernel(plan, turned_ref, own_ref, three_ref, gains_ref, read_ref):
    @pl.when((lax.axis_index("kv") == 1) & jnp.logical_not(among(plan.memory_first)))
    def _():
        read_into(read_ref, [three_ref], turned_ref, own_ref, gains_ref)


def attend_and_store(
    turned_ref, own_ref, earlier_ref, stats_ref, summed_ref, read_ref, out_ref, held, sems
):
    first, same = first_document(block_docs(own_ref))
    attend = attend_before(turned_ref, earlier_ref, stats_ref, summed_ref, first, same)
    rows = (turned_ref.shape[1] // GROUPS)

    def mixed(g):
        attended = attend(g)
        return [
            read_ref[part_of(g * GROUPS + i, HEAD_DIM), :] + attended[:, part_of(i, rows)]
            for i in range(GROUPS)
        ]

    store_heads(mixed, out_ref, held, sems)


def read_and_store(states, turned_ref, gains_ref, same, summed_ref, out_ref, held, sems):
    rows = (turned_ref.shape[1] // GROUPS)
    read = read_memory(states, turned_ref, gains_ref, jnp.where(same, 1.0, 0.0))

    def mixed(g):
        return [
            head + summed_ref[part_of(g, HEAD_DIM), part_of(i, rows)]
            for i, head in enumerate(read(g))
        ]

    store_heads(mixed, out_ref, held, sems)


def early_kernel(
    plan, turned_ref, own_ref, one_ref, three_ref, stats_ref, gains_ref, summed_ref, read_in, out_in,
    read_ref, state_ref, out_ref, held, sems,
):
    kv = lax.axis_index("kv")
    late = among(plan.late)

    @pl.when((kv == 0) & jnp.logical_not(late | among(plan.alone)))
    def _():
        first, same = first_document(block_docs(own_ref))
        states = memory_states([one_ref, three_ref], first)
        read_and_store(states, turned_ref, gains_ref, same, summed_ref, out_ref, held, sems)

    @pl.when((kv == 1) & jnp.logical_not(late))
    def _():
        attend_and_store(
            turned_ref, own_ref, one_ref, stats_ref, summed_ref, read_ref, out_ref, held, sems
        )

    @pl.when((kv == 0) & late)
    def _():
        first, _ = first_document(block_docs(own_ref))
        for g, state in enumerate(memory_states([one_ref, three_ref], first)):
            state_ref[part_of(g, HEAD_DIM), :] = state

    @pl.when((kv == 1) & among(plan.memory_first))
    def _():
        read_into(read_ref, [one_ref, three_ref], turned_ref, own_ref, gains_ref)


def late_kernel(
    plan, turned_ref, own_ref, two_ref, state_ref, summed_ref, stats_ref, gains_ref, read_ref, out_in,
    out_ref, held, sems,
):
    kv = lax.axis_index("kv")
    late = among(plan.late)

    @pl.when((kv == 1) & late)
    def _():
        attend_and_store(
            turned_ref, own_ref, two_ref, stats_ref, summed_ref, read_ref, out_ref, held, sems
        )

    @pl.when((kv == 0) & late)
    def _():
        first, same = first_document(block_docs(own_ref))
        states = [
            state_ref[part_of(g, HEAD_DIM), :] + state
            for g, state in enumerate(memory_states([two_ref], first))
        ]
        read_and_store(states, turned_ref, gains_ref, same, summed_ref, out_ref, held, sems)


def near_device(n_seq, queries, keys, values, doc_ids, beta, lin_gain):
    rows = queries.shape[0]
    vmem = pl.BlockSpec(memory_space=pltpu.VMEM)
    hbm = pl.BlockSpec(memory_space=pltpu.HBM)
    in_hbm = functools.partial(pltpu.with_memory_space_constraint, memory_space=pltpu.HBM)
    params = pltpu.CompilerParams(vmem_limit_bytes=32 * 1024 * 1024)
    wide = GROUPS * rows
    group_shape = jax.ShapeDtypeStruct((KV_HEADS * HEAD_DIM, wide), jnp.float32)
    gains_shape = jax.ShapeDtypeStruct((HEADS * HEAD_DIM, HEAD_DIM), jnp.float32)
    docs = doc_ids.reshape(1, rows)
    gain = lin_gain.reshape(HEADS, HEAD_DIM)
    deep = 2 * KV_HEADS * rows + EXTRA

    def estimate(share):
        return pl.CostEstimate(
            flops=int(share * 4 * HEADS * HEAD_DIM * rows * rows),
            bytes_accessed=int(share * 4 * 1024 * 1024),
            transcendentals=int(share * HEADS * rows * rows),
        )

    def send(payload, pairs):
        return lax.ppermute(payload, ("seq", "kv"), pairs)

    plan = Plan(n_seq)
    block_shape = jax.ShapeDtypeStruct((deep, HEAD_DIM), jnp.bfloat16)
    short_shape = jax.ShapeDtypeStruct((deep - EXTRA, HEAD_DIM), jnp.bfloat16)
    stats_shape = jax.ShapeDtypeStruct((4 * KV_HEADS, wide), jnp.float32)
    state_shape = jax.ShapeDtypeStruct((KV_HEADS * HEAD_DIM, HEAD_DIM), jnp.float32)
    results = [group_shape, stats_shape, gains_shape]
    doc_scratch = pltpu.VMEM((1, rows), jnp.int32)
    beta_scratch = pltpu.SMEM((HEADS,), jnp.float32)
    sems = pltpu.SemaphoreType.DMA((2 * KV_HEADS + 1,))
    block = (in_hbm(keys), in_hbm(values), in_hbm(docs))
    beta = in_hbm(beta)
    packed = pl.pallas_call(
        functools.partial(pack_kernel, plan),
        out_shape=block_shape,
        in_specs=[hbm] * 3,
        out_specs=vmem,
        scratch_shapes=[doc_scratch, sems],
        compiler_params=params,
        cost_estimate=estimate(0.1),
    )(*block)
    one = send(packed, plan.pairs[0])
    own, short, summed, stats, gains = pl.pallas_call(
        functools.partial(settle_kernel, plan),
        out_shape=[block_shape, short_shape] + results,
        in_specs=[vmem] * 2 + [hbm] * 5,
        out_specs=[vmem] * 5,
        scratch_shapes=[
            pltpu.VMEM(queries.shape, queries.dtype),
            beta_scratch,
            doc_scratch,
            sems,
            pltpu.SemaphoreType.DMA((2,)),
        ],
        compiler_params=params,
        cost_estimate=estimate(1.0),
    )(gain, packed, in_hbm(queries), *block, beta)
    two = send(own, plan.pairs[1])
    three = send(short, plan.pairs[2])
    out_shape = jax.ShapeDtypeStruct((rows, HEADS * HEAD_DIM), jnp.float32)
    store_scratch = [
        pltpu.VMEM((rows, HEADS * HEAD_DIM), jnp.float32),
        pltpu.SemaphoreType.DMA((HEADS // 2,)),
    ]
    turned_shape = jax.ShapeDtypeStruct((KV_HEADS * HEAD_DIM, wide), queries.dtype)
    summed, stats, gains, out, turned = pl.pallas_call(
        functools.partial(own_kernel, plan),
        out_shape=results + [out_shape, turned_shape],
        in_specs=[vmem] * 3 + [hbm] + [vmem] * 3,
        out_specs=[vmem] * 3 + [hbm, vmem],
        scratch_shapes=[beta_scratch, pltpu.SemaphoreType.DMA] + store_scratch,
        input_output_aliases={4: 0, 5: 1, 6: 2},
        compiler_params=params,
        cost_estimate=estimate(1.0),
    )(queries, gain, own, beta, summed, stats, gains)
    read = pl.pallas_call(
        functools.partial(read_kernel, plan),
        out_shape=gains_shape,
        in_specs=[vmem] * 4,
        out_specs=vmem,
        compiler_params=params,
    )(turned, own, three, gains)
    read, state, out = pl.pallas_call(
        functools.partial(early_kernel, plan),
        out_shape=[gains_shape, state_shape, out_shape],
        in_specs=[vmem] * 8 + [hbm],
        out_specs=[vmem] * 2 + [hbm],
        scratch_shapes=store_scratch,
        input_output_aliases={7: 0, 8: 2},
        compiler_params=params,
    )(turned, own, one, three, stats, gains, summed, read, out)
    return pl.pallas_call(
        functools.partial(late_kernel, plan),
        out_shape=out_shape,
        in_specs=[vmem] * 8 + [hbm],
        out_specs=hbm,
        scratch_shapes=store_scratch,
        input_output_aliases={8: 0},
        compiler_params=params,
    )(turned, own, two, state, summed, stats, gains, read, out)


def carried_in(part, axis, combine, identity):
    place = lax.axis_index(axis)
    gathered = jax.tree.map(lambda a: lax.all_gather(a, axis), part)
    state = jax.tree.map(lambda a, e: jnp.zeros_like(a) + jnp.asarray(e, a.dtype), part, identity)

    def one(step, state):
        return combine(
            state, jax.tree.map(lambda a: lax.dynamic_index_in_dim(a, step, 0, False), gathered)
        )

    return lax.fori_loop(0, place, one, state)


def join_states(earlier, later):
    state_early, first_early, last_early = earlier
    state_late, first_late, last_late = later
    empty_late = first_late < 0
    joined = (first_late == last_late) & (last_early == first_late)
    merged = state_late + jnp.where(joined, state_early, jnp.zeros_like(state_early))
    combined = jnp.where(empty_late, state_early, merged)
    first_doc = jnp.where(first_early < 0, first_late, first_early)
    last_doc = jnp.where(empty_late, last_early, last_late)
    return (combined, first_doc, last_doc)


def tail_merge(one_side, other_side):
    state_one, first_one, last_one = one_side
    state_other, first_other, last_other = other_side
    top_doc = jnp.maximum(last_one, last_other)
    state_sum = jnp.where(last_one == top_doc, state_one, jnp.zeros_like(state_one))
    state_sum = state_sum + jnp.where(
        last_other == top_doc, state_other, jnp.zeros_like(state_other)
    )
    return (state_sum, jnp.minimum(first_one, first_other), top_doc)


def tail_state(key_rows, value_rows, doc_rows, target_doc):
    count = key_rows.shape[0]
    key_heads = key_rows.reshape(count, KV_HEADS, HEAD_DIM)
    value_heads = value_rows.reshape(count, KV_HEADS, HEAD_DIM)
    live = doc_rows == target_doc
    masked = jnp.where(live[:, None, None], key_heads, jnp.zeros_like(key_heads))
    return jnp.einsum("rgd,rge->gde", masked, value_heads, preferred_element_type=jnp.float32)


def attend_block(
    carry, query_heads, query_pos, query_doc, key_rows, value_rows, key_doc, key_start
):
    running_max, running_sum, accumulated = carry
    key_count = key_rows.shape[0]
    key_heads = key_rows.reshape(key_count, KV_HEADS, HEAD_DIM)
    value_heads = value_rows.reshape(key_count, KV_HEADS, HEAD_DIM)
    scores = jnp.einsum(
        "rgqd,kgd->gqrk", query_heads, key_heads, preferred_element_type=jnp.float32
    )
    scores = scores / jnp.sqrt(jnp.float32(HEAD_DIM))
    key_pos = key_start + jnp.arange(key_count, dtype=jnp.int32)
    allowed = (key_pos[None, :] <= query_pos[:, None]) & (key_doc[None, :] == query_doc[:, None])
    masked = jnp.where(allowed, scores, jnp.float32(-1e30))
    new_max = jnp.maximum(running_max, jnp.max(masked, axis=-1))
    factor = jnp.exp(running_max - new_max)
    weights = jnp.where(allowed, jnp.exp(masked - new_max[..., None]), jnp.float32(0.0))
    new_sum = running_sum * factor + jnp.sum(weights, axis=-1)
    product = jnp.einsum(
        "gqrk,kge->gqre",
        weights.astype(jnp.bfloat16),
        value_heads,
        preferred_element_type=jnp.float32,
    )
    new_accum = accumulated * factor[..., None] + product
    return (new_max, new_sum, new_accum)


def far_device(queries, keys, values, doc_ids, beta, lin_gain):
    row_count = queries.shape[0]
    groups = HEADS // KV_HEADS
    query_heads = queries.reshape(row_count, KV_HEADS, groups, HEAD_DIM)
    position = lax.axis_index("kv") * row_count
    query_pos = position + jnp.arange(row_count, dtype=jnp.int32)
    last_query = position + row_count - 1
    initial = (
        jnp.full((KV_HEADS, groups, row_count), -1e30, jnp.float32),
        jnp.zeros((KV_HEADS, groups, row_count), jnp.float32),
        jnp.zeros((KV_HEADS, groups, row_count, HEAD_DIM), jnp.float32),
    )
    empty_tail = (
        jnp.zeros((KV_HEADS, HEAD_DIM, HEAD_DIM), jnp.float32),
        jnp.array(2**30, jnp.int32),
        jnp.array(-1, jnp.int32),
    )
    key_piece = lax.all_gather(keys, "kv", axis=0, tiled=True)
    value_piece = lax.all_gather(values, "kv", axis=0, tiled=True)
    doc_piece = lax.all_gather(doc_ids, "kv", axis=0, tiled=True)
    blocks = key_piece.shape[0] // row_count

    def one_block(state, item):
        soft_state, tail_now = state
        key_block, value_block, doc_block, number = item
        block_start = number * row_count
        soft_next = lax.cond(
            block_start <= last_query,
            lambda inner: attend_block(
                inner,
                query_heads,
                query_pos,
                doc_ids,
                key_block,
                value_block,
                doc_block,
                block_start,
            ),
            lambda inner: inner,
            soft_state,
        )
        block_tail = (
            tail_state(key_block, value_block, doc_block, doc_block[-1]),
            doc_block[0],
            doc_block[-1],
        )
        tail_now = tail_merge(tail_now, block_tail)
        return ((soft_next, tail_now), None)

    stacked = (
        key_piece.reshape(blocks, row_count, -1),
        value_piece.reshape(blocks, row_count, -1),
        doc_piece.reshape(blocks, row_count),
        jnp.arange(blocks, dtype=jnp.int32),
    )
    result, _ = lax.scan(one_block, (initial, empty_tail), stacked)
    running, segment_tail = result
    running_max, running_sum, accumulated = running
    soft_out = jnp.transpose(accumulated / running_sum[..., None], (2, 0, 1, 3))
    identity = (
        jnp.zeros((KV_HEADS, HEAD_DIM, HEAD_DIM), jnp.float32),
        jnp.array(-1, jnp.int32),
        jnp.array(-1, jnp.int32),
    )
    memory = carried_in(segment_tail, "seq", join_states, identity)
    memory_state, memory_first, memory_last = memory
    query_float = query_heads.astype(jnp.float32)
    recalled = jnp.einsum(
        "rgqd,gde->rgqe", query_float, memory_state, precision=lax.Precision.HIGHEST
    )
    recalled = jnp.where((doc_ids == memory_last)[:, None, None, None], recalled, jnp.float32(0.0))
    mean_square = jnp.mean(recalled * recalled, axis=-1, keepdims=True)
    normed = (
        recalled * lax.rsqrt(mean_square + 1e-06) * lin_gain.reshape(KV_HEADS, groups, HEAD_DIM)
    )
    mixing = jax.nn.sigmoid(beta).reshape(KV_HEADS, groups)[None, :, :, None]
    mixed = mixing * normed + (1.0 - mixing) * soft_out
    return mixed.reshape(row_count, HEADS * HEAD_DIM).astype(jnp.float32)


def solution(mesh):
    n_seq, n_kv = mesh.shape["seq"], mesh.shape["kv"]
    in_specs = (
        P(("dp", "seq", "kv"), None),
        P(("dp", "seq", "kv"), None),
        P(("dp", "seq", "kv"), None),
        P(("dp", "seq", "kv")),
        P(),
        P(),
    )
    out_specs = P(("dp", "seq", "kv"), None)
    if n_kv == 2 and n_seq * n_kv <= 2 * LONGEST:
        on_device = functools.partial(near_device, n_seq)
    else:
        on_device = far_device
    return jax.shard_map(
        on_device, mesh=mesh, in_specs=in_specs, out_specs=out_specs, check_vma=False
    )
```

```python
import functools
import math

import jax
import jax.numpy as jnp
from jax import lax
from jax.experimental import pallas as pl
from jax.experimental.pallas import tpu as pltpu
from jax.sharding import PartitionSpec as P

HEADS = 16
KV_HEADS = 4
HEAD_DIM = 128
GROUPS = HEADS // KV_HEADS
LONGEST = 4
SCALE = math.log2(math.e) / math.sqrt(HEAD_DIM)
LOWEST = -1e30
EXTRA = 16

NT = (((1,), (1,)), ((), ()))
TN = (((0,), (0,)), ((), ()))
NN = (((1,), (0,)), ((), ()))


def dot(a, b, dims):
    return lax.dot_general(a, b, dims, preferred_element_type=jnp.float32)


def column(row):
    return jnp.transpose(jnp.broadcast_to(row, (HEAD_DIM, row.shape[1])))


def part_of(i, size):
    return slice(i * size, (i + 1) * size)


def group_queries(q_ref, g):
    heads = [q_ref[:, part_of(g * GROUPS + i, HEAD_DIM)] for i in range(GROUPS)]
    return jnp.concatenate(heads, axis=0)


def share_of(beta_ref, h):
    return 1.0 / (1.0 + jnp.exp(-jnp.full((1, HEAD_DIM), beta_ref[h], jnp.float32)))


def scaled_gains(beta_ref, gain_ref, out_ref):
    for h in range(HEADS):
        scaled = gain_ref[h : h + 1, :] * share_of(beta_ref, h)
        out_ref[part_of(h, HEAD_DIM), :] = column(scaled)


def suffix(others, least=0.0):
    count = jnp.maximum(jnp.sum(others, axis=1, keepdims=True), least)
    shape = (others.shape[1], HEAD_DIM)
    return lax.broadcasted_iota(jnp.int32, shape, 0).astype(jnp.float32) >= count


def first_document(docs):
    first = jnp.broadcast_to(docs[:, 0:1], docs.shape)
    return first, docs == first


def load_block(key_ref, value_ref, doc_ref, out_ref, doc_scratch, sems):
    rows = key_ref.shape[0]
    doc_copy = pltpu.make_async_copy(doc_ref, doc_scratch, sems.at[0])
    doc_copy.start()
    copies = []
    for g in range(2 * KV_HEADS):
        source = key_ref if g < KV_HEADS else value_ref
        copy = pltpu.make_async_copy(
            source.at[:, part_of(g % KV_HEADS, HEAD_DIM)],
            out_ref.at[part_of(g, rows), :],
            sems.at[1 + g],
        )
        copy.start()
        copies.append(copy)
    doc_copy.wait()
    start = 2 * KV_HEADS * rows
    docs = doc_scratch[...].astype(jnp.float32)
    docs = jnp.broadcast_to(docs, (out_ref.shape[0] - start, rows))
    out_ref[start:, :] = docs.astype(jnp.bfloat16)
    for copy in copies:
        copy.wait()


def block_keys(ref, g):
    return ref[part_of(g, HEAD_DIM), :]


def block_values(ref, g):
    return ref[part_of(KV_HEADS + g, HEAD_DIM), :]


def block_docs(ref):
    start = 2 * KV_HEADS * HEAD_DIM
    return ref[start : start + EXTRA, :].astype(jnp.float32)[0:1, :]


class Plan:
    def __init__(self, n_seq):
        devices = 2 * n_seq
        near = [(b, b + 1) for b in range(devices - 1)]
        far = [(b, b + 2) for b in range(devices - 2)]
        crossing = [p for p in far if p[0] // 2 % 2 == 1]
        touched = {b for p in crossing for b in p}
        targets = {p[1] for p in crossing}
        first = crossing + [p for p in near if p[0] not in touched and p[1] not in targets]
        second = [p for p in near if p not in first]
        last = [p for p in far if p not in first]
        self.pairs = [first, second, last]
        self.senders = sorted({p[0] for p in first})
        busy = {b for p in first for b in p} & {b for p in second for b in p}
        self.early = [b for b in range(devices) if b not in busy]
        self.late = sorted({p[1] for p in second})
        received = {p[1] for pairs in self.pairs for p in pairs}
        self.alone = [b for b in range(devices) if b not in received]
        self.memory_first = [p[1] for p in crossing if p[1] % 2 == 1]


def among(members):
    block = 2 * lax.axis_index("seq") + lax.axis_index("kv")
    return functools.reduce(jnp.logical_or, [block == b for b in members])


def pack_kernel(plan, key_ref, value_ref, doc_ref, out_ref, doc_scratch, sems):
    @pl.when(among(plan.senders))
    def _():
        load_block(key_ref, value_ref, doc_ref, out_ref, doc_scratch, sems)


def attend_own(q_ref, block_ref, g, bias):
    rows = q_ref.shape[0]
    scores = dot(block_keys(block_ref, g), group_queries(q_ref, g), NT)
    tops, totals, weights = [], [], []
    for i in range(GROUPS):
        masked = scores[:, part_of(i, rows)] * SCALE + bias
        top = jnp.max(masked, axis=0, keepdims=True)
        weight = jnp.exp2(masked - top)
        tops.append(top)
        totals.append(jnp.sum(weight, axis=0, keepdims=True))
        weights.append(weight.astype(jnp.bfloat16))
    summed = dot(block_values(block_ref, g), jnp.concatenate(weights, axis=1), TN)
    return summed, jnp.concatenate(tops, axis=1), jnp.concatenate(totals, axis=1)


def own_bias(docs):
    rows = docs.shape[1]
    place = lax.broadcasted_iota(jnp.int32, (rows, rows), 0)
    row = lax.broadcasted_iota(jnp.int32, (rows, rows), 1)
    return jnp.where((place <= row) & (column(docs) == docs), 0.0, LOWEST)


def attend_itself(
    q_ref, block_ref, gain_ref, beta_ref, beta_copy, summed_ref, stats_ref, gains_ref
):
    bias = own_bias(block_docs(block_ref))
    results = [attend_own(q_ref, block_ref, g, bias) for g in range(KV_HEADS)]
    beta_copy.wait()
    scaled_gains(beta_ref, gain_ref, gains_ref)
    done = lax.axis_index("kv") == 0
    for g, (summed, top, total) in enumerate(results):
        rest = [1.0 - share_of(beta_ref, g * GROUPS + i) for i in range(GROUPS)]
        rest = jnp.concatenate(rest, axis=1)
        summed_ref[part_of(g, HEAD_DIM), :] = summed * jnp.where(done, rest / total, 1.0)
        stats_ref[g : g + 1, :] = top
        stats_ref[KV_HEADS + g : KV_HEADS + g + 1, :] = total
        stats_ref[2 * KV_HEADS + g : 2 * KV_HEADS + g + 1, :] = rest


def settle_kernel(
    plan, gain_ref, packed_ref, query_ref, key_ref, value_ref, doc_ref, beta_ref,
    own_ref, short_ref, summed_ref, stats_ref, gains_ref,
    q_scratch, beta_scratch, doc_scratch, sems, early_sems,
):
    sender, early = among(plan.senders), among(plan.early)
    query_copy = pltpu.make_async_copy(query_ref, q_scratch, early_sems.at[0])
    beta_copy = pltpu.make_async_copy(beta_ref, beta_scratch, early_sems.at[1])

    @pl.when(early)
    def _():
        query_copy.start()
        beta_copy.start()

    @pl.when(sender)
    def _():
        own_ref[...] = packed_ref[...]

    @pl.when(jnp.logical_not(sender))
    def _():
        load_block(key_ref, value_ref, doc_ref, own_ref, doc_scratch, sems)

    short_ref[...] = own_ref[0 : short_ref.shape[0], :]
    line = lax.broadcasted_iota(jnp.int32, (EXTRA, HEAD_DIM), 0)
    keys = own_ref[0:EXTRA, :].astype(jnp.float32)
    keys = jnp.where(line == 0, block_docs(own_ref), keys)
    short_ref[0:EXTRA, :] = keys.astype(jnp.bfloat16)

    @pl.when(early)
    def _():
        query_copy.wait()
        attend_itself(
            q_scratch, own_ref, gain_ref, beta_scratch, beta_copy,
            summed_ref, stats_ref, gains_ref,
        )


def own_kernel(
    plan, q_ref, gain_ref, own_ref, beta_ref, summed_in, stats_in, gains_in,
    summed_ref, stats_ref, gains_ref, out_ref, turned_ref, beta_scratch, sem, held, sems,
):
    rows = q_ref.shape[0]
    for g in range(KV_HEADS):
        for i in range(GROUPS):
            head = q_ref[:, part_of(g * GROUPS + i, HEAD_DIM)]
            turned_ref[part_of(g, HEAD_DIM), part_of(i, rows)] = jnp.transpose(head)

    @pl.when(among(plan.alone))
    def _():
        _, same = first_document(block_docs(own_ref))
        states = lambda g: jnp.zeros((HEAD_DIM, HEAD_DIM), jnp.float32)
        read_and_store(states, turned_ref, gains_ref, same, summed_ref, out_ref, held, sems)

    @pl.when(jnp.logical_not(among(plan.early)))
    def _():
        beta_copy = pltpu.make_async_copy(beta_ref, beta_scratch, sem)
        beta_copy.start()
        attend_itself(
            q_ref, own_ref, gain_ref, beta_scratch, beta_copy, summed_ref, stats_ref, gains_ref
        )


def memory_states(refs, first):
    lives = []
    for ref in refs:
        short = ref.shape[0] == 2 * KV_HEADS * HEAD_DIM
        docs = ref[0:EXTRA, :].astype(jnp.float32)[0:1, :] if short else block_docs(ref)
        live = suffix(jnp.where(docs == first, 0.0, 1.0), 1.0 if short else 0.0)
        lives.append(jnp.where(live, 1.0, 0.0).astype(jnp.bfloat16))

    def state(g):
        terms = [
            dot(block_values(ref, g), block_keys(ref, g) * live, TN)
            for ref, live in zip(refs, lives)
        ]
        return functools.reduce(jnp.add, terms)

    return state


def read_memory(states, turned_ref, gains_ref, reads):
    rows = (turned_ref.shape[1] // GROUPS)
    ahead = {}

    def product(g):
        if g < KV_HEADS and g not in ahead:
            state = states(g)
            high = state.astype(jnp.bfloat16)
            state = state - high.astype(jnp.float32)
            middle = state.astype(jnp.bfloat16)
            low = (state - middle.astype(jnp.float32)).astype(jnp.bfloat16)
            pieces = jnp.concatenate([high, middle, low], axis=0)
            ahead[g] = dot(pieces, turned_ref[part_of(g, HEAD_DIM), :], NN)

    def read(g):
        product(g)
        product(g + 1)
        recalled = ahead[g][part_of(0, HEAD_DIM), :] + (
            ahead[g][part_of(1, HEAD_DIM), :] + ahead[g][part_of(2, HEAD_DIM), :]
        )
        heads = []
        for i in range(GROUPS):
            head = recalled[:, part_of(i, rows)]
            square = jnp.sum(head * head, axis=0, keepdims=True) * (1.0 / HEAD_DIM)
            head = head * (lax.rsqrt(square + 1e-06) * reads)
            heads.append(head * gains_ref[part_of(g * GROUPS + i, HEAD_DIM), :])
        return heads

    return read


def attend_before(turned_ref, one_ref, stats_ref, summed_ref, first, same):
    rows = (turned_ref.shape[1] // GROUPS)
    live = suffix(jnp.where(block_docs(one_ref) == first, 0.0, 1.0))
    bias = jnp.where(live & same, 0.0, LOWEST)
    ahead = {}

    def score(g):
        if g < KV_HEADS and g not in ahead:
            ahead[g] = dot(block_keys(one_ref, g), turned_ref[part_of(g, HEAD_DIM), :], NN)

    def attend(g):
        score(g)
        score(g + 1)
        weights, factors, scales = [], [], []
        for i in range(GROUPS):
            cut = part_of(i, rows)
            masked = ahead[g][:, cut] * SCALE + bias
            top_own = stats_ref[g : g + 1, cut]
            top = jnp.maximum(jnp.max(masked, axis=0, keepdims=True), top_own)
            weight = jnp.exp2(masked - top)
            factor = jnp.exp2(top_own - top)
            total = stats_ref[KV_HEADS + g : KV_HEADS + g + 1, cut] * factor
            total = total + jnp.sum(weight, axis=0, keepdims=True)
            factors.append(factor)
            scales.append(stats_ref[2 * KV_HEADS + g : 2 * KV_HEADS + g + 1, cut] / total)
            weights.append(weight.astype(jnp.bfloat16))
        added = dot(block_values(one_ref, g), jnp.concatenate(weights, axis=1), TN)
        summed = summed_ref[part_of(g, HEAD_DIM), :] * jnp.concatenate(factors, axis=1) + added
        return summed * jnp.concatenate(scales, axis=1)

    return attend


def store_heads(mixed, out_ref, held, sems):
    copies = []
    for g in range(KV_HEADS):
        for i, head in enumerate(mixed(g)):
            h = g * GROUPS + i
            held[:, part_of(h, HEAD_DIM)] = jnp.transpose(head)
            if h % 2 == 1:
                wide = part_of(h // 2, 2 * HEAD_DIM)
                copy = pltpu.make_async_copy(
                    held.at[:, wide], out_ref.at[:, wide], sems.at[h // 2]
                )
                copy.start()
                copies.append(copy)
    for copy in copies:
        copy.wait()


def read_into(read_ref, refs, turned_ref, own_ref, gains_ref):
    first, same = first_document(block_docs(own_ref))
    read = read_memory(
        memory_states(refs, first), turned_ref, gains_ref, jnp.where(same, 1.0, 0.0)
    )
    for g in range(KV_HEADS):
        for i, head in enumerate(read(g)):
            read_ref[part_of(g * GROUPS + i, HEAD_DIM), :] = head


def read_kernel(plan, turned_ref, own_ref, three_ref, gains_ref, read_ref):
    @pl.when((lax.axis_index("kv") == 1) & jnp.logical_not(among(plan.memory_first)))
    def _():
        read_into(read_ref, [three_ref], turned_ref, own_ref, gains_ref)


def attend_and_store(
    turned_ref, own_ref, earlier_ref, stats_ref, summed_ref, read_ref, out_ref, held, sems
):
    first, same = first_document(block_docs(own_ref))
    attend = attend_before(turned_ref, earlier_ref, stats_ref, summed_ref, first, same)
    rows = (turned_ref.shape[1] // GROUPS)

    def mixed(g):
        attended = attend(g)
        return [
            read_ref[part_of(g * GROUPS + i, HEAD_DIM), :] + attended[:, part_of(i, rows)]
            for i in range(GROUPS)
        ]

    store_heads(mixed, out_ref, held, sems)


def read_and_store(states, turned_ref, gains_ref, same, summed_ref, out_ref, held, sems):
    rows = (turned_ref.shape[1] // GROUPS)
    read = read_memory(states, turned_ref, gains_ref, jnp.where(same, 1.0, 0.0))

    def mixed(g):
        return [
            head + summed_ref[part_of(g, HEAD_DIM), part_of(i, rows)]
            for i, head in enumerate(read(g))
        ]

    store_heads(mixed, out_ref, held, sems)


def early_kernel(
    plan, turned_ref, own_ref, one_ref, three_ref, stats_ref, gains_ref, summed_ref, read_in, out_in,
    read_ref, state_ref, out_ref, held, sems,
):
    kv = lax.axis_index("kv")
    late = among(plan.late)

    @pl.when((kv == 0) & jnp.logical_not(late | among(plan.alone)))
    def _():
        first, same = first_document(block_docs(own_ref))
        states = memory_states([one_ref, three_ref], first)
        read_and_store(states, turned_ref, gains_ref, same, summed_ref, out_ref, held, sems)

    @pl.when((kv == 1) & jnp.logical_not(late))
    def _():
        attend_and_store(
            turned_ref, own_ref, one_ref, stats_ref, summed_ref, read_ref, out_ref, held, sems
        )

    @pl.when((kv == 0) & late)
    def _():
        first, _ = first_document(block_docs(own_ref))
        states = memory_states([one_ref, three_ref], first)
        for g in range(KV_HEADS):
            state_ref[part_of(g, HEAD_DIM), :] = states(g)

    @pl.when((kv == 1) & among(plan.memory_first))
    def _():
        read_into(read_ref, [one_ref, three_ref], turned_ref, own_ref, gains_ref)


def late_kernel(
    plan, turned_ref, own_ref, two_ref, state_ref, summed_ref, stats_ref, gains_ref, read_ref, out_in,
    out_ref, held, sems,
):
    kv = lax.axis_index("kv")
    late = among(plan.late)

    @pl.when((kv == 1) & late)
    def _():
        attend_and_store(
            turned_ref, own_ref, two_ref, stats_ref, summed_ref, read_ref, out_ref, held, sems
        )

    @pl.when((kv == 0) & late)
    def _():
        first, same = first_document(block_docs(own_ref))
        added = memory_states([two_ref], first)
        states = lambda g: state_ref[part_of(g, HEAD_DIM), :] + added(g)
        read_and_store(states, turned_ref, gains_ref, same, summed_ref, out_ref, held, sems)


def near_device(n_seq, queries, keys, values, doc_ids, beta, lin_gain):
    rows = queries.shape[0]
    vmem = pl.BlockSpec(memory_space=pltpu.VMEM)
    hbm = pl.BlockSpec(memory_space=pltpu.HBM)
    in_hbm = functools.partial(pltpu.with_memory_space_constraint, memory_space=pltpu.HBM)
    params = pltpu.CompilerParams(vmem_limit_bytes=32 * 1024 * 1024)
    wide = GROUPS * rows
    group_shape = jax.ShapeDtypeStruct((KV_HEADS * HEAD_DIM, wide), jnp.float32)
    gains_shape = jax.ShapeDtypeStruct((HEADS * HEAD_DIM, HEAD_DIM), jnp.float32)
    docs = doc_ids.reshape(1, rows)
    gain = lin_gain.reshape(HEADS, HEAD_DIM)
    deep = 2 * KV_HEADS * rows + EXTRA

    def estimate(share):
        return pl.CostEstimate(
            flops=int(share * 4 * HEADS * HEAD_DIM * rows * rows),
            bytes_accessed=int(share * 4 * 1024 * 1024),
            transcendentals=int(share * HEADS * rows * rows),
        )

    def send(payload, pairs):
        return lax.ppermute(payload, ("seq", "kv"), pairs)

    plan = Plan(n_seq)
    block_shape = jax.ShapeDtypeStruct((deep, HEAD_DIM), jnp.bfloat16)
    short_shape = jax.ShapeDtypeStruct((deep - EXTRA, HEAD_DIM), jnp.bfloat16)
    stats_shape = jax.ShapeDtypeStruct((4 * KV_HEADS, wide), jnp.float32)
    state_shape = jax.ShapeDtypeStruct((KV_HEADS * HEAD_DIM, HEAD_DIM), jnp.float32)
    results = [group_shape, stats_shape, gains_shape]
    doc_scratch = pltpu.VMEM((1, rows), jnp.int32)
    beta_scratch = pltpu.SMEM((HEADS,), jnp.float32)
    sems = pltpu.SemaphoreType.DMA((2 * KV_HEADS + 1,))
    block = (in_hbm(keys), in_hbm(values), in_hbm(docs))
    beta = in_hbm(beta)
    packed = pl.pallas_call(
        functools.partial(pack_kernel, plan),
        out_shape=block_shape,
        in_specs=[hbm] * 3,
        out_specs=vmem,
        scratch_shapes=[doc_scratch, sems],
        compiler_params=params,
        cost_estimate=estimate(0.1),
    )(*block)
    one = send(packed, plan.pairs[0])
    own, short, summed, stats, gains = pl.pallas_call(
        functools.partial(settle_kernel, plan),
        out_shape=[block_shape, short_shape] + results,
        in_specs=[vmem] * 2 + [hbm] * 5,
        out_specs=[vmem] * 5,
        scratch_shapes=[
            pltpu.VMEM(queries.shape, queries.dtype),
            beta_scratch,
            doc_scratch,
            sems,
            pltpu.SemaphoreType.DMA((2,)),
        ],
        compiler_params=params,
        cost_estimate=estimate(1.0),
    )(gain, packed, in_hbm(queries), *block, beta)
    two = send(own, plan.pairs[1])
    three = send(short, plan.pairs[2])
    out_shape = jax.ShapeDtypeStruct((rows, HEADS * HEAD_DIM), jnp.float32)
    store_scratch = [
        pltpu.VMEM((rows, HEADS * HEAD_DIM), jnp.float32),
        pltpu.SemaphoreType.DMA((HEADS // 2,)),
    ]
    turned_shape = jax.ShapeDtypeStruct((KV_HEADS * HEAD_DIM, wide), queries.dtype)
    summed, stats, gains, out, turned = pl.pallas_call(
        functools.partial(own_kernel, plan),
        out_shape=results + [out_shape, turned_shape],
        in_specs=[vmem] * 3 + [hbm] + [vmem] * 3,
        out_specs=[vmem] * 3 + [hbm, vmem],
        scratch_shapes=[beta_scratch, pltpu.SemaphoreType.DMA] + store_scratch,
        input_output_aliases={4: 0, 5: 1, 6: 2},
        compiler_params=params,
        cost_estimate=estimate(1.0),
    )(queries, gain, own, beta, summed, stats, gains)
    read = pl.pallas_call(
        functools.partial(read_kernel, plan),
        out_shape=gains_shape,
        in_specs=[vmem] * 4,
        out_specs=vmem,
        compiler_params=params,
    )(turned, own, three, gains)
    read, state, out = pl.pallas_call(
        functools.partial(early_kernel, plan),
        out_shape=[gains_shape, state_shape, out_shape],
        in_specs=[vmem] * 8 + [hbm],
        out_specs=[vmem] * 2 + [hbm],
        scratch_shapes=store_scratch,
        input_output_aliases={7: 0, 8: 2},
        compiler_params=params,
    )(turned, own, one, three, stats, gains, summed, read, out)
    return pl.pallas_call(
        functools.partial(late_kernel, plan),
        out_shape=out_shape,
        in_specs=[vmem] * 8 + [hbm],
        out_specs=hbm,
        scratch_shapes=store_scratch,
        input_output_aliases={8: 0},
        compiler_params=params,
    )(turned, own, two, state, summed, stats, gains, read, out)


def carried_in(part, axis, combine, identity):
    place = lax.axis_index(axis)
    gathered = jax.tree.map(lambda a: lax.all_gather(a, axis), part)
    state = jax.tree.map(lambda a, e: jnp.zeros_like(a) + jnp.asarray(e, a.dtype), part, identity)

    def one(step, state):
        return combine(
            state, jax.tree.map(lambda a: lax.dynamic_index_in_dim(a, step, 0, False), gathered)
        )

    return lax.fori_loop(0, place, one, state)


def join_states(earlier, later):
    state_early, first_early, last_early = earlier
    state_late, first_late, last_late = later
    empty_late = first_late < 0
    joined = (first_late == last_late) & (last_early == first_late)
    merged = state_late + jnp.where(joined, state_early, jnp.zeros_like(state_early))
    combined = jnp.where(empty_late, state_early, merged)
    first_doc = jnp.where(first_early < 0, first_late, first_early)
    last_doc = jnp.where(empty_late, last_early, last_late)
    return (combined, first_doc, last_doc)


def tail_merge(one_side, other_side):
    state_one, first_one, last_one = one_side
    state_other, first_other, last_other = other_side
    top_doc = jnp.maximum(last_one, last_other)
    state_sum = jnp.where(last_one == top_doc, state_one, jnp.zeros_like(state_one))
    state_sum = state_sum + jnp.where(
        last_other == top_doc, state_other, jnp.zeros_like(state_other)
    )
    return (state_sum, jnp.minimum(first_one, first_other), top_doc)


def tail_state(key_rows, value_rows, doc_rows, target_doc):
    count = key_rows.shape[0]
    key_heads = key_rows.reshape(count, KV_HEADS, HEAD_DIM)
    value_heads = value_rows.reshape(count, KV_HEADS, HEAD_DIM)
    live = doc_rows == target_doc
    masked = jnp.where(live[:, None, None], key_heads, jnp.zeros_like(key_heads))
    return jnp.einsum("rgd,rge->gde", masked, value_heads, preferred_element_type=jnp.float32)


def attend_block(
    carry, query_heads, query_pos, query_doc, key_rows, value_rows, key_doc, key_start
):
    running_max, running_sum, accumulated = carry
    key_count = key_rows.shape[0]
    key_heads = key_rows.reshape(key_count, KV_HEADS, HEAD_DIM)
    value_heads = value_rows.reshape(key_count, KV_HEADS, HEAD_DIM)
    scores = jnp.einsum(
        "rgqd,kgd->gqrk", query_heads, key_heads, preferred_element_type=jnp.float32
    )
    scores = scores / jnp.sqrt(jnp.float32(HEAD_DIM))
    key_pos = key_start + jnp.arange(key_count, dtype=jnp.int32)
    allowed = (key_pos[None, :] <= query_pos[:, None]) & (key_doc[None, :] == query_doc[:, None])
    masked = jnp.where(allowed, scores, jnp.float32(-1e30))
    new_max = jnp.maximum(running_max, jnp.max(masked, axis=-1))
    factor = jnp.exp(running_max - new_max)
    weights = jnp.where(allowed, jnp.exp(masked - new_max[..., None]), jnp.float32(0.0))
    new_sum = running_sum * factor + jnp.sum(weights, axis=-1)
    product = jnp.einsum(
        "gqrk,kge->gqre",
        weights.astype(jnp.bfloat16),
        value_heads,
        preferred_element_type=jnp.float32,
    )
    new_accum = accumulated * factor[..., None] + product
    return (new_max, new_sum, new_accum)


def far_device(queries, keys, values, doc_ids, beta, lin_gain):
    row_count = queries.shape[0]
    groups = HEADS // KV_HEADS
    query_heads = queries.reshape(row_count, KV_HEADS, groups, HEAD_DIM)
    position = lax.axis_index("kv") * row_count
    query_pos = position + jnp.arange(row_count, dtype=jnp.int32)
    last_query = position + row_count - 1
    initial = (
        jnp.full((KV_HEADS, groups, row_count), -1e30, jnp.float32),
        jnp.zeros((KV_HEADS, groups, row_count), jnp.float32),
        jnp.zeros((KV_HEADS, groups, row_count, HEAD_DIM), jnp.float32),
    )
    empty_tail = (
        jnp.zeros((KV_HEADS, HEAD_DIM, HEAD_DIM), jnp.float32),
        jnp.array(2**30, jnp.int32),
        jnp.array(-1, jnp.int32),
    )
    key_piece = lax.all_gather(keys, "kv", axis=0, tiled=True)
    value_piece = lax.all_gather(values, "kv", axis=0, tiled=True)
    doc_piece = lax.all_gather(doc_ids, "kv", axis=0, tiled=True)
    blocks = key_piece.shape[0] // row_count

    def one_block(state, item):
        soft_state, tail_now = state
        key_block, value_block, doc_block, number = item
        block_start = number * row_count
        soft_next = lax.cond(
            block_start <= last_query,
            lambda inner: attend_block(
                inner,
                query_heads,
                query_pos,
                doc_ids,
                key_block,
                value_block,
                doc_block,
                block_start,
            ),
            lambda inner: inner,
            soft_state,
        )
        block_tail = (
            tail_state(key_block, value_block, doc_block, doc_block[-1]),
            doc_block[0],
            doc_block[-1],
        )
        tail_now = tail_merge(tail_now, block_tail)
        return ((soft_next, tail_now), None)

    stacked = (
        key_piece.reshape(blocks, row_count, -1),
        value_piece.reshape(blocks, row_count, -1),
        doc_piece.reshape(blocks, row_count),
        jnp.arange(blocks, dtype=jnp.int32),
    )
    result, _ = lax.scan(one_block, (initial, empty_tail), stacked)
    running, segment_tail = result
    running_max, running_sum, accumulated = running
    soft_out = jnp.transpose(accumulated / running_sum[..., None], (2, 0, 1, 3))
    identity = (
        jnp.zeros((KV_HEADS, HEAD_DIM, HEAD_DIM), jnp.float32),
        jnp.array(-1, jnp.int32),
        jnp.array(-1, jnp.int32),
    )
    memory = carried_in(segment_tail, "seq", join_states, identity)
    memory_state, memory_first, memory_last = memory
    query_float = query_heads.astype(jnp.float32)
    recalled = jnp.einsum(
        "rgqd,gde->rgqe", query_float, memory_state, precision=lax.Precision.HIGHEST
    )
    recalled = jnp.where((doc_ids == memory_last)[:, None, None, None], recalled, jnp.float32(0.0))
    mean_square = jnp.mean(recalled * recalled, axis=-1, keepdims=True)
    normed = (
        recalled * lax.rsqrt(mean_square + 1e-06) * lin_gain.reshape(KV_HEADS, groups, HEAD_DIM)
    )
    mixing = jax.nn.sigmoid(beta).reshape(KV_HEADS, groups)[None, :, :, None]
    mixed = mixing * normed + (1.0 - mixing) * soft_out
    return mixed.reshape(row_count, HEADS * HEAD_DIM).astype(jnp.float32)


def solution(mesh):
    n_seq, n_kv = mesh.shape["seq"], mesh.shape["kv"]
    in_specs = (
        P(("dp", "seq", "kv"), None),
        P(("dp", "seq", "kv"), None),
        P(("dp", "seq", "kv"), None),
        P(("dp", "seq", "kv")),
        P(),
        P(),
    )
    out_specs = P(("dp", "seq", "kv"), None)
    if n_kv == 2 and n_seq * n_kv <= 2 * LONGEST:
        on_device = functools.partial(near_device, n_seq)
    else:
        on_device = far_device
    return jax.shard_map(
        on_device, mesh=mesh, in_specs=in_specs, out_specs=out_specs, check_vma=False
    )
```

```python
import functools
import math

import jax
import jax.numpy as jnp
from jax import lax
from jax.experimental import pallas as pl
from jax.experimental.pallas import tpu as pltpu
from jax.sharding import PartitionSpec as P

HEADS = 16
KV_HEADS = 4
HEAD_DIM = 128
GROUPS = HEADS // KV_HEADS
LONGEST = 4
SCALE = math.log2(math.e) / math.sqrt(HEAD_DIM)
LOWEST = -1e30
EXTRA = 16

NT = (((1,), (1,)), ((), ()))
TN = (((0,), (0,)), ((), ()))
NN = (((1,), (0,)), ((), ()))


def dot(a, b, dims):
    return lax.dot_general(a, b, dims, preferred_element_type=jnp.float32)


def column(row):
    return jnp.transpose(jnp.broadcast_to(row, (HEAD_DIM, row.shape[1])))


def part_of(i, size):
    return slice(i * size, (i + 1) * size)


def group_queries(q_ref, g):
    heads = [q_ref[:, part_of(g * GROUPS + i, HEAD_DIM)] for i in range(GROUPS)]
    return jnp.concatenate(heads, axis=0)


def share_of(beta_ref, h):
    return 1.0 / (1.0 + jnp.exp(-jnp.full((1, HEAD_DIM), beta_ref[h], jnp.float32)))


def scaled_gains(beta_ref, gain_ref, out_ref):
    for h in range(HEADS):
        scaled = gain_ref[h : h + 1, :] * share_of(beta_ref, h)
        out_ref[part_of(h, HEAD_DIM), :] = column(scaled)


def suffix(others, least=0.0):
    count = jnp.maximum(jnp.sum(others, axis=1, keepdims=True), least)
    shape = (others.shape[1], HEAD_DIM)
    return lax.broadcasted_iota(jnp.int32, shape, 0).astype(jnp.float32) >= count


def first_document(docs):
    first = jnp.broadcast_to(docs[:, 0:1], docs.shape)
    return first, docs == first


def load_block(key_ref, value_ref, doc_ref, out_ref, doc_scratch, sems):
    rows = key_ref.shape[0]
    doc_copy = pltpu.make_async_copy(doc_ref, doc_scratch, sems.at[0])
    doc_copy.start()
    copies = []
    for g in range(2 * KV_HEADS):
        source = key_ref if g < KV_HEADS else value_ref
        copy = pltpu.make_async_copy(
            source.at[:, part_of(g % KV_HEADS, HEAD_DIM)],
            out_ref.at[part_of(g, rows), :],
            sems.at[1 + g],
        )
        copy.start()
        copies.append(copy)
    doc_copy.wait()
    start = 2 * KV_HEADS * rows
    docs = doc_scratch[...].astype(jnp.float32)
    docs = jnp.broadcast_to(docs, (out_ref.shape[0] - start, rows))
    out_ref[start:, :] = docs.astype(jnp.bfloat16)
    for copy in copies:
        copy.wait()


def block_keys(ref, g):
    return ref[part_of(g, HEAD_DIM), :]


def block_values(ref, g):
    return ref[part_of(KV_HEADS + g, HEAD_DIM), :]


def block_docs(ref):
    start = 2 * KV_HEADS * HEAD_DIM
    return ref[start : start + EXTRA, :].astype(jnp.float32)[0:1, :]


class Plan:
    def __init__(self, n_seq):
        devices = 2 * n_seq
        near = [(b, b + 1) for b in range(devices - 1)]
        far = [(b, b + 2) for b in range(devices - 2)]
        crossing = [p for p in far if p[0] // 2 % 2 == 1]
        touched = {b for p in crossing for b in p}
        targets = {p[1] for p in crossing}
        first = crossing + [p for p in near if p[0] not in touched and p[1] not in targets]
        second = [p for p in near if p not in first]
        last = [p for p in far if p not in first]
        self.pairs = [first, second, last]
        self.senders = sorted({p[0] for p in first})
        busy = {b for p in first for b in p} & {b for p in second for b in p}
        self.early = [b for b in range(devices) if b not in busy]
        self.late = sorted({p[1] for p in second})
        received = {p[1] for pairs in self.pairs for p in pairs}
        self.alone = [b for b in range(devices) if b not in received]
        self.memory_first = [p[1] for p in crossing if p[1] % 2 == 1]


def among(members):
    block = 2 * lax.axis_index("seq") + lax.axis_index("kv")
    return functools.reduce(jnp.logical_or, [block == b for b in members])


def pack_kernel(plan, key_ref, value_ref, doc_ref, out_ref, doc_scratch, sems):
    @pl.when(among(plan.senders))
    def _():
        load_block(key_ref, value_ref, doc_ref, out_ref, doc_scratch, sems)


def attend_own(q_ref, block_ref, g, bias):
    rows = q_ref.shape[0]
    scores = dot(block_keys(block_ref, g), group_queries(q_ref, g), NT)
    tops, totals, weights = [], [], []
    for i in range(GROUPS):
        masked = scores[:, part_of(i, rows)] * SCALE + bias
        top = jnp.max(masked, axis=0, keepdims=True)
        weight = jnp.exp2(masked - top)
        tops.append(top)
        totals.append(jnp.sum(weight, axis=0, keepdims=True))
        weights.append(weight.astype(jnp.bfloat16))
    summed = dot(block_values(block_ref, g), jnp.concatenate(weights, axis=1), TN)
    return summed, jnp.concatenate(tops, axis=1), jnp.concatenate(totals, axis=1)


def own_bias(docs):
    rows = docs.shape[1]
    place = lax.broadcasted_iota(jnp.int32, (rows, rows), 0)
    row = lax.broadcasted_iota(jnp.int32, (rows, rows), 1)
    return jnp.where((place <= row) & (column(docs) == docs), 0.0, LOWEST)


def attend_itself(
    q_ref, block_ref, gain_ref, beta_ref, beta_copy, summed_ref, stats_ref, gains_ref
):
    bias = own_bias(block_docs(block_ref))
    results = [attend_own(q_ref, block_ref, g, bias) for g in range(KV_HEADS)]
    beta_copy.wait()
    scaled_gains(beta_ref, gain_ref, gains_ref)
    done = lax.axis_index("kv") == 0
    for g, (summed, top, total) in enumerate(results):
        rest = [1.0 - share_of(beta_ref, g * GROUPS + i) for i in range(GROUPS)]
        rest = jnp.concatenate(rest, axis=1)
        summed_ref[part_of(g, HEAD_DIM), :] = summed * jnp.where(done, rest / total, 1.0)
        stats_ref[g : g + 1, :] = top
        stats_ref[KV_HEADS + g : KV_HEADS + g + 1, :] = total
        stats_ref[2 * KV_HEADS + g : 2 * KV_HEADS + g + 1, :] = rest


def settle_kernel(
    plan, gain_ref, packed_ref, query_ref, key_ref, value_ref, doc_ref, beta_ref,
    own_ref, short_ref, summed_ref, stats_ref, gains_ref,
    q_scratch, beta_scratch, doc_scratch, sems, early_sems,
):
    sender, early = among(plan.senders), among(plan.early)
    query_copy = pltpu.make_async_copy(query_ref, q_scratch, early_sems.at[0])
    beta_copy = pltpu.make_async_copy(beta_ref, beta_scratch, early_sems.at[1])

    @pl.when(early)
    def _():
        query_copy.start()
        beta_copy.start()

    @pl.when(sender)
    def _():
        own_ref[...] = packed_ref[...]

    @pl.when(jnp.logical_not(sender))
    def _():
        load_block(key_ref, value_ref, doc_ref, own_ref, doc_scratch, sems)

    short_ref[...] = own_ref[0 : short_ref.shape[0], :]
    line = lax.broadcasted_iota(jnp.int32, (EXTRA, HEAD_DIM), 0)
    keys = own_ref[0:EXTRA, :].astype(jnp.float32)
    keys = jnp.where(line == 0, block_docs(own_ref), keys)
    short_ref[0:EXTRA, :] = keys.astype(jnp.bfloat16)

    @pl.when(early)
    def _():
        query_copy.wait()
        attend_itself(
            q_scratch, own_ref, gain_ref, beta_scratch, beta_copy,
            summed_ref, stats_ref, gains_ref,
        )


def own_kernel(
    plan, q_ref, gain_ref, own_ref, beta_ref, summed_in, stats_in, gains_in,
    summed_ref, stats_ref, gains_ref, out_ref, turned_ref, beta_scratch, sem, held, sems,
):
    rows = q_ref.shape[0]
    for g in range(KV_HEADS):
        for i in range(GROUPS):
            head = q_ref[:, part_of(g * GROUPS + i, HEAD_DIM)]
            turned_ref[part_of(g, HEAD_DIM), part_of(i, rows)] = jnp.transpose(head)

    @pl.when(among(plan.alone))
    def _():
        _, same = first_document(block_docs(own_ref))
        states = [jnp.zeros((HEAD_DIM, HEAD_DIM), jnp.float32)] * KV_HEADS
        read_and_store(states, turned_ref, gains_ref, same, summed_ref, out_ref, held, sems)

    @pl.when(jnp.logical_not(among(plan.early)))
    def _():
        beta_copy = pltpu.make_async_copy(beta_ref, beta_scratch, sem)
        beta_copy.start()
        attend_itself(
            q_ref, own_ref, gain_ref, beta_scratch, beta_copy, summed_ref, stats_ref, gains_ref
        )


def memory_states(refs, first):
    lives = []
    for ref in refs:
        short = ref.shape[0] == 2 * KV_HEADS * HEAD_DIM
        docs = ref[0:EXTRA, :].astype(jnp.float32)[0:1, :] if short else block_docs(ref)
        live = suffix(jnp.where(docs == first, 0.0, 1.0), 1.0 if short else 0.0)
        lives.append(jnp.where(live, 1.0, 0.0).astype(jnp.bfloat16))
    return [
        functools.reduce(
            jnp.add,
            [
                dot(block_values(ref, g), block_keys(ref, g) * live, TN)
                for ref, live in zip(refs, lives)
            ],
        )
        for g in range(KV_HEADS)
    ]


def read_memory(states, turned_ref, gains_ref, reads):
    rows = turned_ref.shape[1] // GROUPS
    pieces = []
    for state in states:
        high = state.astype(jnp.bfloat16)
        state = state - high.astype(jnp.float32)
        middle = state.astype(jnp.bfloat16)
        low = (state - middle.astype(jnp.float32)).astype(jnp.bfloat16)
        pieces.append(jnp.concatenate([high, middle, low], axis=0))
    products = [
        dot(pieces[g], turned_ref[part_of(g, HEAD_DIM), :], NN) for g in range(KV_HEADS)
    ]

    def read(g):
        recalled = products[g][part_of(0, HEAD_DIM), :] + (
            products[g][part_of(1, HEAD_DIM), :] + products[g][part_of(2, HEAD_DIM), :]
        )
        heads = []
        for i in range(GROUPS):
            head = recalled[:, part_of(i, rows)]
            square = jnp.sum(head * head, axis=0, keepdims=True) * (1.0 / HEAD_DIM)
            head = head * (lax.rsqrt(square + 1e-06) * reads)
            heads.append(head * gains_ref[part_of(g * GROUPS + i, HEAD_DIM), :])
        return heads

    return read


def attend_before(turned_ref, one_ref, stats_ref, summed_ref, first, same):
    rows = (turned_ref.shape[1] // GROUPS)
    live = suffix(jnp.where(block_docs(one_ref) == first, 0.0, 1.0))
    bias = jnp.where(live & same, 0.0, LOWEST)
    ahead = {}

    def score(g):
        if g < KV_HEADS and g not in ahead:
            ahead[g] = dot(block_keys(one_ref, g), turned_ref[part_of(g, HEAD_DIM), :], NN)

    def attend(g):
        for later in range(3):
            score(g + later)
        weights, factors, scales = [], [], []
        for i in range(GROUPS):
            cut = part_of(i, rows)
            masked = ahead[g][:, cut] * SCALE + bias
            top_own = stats_ref[g : g + 1, cut]
            top = jnp.maximum(jnp.max(masked, axis=0, keepdims=True), top_own)
            weight = jnp.exp2(masked - top)
            factor = jnp.exp2(top_own - top)
            total = stats_ref[KV_HEADS + g : KV_HEADS + g + 1, cut] * factor
            total = total + jnp.sum(weight, axis=0, keepdims=True)
            factors.append(factor)
            scales.append(stats_ref[2 * KV_HEADS + g : 2 * KV_HEADS + g + 1, cut] / total)
            weights.append(weight.astype(jnp.bfloat16))
        added = dot(block_values(one_ref, g), jnp.concatenate(weights, axis=1), TN)
        summed = summed_ref[part_of(g, HEAD_DIM), :] * jnp.concatenate(factors, axis=1) + added
        return summed * jnp.concatenate(scales, axis=1)

    return attend


def store_heads(mixed, out_ref, held, sems):
    copies = []
    ahead = mixed(0)
    for g in range(KV_HEADS):
        heads, ahead = ahead, mixed(g + 1) if g + 1 < KV_HEADS else None
        for i, head in enumerate(heads):
            held[:, part_of(g * GROUPS + i, HEAD_DIM)] = jnp.transpose(head)
        wide = part_of(g, GROUPS * HEAD_DIM)
        copies.append(pltpu.make_async_copy(held.at[:, wide], out_ref.at[:, wide], sems.at[g]))
        copies[g].start()
    for copy in copies:
        copy.wait()


def read_into(read_ref, refs, turned_ref, own_ref, gains_ref):
    first, same = first_document(block_docs(own_ref))
    read = read_memory(
        memory_states(refs, first), turned_ref, gains_ref, jnp.where(same, 1.0, 0.0)
    )
    for g in range(KV_HEADS):
        for i, head in enumerate(read(g)):
            read_ref[part_of(g * GROUPS + i, HEAD_DIM), :] = head


def read_kernel(plan, turned_ref, own_ref, three_ref, gains_ref, read_ref):
    @pl.when((lax.axis_index("kv") == 1) & jnp.logical_not(among(plan.memory_first)))
    def _():
        read_into(read_ref, [three_ref], turned_ref, own_ref, gains_ref)


def attend_and_store(
    turned_ref, own_ref, earlier_ref, stats_ref, summed_ref, read_ref, out_ref, held, sems
):
    first, same = first_document(block_docs(own_ref))
    attend = attend_before(turned_ref, earlier_ref, stats_ref, summed_ref, first, same)
    rows = (turned_ref.shape[1] // GROUPS)

    def mixed(g):
        attended = attend(g)
        return [
            read_ref[part_of(g * GROUPS + i, HEAD_DIM), :] + attended[:, part_of(i, rows)]
            for i in range(GROUPS)
        ]

    store_heads(mixed, out_ref, held, sems)


def read_and_store(states, turned_ref, gains_ref, same, summed_ref, out_ref, held, sems):
    rows = (turned_ref.shape[1] // GROUPS)
    read = read_memory(states, turned_ref, gains_ref, jnp.where(same, 1.0, 0.0))

    def mixed(g):
        return [
            head + summed_ref[part_of(g, HEAD_DIM), part_of(i, rows)]
            for i, head in enumerate(read(g))
        ]

    store_heads(mixed, out_ref, held, sems)


def early_kernel(
    plan, turned_ref, own_ref, one_ref, three_ref, stats_ref, gains_ref, summed_ref, read_in, out_in,
    read_ref, state_ref, out_ref, held, sems,
):
    kv = lax.axis_index("kv")
    late = among(plan.late)

    @pl.when((kv == 0) & jnp.logical_not(late | among(plan.alone)))
    def _():
        first, same = first_document(block_docs(own_ref))
        states = memory_states([one_ref, three_ref], first)
        read_and_store(states, turned_ref, gains_ref, same, summed_ref, out_ref, held, sems)

    @pl.when((kv == 1) & jnp.logical_not(late))
    def _():
        attend_and_store(
            turned_ref, own_ref, one_ref, stats_ref, summed_ref, read_ref, out_ref, held, sems
        )

    @pl.when((kv == 0) & late)
    def _():
        first, _ = first_document(block_docs(own_ref))
        for g, state in enumerate(memory_states([one_ref, three_ref], first)):
            state_ref[part_of(g, HEAD_DIM), :] = state

    @pl.when((kv == 1) & among(plan.memory_first))
    def _():
        read_into(read_ref, [one_ref, three_ref], turned_ref, own_ref, gains_ref)


def late_kernel(
    plan, turned_ref, own_ref, two_ref, state_ref, summed_ref, stats_ref, gains_ref, read_ref, out_in,
    out_ref, held, sems,
):
    kv = lax.axis_index("kv")
    late = among(plan.late)

    @pl.when((kv == 1) & late)
    def _():
        attend_and_store(
            turned_ref, own_ref, two_ref, stats_ref, summed_ref, read_ref, out_ref, held, sems
        )

    @pl.when((kv == 0) & late)
    def _():
        first, same = first_document(block_docs(own_ref))
        states = [
            state_ref[part_of(g, HEAD_DIM), :] + state
            for g, state in enumerate(memory_states([two_ref], first))
        ]
        read_and_store(states, turned_ref, gains_ref, same, summed_ref, out_ref, held, sems)


def near_device(n_seq, queries, keys, values, doc_ids, beta, lin_gain):
    rows = queries.shape[0]
    vmem = pl.BlockSpec(memory_space=pltpu.VMEM)
    hbm = pl.BlockSpec(memory_space=pltpu.HBM)
    in_hbm = functools.partial(pltpu.with_memory_space_constraint, memory_space=pltpu.HBM)
    params = pltpu.CompilerParams(vmem_limit_bytes=32 * 1024 * 1024)
    wide = GROUPS * rows
    group_shape = jax.ShapeDtypeStruct((KV_HEADS * HEAD_DIM, wide), jnp.float32)
    gains_shape = jax.ShapeDtypeStruct((HEADS * HEAD_DIM, HEAD_DIM), jnp.float32)
    docs = doc_ids.reshape(1, rows)
    gain = lin_gain.reshape(HEADS, HEAD_DIM)
    deep = 2 * KV_HEADS * rows + EXTRA

    def estimate(share):
        return pl.CostEstimate(
            flops=int(share * 4 * HEADS * HEAD_DIM * rows * rows),
            bytes_accessed=int(share * 4 * 1024 * 1024),
            transcendentals=int(share * HEADS * rows * rows),
        )

    def send(payload, pairs):
        return lax.ppermute(payload, ("seq", "kv"), pairs)

    plan = Plan(n_seq)
    block_shape = jax.ShapeDtypeStruct((deep, HEAD_DIM), jnp.bfloat16)
    short_shape = jax.ShapeDtypeStruct((deep - EXTRA, HEAD_DIM), jnp.bfloat16)
    stats_shape = jax.ShapeDtypeStruct((4 * KV_HEADS, wide), jnp.float32)
    state_shape = jax.ShapeDtypeStruct((KV_HEADS * HEAD_DIM, HEAD_DIM), jnp.float32)
    results = [group_shape, stats_shape, gains_shape]
    doc_scratch = pltpu.VMEM((1, rows), jnp.int32)
    beta_scratch = pltpu.SMEM((HEADS,), jnp.float32)
    sems = pltpu.SemaphoreType.DMA((2 * KV_HEADS + 1,))
    block = (in_hbm(keys), in_hbm(values), in_hbm(docs))
    beta = in_hbm(beta)
    packed = pl.pallas_call(
        functools.partial(pack_kernel, plan),
        out_shape=block_shape,
        in_specs=[hbm] * 3,
        out_specs=vmem,
        scratch_shapes=[doc_scratch, sems],
        compiler_params=params,
        cost_estimate=estimate(0.1),
    )(*block)
    one = send(packed, plan.pairs[0])
    own, short, summed, stats, gains = pl.pallas_call(
        functools.partial(settle_kernel, plan),
        out_shape=[block_shape, short_shape] + results,
        in_specs=[vmem] * 2 + [hbm] * 5,
        out_specs=[vmem] * 5,
        scratch_shapes=[
            pltpu.VMEM(queries.shape, queries.dtype),
            beta_scratch,
            doc_scratch,
            sems,
            pltpu.SemaphoreType.DMA((2,)),
        ],
        compiler_params=params,
        cost_estimate=estimate(1.0),
    )(gain, packed, in_hbm(queries), *block, beta)
    two = send(own, plan.pairs[1])
    three = send(short, plan.pairs[2])
    out_shape = jax.ShapeDtypeStruct((rows, HEADS * HEAD_DIM), jnp.float32)
    store_scratch = [
        pltpu.VMEM((rows, HEADS * HEAD_DIM), jnp.float32),
        pltpu.SemaphoreType.DMA((KV_HEADS,)),
    ]
    turned_shape = jax.ShapeDtypeStruct((KV_HEADS * HEAD_DIM, wide), queries.dtype)
    summed, stats, gains, out, turned = pl.pallas_call(
        functools.partial(own_kernel, plan),
        out_shape=results + [out_shape, turned_shape],
        in_specs=[vmem] * 3 + [hbm] + [vmem] * 3,
        out_specs=[vmem] * 3 + [hbm, vmem],
        scratch_shapes=[beta_scratch, pltpu.SemaphoreType.DMA] + store_scratch,
        input_output_aliases={4: 0, 5: 1, 6: 2},
        compiler_params=params,
        cost_estimate=estimate(1.0),
    )(queries, gain, own, beta, summed, stats, gains)
    read = pl.pallas_call(
        functools.partial(read_kernel, plan),
        out_shape=gains_shape,
        in_specs=[vmem] * 4,
        out_specs=vmem,
        compiler_params=params,
    )(turned, own, three, gains)
    read, state, out = pl.pallas_call(
        functools.partial(early_kernel, plan),
        out_shape=[gains_shape, state_shape, out_shape],
        in_specs=[vmem] * 8 + [hbm],
        out_specs=[vmem] * 2 + [hbm],
        scratch_shapes=store_scratch,
        input_output_aliases={7: 0, 8: 2},
        compiler_params=params,
    )(turned, own, one, three, stats, gains, summed, read, out)
    return pl.pallas_call(
        functools.partial(late_kernel, plan),
        out_shape=out_shape,
        in_specs=[vmem] * 8 + [hbm],
        out_specs=hbm,
        scratch_shapes=store_scratch,
        input_output_aliases={8: 0},
        compiler_params=params,
    )(turned, own, two, state, summed, stats, gains, read, out)


def carried_in(part, axis, combine, identity):
    place = lax.axis_index(axis)
    gathered = jax.tree.map(lambda a: lax.all_gather(a, axis), part)
    state = jax.tree.map(lambda a, e: jnp.zeros_like(a) + jnp.asarray(e, a.dtype), part, identity)

    def one(step, state):
        return combine(
            state, jax.tree.map(lambda a: lax.dynamic_index_in_dim(a, step, 0, False), gathered)
        )

    return lax.fori_loop(0, place, one, state)


def join_states(earlier, later):
    state_early, first_early, last_early = earlier
    state_late, first_late, last_late = later
    empty_late = first_late < 0
    joined = (first_late == last_late) & (last_early == first_late)
    merged = state_late + jnp.where(joined, state_early, jnp.zeros_like(state_early))
    combined = jnp.where(empty_late, state_early, merged)
    first_doc = jnp.where(first_early < 0, first_late, first_early)
    last_doc = jnp.where(empty_late, last_early, last_late)
    return (combined, first_doc, last_doc)


def tail_merge(one_side, other_side):
    state_one, first_one, last_one = one_side
    state_other, first_other, last_other = other_side
    top_doc = jnp.maximum(last_one, last_other)
    state_sum = jnp.where(last_one == top_doc, state_one, jnp.zeros_like(state_one))
    state_sum = state_sum + jnp.where(
        last_other == top_doc, state_other, jnp.zeros_like(state_other)
    )
    return (state_sum, jnp.minimum(first_one, first_other), top_doc)


def tail_state(key_rows, value_rows, doc_rows, target_doc):
    count = key_rows.shape[0]
    key_heads = key_rows.reshape(count, KV_HEADS, HEAD_DIM)
    value_heads = value_rows.reshape(count, KV_HEADS, HEAD_DIM)
    live = doc_rows == target_doc
    masked = jnp.where(live[:, None, None], key_heads, jnp.zeros_like(key_heads))
    return jnp.einsum("rgd,rge->gde", masked, value_heads, preferred_element_type=jnp.float32)


def attend_block(
    carry, query_heads, query_pos, query_doc, key_rows, value_rows, key_doc, key_start
):
    running_max, running_sum, accumulated = carry
    key_count = key_rows.shape[0]
    key_heads = key_rows.reshape(key_count, KV_HEADS, HEAD_DIM)
    value_heads = value_rows.reshape(key_count, KV_HEADS, HEAD_DIM)
    scores = jnp.einsum(
        "rgqd,kgd->gqrk", query_heads, key_heads, preferred_element_type=jnp.float32
    )
    scores = scores / jnp.sqrt(jnp.float32(HEAD_DIM))
    key_pos = key_start + jnp.arange(key_count, dtype=jnp.int32)
    allowed = (key_pos[None, :] <= query_pos[:, None]) & (key_doc[None, :] == query_doc[:, None])
    masked = jnp.where(allowed, scores, jnp.float32(-1e30))
    new_max = jnp.maximum(running_max, jnp.max(masked, axis=-1))
    factor = jnp.exp(running_max - new_max)
    weights = jnp.where(allowed, jnp.exp(masked - new_max[..., None]), jnp.float32(0.0))
    new_sum = running_sum * factor + jnp.sum(weights, axis=-1)
    product = jnp.einsum(
        "gqrk,kge->gqre",
        weights.astype(jnp.bfloat16),
        value_heads,
        preferred_element_type=jnp.float32,
    )
    new_accum = accumulated * factor[..., None] + product
    return (new_max, new_sum, new_accum)


def far_device(queries, keys, values, doc_ids, beta, lin_gain):
    row_count = queries.shape[0]
    groups = HEADS // KV_HEADS
    query_heads = queries.reshape(row_count, KV_HEADS, groups, HEAD_DIM)
    position = lax.axis_index("kv") * row_count
    query_pos = position + jnp.arange(row_count, dtype=jnp.int32)
    last_query = position + row_count - 1
    initial = (
        jnp.full((KV_HEADS, groups, row_count), -1e30, jnp.float32),
        jnp.zeros((KV_HEADS, groups, row_count), jnp.float32),
        jnp.zeros((KV_HEADS, groups, row_count, HEAD_DIM), jnp.float32),
    )
    empty_tail = (
        jnp.zeros((KV_HEADS, HEAD_DIM, HEAD_DIM), jnp.float32),
        jnp.array(2**30, jnp.int32),
        jnp.array(-1, jnp.int32),
    )
    key_piece = lax.all_gather(keys, "kv", axis=0, tiled=True)
    value_piece = lax.all_gather(values, "kv", axis=0, tiled=True)
    doc_piece = lax.all_gather(doc_ids, "kv", axis=0, tiled=True)
    blocks = key_piece.shape[0] // row_count

    def one_block(state, item):
        soft_state, tail_now = state
        key_block, value_block, doc_block, number = item
        block_start = number * row_count
        soft_next = lax.cond(
            block_start <= last_query,
            lambda inner: attend_block(
                inner,
                query_heads,
                query_pos,
                doc_ids,
                key_block,
                value_block,
                doc_block,
                block_start,
            ),
            lambda inner: inner,
            soft_state,
        )
        block_tail = (
            tail_state(key_block, value_block, doc_block, doc_block[-1]),
            doc_block[0],
            doc_block[-1],
        )
        tail_now = tail_merge(tail_now, block_tail)
        return ((soft_next, tail_now), None)

    stacked = (
        key_piece.reshape(blocks, row_count, -1),
        value_piece.reshape(blocks, row_count, -1),
        doc_piece.reshape(blocks, row_count),
        jnp.arange(blocks, dtype=jnp.int32),
    )
    result, _ = lax.scan(one_block, (initial, empty_tail), stacked)
    running, segment_tail = result
    running_max, running_sum, accumulated = running
    soft_out = jnp.transpose(accumulated / running_sum[..., None], (2, 0, 1, 3))
    identity = (
        jnp.zeros((KV_HEADS, HEAD_DIM, HEAD_DIM), jnp.float32),
        jnp.array(-1, jnp.int32),
        jnp.array(-1, jnp.int32),
    )
    memory = carried_in(segment_tail, "seq", join_states, identity)
    memory_state, memory_first, memory_last = memory
    query_float = query_heads.astype(jnp.float32)
    recalled = jnp.einsum(
        "rgqd,gde->rgqe", query_float, memory_state, precision=lax.Precision.HIGHEST
    )
    recalled = jnp.where((doc_ids == memory_last)[:, None, None, None], recalled, jnp.float32(0.0))
    mean_square = jnp.mean(recalled * recalled, axis=-1, keepdims=True)
    normed = (
        recalled * lax.rsqrt(mean_square + 1e-06) * lin_gain.reshape(KV_HEADS, groups, HEAD_DIM)
    )
    mixing = jax.nn.sigmoid(beta).reshape(KV_HEADS, groups)[None, :, :, None]
    mixed = mixing * normed + (1.0 - mixing) * soft_out
    return mixed.reshape(row_count, HEADS * HEAD_DIM).astype(jnp.float32)


def solution(mesh):
    n_seq, n_kv = mesh.shape["seq"], mesh.shape["kv"]
    in_specs = (
        P(("dp", "seq", "kv"), None),
        P(("dp", "seq", "kv"), None),
        P(("dp", "seq", "kv"), None),
        P(("dp", "seq", "kv")),
        P(),
        P(),
    )
    out_specs = P(("dp", "seq", "kv"), None)
    if n_kv == 2 and n_seq * n_kv <= 2 * LONGEST:
        on_device = functools.partial(near_device, n_seq)
    else:
        on_device = far_device
    return jax.shard_map(
        on_device, mesh=mesh, in_specs=in_specs, out_specs=out_specs, check_vma=False
    )
```

```python
import functools
import math

import jax
import jax.numpy as jnp
from jax import lax
from jax.experimental import pallas as pl
from jax.experimental.pallas import tpu as pltpu
from jax.sharding import PartitionSpec as P

HEADS = 16
KV_HEADS = 4
HEAD_DIM = 128
GROUPS = HEADS // KV_HEADS
LONGEST = 4
SCALE = math.log2(math.e) / math.sqrt(HEAD_DIM)
LOWEST = -1e30
EXTRA = 16

NT = (((1,), (1,)), ((), ()))
TN = (((0,), (0,)), ((), ()))
NN = (((1,), (0,)), ((), ()))


def dot(a, b, dims):
    return lax.dot_general(a, b, dims, preferred_element_type=jnp.float32)


def column(row):
    return jnp.transpose(jnp.broadcast_to(row, (HEAD_DIM, row.shape[1])))


def part_of(i, size):
    return slice(i * size, (i + 1) * size)


def group_queries(q_ref, g):
    heads = [q_ref[:, part_of(g * GROUPS + i, HEAD_DIM)] for i in range(GROUPS)]
    return jnp.concatenate(heads, axis=0)


def share_of(beta_ref, h):
    return 1.0 / (1.0 + jnp.exp(-jnp.full((1, HEAD_DIM), beta_ref[h], jnp.float32)))


def scaled_gains(beta_ref, gain_ref, out_ref):
    for h in range(HEADS):
        scaled = gain_ref[h : h + 1, :] * share_of(beta_ref, h)
        out_ref[part_of(h, HEAD_DIM), :] = column(scaled)


def suffix(others, least=0.0):
    count = jnp.maximum(jnp.sum(others, axis=1, keepdims=True), least)
    shape = (others.shape[1], HEAD_DIM)
    return lax.broadcasted_iota(jnp.int32, shape, 0).astype(jnp.float32) >= count


def first_document(docs):
    first = jnp.broadcast_to(docs[:, 0:1], docs.shape)
    return first, docs == first


def load_block(key_ref, value_ref, doc_ref, out_ref, doc_scratch, sems):
    rows = key_ref.shape[0]
    doc_copy = pltpu.make_async_copy(doc_ref, doc_scratch, sems.at[0])
    doc_copy.start()
    copies = []
    for g in range(2 * KV_HEADS):
        source = key_ref if g < KV_HEADS else value_ref
        copy = pltpu.make_async_copy(
            source.at[:, part_of(g % KV_HEADS, HEAD_DIM)],
            out_ref.at[part_of(g, rows), :],
            sems.at[1 + g],
        )
        copy.start()
        copies.append(copy)
    doc_copy.wait()
    start = 2 * KV_HEADS * rows
    docs = doc_scratch[...].astype(jnp.float32)
    docs = jnp.broadcast_to(docs, (out_ref.shape[0] - start, rows))
    out_ref[start:, :] = docs.astype(jnp.bfloat16)
    for copy in copies:
        copy.wait()


def block_keys(ref, g):
    return ref[part_of(g, HEAD_DIM), :]


def block_values(ref, g):
    return ref[part_of(KV_HEADS + g, HEAD_DIM), :]


def block_docs(ref):
    start = 2 * KV_HEADS * HEAD_DIM
    return ref[start : start + EXTRA, :].astype(jnp.float32)[0:1, :]


class Plan:
    def __init__(self, n_seq):
        devices = 2 * n_seq
        near = [(b, b + 1) for b in range(devices - 1)]
        far = [(b, b + 2) for b in range(devices - 2)]
        crossing = [p for p in far if p[0] // 2 % 2 == 1]
        touched = {b for p in crossing for b in p}
        targets = {p[1] for p in crossing}
        first = crossing + [p for p in near if p[0] not in touched and p[1] not in targets]
        second = [p for p in near if p not in first]
        last = [p for p in far if p not in first]
        self.pairs = [first, second, last]
        self.senders = sorted({p[0] for p in first})
        busy = {b for p in first for b in p} & {b for p in second for b in p}
        self.early = [b for b in range(devices) if b not in busy]
        self.late = sorted({p[1] for p in second})
        received = {p[1] for pairs in self.pairs for p in pairs}
        self.alone = [b for b in range(devices) if b not in received]
        self.memory_first = [p[1] for p in crossing if p[1] % 2 == 1]


def among(members):
    block = 2 * lax.axis_index("seq") + lax.axis_index("kv")
    return functools.reduce(jnp.logical_or, [block == b for b in members])


def pack_kernel(plan, key_ref, value_ref, doc_ref, out_ref, doc_scratch, sems):
    @pl.when(among(plan.senders))
    def _():
        load_block(key_ref, value_ref, doc_ref, out_ref, doc_scratch, sems)


def attend_own(q_ref, block_ref, g, bias):
    rows = q_ref.shape[0]
    scores = dot(block_keys(block_ref, g), group_queries(q_ref, g), NT)
    tops, totals, weights = [], [], []
    for i in range(GROUPS):
        masked = scores[:, part_of(i, rows)] * SCALE + bias
        top = jnp.max(masked, axis=0, keepdims=True)
        weight = jnp.exp2(masked - top)
        tops.append(top)
        totals.append(jnp.sum(weight, axis=0, keepdims=True))
        weights.append(weight.astype(jnp.bfloat16))
    summed = dot(block_values(block_ref, g), jnp.concatenate(weights, axis=1), TN)
    return summed, jnp.concatenate(tops, axis=1), jnp.concatenate(totals, axis=1)


def own_bias(docs):
    rows = docs.shape[1]
    place = lax.broadcasted_iota(jnp.int32, (rows, rows), 0)
    row = lax.broadcasted_iota(jnp.int32, (rows, rows), 1)
    return jnp.where((place <= row) & (column(docs) == docs), 0.0, LOWEST)


def attend_itself(
    q_ref, block_ref, gain_ref, beta_ref, beta_copy, summed_ref, stats_ref, gains_ref
):
    bias = own_bias(block_docs(block_ref))
    results = [attend_own(q_ref, block_ref, g, bias) for g in range(KV_HEADS)]
    beta_copy.wait()
    scaled_gains(beta_ref, gain_ref, gains_ref)
    done = lax.axis_index("kv") == 0
    for g, (summed, top, total) in enumerate(results):
        rest = [1.0 - share_of(beta_ref, g * GROUPS + i) for i in range(GROUPS)]
        rest = jnp.concatenate(rest, axis=1)
        summed_ref[part_of(g, HEAD_DIM), :] = summed * jnp.where(done, rest / total, 1.0)
        stats_ref[g : g + 1, :] = top
        stats_ref[KV_HEADS + g : KV_HEADS + g + 1, :] = total
        stats_ref[2 * KV_HEADS + g : 2 * KV_HEADS + g + 1, :] = rest


def settle_kernel(
    plan, gain_ref, packed_ref, query_ref, key_ref, value_ref, doc_ref, beta_ref,
    own_ref, short_ref, summed_ref, stats_ref, gains_ref,
    q_scratch, beta_scratch, doc_scratch, sems, early_sems,
):
    sender, early = among(plan.senders), among(plan.early)
    query_copy = pltpu.make_async_copy(query_ref, q_scratch, early_sems.at[0])
    beta_copy = pltpu.make_async_copy(beta_ref, beta_scratch, early_sems.at[1])

    @pl.when(early)
    def _():
        query_copy.start()
        beta_copy.start()

    @pl.when(sender)
    def _():
        own_ref[...] = packed_ref[...]

    @pl.when(jnp.logical_not(sender))
    def _():
        load_block(key_ref, value_ref, doc_ref, own_ref, doc_scratch, sems)

    short_ref[...] = own_ref[0 : short_ref.shape[0], :]
    line = lax.broadcasted_iota(jnp.int32, (EXTRA, HEAD_DIM), 0)
    keys = own_ref[0:EXTRA, :].astype(jnp.float32)
    keys = jnp.where(line == 0, block_docs(own_ref), keys)
    short_ref[0:EXTRA, :] = keys.astype(jnp.bfloat16)

    @pl.when(early)
    def _():
        query_copy.wait()
        attend_itself(
            q_scratch, own_ref, gain_ref, beta_scratch, beta_copy,
            summed_ref, stats_ref, gains_ref,
        )


def own_kernel(
    plan, q_ref, gain_ref, own_ref, beta_ref, summed_in, stats_in, gains_in,
    summed_ref, stats_ref, gains_ref, out_ref, turned_ref, beta_scratch, sem, held, sems,
):
    rows = q_ref.shape[0]
    for g in range(KV_HEADS):
        for i in range(GROUPS):
            head = q_ref[:, part_of(g * GROUPS + i, HEAD_DIM)]
            turned_ref[part_of(g, HEAD_DIM), part_of(i, rows)] = jnp.transpose(head)

    @pl.when(among(plan.alone))
    def _():
        _, same = first_document(block_docs(own_ref))
        states = [jnp.zeros((HEAD_DIM, HEAD_DIM), jnp.float32)] * KV_HEADS
        read_and_store(states, turned_ref, gains_ref, same, summed_ref, out_ref, held, sems)

    @pl.when(jnp.logical_not(among(plan.early)))
    def _():
        beta_copy = pltpu.make_async_copy(beta_ref, beta_scratch, sem)
        beta_copy.start()
        attend_itself(
            q_ref, own_ref, gain_ref, beta_scratch, beta_copy, summed_ref, stats_ref, gains_ref
        )


def memory_states(refs, first):
    lives = []
    for ref in refs:
        short = ref.shape[0] == 2 * KV_HEADS * HEAD_DIM
        docs = ref[0:EXTRA, :].astype(jnp.float32)[0:1, :] if short else block_docs(ref)
        live = suffix(jnp.where(docs == first, 0.0, 1.0), 1.0 if short else 0.0)
        lives.append(jnp.where(live, 1.0, 0.0).astype(jnp.bfloat16))
    return [
        functools.reduce(
            jnp.add,
            [
                dot(block_values(ref, g), block_keys(ref, g) * live, TN)
                for ref, live in zip(refs, lives)
            ],
        )
        for g in range(KV_HEADS)
    ]


def read_memory(states, turned_ref, gains_ref, reads):
    rows = turned_ref.shape[1] // GROUPS
    pieces = []
    for state in states:
        high = state.astype(jnp.bfloat16)
        state = state - high.astype(jnp.float32)
        middle = state.astype(jnp.bfloat16)
        low = (state - middle.astype(jnp.float32)).astype(jnp.bfloat16)
        pieces.append(jnp.concatenate([high, middle, low], axis=0))
    products = [
        dot(pieces[g], turned_ref[part_of(g, HEAD_DIM), :], NN) for g in range(KV_HEADS)
    ]

    def read(g):
        recalled = products[g][part_of(0, HEAD_DIM), :] + (
            products[g][part_of(1, HEAD_DIM), :] + products[g][part_of(2, HEAD_DIM), :]
        )
        heads = []
        for i in range(GROUPS):
            head = recalled[:, part_of(i, rows)]
            square = jnp.sum(head * head, axis=0, keepdims=True) * (1.0 / HEAD_DIM)
            head = head * (lax.rsqrt(square + 1e-06) * reads)
            heads.append(head * gains_ref[part_of(g * GROUPS + i, HEAD_DIM), :])
        return heads

    return read


def attend_before(turned_ref, one_ref, stats_ref, summed_ref, first, same):
    rows = (turned_ref.shape[1] // GROUPS)
    live = suffix(jnp.where(block_docs(one_ref) == first, 0.0, 1.0))
    bias = jnp.where(live & same, 0.0, LOWEST)
    ahead = {}

    def score(g):
        if g < KV_HEADS and g not in ahead:
            ahead[g] = dot(block_keys(one_ref, g), turned_ref[part_of(g, HEAD_DIM), :], NN)

    def attend(g):
        for later in range(3):
            score(g + later)
        weights, factors, scales = [], [], []
        for i in range(GROUPS):
            cut = part_of(i, rows)
            masked = ahead[g][:, cut] * SCALE + bias
            top_own = stats_ref[g : g + 1, cut]
            top = jnp.maximum(jnp.max(masked, axis=0, keepdims=True), top_own)
            weight = jnp.exp2(masked - top)
            factor = jnp.exp2(top_own - top)
            total = stats_ref[KV_HEADS + g : KV_HEADS + g + 1, cut] * factor
            total = total + jnp.sum(weight, axis=0, keepdims=True)
            factors.append(factor)
            scales.append(stats_ref[2 * KV_HEADS + g : 2 * KV_HEADS + g + 1, cut] / total)
            weights.append(weight.astype(jnp.bfloat16))
        added = dot(block_values(one_ref, g), jnp.concatenate(weights, axis=1), TN)
        summed = summed_ref[part_of(g, HEAD_DIM), :] * jnp.concatenate(factors, axis=1) + added
        return summed * jnp.concatenate(scales, axis=1)

    return attend


def store_heads(mixed, out_ref, held, sems):
    copies = []
    ahead = mixed(0)
    for g in range(KV_HEADS):
        heads, ahead = ahead, mixed(g + 1) if g + 1 < KV_HEADS else None
        for i, head in enumerate(heads):
            held[:, part_of(g * GROUPS + i, HEAD_DIM)] = jnp.transpose(head)
        for half in range(2 * g, 2 * g + 2):
            wide = part_of(half, GROUPS // 2 * HEAD_DIM)
            copy = pltpu.make_async_copy(held.at[:, wide], out_ref.at[:, wide], sems.at[half])
            copy.start(priority=half % 2)
            copies.append(copy)
    for copy in copies:
        copy.wait()


def read_into(read_ref, refs, turned_ref, own_ref, gains_ref):
    first, same = first_document(block_docs(own_ref))
    read = read_memory(
        memory_states(refs, first), turned_ref, gains_ref, jnp.where(same, 1.0, 0.0)
    )
    for g in range(KV_HEADS):
        for i, head in enumerate(read(g)):
            read_ref[part_of(g * GROUPS + i, HEAD_DIM), :] = head


def read_kernel(plan, turned_ref, own_ref, three_ref, gains_ref, read_ref):
    @pl.when((lax.axis_index("kv") == 1) & jnp.logical_not(among(plan.memory_first)))
    def _():
        read_into(read_ref, [three_ref], turned_ref, own_ref, gains_ref)


def attend_and_store(
    turned_ref, own_ref, earlier_ref, stats_ref, summed_ref, read_ref, out_ref, held, sems
):
    first, same = first_document(block_docs(own_ref))
    attend = attend_before(turned_ref, earlier_ref, stats_ref, summed_ref, first, same)
    rows = (turned_ref.shape[1] // GROUPS)

    def mixed(g):
        attended = attend(g)
        return [
            read_ref[part_of(g * GROUPS + i, HEAD_DIM), :] + attended[:, part_of(i, rows)]
            for i in range(GROUPS)
        ]

    store_heads(mixed, out_ref, held, sems)


def read_and_store(states, turned_ref, gains_ref, same, summed_ref, out_ref, held, sems):
    rows = (turned_ref.shape[1] // GROUPS)
    read = read_memory(states, turned_ref, gains_ref, jnp.where(same, 1.0, 0.0))

    def mixed(g):
        return [
            head + summed_ref[part_of(g, HEAD_DIM), part_of(i, rows)]
            for i, head in enumerate(read(g))
        ]

    store_heads(mixed, out_ref, held, sems)


def early_kernel(
    plan, turned_ref, own_ref, one_ref, three_ref, stats_ref, gains_ref, summed_ref, read_in, out_in,
    read_ref, state_ref, out_ref, held, sems,
):
    kv = lax.axis_index("kv")
    late = among(plan.late)

    @pl.when((kv == 0) & jnp.logical_not(late | among(plan.alone)))
    def _():
        first, same = first_document(block_docs(own_ref))
        states = memory_states([one_ref, three_ref], first)
        read_and_store(states, turned_ref, gains_ref, same, summed_ref, out_ref, held, sems)

    @pl.when((kv == 1) & jnp.logical_not(late))
    def _():
        attend_and_store(
            turned_ref, own_ref, one_ref, stats_ref, summed_ref, read_ref, out_ref, held, sems
        )

    @pl.when((kv == 0) & late)
    def _():
        first, _ = first_document(block_docs(own_ref))
        for g, state in enumerate(memory_states([one_ref, three_ref], first)):
            state_ref[part_of(g, HEAD_DIM), :] = state

    @pl.when((kv == 1) & among(plan.memory_first))
    def _():
        read_into(read_ref, [one_ref, three_ref], turned_ref, own_ref, gains_ref)


def late_kernel(
    plan, turned_ref, own_ref, two_ref, state_ref, summed_ref, stats_ref, gains_ref, read_ref, out_in,
    out_ref, held, sems,
):
    kv = lax.axis_index("kv")
    late = among(plan.late)

    @pl.when((kv == 1) & late)
    def _():
        attend_and_store(
            turned_ref, own_ref, two_ref, stats_ref, summed_ref, read_ref, out_ref, held, sems
        )

    @pl.when((kv == 0) & late)
    def _():
        first, same = first_document(block_docs(own_ref))
        states = [
            state_ref[part_of(g, HEAD_DIM), :] + state
            for g, state in enumerate(memory_states([two_ref], first))
        ]
        read_and_store(states, turned_ref, gains_ref, same, summed_ref, out_ref, held, sems)


def near_device(n_seq, queries, keys, values, doc_ids, beta, lin_gain):
    rows = queries.shape[0]
    vmem = pl.BlockSpec(memory_space=pltpu.VMEM)
    hbm = pl.BlockSpec(memory_space=pltpu.HBM)
    in_hbm = functools.partial(pltpu.with_memory_space_constraint, memory_space=pltpu.HBM)
    params = pltpu.CompilerParams(vmem_limit_bytes=32 * 1024 * 1024)
    wide = GROUPS * rows
    group_shape = jax.ShapeDtypeStruct((KV_HEADS * HEAD_DIM, wide), jnp.float32)
    gains_shape = jax.ShapeDtypeStruct((HEADS * HEAD_DIM, HEAD_DIM), jnp.float32)
    docs = doc_ids.reshape(1, rows)
    gain = lin_gain.reshape(HEADS, HEAD_DIM)
    deep = 2 * KV_HEADS * rows + EXTRA

    def estimate(share):
        return pl.CostEstimate(
            flops=int(share * 4 * HEADS * HEAD_DIM * rows * rows),
            bytes_accessed=int(share * 4 * 1024 * 1024),
            transcendentals=int(share * HEADS * rows * rows),
        )

    def send(payload, pairs):
        return lax.ppermute(payload, ("seq", "kv"), pairs)

    plan = Plan(n_seq)
    block_shape = jax.ShapeDtypeStruct((deep, HEAD_DIM), jnp.bfloat16)
    short_shape = jax.ShapeDtypeStruct((deep - EXTRA, HEAD_DIM), jnp.bfloat16)
    stats_shape = jax.ShapeDtypeStruct((4 * KV_HEADS, wide), jnp.float32)
    state_shape = jax.ShapeDtypeStruct((KV_HEADS * HEAD_DIM, HEAD_DIM), jnp.float32)
    results = [group_shape, stats_shape, gains_shape]
    doc_scratch = pltpu.VMEM((1, rows), jnp.int32)
    beta_scratch = pltpu.SMEM((HEADS,), jnp.float32)
    sems = pltpu.SemaphoreType.DMA((2 * KV_HEADS + 1,))
    block = (in_hbm(keys), in_hbm(values), in_hbm(docs))
    beta = in_hbm(beta)
    packed = pl.pallas_call(
        functools.partial(pack_kernel, plan),
        out_shape=block_shape,
        in_specs=[hbm] * 3,
        out_specs=vmem,
        scratch_shapes=[doc_scratch, sems],
        compiler_params=params,
        cost_estimate=estimate(0.1),
    )(*block)
    one = send(packed, plan.pairs[0])
    own, short, summed, stats, gains = pl.pallas_call(
        functools.partial(settle_kernel, plan),
        out_shape=[block_shape, short_shape] + results,
        in_specs=[vmem] * 2 + [hbm] * 5,
        out_specs=[vmem] * 5,
        scratch_shapes=[
            pltpu.VMEM(queries.shape, queries.dtype),
            beta_scratch,
            doc_scratch,
            sems,
            pltpu.SemaphoreType.DMA((2,)),
        ],
        compiler_params=params,
        cost_estimate=estimate(1.0),
    )(gain, packed, in_hbm(queries), *block, beta)
    two = send(own, plan.pairs[1])
    three = send(short, plan.pairs[2])
    out_shape = jax.ShapeDtypeStruct((rows, HEADS * HEAD_DIM), jnp.float32)
    store_scratch = [
        pltpu.VMEM((rows, HEADS * HEAD_DIM), jnp.float32),
        pltpu.SemaphoreType.DMA((2 * KV_HEADS,)),
    ]
    turned_shape = jax.ShapeDtypeStruct((KV_HEADS * HEAD_DIM, wide), queries.dtype)
    summed, stats, gains, out, turned = pl.pallas_call(
        functools.partial(own_kernel, plan),
        out_shape=results + [out_shape, turned_shape],
        in_specs=[vmem] * 3 + [hbm] + [vmem] * 3,
        out_specs=[vmem] * 3 + [hbm, vmem],
        scratch_shapes=[beta_scratch, pltpu.SemaphoreType.DMA] + store_scratch,
        input_output_aliases={4: 0, 5: 1, 6: 2},
        compiler_params=params,
        cost_estimate=estimate(1.0),
    )(queries, gain, own, beta, summed, stats, gains)
    read = pl.pallas_call(
        functools.partial(read_kernel, plan),
        out_shape=gains_shape,
        in_specs=[vmem] * 4,
        out_specs=vmem,
        compiler_params=params,
    )(turned, own, three, gains)
    read, state, out = pl.pallas_call(
        functools.partial(early_kernel, plan),
        out_shape=[gains_shape, state_shape, out_shape],
        in_specs=[vmem] * 8 + [hbm],
        out_specs=[vmem] * 2 + [hbm],
        scratch_shapes=store_scratch,
        input_output_aliases={7: 0, 8: 2},
        compiler_params=params,
    )(turned, own, one, three, stats, gains, summed, read, out)
    return pl.pallas_call(
        functools.partial(late_kernel, plan),
        out_shape=out_shape,
        in_specs=[vmem] * 8 + [hbm],
        out_specs=hbm,
        scratch_shapes=store_scratch,
        input_output_aliases={8: 0},
        compiler_params=params,
    )(turned, own, two, state, summed, stats, gains, read, out)


def carried_in(part, axis, combine, identity):
    place = lax.axis_index(axis)
    gathered = jax.tree.map(lambda a: lax.all_gather(a, axis), part)
    state = jax.tree.map(lambda a, e: jnp.zeros_like(a) + jnp.asarray(e, a.dtype), part, identity)

    def one(step, state):
        return combine(
            state, jax.tree.map(lambda a: lax.dynamic_index_in_dim(a, step, 0, False), gathered)
        )

    return lax.fori_loop(0, place, one, state)


def join_states(earlier, later):
    state_early, first_early, last_early = earlier
    state_late, first_late, last_late = later
    empty_late = first_late < 0
    joined = (first_late == last_late) & (last_early == first_late)
    merged = state_late + jnp.where(joined, state_early, jnp.zeros_like(state_early))
    combined = jnp.where(empty_late, state_early, merged)
    first_doc = jnp.where(first_early < 0, first_late, first_early)
    last_doc = jnp.where(empty_late, last_early, last_late)
    return (combined, first_doc, last_doc)


def tail_merge(one_side, other_side):
    state_one, first_one, last_one = one_side
    state_other, first_other, last_other = other_side
    top_doc = jnp.maximum(last_one, last_other)
    state_sum = jnp.where(last_one == top_doc, state_one, jnp.zeros_like(state_one))
    state_sum = state_sum + jnp.where(
        last_other == top_doc, state_other, jnp.zeros_like(state_other)
    )
    return (state_sum, jnp.minimum(first_one, first_other), top_doc)


def tail_state(key_rows, value_rows, doc_rows, target_doc):
    count = key_rows.shape[0]
    key_heads = key_rows.reshape(count, KV_HEADS, HEAD_DIM)
    value_heads = value_rows.reshape(count, KV_HEADS, HEAD_DIM)
    live = doc_rows == target_doc
    masked = jnp.where(live[:, None, None], key_heads, jnp.zeros_like(key_heads))
    return jnp.einsum("rgd,rge->gde", masked, value_heads, preferred_element_type=jnp.float32)


def attend_block(
    carry, query_heads, query_pos, query_doc, key_rows, value_rows, key_doc, key_start
):
    running_max, running_sum, accumulated = carry
    key_count = key_rows.shape[0]
    key_heads = key_rows.reshape(key_count, KV_HEADS, HEAD_DIM)
    value_heads = value_rows.reshape(key_count, KV_HEADS, HEAD_DIM)
    scores = jnp.einsum(
        "rgqd,kgd->gqrk", query_heads, key_heads, preferred_element_type=jnp.float32
    )
    scores = scores / jnp.sqrt(jnp.float32(HEAD_DIM))
    key_pos = key_start + jnp.arange(key_count, dtype=jnp.int32)
    allowed = (key_pos[None, :] <= query_pos[:, None]) & (key_doc[None, :] == query_doc[:, None])
    masked = jnp.where(allowed, scores, jnp.float32(-1e30))
    new_max = jnp.maximum(running_max, jnp.max(masked, axis=-1))
    factor = jnp.exp(running_max - new_max)
    weights = jnp.where(allowed, jnp.exp(masked - new_max[..., None]), jnp.float32(0.0))
    new_sum = running_sum * factor + jnp.sum(weights, axis=-1)
    product = jnp.einsum(
        "gqrk,kge->gqre",
        weights.astype(jnp.bfloat16),
        value_heads,
        preferred_element_type=jnp.float32,
    )
    new_accum = accumulated * factor[..., None] + product
    return (new_max, new_sum, new_accum)


def far_device(queries, keys, values, doc_ids, beta, lin_gain):
    row_count = queries.shape[0]
    groups = HEADS // KV_HEADS
    query_heads = queries.reshape(row_count, KV_HEADS, groups, HEAD_DIM)
    position = lax.axis_index("kv") * row_count
    query_pos = position + jnp.arange(row_count, dtype=jnp.int32)
    last_query = position + row_count - 1
    initial = (
        jnp.full((KV_HEADS, groups, row_count), -1e30, jnp.float32),
        jnp.zeros((KV_HEADS, groups, row_count), jnp.float32),
        jnp.zeros((KV_HEADS, groups, row_count, HEAD_DIM), jnp.float32),
    )
    empty_tail = (
        jnp.zeros((KV_HEADS, HEAD_DIM, HEAD_DIM), jnp.float32),
        jnp.array(2**30, jnp.int32),
        jnp.array(-1, jnp.int32),
    )
    key_piece = lax.all_gather(keys, "kv", axis=0, tiled=True)
    value_piece = lax.all_gather(values, "kv", axis=0, tiled=True)
    doc_piece = lax.all_gather(doc_ids, "kv", axis=0, tiled=True)
    blocks = key_piece.shape[0] // row_count

    def one_block(state, item):
        soft_state, tail_now = state
        key_block, value_block, doc_block, number = item
        block_start = number * row_count
        soft_next = lax.cond(
            block_start <= last_query,
            lambda inner: attend_block(
                inner,
                query_heads,
                query_pos,
                doc_ids,
                key_block,
                value_block,
                doc_block,
                block_start,
            ),
            lambda inner: inner,
            soft_state,
        )
        block_tail = (
            tail_state(key_block, value_block, doc_block, doc_block[-1]),
            doc_block[0],
            doc_block[-1],
        )
        tail_now = tail_merge(tail_now, block_tail)
        return ((soft_next, tail_now), None)

    stacked = (
        key_piece.reshape(blocks, row_count, -1),
        value_piece.reshape(blocks, row_count, -1),
        doc_piece.reshape(blocks, row_count),
        jnp.arange(blocks, dtype=jnp.int32),
    )
    result, _ = lax.scan(one_block, (initial, empty_tail), stacked)
    running, segment_tail = result
    running_max, running_sum, accumulated = running
    soft_out = jnp.transpose(accumulated / running_sum[..., None], (2, 0, 1, 3))
    identity = (
        jnp.zeros((KV_HEADS, HEAD_DIM, HEAD_DIM), jnp.float32),
        jnp.array(-1, jnp.int32),
        jnp.array(-1, jnp.int32),
    )
    memory = carried_in(segment_tail, "seq", join_states, identity)
    memory_state, memory_first, memory_last = memory
    query_float = query_heads.astype(jnp.float32)
    recalled = jnp.einsum(
        "rgqd,gde->rgqe", query_float, memory_state, precision=lax.Precision.HIGHEST
    )
    recalled = jnp.where((doc_ids == memory_last)[:, None, None, None], recalled, jnp.float32(0.0))
    mean_square = jnp.mean(recalled * recalled, axis=-1, keepdims=True)
    normed = (
        recalled * lax.rsqrt(mean_square + 1e-06) * lin_gain.reshape(KV_HEADS, groups, HEAD_DIM)
    )
    mixing = jax.nn.sigmoid(beta).reshape(KV_HEADS, groups)[None, :, :, None]
    mixed = mixing * normed + (1.0 - mixing) * soft_out
    return mixed.reshape(row_count, HEADS * HEAD_DIM).astype(jnp.float32)


def solution(mesh):
    n_seq, n_kv = mesh.shape["seq"], mesh.shape["kv"]
    in_specs = (
        P(("dp", "seq", "kv"), None),
        P(("dp", "seq", "kv"), None),
        P(("dp", "seq", "kv"), None),
        P(("dp", "seq", "kv")),
        P(),
        P(),
    )
    out_specs = P(("dp", "seq", "kv"), None)
    if n_kv == 2 and n_seq * n_kv <= 2 * LONGEST:
        on_device = functools.partial(near_device, n_seq)
    else:
        on_device = far_device
    return jax.shard_map(
        on_device, mesh=mesh, in_specs=in_specs, out_specs=out_specs, check_vma=False
    )
```

```python
import functools
import math

import jax
import jax.numpy as jnp
from jax import lax
from jax.experimental import pallas as pl
from jax.experimental.pallas import tpu as pltpu
from jax.sharding import PartitionSpec as P

HEADS = 16
KV_HEADS = 4
HEAD_DIM = 128
GROUPS = HEADS // KV_HEADS
LONGEST = 4
SCALE = math.log2(math.e) / math.sqrt(HEAD_DIM)
LOWEST = -1e30
EXTRA = 16

NT = (((1,), (1,)), ((), ()))
TN = (((0,), (0,)), ((), ()))
NN = (((1,), (0,)), ((), ()))


def dot(a, b, dims):
    return lax.dot_general(a, b, dims, preferred_element_type=jnp.float32)


def column(row):
    return jnp.transpose(jnp.broadcast_to(row, (HEAD_DIM, row.shape[1])))


def part_of(i, size):
    return slice(i * size, (i + 1) * size)


def group_queries(q_ref, g):
    heads = [q_ref[:, part_of(g * GROUPS + i, HEAD_DIM)] for i in range(GROUPS)]
    return jnp.concatenate(heads, axis=0)


def share_of(beta_ref, h):
    return 1.0 / (1.0 + jnp.exp(-jnp.full((1, HEAD_DIM), beta_ref[h], jnp.float32)))


def scaled_gains(beta_ref, gain_ref, out_ref):
    for h in range(HEADS):
        scaled = gain_ref[h : h + 1, :] * share_of(beta_ref, h)
        out_ref[part_of(h, HEAD_DIM), :] = column(scaled)


def suffix(others, least=0.0):
    count = jnp.maximum(jnp.sum(others, axis=1, keepdims=True), least)
    shape = (others.shape[1], HEAD_DIM)
    return lax.broadcasted_iota(jnp.int32, shape, 0).astype(jnp.float32) >= count


def first_document(docs):
    first = jnp.broadcast_to(docs[:, 0:1], docs.shape)
    return first, docs == first


def load_block(key_ref, value_ref, doc_ref, out_ref, doc_scratch, sems):
    rows = key_ref.shape[0]
    doc_copy = pltpu.make_async_copy(doc_ref, doc_scratch, sems.at[0])
    doc_copy.start()
    copies = []
    for g in range(2 * KV_HEADS):
        source = key_ref if g < KV_HEADS else value_ref
        copy = pltpu.make_async_copy(
            source.at[:, part_of(g % KV_HEADS, HEAD_DIM)],
            out_ref.at[part_of(g, rows), :],
            sems.at[1 + g],
        )
        copy.start()
        copies.append(copy)
    doc_copy.wait()
    start = 2 * KV_HEADS * rows
    docs = doc_scratch[...].astype(jnp.float32)
    docs = jnp.broadcast_to(docs, (out_ref.shape[0] - start, rows))
    out_ref[start:, :] = docs.astype(jnp.bfloat16)
    for copy in copies:
        copy.wait()


def block_keys(ref, g):
    return ref[part_of(g, HEAD_DIM), :]


def block_values(ref, g):
    return ref[part_of(KV_HEADS + g, HEAD_DIM), :]


def block_docs(ref):
    start = 2 * KV_HEADS * HEAD_DIM
    return ref[start : start + EXTRA, :].astype(jnp.float32)[0:1, :]


class Plan:
    def __init__(self, n_seq):
        devices = 2 * n_seq
        near = [(b, b + 1) for b in range(devices - 1)]
        far = [(b, b + 2) for b in range(devices - 2)]
        crossing = [p for p in far if p[0] // 2 % 2 == 1]
        touched = {b for p in crossing for b in p}
        targets = {p[1] for p in crossing}
        first = crossing + [p for p in near if p[0] not in touched and p[1] not in targets]
        second = [p for p in near if p not in first]
        last = [p for p in far if p not in first]
        self.pairs = [first, second, last]
        self.senders = sorted({p[0] for p in first})
        busy = {b for p in first for b in p} & {b for p in second for b in p}
        self.early = [b for b in range(devices) if b not in busy]
        self.late = sorted({p[1] for p in second})
        received = {p[1] for pairs in self.pairs for p in pairs}
        self.alone = [b for b in range(devices) if b not in received]
        self.memory_first = [p[1] for p in crossing if p[1] % 2 == 1]


def among(members):
    block = 2 * lax.axis_index("seq") + lax.axis_index("kv")
    return functools.reduce(jnp.logical_or, [block == b for b in members])


def pack_kernel(plan, key_ref, value_ref, doc_ref, out_ref, doc_scratch, sems):
    @pl.when(among(plan.senders))
    def _():
        load_block(key_ref, value_ref, doc_ref, out_ref, doc_scratch, sems)


def attend_own(q_ref, block_ref, g, bias):
    rows = q_ref.shape[0]
    scores = dot(block_keys(block_ref, g), group_queries(q_ref, g), NT)
    tops, totals, weights = [], [], []
    for i in range(GROUPS):
        masked = scores[:, part_of(i, rows)] * SCALE + bias
        top = jnp.max(masked, axis=0, keepdims=True)
        weight = jnp.exp2(masked - top)
        tops.append(top)
        totals.append(jnp.sum(weight, axis=0, keepdims=True))
        weights.append(weight.astype(jnp.bfloat16))
    summed = dot(block_values(block_ref, g), jnp.concatenate(weights, axis=1), TN)
    return summed, jnp.concatenate(tops, axis=1), jnp.concatenate(totals, axis=1)


def own_bias(docs):
    rows = docs.shape[1]
    place = lax.broadcasted_iota(jnp.int32, (rows, rows), 0)
    row = lax.broadcasted_iota(jnp.int32, (rows, rows), 1)
    return jnp.where((place <= row) & (column(docs) == docs), 0.0, LOWEST)


def attend_itself(
    q_ref, block_ref, gain_ref, beta_ref, beta_copy, summed_ref, stats_ref, gains_ref
):
    bias = own_bias(block_docs(block_ref))
    results = [attend_own(q_ref, block_ref, g, bias) for g in range(KV_HEADS)]
    beta_copy.wait()
    scaled_gains(beta_ref, gain_ref, gains_ref)
    done = lax.axis_index("kv") == 0
    for g, (summed, top, total) in enumerate(results):
        rest = [1.0 - share_of(beta_ref, g * GROUPS + i) for i in range(GROUPS)]
        rest = jnp.concatenate(rest, axis=1)
        summed_ref[part_of(g, HEAD_DIM), :] = summed * jnp.where(done, rest / total, 1.0)
        stats_ref[g : g + 1, :] = top
        stats_ref[KV_HEADS + g : KV_HEADS + g + 1, :] = total
        stats_ref[2 * KV_HEADS + g : 2 * KV_HEADS + g + 1, :] = rest


def settle_kernel(
    plan, gain_ref, packed_ref, key_ref, value_ref, doc_ref, query_ref, beta_ref,
    own_ref, short_ref, summed_ref, stats_ref, gains_ref,
    q_scratch, beta_scratch, early_sems,
):
    sender, early = among(plan.senders), among(plan.early)
    query_copy = pltpu.make_async_copy(query_ref, q_scratch, early_sems.at[0])
    beta_copy = pltpu.make_async_copy(beta_ref, beta_scratch, early_sems.at[1])

    @pl.when(early)
    def _():
        query_copy.start()
        beta_copy.start()

    @pl.when(sender)
    def _():
        own_ref[...] = packed_ref[...]

    @pl.when(jnp.logical_not(sender))
    def _():
        for g in range(KV_HEADS):
            cols = part_of(g, HEAD_DIM)
            own_ref[part_of(g, HEAD_DIM), :] = key_ref[:, cols]
            own_ref[part_of(KV_HEADS + g, HEAD_DIM), :] = value_ref[:, cols]
        start = 2 * KV_HEADS * HEAD_DIM
        docs = jnp.broadcast_to(doc_ref[...].astype(jnp.float32), (EXTRA, HEAD_DIM))
        own_ref[start:, :] = docs.astype(jnp.bfloat16)

    short_ref[...] = own_ref[0 : short_ref.shape[0], :]
    line = lax.broadcasted_iota(jnp.int32, (EXTRA, HEAD_DIM), 0)
    keys = own_ref[0:EXTRA, :].astype(jnp.float32)
    keys = jnp.where(line == 0, block_docs(own_ref), keys)
    short_ref[0:EXTRA, :] = keys.astype(jnp.bfloat16)

    @pl.when(early)
    def _():
        query_copy.wait()
        attend_itself(
            q_scratch, own_ref, gain_ref, beta_scratch, beta_copy,
            summed_ref, stats_ref, gains_ref,
        )


def own_kernel(
    plan, q_ref, gain_ref, own_ref, beta_ref, summed_in, stats_in, gains_in,
    summed_ref, stats_ref, gains_ref, out_ref, turned_ref, beta_scratch, sem, held, sems,
):
    rows = q_ref.shape[0]
    for g in range(KV_HEADS):
        for i in range(GROUPS):
            head = q_ref[:, part_of(g * GROUPS + i, HEAD_DIM)]
            turned_ref[part_of(g, HEAD_DIM), part_of(i, rows)] = jnp.transpose(head)

    @pl.when(among(plan.alone))
    def _():
        _, same = first_document(block_docs(own_ref))
        states = [jnp.zeros((HEAD_DIM, HEAD_DIM), jnp.float32)] * KV_HEADS
        read_and_store(states, turned_ref, gains_ref, same, summed_ref, out_ref, held, sems)

    @pl.when(jnp.logical_not(among(plan.early)))
    def _():
        beta_copy = pltpu.make_async_copy(beta_ref, beta_scratch, sem)
        beta_copy.start()
        attend_itself(
            q_ref, own_ref, gain_ref, beta_scratch, beta_copy, summed_ref, stats_ref, gains_ref
        )


def memory_states(refs, first):
    lives = []
    for ref in refs:
        short = ref.shape[0] == 2 * KV_HEADS * HEAD_DIM
        docs = ref[0:EXTRA, :].astype(jnp.float32)[0:1, :] if short else block_docs(ref)
        live = suffix(jnp.where(docs == first, 0.0, 1.0), 1.0 if short else 0.0)
        lives.append(jnp.where(live, 1.0, 0.0).astype(jnp.bfloat16))
    return [
        functools.reduce(
            jnp.add,
            [
                dot(block_values(ref, g), block_keys(ref, g) * live, TN)
                for ref, live in zip(refs, lives)
            ],
        )
        for g in range(KV_HEADS)
    ]


def read_memory(states, turned_ref, gains_ref, reads):
    rows = turned_ref.shape[1] // GROUPS
    pieces = []
    for state in states:
        high = state.astype(jnp.bfloat16)
        state = state - high.astype(jnp.float32)
        middle = state.astype(jnp.bfloat16)
        low = (state - middle.astype(jnp.float32)).astype(jnp.bfloat16)
        pieces.append(jnp.concatenate([high, middle, low], axis=0))
    products = [
        dot(pieces[g], turned_ref[part_of(g, HEAD_DIM), :], NN) for g in range(KV_HEADS)
    ]

    def read(g):
        recalled = products[g][part_of(0, HEAD_DIM), :] + (
            products[g][part_of(1, HEAD_DIM), :] + products[g][part_of(2, HEAD_DIM), :]
        )
        heads = []
        for i in range(GROUPS):
            head = recalled[:, part_of(i, rows)]
            square = jnp.sum(head * head, axis=0, keepdims=True) * (1.0 / HEAD_DIM)
            head = head * (lax.rsqrt(square + 1e-06) * reads)
            heads.append(head * gains_ref[part_of(g * GROUPS + i, HEAD_DIM), :])
        return heads

    return read


def attend_before(turned_ref, one_ref, stats_ref, summed_ref, first, same):
    rows = (turned_ref.shape[1] // GROUPS)
    live = suffix(jnp.where(block_docs(one_ref) == first, 0.0, 1.0))
    bias = jnp.where(live & same, 0.0, LOWEST)
    ahead = {}

    def score(g):
        if g < KV_HEADS and g not in ahead:
            ahead[g] = dot(block_keys(one_ref, g), turned_ref[part_of(g, HEAD_DIM), :], NN)

    def attend(g):
        for later in range(3):
            score(g + later)
        weights, factors, scales = [], [], []
        for i in range(GROUPS):
            cut = part_of(i, rows)
            masked = ahead[g][:, cut] * SCALE + bias
            top_own = stats_ref[g : g + 1, cut]
            top = jnp.maximum(jnp.max(masked, axis=0, keepdims=True), top_own)
            weight = jnp.exp2(masked - top)
            factor = jnp.exp2(top_own - top)
            total = stats_ref[KV_HEADS + g : KV_HEADS + g + 1, cut] * factor
            total = total + jnp.sum(weight, axis=0, keepdims=True)
            factors.append(factor)
            scales.append(stats_ref[2 * KV_HEADS + g : 2 * KV_HEADS + g + 1, cut] / total)
            weights.append(weight.astype(jnp.bfloat16))
        added = dot(block_values(one_ref, g), jnp.concatenate(weights, axis=1), TN)
        summed = summed_ref[part_of(g, HEAD_DIM), :] * jnp.concatenate(factors, axis=1) + added
        return summed * jnp.concatenate(scales, axis=1)

    return attend


def store_heads(mixed, out_ref, held, sems):
    copies = []
    ahead = mixed(0)
    for g in range(KV_HEADS):
        heads, ahead = ahead, mixed(g + 1) if g + 1 < KV_HEADS else None
        for i, head in enumerate(heads):
            held[:, part_of(g * GROUPS + i, HEAD_DIM)] = jnp.transpose(head)
        wide = part_of(g, GROUPS * HEAD_DIM)
        copies.append(pltpu.make_async_copy(held.at[:, wide], out_ref.at[:, wide], sems.at[g]))
        copies[g].start()
    for copy in copies:
        copy.wait()


def read_into(read_ref, refs, turned_ref, own_ref, gains_ref):
    first, same = first_document(block_docs(own_ref))
    read = read_memory(
        memory_states(refs, first), turned_ref, gains_ref, jnp.where(same, 1.0, 0.0)
    )
    for g in range(KV_HEADS):
        for i, head in enumerate(read(g)):
            read_ref[part_of(g * GROUPS + i, HEAD_DIM), :] = head


def read_kernel(plan, turned_ref, own_ref, three_ref, gains_ref, read_ref):
    @pl.when((lax.axis_index("kv") == 1) & jnp.logical_not(among(plan.memory_first)))
    def _():
        read_into(read_ref, [three_ref], turned_ref, own_ref, gains_ref)


def attend_and_store(
    turned_ref, own_ref, earlier_ref, stats_ref, summed_ref, read_ref, out_ref, held, sems
):
    first, same = first_document(block_docs(own_ref))
    attend = attend_before(turned_ref, earlier_ref, stats_ref, summed_ref, first, same)
    rows = (turned_ref.shape[1] // GROUPS)

    def mixed(g):
        attended = attend(g)
        return [
            read_ref[part_of(g * GROUPS + i, HEAD_DIM), :] + attended[:, part_of(i, rows)]
            for i in range(GROUPS)
        ]

    store_heads(mixed, out_ref, held, sems)


def read_and_store(states, turned_ref, gains_ref, same, summed_ref, out_ref, held, sems):
    rows = (turned_ref.shape[1] // GROUPS)
    read = read_memory(states, turned_ref, gains_ref, jnp.where(same, 1.0, 0.0))

    def mixed(g):
        return [
            head + summed_ref[part_of(g, HEAD_DIM), part_of(i, rows)]
            for i, head in enumerate(read(g))
        ]

    store_heads(mixed, out_ref, held, sems)


def early_kernel(
    plan, turned_ref, own_ref, one_ref, three_ref, stats_ref, gains_ref, summed_ref, read_in, out_in,
    read_ref, state_ref, out_ref, held, sems,
):
    kv = lax.axis_index("kv")
    late = among(plan.late)

    @pl.when((kv == 0) & jnp.logical_not(late | among(plan.alone)))
    def _():
        first, same = first_document(block_docs(own_ref))
        states = memory_states([one_ref, three_ref], first)
        read_and_store(states, turned_ref, gains_ref, same, summed_ref, out_ref, held, sems)

    @pl.when((kv == 1) & jnp.logical_not(late))
    def _():
        attend_and_store(
            turned_ref, own_ref, one_ref, stats_ref, summed_ref, read_ref, out_ref, held, sems
        )

    @pl.when((kv == 0) & late)
    def _():
        first, _ = first_document(block_docs(own_ref))
        for g, state in enumerate(memory_states([one_ref, three_ref], first)):
            state_ref[part_of(g, HEAD_DIM), :] = state

    @pl.when((kv == 1) & among(plan.memory_first))
    def _():
        read_into(read_ref, [one_ref, three_ref], turned_ref, own_ref, gains_ref)


def late_kernel(
    plan, turned_ref, own_ref, two_ref, state_ref, summed_ref, stats_ref, gains_ref, read_ref, out_in,
    out_ref, held, sems,
):
    kv = lax.axis_index("kv")
    late = among(plan.late)

    @pl.when((kv == 1) & late)
    def _():
        attend_and_store(
            turned_ref, own_ref, two_ref, stats_ref, summed_ref, read_ref, out_ref, held, sems
        )

    @pl.when((kv == 0) & late)
    def _():
        first, same = first_document(block_docs(own_ref))
        states = [
            state_ref[part_of(g, HEAD_DIM), :] + state
            for g, state in enumerate(memory_states([two_ref], first))
        ]
        read_and_store(states, turned_ref, gains_ref, same, summed_ref, out_ref, held, sems)


def near_device(n_seq, queries, keys, values, doc_ids, beta, lin_gain):
    rows = queries.shape[0]
    vmem = pl.BlockSpec(memory_space=pltpu.VMEM)
    hbm = pl.BlockSpec(memory_space=pltpu.HBM)
    in_hbm = functools.partial(pltpu.with_memory_space_constraint, memory_space=pltpu.HBM)
    params = pltpu.CompilerParams(vmem_limit_bytes=32 * 1024 * 1024)
    wide = GROUPS * rows
    group_shape = jax.ShapeDtypeStruct((KV_HEADS * HEAD_DIM, wide), jnp.float32)
    gains_shape = jax.ShapeDtypeStruct((HEADS * HEAD_DIM, HEAD_DIM), jnp.float32)
    docs = doc_ids.reshape(1, rows)
    gain = lin_gain.reshape(HEADS, HEAD_DIM)
    deep = 2 * KV_HEADS * rows + EXTRA

    def estimate(share):
        return pl.CostEstimate(
            flops=int(share * 4 * HEADS * HEAD_DIM * rows * rows),
            bytes_accessed=int(share * 4 * 1024 * 1024),
            transcendentals=int(share * HEADS * rows * rows),
        )

    def send(payload, pairs):
        return lax.ppermute(payload, ("seq", "kv"), pairs)

    plan = Plan(n_seq)
    block_shape = jax.ShapeDtypeStruct((deep, HEAD_DIM), jnp.bfloat16)
    short_shape = jax.ShapeDtypeStruct((deep - EXTRA, HEAD_DIM), jnp.bfloat16)
    stats_shape = jax.ShapeDtypeStruct((4 * KV_HEADS, wide), jnp.float32)
    state_shape = jax.ShapeDtypeStruct((KV_HEADS * HEAD_DIM, HEAD_DIM), jnp.float32)
    results = [group_shape, stats_shape, gains_shape]
    doc_scratch = pltpu.VMEM((1, rows), jnp.int32)
    beta_scratch = pltpu.SMEM((HEADS,), jnp.float32)
    sems = pltpu.SemaphoreType.DMA((2 * KV_HEADS + 1,))
    block = (in_hbm(keys), in_hbm(values), in_hbm(docs))
    beta = in_hbm(beta)
    packed = pl.pallas_call(
        functools.partial(pack_kernel, plan),
        out_shape=block_shape,
        in_specs=[hbm] * 3,
        out_specs=vmem,
        scratch_shapes=[doc_scratch, sems],
        compiler_params=params,
        cost_estimate=estimate(0.1),
    )(*block)
    one = send(packed, plan.pairs[0])
    own, short, summed, stats, gains = pl.pallas_call(
        functools.partial(settle_kernel, plan),
        out_shape=[block_shape, short_shape] + results,
        in_specs=[vmem] * 5 + [hbm] * 2,
        out_specs=[vmem] * 5,
        scratch_shapes=[
            pltpu.VMEM(queries.shape, queries.dtype),
            beta_scratch,
            pltpu.SemaphoreType.DMA((2,)),
        ],
        compiler_params=params,
        cost_estimate=estimate(1.0),
    )(gain, packed, keys, values, docs, in_hbm(queries), beta)
    two = send(own, plan.pairs[1])
    three = send(short, plan.pairs[2])
    out_shape = jax.ShapeDtypeStruct((rows, HEADS * HEAD_DIM), jnp.float32)
    store_scratch = [
        pltpu.VMEM((rows, HEADS * HEAD_DIM), jnp.float32),
        pltpu.SemaphoreType.DMA((KV_HEADS,)),
    ]
    turned_shape = jax.ShapeDtypeStruct((KV_HEADS * HEAD_DIM, wide), queries.dtype)
    summed, stats, gains, out, turned = pl.pallas_call(
        functools.partial(own_kernel, plan),
        out_shape=results + [out_shape, turned_shape],
        in_specs=[vmem] * 3 + [hbm] + [vmem] * 3,
        out_specs=[vmem] * 3 + [hbm, vmem],
        scratch_shapes=[beta_scratch, pltpu.SemaphoreType.DMA] + store_scratch,
        input_output_aliases={4: 0, 5: 1, 6: 2},
        compiler_params=params,
        cost_estimate=estimate(1.0),
    )(queries, gain, own, beta, summed, stats, gains)
    read = pl.pallas_call(
        functools.partial(read_kernel, plan),
        out_shape=gains_shape,
        in_specs=[vmem] * 4,
        out_specs=vmem,
        compiler_params=params,
    )(turned, own, three, gains)
    read, state, out = pl.pallas_call(
        functools.partial(early_kernel, plan),
        out_shape=[gains_shape, state_shape, out_shape],
        in_specs=[vmem] * 8 + [hbm],
        out_specs=[vmem] * 2 + [hbm],
        scratch_shapes=store_scratch,
        input_output_aliases={7: 0, 8: 2},
        compiler_params=params,
    )(turned, own, one, three, stats, gains, summed, read, out)
    return pl.pallas_call(
        functools.partial(late_kernel, plan),
        out_shape=out_shape,
        in_specs=[vmem] * 8 + [hbm],
        out_specs=hbm,
        scratch_shapes=store_scratch,
        input_output_aliases={8: 0},
        compiler_params=params,
    )(turned, own, two, state, summed, stats, gains, read, out)


def carried_in(part, axis, combine, identity):
    place = lax.axis_index(axis)
    gathered = jax.tree.map(lambda a: lax.all_gather(a, axis), part)
    state = jax.tree.map(lambda a, e: jnp.zeros_like(a) + jnp.asarray(e, a.dtype), part, identity)

    def one(step, state):
        return combine(
            state, jax.tree.map(lambda a: lax.dynamic_index_in_dim(a, step, 0, False), gathered)
        )

    return lax.fori_loop(0, place, one, state)


def join_states(earlier, later):
    state_early, first_early, last_early = earlier
    state_late, first_late, last_late = later
    empty_late = first_late < 0
    joined = (first_late == last_late) & (last_early == first_late)
    merged = state_late + jnp.where(joined, state_early, jnp.zeros_like(state_early))
    combined = jnp.where(empty_late, state_early, merged)
    first_doc = jnp.where(first_early < 0, first_late, first_early)
    last_doc = jnp.where(empty_late, last_early, last_late)
    return (combined, first_doc, last_doc)


def tail_merge(one_side, other_side):
    state_one, first_one, last_one = one_side
    state_other, first_other, last_other = other_side
    top_doc = jnp.maximum(last_one, last_other)
    state_sum = jnp.where(last_one == top_doc, state_one, jnp.zeros_like(state_one))
    state_sum = state_sum + jnp.where(
        last_other == top_doc, state_other, jnp.zeros_like(state_other)
    )
    return (state_sum, jnp.minimum(first_one, first_other), top_doc)


def tail_state(key_rows, value_rows, doc_rows, target_doc):
    count = key_rows.shape[0]
    key_heads = key_rows.reshape(count, KV_HEADS, HEAD_DIM)
    value_heads = value_rows.reshape(count, KV_HEADS, HEAD_DIM)
    live = doc_rows == target_doc
    masked = jnp.where(live[:, None, None], key_heads, jnp.zeros_like(key_heads))
    return jnp.einsum("rgd,rge->gde", masked, value_heads, preferred_element_type=jnp.float32)


def attend_block(
    carry, query_heads, query_pos, query_doc, key_rows, value_rows, key_doc, key_start
):
    running_max, running_sum, accumulated = carry
    key_count = key_rows.shape[0]
    key_heads = key_rows.reshape(key_count, KV_HEADS, HEAD_DIM)
    value_heads = value_rows.reshape(key_count, KV_HEADS, HEAD_DIM)
    scores = jnp.einsum(
        "rgqd,kgd->gqrk", query_heads, key_heads, preferred_element_type=jnp.float32
    )
    scores = scores / jnp.sqrt(jnp.float32(HEAD_DIM))
    key_pos = key_start + jnp.arange(key_count, dtype=jnp.int32)
    allowed = (key_pos[None, :] <= query_pos[:, None]) & (key_doc[None, :] == query_doc[:, None])
    masked = jnp.where(allowed, scores, jnp.float32(-1e30))
    new_max = jnp.maximum(running_max, jnp.max(masked, axis=-1))
    factor = jnp.exp(running_max - new_max)
    weights = jnp.where(allowed, jnp.exp(masked - new_max[..., None]), jnp.float32(0.0))
    new_sum = running_sum * factor + jnp.sum(weights, axis=-1)
    product = jnp.einsum(
        "gqrk,kge->gqre",
        weights.astype(jnp.bfloat16),
        value_heads,
        preferred_element_type=jnp.float32,
    )
    new_accum = accumulated * factor[..., None] + product
    return (new_max, new_sum, new_accum)


def far_device(queries, keys, values, doc_ids, beta, lin_gain):
    row_count = queries.shape[0]
    groups = HEADS // KV_HEADS
    query_heads = queries.reshape(row_count, KV_HEADS, groups, HEAD_DIM)
    position = lax.axis_index("kv") * row_count
    query_pos = position + jnp.arange(row_count, dtype=jnp.int32)
    last_query = position + row_count - 1
    initial = (
        jnp.full((KV_HEADS, groups, row_count), -1e30, jnp.float32),
        jnp.zeros((KV_HEADS, groups, row_count), jnp.float32),
        jnp.zeros((KV_HEADS, groups, row_count, HEAD_DIM), jnp.float32),
    )
    empty_tail = (
        jnp.zeros((KV_HEADS, HEAD_DIM, HEAD_DIM), jnp.float32),
        jnp.array(2**30, jnp.int32),
        jnp.array(-1, jnp.int32),
    )
    key_piece = lax.all_gather(keys, "kv", axis=0, tiled=True)
    value_piece = lax.all_gather(values, "kv", axis=0, tiled=True)
    doc_piece = lax.all_gather(doc_ids, "kv", axis=0, tiled=True)
    blocks = key_piece.shape[0] // row_count

    def one_block(state, item):
        soft_state, tail_now = state
        key_block, value_block, doc_block, number = item
        block_start = number * row_count
        soft_next = lax.cond(
            block_start <= last_query,
            lambda inner: attend_block(
                inner,
                query_heads,
                query_pos,
                doc_ids,
                key_block,
                value_block,
                doc_block,
                block_start,
            ),
            lambda inner: inner,
            soft_state,
        )
        block_tail = (
            tail_state(key_block, value_block, doc_block, doc_block[-1]),
            doc_block[0],
            doc_block[-1],
        )
        tail_now = tail_merge(tail_now, block_tail)
        return ((soft_next, tail_now), None)

    stacked = (
        key_piece.reshape(blocks, row_count, -1),
        value_piece.reshape(blocks, row_count, -1),
        doc_piece.reshape(blocks, row_count),
        jnp.arange(blocks, dtype=jnp.int32),
    )
    result, _ = lax.scan(one_block, (initial, empty_tail), stacked)
    running, segment_tail = result
    running_max, running_sum, accumulated = running
    soft_out = jnp.transpose(accumulated / running_sum[..., None], (2, 0, 1, 3))
    identity = (
        jnp.zeros((KV_HEADS, HEAD_DIM, HEAD_DIM), jnp.float32),
        jnp.array(-1, jnp.int32),
        jnp.array(-1, jnp.int32),
    )
    memory = carried_in(segment_tail, "seq", join_states, identity)
    memory_state, memory_first, memory_last = memory
    query_float = query_heads.astype(jnp.float32)
    recalled = jnp.einsum(
        "rgqd,gde->rgqe", query_float, memory_state, precision=lax.Precision.HIGHEST
    )
    recalled = jnp.where((doc_ids == memory_last)[:, None, None, None], recalled, jnp.float32(0.0))
    mean_square = jnp.mean(recalled * recalled, axis=-1, keepdims=True)
    normed = (
        recalled * lax.rsqrt(mean_square + 1e-06) * lin_gain.reshape(KV_HEADS, groups, HEAD_DIM)
    )
    mixing = jax.nn.sigmoid(beta).reshape(KV_HEADS, groups)[None, :, :, None]
    mixed = mixing * normed + (1.0 - mixing) * soft_out
    return mixed.reshape(row_count, HEADS * HEAD_DIM).astype(jnp.float32)


def solution(mesh):
    n_seq, n_kv = mesh.shape["seq"], mesh.shape["kv"]
    in_specs = (
        P(("dp", "seq", "kv"), None),
        P(("dp", "seq", "kv"), None),
        P(("dp", "seq", "kv"), None),
        P(("dp", "seq", "kv")),
        P(),
        P(),
    )
    out_specs = P(("dp", "seq", "kv"), None)
    if n_kv == 2 and n_seq * n_kv <= 2 * LONGEST:
        on_device = functools.partial(near_device, n_seq)
    else:
        on_device = far_device
    return jax.shard_map(
        on_device, mesh=mesh, in_specs=in_specs, out_specs=out_specs, check_vma=False
    )
```

```python
import functools
import math

import jax
import jax.numpy as jnp
from jax import lax
from jax.experimental import pallas as pl
from jax.experimental.pallas import tpu as pltpu
from jax.sharding import PartitionSpec as P

HEADS = 16
KV_HEADS = 4
HEAD_DIM = 128
GROUPS = HEADS // KV_HEADS
LONGEST = 4
SCALE = math.log2(math.e) / math.sqrt(HEAD_DIM)
LOWEST = -1e30
EXTRA = 16

NT = (((1,), (1,)), ((), ()))
TN = (((0,), (0,)), ((), ()))
NN = (((1,), (0,)), ((), ()))


def dot(a, b, dims):
    return lax.dot_general(a, b, dims, preferred_element_type=jnp.float32)


def column(row):
    return jnp.transpose(jnp.broadcast_to(row, (HEAD_DIM, row.shape[1])))


def part_of(i, size):
    return slice(i * size, (i + 1) * size)


def group_queries(q_ref, g):
    heads = [q_ref[:, part_of(g * GROUPS + i, HEAD_DIM)] for i in range(GROUPS)]
    return jnp.concatenate(heads, axis=0)


def share_of(beta_ref, h):
    return 1.0 / (1.0 + jnp.exp(-jnp.full((1, HEAD_DIM), beta_ref[h], jnp.float32)))


def scaled_gains(beta_ref, gain_ref, out_ref):
    for h in range(HEADS):
        scaled = gain_ref[h : h + 1, :] * share_of(beta_ref, h)
        out_ref[part_of(h, HEAD_DIM), :] = column(scaled)


def suffix(others, least=0.0):
    count = jnp.maximum(jnp.sum(others, axis=1, keepdims=True), least)
    shape = (others.shape[1], HEAD_DIM)
    return lax.broadcasted_iota(jnp.int32, shape, 0).astype(jnp.float32) >= count


def first_document(docs):
    first = jnp.broadcast_to(docs[:, 0:1], docs.shape)
    return first, docs == first


def load_block(key_ref, value_ref, doc_ref, out_ref, doc_scratch, sems):
    rows = key_ref.shape[0]
    doc_copy = pltpu.make_async_copy(doc_ref, doc_scratch, sems.at[0])
    doc_copy.start()
    copies = []
    for g in range(2 * KV_HEADS):
        source = key_ref if g < KV_HEADS else value_ref
        copy = pltpu.make_async_copy(
            source.at[:, part_of(g % KV_HEADS, HEAD_DIM)],
            out_ref.at[part_of(g, rows), :],
            sems.at[1 + g],
        )
        copy.start()
        copies.append(copy)
    doc_copy.wait()
    start = 2 * KV_HEADS * rows
    docs = doc_scratch[...].astype(jnp.float32)
    docs = jnp.broadcast_to(docs, (out_ref.shape[0] - start, rows))
    out_ref[start:, :] = docs.astype(jnp.bfloat16)
    for copy in copies:
        copy.wait()


def block_keys(ref, g):
    return ref[part_of(g, HEAD_DIM), :]


def block_values(ref, g):
    return ref[part_of(KV_HEADS + g, HEAD_DIM), :]


def block_docs(ref):
    start = 2 * KV_HEADS * HEAD_DIM
    return ref[start : start + EXTRA, :].astype(jnp.float32)[0:1, :]


class Plan:
    def __init__(self, n_seq):
        devices = 2 * n_seq
        near = [(b, b + 1) for b in range(devices - 1)]
        far = [(b, b + 2) for b in range(devices - 2)]
        crossing = [p for p in far if p[0] // 2 % 2 == 1]
        touched = {b for p in crossing for b in p}
        targets = {p[1] for p in crossing}
        first = [p for p in crossing if p[0] % 2 == 0]
        first += [p for p in near if p[0] not in touched and p[1] not in targets]
        after = [p for p in near if p not in first]
        third = [p for p in crossing if p[0] % 2 == 1]
        third += [p for p in after if p[0] in targets and p[0] % 2 == 1]
        second = [p for p in after if p not in third]
        last = [p for p in far if p not in first + third]
        self.pairs = [first, second, third, last]
        self.senders = sorted({p[0] for p in first})
        busy = {b for p in second + third for b in p}
        self.early = [b for b in range(devices) if b not in busy]
        self.late = sorted({p[1] for p in second + third})
        self.latest = sorted({p[1] for p in third})
        received = {p[1] for pairs in self.pairs for p in pairs}
        self.alone = [b for b in range(devices) if b not in received]
        self.memory_third = [p[1] for p in crossing if p[1] % 2 == 1]


def among(members):
    block = 2 * lax.axis_index("seq") + lax.axis_index("kv")
    return functools.reduce(jnp.logical_or, [block == b for b in members])


def pack_kernel(plan, key_ref, value_ref, doc_ref, out_ref, doc_scratch, sems):
    @pl.when(among(plan.senders))
    def _():
        load_block(key_ref, value_ref, doc_ref, out_ref, doc_scratch, sems)


def attend_own(q_ref, block_ref, g, bias):
    rows = q_ref.shape[0]
    scores = dot(block_keys(block_ref, g), group_queries(q_ref, g), NT)
    tops, totals, weights = [], [], []
    for i in range(GROUPS):
        masked = scores[:, part_of(i, rows)] * SCALE + bias
        top = jnp.max(masked, axis=0, keepdims=True)
        weight = jnp.exp2(masked - top)
        tops.append(top)
        totals.append(jnp.sum(weight, axis=0, keepdims=True))
        weights.append(weight.astype(jnp.bfloat16))
    summed = dot(block_values(block_ref, g), jnp.concatenate(weights, axis=1), TN)
    return summed, jnp.concatenate(tops, axis=1), jnp.concatenate(totals, axis=1)


def own_bias(docs):
    rows = docs.shape[1]
    place = lax.broadcasted_iota(jnp.int32, (rows, rows), 0)
    row = lax.broadcasted_iota(jnp.int32, (rows, rows), 1)
    return jnp.where((place <= row) & (column(docs) == docs), 0.0, LOWEST)


def attend_itself(
    q_ref, block_ref, gain_ref, beta_ref, beta_copy, summed_ref, stats_ref, gains_ref
):
    bias = own_bias(block_docs(block_ref))
    results = [attend_own(q_ref, block_ref, g, bias) for g in range(KV_HEADS)]
    beta_copy.wait()
    scaled_gains(beta_ref, gain_ref, gains_ref)
    done = lax.axis_index("kv") == 0
    for g, (summed, top, total) in enumerate(results):
        rest = [1.0 - share_of(beta_ref, g * GROUPS + i) for i in range(GROUPS)]
        rest = jnp.concatenate(rest, axis=1)
        summed_ref[part_of(g, HEAD_DIM), :] = summed * jnp.where(done, rest / total, 1.0)
        stats_ref[g : g + 1, :] = top
        stats_ref[KV_HEADS + g : KV_HEADS + g + 1, :] = total
        stats_ref[2 * KV_HEADS + g : 2 * KV_HEADS + g + 1, :] = rest


def settle_kernel(
    plan, gain_ref, packed_ref, key_ref, value_ref, doc_ref, query_ref, beta_ref,
    own_ref, short_ref, summed_ref, stats_ref, gains_ref,
    q_scratch, beta_scratch, early_sems,
):
    sender, early = among(plan.senders), among(plan.early)
    query_copy = pltpu.make_async_copy(query_ref, q_scratch, early_sems.at[0])
    beta_copy = pltpu.make_async_copy(beta_ref, beta_scratch, early_sems.at[1])

    @pl.when(early)
    def _():
        query_copy.start()
        beta_copy.start()

    @pl.when(sender)
    def _():
        own_ref[...] = packed_ref[...]

    @pl.when(jnp.logical_not(sender))
    def _():
        for g in range(KV_HEADS):
            cols = part_of(g, HEAD_DIM)
            own_ref[part_of(g, HEAD_DIM), :] = key_ref[:, cols]
            own_ref[part_of(KV_HEADS + g, HEAD_DIM), :] = value_ref[:, cols]
        start = 2 * KV_HEADS * HEAD_DIM
        docs = jnp.broadcast_to(doc_ref[...].astype(jnp.float32), (EXTRA, HEAD_DIM))
        own_ref[start:, :] = docs.astype(jnp.bfloat16)

    short_ref[...] = own_ref[0 : short_ref.shape[0], :]
    line = lax.broadcasted_iota(jnp.int32, (EXTRA, HEAD_DIM), 0)
    keys = own_ref[0:EXTRA, :].astype(jnp.float32)
    keys = jnp.where(line == 0, block_docs(own_ref), keys)
    short_ref[0:EXTRA, :] = keys.astype(jnp.bfloat16)

    @pl.when(early)
    def _():
        query_copy.wait()
        attend_itself(
            q_scratch, own_ref, gain_ref, beta_scratch, beta_copy,
            summed_ref, stats_ref, gains_ref,
        )


def own_kernel(
    plan, q_ref, gain_ref, own_ref, beta_ref, summed_in, stats_in, gains_in,
    summed_ref, stats_ref, gains_ref, out_ref, turned_ref, beta_scratch, sem, held, sems,
):
    rows = q_ref.shape[0]
    for g in range(KV_HEADS):
        for i in range(GROUPS):
            head = q_ref[:, part_of(g * GROUPS + i, HEAD_DIM)]
            turned_ref[part_of(g, HEAD_DIM), part_of(i, rows)] = jnp.transpose(head)

    @pl.when(among(plan.alone))
    def _():
        _, same = first_document(block_docs(own_ref))
        states = [jnp.zeros((HEAD_DIM, HEAD_DIM), jnp.float32)] * KV_HEADS
        read_and_store(states, turned_ref, gains_ref, same, summed_ref, out_ref, held, sems)

    @pl.when(jnp.logical_not(among(plan.early)))
    def _():
        beta_copy = pltpu.make_async_copy(beta_ref, beta_scratch, sem)
        beta_copy.start()
        attend_itself(
            q_ref, own_ref, gain_ref, beta_scratch, beta_copy, summed_ref, stats_ref, gains_ref
        )


def memory_states(refs, first):
    lives = []
    for ref in refs:
        short = ref.shape[0] == 2 * KV_HEADS * HEAD_DIM
        docs = ref[0:EXTRA, :].astype(jnp.float32)[0:1, :] if short else block_docs(ref)
        live = suffix(jnp.where(docs == first, 0.0, 1.0), 1.0 if short else 0.0)
        lives.append(jnp.where(live, 1.0, 0.0).astype(jnp.bfloat16))
    return [
        functools.reduce(
            jnp.add,
            [
                dot(block_values(ref, g), block_keys(ref, g) * live, TN)
                for ref, live in zip(refs, lives)
            ],
        )
        for g in range(KV_HEADS)
    ]


def read_memory(states, turned_ref, gains_ref, reads):
    rows = turned_ref.shape[1] // GROUPS
    pieces = []
    for state in states:
        high = state.astype(jnp.bfloat16)
        state = state - high.astype(jnp.float32)
        middle = state.astype(jnp.bfloat16)
        low = (state - middle.astype(jnp.float32)).astype(jnp.bfloat16)
        pieces.append(jnp.concatenate([high, middle, low], axis=0))
    products = [
        dot(pieces[g], turned_ref[part_of(g, HEAD_DIM), :], NN) for g in range(KV_HEADS)
    ]

    def read(g):
        recalled = products[g][part_of(0, HEAD_DIM), :] + (
            products[g][part_of(1, HEAD_DIM), :] + products[g][part_of(2, HEAD_DIM), :]
        )
        heads = []
        for i in range(GROUPS):
            head = recalled[:, part_of(i, rows)]
            square = jnp.sum(head * head, axis=0, keepdims=True) * (1.0 / HEAD_DIM)
            head = head * (lax.rsqrt(square + 1e-06) * reads)
            heads.append(head * gains_ref[part_of(g * GROUPS + i, HEAD_DIM), :])
        return heads

    return read


def attend_before(turned_ref, one_ref, stats_ref, summed_ref, first, same):
    rows = (turned_ref.shape[1] // GROUPS)
    live = suffix(jnp.where(block_docs(one_ref) == first, 0.0, 1.0))
    bias = jnp.where(live & same, 0.0, LOWEST)
    ahead = {}

    def score(g):
        if g < KV_HEADS and g not in ahead:
            ahead[g] = dot(block_keys(one_ref, g), turned_ref[part_of(g, HEAD_DIM), :], NN)

    def attend(g):
        for later in range(3):
            score(g + later)
        weights, factors, scales = [], [], []
        for i in range(GROUPS):
            cut = part_of(i, rows)
            masked = ahead[g][:, cut] * SCALE + bias
            top_own = stats_ref[g : g + 1, cut]
            top = jnp.maximum(jnp.max(masked, axis=0, keepdims=True), top_own)
            weight = jnp.exp2(masked - top)
            factor = jnp.exp2(top_own - top)
            total = stats_ref[KV_HEADS + g : KV_HEADS + g + 1, cut] * factor
            total = total + jnp.sum(weight, axis=0, keepdims=True)
            factors.append(factor)
            scales.append(stats_ref[2 * KV_HEADS + g : 2 * KV_HEADS + g + 1, cut] / total)
            weights.append(weight.astype(jnp.bfloat16))
        added = dot(block_values(one_ref, g), jnp.concatenate(weights, axis=1), TN)
        summed = summed_ref[part_of(g, HEAD_DIM), :] * jnp.concatenate(factors, axis=1) + added
        return summed * jnp.concatenate(scales, axis=1)

    return attend


def store_heads(mixed, out_ref, held, sems):
    copies = []
    ahead = mixed(0)
    for g in range(KV_HEADS):
        heads, ahead = ahead, mixed(g + 1) if g + 1 < KV_HEADS else None
        for i, head in enumerate(heads):
            held[:, part_of(g * GROUPS + i, HEAD_DIM)] = jnp.transpose(head)
        wide = part_of(g, GROUPS * HEAD_DIM)
        copies.append(pltpu.make_async_copy(held.at[:, wide], out_ref.at[:, wide], sems.at[g]))
        copies[g].start()
    for copy in copies:
        copy.wait()


def read_into(read_ref, refs, turned_ref, own_ref, gains_ref):
    first, same = first_document(block_docs(own_ref))
    read = read_memory(
        memory_states(refs, first), turned_ref, gains_ref, jnp.where(same, 1.0, 0.0)
    )
    for g in range(KV_HEADS):
        for i, head in enumerate(read(g)):
            read_ref[part_of(g * GROUPS + i, HEAD_DIM), :] = head


def read_kernel(plan, turned_ref, own_ref, three_ref, gains_ref, read_ref):
    @pl.when((lax.axis_index("kv") == 1) & jnp.logical_not(among(plan.memory_third)))
    def _():
        read_into(read_ref, [three_ref], turned_ref, own_ref, gains_ref)


def attend_and_store(
    turned_ref, own_ref, earlier_ref, stats_ref, summed_ref, read_ref, out_ref, held, sems
):
    first, same = first_document(block_docs(own_ref))
    attend = attend_before(turned_ref, earlier_ref, stats_ref, summed_ref, first, same)
    rows = (turned_ref.shape[1] // GROUPS)

    def mixed(g):
        attended = attend(g)
        return [
            read_ref[part_of(g * GROUPS + i, HEAD_DIM), :] + attended[:, part_of(i, rows)]
            for i in range(GROUPS)
        ]

    store_heads(mixed, out_ref, held, sems)


def read_and_store(states, turned_ref, gains_ref, same, summed_ref, out_ref, held, sems):
    rows = (turned_ref.shape[1] // GROUPS)
    read = read_memory(states, turned_ref, gains_ref, jnp.where(same, 1.0, 0.0))

    def mixed(g):
        return [
            head + summed_ref[part_of(g, HEAD_DIM), part_of(i, rows)]
            for i, head in enumerate(read(g))
        ]

    store_heads(mixed, out_ref, held, sems)


def early_kernel(
    plan, turned_ref, own_ref, one_ref, three_ref, stats_ref, gains_ref, summed_ref, read_in, out_in,
    read_ref, state_ref, out_ref, held, sems,
):
    kv = lax.axis_index("kv")
    late = among(plan.late)

    @pl.when((kv == 0) & jnp.logical_not(late | among(plan.alone)))
    def _():
        first, same = first_document(block_docs(own_ref))
        states = memory_states([one_ref, three_ref], first)
        read_and_store(states, turned_ref, gains_ref, same, summed_ref, out_ref, held, sems)

    @pl.when((kv == 1) & jnp.logical_not(late))
    def _():
        attend_and_store(
            turned_ref, own_ref, one_ref, stats_ref, summed_ref, read_ref, out_ref, held, sems
        )

    @pl.when((kv == 0) & late)
    def _():
        first, _ = first_document(block_docs(own_ref))
        for g, state in enumerate(memory_states([one_ref, three_ref], first)):
            state_ref[part_of(g, HEAD_DIM), :] = state


def late_kernel(
    plan, turned_ref, own_ref, two_ref, state_ref, stats_ref, gains_ref, read_ref, summed_in,
    out_in, summed_ref, out_ref, held, sems,
):
    kv = lax.axis_index("kv")
    latest = among(plan.latest)
    late = among(plan.late) & jnp.logical_not(latest)

    @pl.when((kv == 1) & late)
    def _():
        attend_and_store(
            turned_ref, own_ref, two_ref, stats_ref, summed_ref, read_ref, out_ref, held, sems
        )

    @pl.when((kv == 0) & late)
    def _():
        first, same = first_document(block_docs(own_ref))
        added = memory_states([two_ref], first)
        states = [state_ref[part_of(g, HEAD_DIM), :] + added[g] for g in range(KV_HEADS)]
        read_and_store(states, turned_ref, gains_ref, same, summed_ref, out_ref, held, sems)

    @pl.when((kv == 1) & latest)
    def _():
        first, same = first_document(block_docs(own_ref))
        attend = attend_before(turned_ref, two_ref, stats_ref, summed_ref, first, same)
        for g in range(KV_HEADS):
            summed_ref[part_of(g, HEAD_DIM), :] = attend(g)


def latest_kernel(
    plan, turned_ref, own_ref, three_ref, state_ref, gains_ref, summed_ref, out_in,
    out_ref, held, sems,
):
    latest = among(plan.latest)
    kv = lax.axis_index("kv")

    @pl.when((kv == 1) & latest)
    def _():
        first, same = first_document(block_docs(own_ref))
        states = memory_states([three_ref], first)
        read_and_store(states, turned_ref, gains_ref, same, summed_ref, out_ref, held, sems)

    @pl.when((kv == 0) & latest)
    def _():
        first, same = first_document(block_docs(own_ref))
        added = memory_states([three_ref], first)
        states = [state_ref[part_of(g, HEAD_DIM), :] + added[g] for g in range(KV_HEADS)]
        read_and_store(states, turned_ref, gains_ref, same, summed_ref, out_ref, held, sems)


def near_device(n_seq, queries, keys, values, doc_ids, beta, lin_gain):
    rows = queries.shape[0]
    vmem = pl.BlockSpec(memory_space=pltpu.VMEM)
    hbm = pl.BlockSpec(memory_space=pltpu.HBM)
    in_hbm = functools.partial(pltpu.with_memory_space_constraint, memory_space=pltpu.HBM)
    params = pltpu.CompilerParams(vmem_limit_bytes=32 * 1024 * 1024)
    wide = GROUPS * rows
    group_shape = jax.ShapeDtypeStruct((KV_HEADS * HEAD_DIM, wide), jnp.float32)
    gains_shape = jax.ShapeDtypeStruct((HEADS * HEAD_DIM, HEAD_DIM), jnp.float32)
    docs = doc_ids.reshape(1, rows)
    gain = lin_gain.reshape(HEADS, HEAD_DIM)
    deep = 2 * KV_HEADS * rows + EXTRA

    def estimate(share):
        return pl.CostEstimate(
            flops=int(share * 4 * HEADS * HEAD_DIM * rows * rows),
            bytes_accessed=int(share * 4 * 1024 * 1024),
            transcendentals=int(share * HEADS * rows * rows),
        )

    def send(payload, pairs):
        return lax.ppermute(payload, ("seq", "kv"), pairs)

    plan = Plan(n_seq)
    block_shape = jax.ShapeDtypeStruct((deep, HEAD_DIM), jnp.bfloat16)
    short_shape = jax.ShapeDtypeStruct((deep - EXTRA, HEAD_DIM), jnp.bfloat16)
    stats_shape = jax.ShapeDtypeStruct((4 * KV_HEADS, wide), jnp.float32)
    state_shape = jax.ShapeDtypeStruct((KV_HEADS * HEAD_DIM, HEAD_DIM), jnp.float32)
    results = [group_shape, stats_shape, gains_shape]
    doc_scratch = pltpu.VMEM((1, rows), jnp.int32)
    beta_scratch = pltpu.SMEM((HEADS,), jnp.float32)
    sems = pltpu.SemaphoreType.DMA((2 * KV_HEADS + 1,))
    block = (in_hbm(keys), in_hbm(values), in_hbm(docs))
    beta = in_hbm(beta)
    packed = pl.pallas_call(
        functools.partial(pack_kernel, plan),
        out_shape=block_shape,
        in_specs=[hbm] * 3,
        out_specs=vmem,
        scratch_shapes=[doc_scratch, sems],
        compiler_params=params,
        cost_estimate=estimate(0.1),
    )(*block)
    one = send(packed, plan.pairs[0])
    own, short, summed, stats, gains = pl.pallas_call(
        functools.partial(settle_kernel, plan),
        out_shape=[block_shape, short_shape] + results,
        in_specs=[vmem] * 5 + [hbm] * 2,
        out_specs=[vmem] * 5,
        scratch_shapes=[
            pltpu.VMEM(queries.shape, queries.dtype),
            beta_scratch,
            pltpu.SemaphoreType.DMA((2,)),
        ],
        compiler_params=params,
        cost_estimate=estimate(1.0),
    )(gain, packed, keys, values, docs, in_hbm(queries), beta)
    two = send(own, plan.pairs[1])
    three = send(own, plan.pairs[2])
    four = send(short, plan.pairs[3])
    out_shape = jax.ShapeDtypeStruct((rows, HEADS * HEAD_DIM), jnp.float32)
    store_scratch = [
        pltpu.VMEM((rows, HEADS * HEAD_DIM), jnp.float32),
        pltpu.SemaphoreType.DMA((KV_HEADS,)),
    ]
    turned_shape = jax.ShapeDtypeStruct((KV_HEADS * HEAD_DIM, wide), queries.dtype)
    summed, stats, gains, out, turned = pl.pallas_call(
        functools.partial(own_kernel, plan),
        out_shape=results + [out_shape, turned_shape],
        in_specs=[vmem] * 3 + [hbm] + [vmem] * 3,
        out_specs=[vmem] * 3 + [hbm, vmem],
        scratch_shapes=[beta_scratch, pltpu.SemaphoreType.DMA] + store_scratch,
        input_output_aliases={4: 0, 5: 1, 6: 2},
        compiler_params=params,
        cost_estimate=estimate(1.0),
    )(queries, gain, own, beta, summed, stats, gains)
    read = pl.pallas_call(
        functools.partial(read_kernel, plan),
        out_shape=gains_shape,
        in_specs=[vmem] * 4,
        out_specs=vmem,
        compiler_params=params,
    )(turned, own, four, gains)
    read, state, out = pl.pallas_call(
        functools.partial(early_kernel, plan),
        out_shape=[gains_shape, state_shape, out_shape],
        in_specs=[vmem] * 8 + [hbm],
        out_specs=[vmem] * 2 + [hbm],
        scratch_shapes=store_scratch,
        input_output_aliases={7: 0, 8: 2},
        compiler_params=params,
    )(turned, own, one, four, stats, gains, summed, read, out)
    summed, out = pl.pallas_call(
        functools.partial(late_kernel, plan),
        out_shape=[group_shape, out_shape],
        in_specs=[vmem] * 8 + [hbm],
        out_specs=[vmem, hbm],
        scratch_shapes=store_scratch,
        input_output_aliases={7: 0, 8: 1},
        compiler_params=params,
    )(turned, own, two, state, stats, gains, read, summed, out)
    return pl.pallas_call(
        functools.partial(latest_kernel, plan),
        out_shape=out_shape,
        in_specs=[vmem] * 6 + [hbm],
        out_specs=hbm,
        scratch_shapes=store_scratch,
        input_output_aliases={6: 0},
        compiler_params=params,
    )(turned, own, three, state, gains, summed, out)


def carried_in(part, axis, combine, identity):
    place = lax.axis_index(axis)
    gathered = jax.tree.map(lambda a: lax.all_gather(a, axis), part)
    state = jax.tree.map(lambda a, e: jnp.zeros_like(a) + jnp.asarray(e, a.dtype), part, identity)

    def one(step, state):
        return combine(
            state, jax.tree.map(lambda a: lax.dynamic_index_in_dim(a, step, 0, False), gathered)
        )

    return lax.fori_loop(0, place, one, state)


def join_states(earlier, later):
    state_early, first_early, last_early = earlier
    state_late, first_late, last_late = later
    empty_late = first_late < 0
    joined = (first_late == last_late) & (last_early == first_late)
    merged = state_late + jnp.where(joined, state_early, jnp.zeros_like(state_early))
    combined = jnp.where(empty_late, state_early, merged)
    first_doc = jnp.where(first_early < 0, first_late, first_early)
    last_doc = jnp.where(empty_late, last_early, last_late)
    return (combined, first_doc, last_doc)


def tail_merge(one_side, other_side):
    state_one, first_one, last_one = one_side
    state_other, first_other, last_other = other_side
    top_doc = jnp.maximum(last_one, last_other)
    state_sum = jnp.where(last_one == top_doc, state_one, jnp.zeros_like(state_one))
    state_sum = state_sum + jnp.where(
        last_other == top_doc, state_other, jnp.zeros_like(state_other)
    )
    return (state_sum, jnp.minimum(first_one, first_other), top_doc)


def tail_state(key_rows, value_rows, doc_rows, target_doc):
    count = key_rows.shape[0]
    key_heads = key_rows.reshape(count, KV_HEADS, HEAD_DIM)
    value_heads = value_rows.reshape(count, KV_HEADS, HEAD_DIM)
    live = doc_rows == target_doc
    masked = jnp.where(live[:, None, None], key_heads, jnp.zeros_like(key_heads))
    return jnp.einsum("rgd,rge->gde", masked, value_heads, preferred_element_type=jnp.float32)


def attend_block(
    carry, query_heads, query_pos, query_doc, key_rows, value_rows, key_doc, key_start
):
    running_max, running_sum, accumulated = carry
    key_count = key_rows.shape[0]
    key_heads = key_rows.reshape(key_count, KV_HEADS, HEAD_DIM)
    value_heads = value_rows.reshape(key_count, KV_HEADS, HEAD_DIM)
    scores = jnp.einsum(
        "rgqd,kgd->gqrk", query_heads, key_heads, preferred_element_type=jnp.float32
    )
    scores = scores / jnp.sqrt(jnp.float32(HEAD_DIM))
    key_pos = key_start + jnp.arange(key_count, dtype=jnp.int32)
    allowed = (key_pos[None, :] <= query_pos[:, None]) & (key_doc[None, :] == query_doc[:, None])
    masked = jnp.where(allowed, scores, jnp.float32(-1e30))
    new_max = jnp.maximum(running_max, jnp.max(masked, axis=-1))
    factor = jnp.exp(running_max - new_max)
    weights = jnp.where(allowed, jnp.exp(masked - new_max[..., None]), jnp.float32(0.0))
    new_sum = running_sum * factor + jnp.sum(weights, axis=-1)
    product = jnp.einsum(
        "gqrk,kge->gqre",
        weights.astype(jnp.bfloat16),
        value_heads,
        preferred_element_type=jnp.float32,
    )
    new_accum = accumulated * factor[..., None] + product
    return (new_max, new_sum, new_accum)


def far_device(queries, keys, values, doc_ids, beta, lin_gain):
    row_count = queries.shape[0]
    groups = HEADS // KV_HEADS
    query_heads = queries.reshape(row_count, KV_HEADS, groups, HEAD_DIM)
    position = lax.axis_index("kv") * row_count
    query_pos = position + jnp.arange(row_count, dtype=jnp.int32)
    last_query = position + row_count - 1
    initial = (
        jnp.full((KV_HEADS, groups, row_count), -1e30, jnp.float32),
        jnp.zeros((KV_HEADS, groups, row_count), jnp.float32),
        jnp.zeros((KV_HEADS, groups, row_count, HEAD_DIM), jnp.float32),
    )
    empty_tail = (
        jnp.zeros((KV_HEADS, HEAD_DIM, HEAD_DIM), jnp.float32),
        jnp.array(2**30, jnp.int32),
        jnp.array(-1, jnp.int32),
    )
    key_piece = lax.all_gather(keys, "kv", axis=0, tiled=True)
    value_piece = lax.all_gather(values, "kv", axis=0, tiled=True)
    doc_piece = lax.all_gather(doc_ids, "kv", axis=0, tiled=True)
    blocks = key_piece.shape[0] // row_count

    def one_block(state, item):
        soft_state, tail_now = state
        key_block, value_block, doc_block, number = item
        block_start = number * row_count
        soft_next = lax.cond(
            block_start <= last_query,
            lambda inner: attend_block(
                inner,
                query_heads,
                query_pos,
                doc_ids,
                key_block,
                value_block,
                doc_block,
                block_start,
            ),
            lambda inner: inner,
            soft_state,
        )
        block_tail = (
            tail_state(key_block, value_block, doc_block, doc_block[-1]),
            doc_block[0],
            doc_block[-1],
        )
        tail_now = tail_merge(tail_now, block_tail)
        return ((soft_next, tail_now), None)

    stacked = (
        key_piece.reshape(blocks, row_count, -1),
        value_piece.reshape(blocks, row_count, -1),
        doc_piece.reshape(blocks, row_count),
        jnp.arange(blocks, dtype=jnp.int32),
    )
    result, _ = lax.scan(one_block, (initial, empty_tail), stacked)
    running, segment_tail = result
    running_max, running_sum, accumulated = running
    soft_out = jnp.transpose(accumulated / running_sum[..., None], (2, 0, 1, 3))
    identity = (
        jnp.zeros((KV_HEADS, HEAD_DIM, HEAD_DIM), jnp.float32),
        jnp.array(-1, jnp.int32),
        jnp.array(-1, jnp.int32),
    )
    memory = carried_in(segment_tail, "seq", join_states, identity)
    memory_state, memory_first, memory_last = memory
    query_float = query_heads.astype(jnp.float32)
    recalled = jnp.einsum(
        "rgqd,gde->rgqe", query_float, memory_state, precision=lax.Precision.HIGHEST
    )
    recalled = jnp.where((doc_ids == memory_last)[:, None, None, None], recalled, jnp.float32(0.0))
    mean_square = jnp.mean(recalled * recalled, axis=-1, keepdims=True)
    normed = (
        recalled * lax.rsqrt(mean_square + 1e-06) * lin_gain.reshape(KV_HEADS, groups, HEAD_DIM)
    )
    mixing = jax.nn.sigmoid(beta).reshape(KV_HEADS, groups)[None, :, :, None]
    mixed = mixing * normed + (1.0 - mixing) * soft_out
    return mixed.reshape(row_count, HEADS * HEAD_DIM).astype(jnp.float32)


def solution(mesh):
    n_seq, n_kv = mesh.shape["seq"], mesh.shape["kv"]
    in_specs = (
        P(("dp", "seq", "kv"), None),
        P(("dp", "seq", "kv"), None),
        P(("dp", "seq", "kv"), None),
        P(("dp", "seq", "kv")),
        P(),
        P(),
    )
    out_specs = P(("dp", "seq", "kv"), None)
    if n_kv == 2 and n_seq * n_kv <= 2 * LONGEST:
        on_device = functools.partial(near_device, n_seq)
    else:
        on_device = far_device
    return jax.shard_map(
        on_device, mesh=mesh, in_specs=in_specs, out_specs=out_specs, check_vma=False
    )
```

```python
import functools
import math

import jax
import jax.numpy as jnp
from jax import lax
from jax.experimental import pallas as pl
from jax.experimental.pallas import tpu as pltpu
from jax.sharding import PartitionSpec as P

HEADS = 16
KV_HEADS = 4
HEAD_DIM = 128
GROUPS = HEADS // KV_HEADS
LONGEST = 4
SCALE = math.log2(math.e) / math.sqrt(HEAD_DIM)
LOWEST = -1e30
EXTRA = 16

NT = (((1,), (1,)), ((), ()))
TN = (((0,), (0,)), ((), ()))
NN = (((1,), (0,)), ((), ()))


def dot(a, b, dims):
    return lax.dot_general(a, b, dims, preferred_element_type=jnp.float32)


def column(row):
    return jnp.transpose(jnp.broadcast_to(row, (HEAD_DIM, row.shape[1])))


def part_of(i, size):
    return slice(i * size, (i + 1) * size)


def group_queries(q_ref, g):
    heads = [q_ref[:, part_of(g * GROUPS + i, HEAD_DIM)] for i in range(GROUPS)]
    return jnp.concatenate(heads, axis=0)


def share_of(beta_ref, h):
    return 1.0 / (1.0 + jnp.exp(-jnp.full((1, HEAD_DIM), beta_ref[h], jnp.float32)))


def scaled_gains(beta_ref, gain_ref, out_ref):
    for h in range(HEADS):
        scaled = gain_ref[h : h + 1, :] * share_of(beta_ref, h)
        out_ref[part_of(h, HEAD_DIM), :] = column(scaled)


def suffix(others, least=0.0):
    count = jnp.maximum(jnp.sum(others, axis=1, keepdims=True), least)
    shape = (others.shape[1], HEAD_DIM)
    return lax.broadcasted_iota(jnp.int32, shape, 0).astype(jnp.float32) >= count


def first_document(docs):
    first = jnp.broadcast_to(docs[:, 0:1], docs.shape)
    return first, docs == first


def spread_heads(key_rows, value_rows, doc_row, out_ref):
    for g in range(KV_HEADS):
        out_ref[part_of(g, HEAD_DIM), :] = key_rows[:, part_of(g, HEAD_DIM)]
    for g in range(KV_HEADS):
        out_ref[part_of(KV_HEADS + g, HEAD_DIM), :] = value_rows[:, part_of(g, HEAD_DIM)]
    docs = jnp.broadcast_to(doc_row[...].astype(jnp.float32), (EXTRA, HEAD_DIM))
    out_ref[2 * KV_HEADS * HEAD_DIM :, :] = docs.astype(jnp.bfloat16)


def block_keys(ref, g):
    return ref[part_of(g, HEAD_DIM), :]


def block_values(ref, g):
    return ref[part_of(KV_HEADS + g, HEAD_DIM), :]


def block_docs(ref):
    start = 2 * KV_HEADS * HEAD_DIM
    return ref[start : start + EXTRA, :].astype(jnp.float32)[0:1, :]


class Plan:
    def __init__(self, n_seq):
        devices = 2 * n_seq
        near = [(b, b + 1) for b in range(devices - 1)]
        far = [(b, b + 2) for b in range(devices - 2)]
        crossing = [p for p in far if p[0] // 2 % 2 == 1]
        touched = {b for p in crossing for b in p}
        targets = {p[1] for p in crossing}
        first = crossing + [p for p in near if p[0] not in touched and p[1] not in targets]
        second = [p for p in near if p not in first]
        last = [p for p in far if p not in first]
        self.pairs = [first, second, last]
        self.senders = sorted({p[0] for p in first})
        busy = {b for p in first for b in p} & {b for p in second for b in p}
        self.early = [b for b in range(devices) if b not in busy]
        self.late = sorted({p[1] for p in second})
        received = {p[1] for pairs in self.pairs for p in pairs}
        self.alone = [b for b in range(devices) if b not in received]
        self.memory_first = [p[1] for p in crossing if p[1] % 2 == 1]


def among(members):
    block = 2 * lax.axis_index("seq") + lax.axis_index("kv")
    return functools.reduce(jnp.logical_or, [block == b for b in members])


def pack_kernel(
    plan, key_ref, value_ref, doc_ref, out_ref, key_scratch, value_scratch, doc_scratch, sems
):
    @pl.when(among(plan.senders))
    def _():
        pairs = ((key_ref, key_scratch), (value_ref, value_scratch), (doc_ref, doc_scratch))
        copies = [pltpu.make_async_copy(a, b, sems.at[i]) for i, (a, b) in enumerate(pairs)]
        for copy in copies:
            copy.start()
        for copy in copies:
            copy.wait()
        spread_heads(key_scratch, value_scratch, doc_scratch, out_ref)


def attend_own(q_ref, block_ref, g, bias):
    rows = q_ref.shape[0]
    scores = dot(block_keys(block_ref, g), group_queries(q_ref, g), NT)
    tops, totals, weights = [], [], []
    for i in range(GROUPS):
        masked = scores[:, part_of(i, rows)] * SCALE + bias
        top = jnp.max(masked, axis=0, keepdims=True)
        weight = jnp.exp2(masked - top)
        tops.append(top)
        totals.append(jnp.sum(weight, axis=0, keepdims=True))
        weights.append(weight.astype(jnp.bfloat16))
    summed = dot(block_values(block_ref, g), jnp.concatenate(weights, axis=1), TN)
    return summed, jnp.concatenate(tops, axis=1), jnp.concatenate(totals, axis=1)


def own_bias(docs):
    rows = docs.shape[1]
    place = lax.broadcasted_iota(jnp.int32, (rows, rows), 0)
    row = lax.broadcasted_iota(jnp.int32, (rows, rows), 1)
    return jnp.where((place <= row) & (column(docs) == docs), 0.0, LOWEST)


def attend_itself(
    q_ref, block_ref, gain_ref, beta_ref, beta_copy, summed_ref, stats_ref, gains_ref
):
    bias = own_bias(block_docs(block_ref))
    results = [attend_own(q_ref, block_ref, g, bias) for g in range(KV_HEADS)]
    beta_copy.wait()
    scaled_gains(beta_ref, gain_ref, gains_ref)
    done = lax.axis_index("kv") == 0
    for g, (summed, top, total) in enumerate(results):
        rest = [1.0 - share_of(beta_ref, g * GROUPS + i) for i in range(GROUPS)]
        rest = jnp.concatenate(rest, axis=1)
        summed_ref[part_of(g, HEAD_DIM), :] = summed * jnp.where(done, rest / total, 1.0)
        stats_ref[g : g + 1, :] = top
        stats_ref[KV_HEADS + g : KV_HEADS + g + 1, :] = total
        stats_ref[2 * KV_HEADS + g : 2 * KV_HEADS + g + 1, :] = rest


def settle_kernel(
    plan, gain_ref, packed_ref, key_ref, value_ref, doc_ref, query_ref, beta_ref,
    own_ref, short_ref, summed_ref, stats_ref, gains_ref,
    q_scratch, beta_scratch, early_sems,
):
    sender, early = among(plan.senders), among(plan.early)
    query_copy = pltpu.make_async_copy(query_ref, q_scratch, early_sems.at[0])
    beta_copy = pltpu.make_async_copy(beta_ref, beta_scratch, early_sems.at[1])

    @pl.when(early)
    def _():
        query_copy.start()
        beta_copy.start()

    @pl.when(sender)
    def _():
        own_ref[...] = packed_ref[...]

    @pl.when(jnp.logical_not(sender))
    def _():
        spread_heads(key_ref, value_ref, doc_ref, own_ref)

    short_ref[...] = own_ref[0 : short_ref.shape[0], :]
    line = lax.broadcasted_iota(jnp.int32, (EXTRA, HEAD_DIM), 0)
    keys = own_ref[0:EXTRA, :].astype(jnp.float32)
    keys = jnp.where(line == 0, block_docs(own_ref), keys)
    short_ref[0:EXTRA, :] = keys.astype(jnp.bfloat16)

    @pl.when(early)
    def _():
        query_copy.wait()
        attend_itself(
            q_scratch, own_ref, gain_ref, beta_scratch, beta_copy,
            summed_ref, stats_ref, gains_ref,
        )


def own_kernel(
    plan, q_ref, gain_ref, own_ref, beta_ref, summed_in, stats_in, gains_in,
    summed_ref, stats_ref, gains_ref, out_ref, turned_ref, beta_scratch, sem, held, sems,
):
    rows = q_ref.shape[0]
    for g in range(KV_HEADS):
        for i in range(GROUPS):
            head = q_ref[:, part_of(g * GROUPS + i, HEAD_DIM)]
            turned_ref[part_of(g, HEAD_DIM), part_of(i, rows)] = jnp.transpose(head)

    @pl.when(among(plan.alone))
    def _():
        _, same = first_document(block_docs(own_ref))
        states = [jnp.zeros((HEAD_DIM, HEAD_DIM), jnp.float32)] * KV_HEADS
        read_and_store(states, turned_ref, gains_ref, same, summed_ref, out_ref, held, sems)

    @pl.when(jnp.logical_not(among(plan.early)))
    def _():
        beta_copy = pltpu.make_async_copy(beta_ref, beta_scratch, sem)
        beta_copy.start()
        attend_itself(
            q_ref, own_ref, gain_ref, beta_scratch, beta_copy, summed_ref, stats_ref, gains_ref
        )


def memory_states(refs, first):
    lives = []
    for ref in refs:
        short = ref.shape[0] == 2 * KV_HEADS * HEAD_DIM
        docs = ref[0:EXTRA, :].astype(jnp.float32)[0:1, :] if short else block_docs(ref)
        live = suffix(jnp.where(docs == first, 0.0, 1.0), 1.0 if short else 0.0)
        lives.append(jnp.where(live, 1.0, 0.0).astype(jnp.bfloat16))
    return [
        functools.reduce(
            jnp.add,
            [
                dot(block_values(ref, g), block_keys(ref, g) * live, TN)
                for ref, live in zip(refs, lives)
            ],
        )
        for g in range(KV_HEADS)
    ]


def read_memory(states, turned_ref, gains_ref, reads):
    rows = turned_ref.shape[1] // GROUPS
    pieces = []
    for state in states:
        high = state.astype(jnp.bfloat16)
        state = state - high.astype(jnp.float32)
        middle = state.astype(jnp.bfloat16)
        low = (state - middle.astype(jnp.float32)).astype(jnp.bfloat16)
        pieces.append(jnp.concatenate([high, middle, low], axis=0))
    products = [
        dot(pieces[g], turned_ref[part_of(g, HEAD_DIM), :], NN) for g in range(KV_HEADS)
    ]

    def read(g):
        recalled = products[g][part_of(0, HEAD_DIM), :] + (
            products[g][part_of(1, HEAD_DIM), :] + products[g][part_of(2, HEAD_DIM), :]
        )
        heads = []
        for i in range(GROUPS):
            head = recalled[:, part_of(i, rows)]
            square = jnp.sum(head * head, axis=0, keepdims=True) * (1.0 / HEAD_DIM)
            head = head * (lax.rsqrt(square + 1e-06) * reads)
            heads.append(head * gains_ref[part_of(g * GROUPS + i, HEAD_DIM), :])
        return heads

    return read


def attend_before(turned_ref, one_ref, stats_ref, summed_ref, first, same):
    rows = (turned_ref.shape[1] // GROUPS)
    live = suffix(jnp.where(block_docs(one_ref) == first, 0.0, 1.0))
    bias = jnp.where(live & same, 0.0, LOWEST)
    ahead = {}

    def score(g):
        if g < KV_HEADS and g not in ahead:
            ahead[g] = dot(block_keys(one_ref, g), turned_ref[part_of(g, HEAD_DIM), :], NN)

    def attend(g):
        for later in range(3):
            score(g + later)
        weights, factors, scales = [], [], []
        for i in range(GROUPS):
            cut = part_of(i, rows)
            masked = ahead[g][:, cut] * SCALE + bias
            top_own = stats_ref[g : g + 1, cut]
            top = jnp.maximum(jnp.max(masked, axis=0, keepdims=True), top_own)
            weight = jnp.exp2(masked - top)
            factor = jnp.exp2(top_own - top)
            total = stats_ref[KV_HEADS + g : KV_HEADS + g + 1, cut] * factor
            total = total + jnp.sum(weight, axis=0, keepdims=True)
            factors.append(factor)
            scales.append(stats_ref[2 * KV_HEADS + g : 2 * KV_HEADS + g + 1, cut] / total)
            weights.append(weight.astype(jnp.bfloat16))
        added = dot(block_values(one_ref, g), jnp.concatenate(weights, axis=1), TN)
        summed = summed_ref[part_of(g, HEAD_DIM), :] * jnp.concatenate(factors, axis=1) + added
        return summed * jnp.concatenate(scales, axis=1)

    return attend


def store_heads(mixed, out_ref, held, sems):
    copies = []
    ahead = mixed(0)
    for g in range(KV_HEADS):
        heads, ahead = ahead, mixed(g + 1) if g + 1 < KV_HEADS else None
        for i, head in enumerate(heads):
            held[:, part_of(g * GROUPS + i, HEAD_DIM)] = jnp.transpose(head)
        wide = part_of(g, GROUPS * HEAD_DIM)
        copies.append(pltpu.make_async_copy(held.at[:, wide], out_ref.at[:, wide], sems.at[g]))
        copies[g].start()
    for copy in copies:
        copy.wait()


def read_into(read_ref, refs, turned_ref, own_ref, gains_ref):
    first, same = first_document(block_docs(own_ref))
    read = read_memory(
        memory_states(refs, first), turned_ref, gains_ref, jnp.where(same, 1.0, 0.0)
    )
    for g in range(KV_HEADS):
        for i, head in enumerate(read(g)):
            read_ref[part_of(g * GROUPS + i, HEAD_DIM), :] = head


def read_kernel(plan, turned_ref, own_ref, three_ref, gains_ref, read_ref):
    @pl.when((lax.axis_index("kv") == 1) & jnp.logical_not(among(plan.memory_first)))
    def _():
        read_into(read_ref, [three_ref], turned_ref, own_ref, gains_ref)


def attend_and_store(
    turned_ref, own_ref, earlier_ref, stats_ref, summed_ref, read_ref, out_ref, held, sems
):
    first, same = first_document(block_docs(own_ref))
    attend = attend_before(turned_ref, earlier_ref, stats_ref, summed_ref, first, same)
    rows = (turned_ref.shape[1] // GROUPS)

    def mixed(g):
        attended = attend(g)
        return [
            read_ref[part_of(g * GROUPS + i, HEAD_DIM), :] + attended[:, part_of(i, rows)]
            for i in range(GROUPS)
        ]

    store_heads(mixed, out_ref, held, sems)


def read_and_store(states, turned_ref, gains_ref, same, summed_ref, out_ref, held, sems):
    rows = (turned_ref.shape[1] // GROUPS)
    read = read_memory(states, turned_ref, gains_ref, jnp.where(same, 1.0, 0.0))

    def mixed(g):
        return [
            head + summed_ref[part_of(g, HEAD_DIM), part_of(i, rows)]
            for i, head in enumerate(read(g))
        ]

    store_heads(mixed, out_ref, held, sems)


def early_kernel(
    plan, turned_ref, own_ref, one_ref, three_ref, stats_ref, gains_ref, summed_ref, read_in, out_in,
    read_ref, state_ref, out_ref, held, sems,
):
    kv = lax.axis_index("kv")
    late = among(plan.late)

    @pl.when((kv == 0) & jnp.logical_not(late | among(plan.alone)))
    def _():
        first, same = first_document(block_docs(own_ref))
        states = memory_states([one_ref, three_ref], first)
        read_and_store(states, turned_ref, gains_ref, same, summed_ref, out_ref, held, sems)

    @pl.when((kv == 1) & jnp.logical_not(late))
    def _():
        attend_and_store(
            turned_ref, own_ref, one_ref, stats_ref, summed_ref, read_ref, out_ref, held, sems
        )

    @pl.when((kv == 0) & late)
    def _():
        first, _ = first_document(block_docs(own_ref))
        for g, state in enumerate(memory_states([one_ref, three_ref], first)):
            state_ref[part_of(g, HEAD_DIM), :] = state

    @pl.when((kv == 1) & among(plan.memory_first))
    def _():
        read_into(read_ref, [one_ref, three_ref], turned_ref, own_ref, gains_ref)


def late_kernel(
    plan, turned_ref, own_ref, two_ref, state_ref, summed_ref, stats_ref, gains_ref, read_ref, out_in,
    out_ref, held, sems,
):
    kv = lax.axis_index("kv")
    late = among(plan.late)

    @pl.when((kv == 1) & late)
    def _():
        attend_and_store(
            turned_ref, own_ref, two_ref, stats_ref, summed_ref, read_ref, out_ref, held, sems
        )

    @pl.when((kv == 0) & late)
    def _():
        first, same = first_document(block_docs(own_ref))
        states = [
            state_ref[part_of(g, HEAD_DIM), :] + state
            for g, state in enumerate(memory_states([two_ref], first))
        ]
        read_and_store(states, turned_ref, gains_ref, same, summed_ref, out_ref, held, sems)


def near_device(n_seq, queries, keys, values, doc_ids, beta, lin_gain):
    rows = queries.shape[0]
    vmem = pl.BlockSpec(memory_space=pltpu.VMEM)
    hbm = pl.BlockSpec(memory_space=pltpu.HBM)
    in_hbm = functools.partial(pltpu.with_memory_space_constraint, memory_space=pltpu.HBM)
    params = pltpu.CompilerParams(vmem_limit_bytes=32 * 1024 * 1024)
    wide = GROUPS * rows
    group_shape = jax.ShapeDtypeStruct((KV_HEADS * HEAD_DIM, wide), jnp.float32)
    gains_shape = jax.ShapeDtypeStruct((HEADS * HEAD_DIM, HEAD_DIM), jnp.float32)
    docs = doc_ids.reshape(1, rows)
    gain = lin_gain.reshape(HEADS, HEAD_DIM)
    deep = 2 * KV_HEADS * rows + EXTRA

    def estimate(share):
        return pl.CostEstimate(
            flops=int(share * 4 * HEADS * HEAD_DIM * rows * rows),
            bytes_accessed=int(share * 4 * 1024 * 1024),
            transcendentals=int(share * HEADS * rows * rows),
        )

    def send(payload, pairs):
        return lax.ppermute(payload, ("seq", "kv"), pairs)

    plan = Plan(n_seq)
    block_shape = jax.ShapeDtypeStruct((deep, HEAD_DIM), jnp.bfloat16)
    short_shape = jax.ShapeDtypeStruct((deep - EXTRA, HEAD_DIM), jnp.bfloat16)
    stats_shape = jax.ShapeDtypeStruct((4 * KV_HEADS, wide), jnp.float32)
    state_shape = jax.ShapeDtypeStruct((KV_HEADS * HEAD_DIM, HEAD_DIM), jnp.float32)
    results = [group_shape, stats_shape, gains_shape]
    beta_scratch = pltpu.SMEM((HEADS,), jnp.float32)
    block = (in_hbm(keys), in_hbm(values), in_hbm(docs))
    beta = in_hbm(beta)
    packed = pl.pallas_call(
        functools.partial(pack_kernel, plan),
        out_shape=block_shape,
        in_specs=[hbm] * 3,
        out_specs=vmem,
        scratch_shapes=[
            pltpu.VMEM(keys.shape, keys.dtype),
            pltpu.VMEM(values.shape, values.dtype),
            pltpu.VMEM((1, rows), jnp.int32),
            pltpu.SemaphoreType.DMA((3,)),
        ],
        compiler_params=params,
        cost_estimate=estimate(0.1),
    )(*block)
    one = send(packed, plan.pairs[0])
    own, short, summed, stats, gains = pl.pallas_call(
        functools.partial(settle_kernel, plan),
        out_shape=[block_shape, short_shape] + results,
        in_specs=[vmem] * 5 + [hbm] * 2,
        out_specs=[vmem] * 5,
        scratch_shapes=[
            pltpu.VMEM(queries.shape, queries.dtype),
            beta_scratch,
            pltpu.SemaphoreType.DMA((2,)),
        ],
        compiler_params=params,
        cost_estimate=estimate(1.0),
    )(gain, packed, keys, values, docs, in_hbm(queries), beta)
    two = send(own, plan.pairs[1])
    three = send(short, plan.pairs[2])
    out_shape = jax.ShapeDtypeStruct((rows, HEADS * HEAD_DIM), jnp.float32)
    store_scratch = [
        pltpu.VMEM((rows, HEADS * HEAD_DIM), jnp.float32),
        pltpu.SemaphoreType.DMA((KV_HEADS,)),
    ]
    turned_shape = jax.ShapeDtypeStruct((KV_HEADS * HEAD_DIM, wide), queries.dtype)
    summed, stats, gains, out, turned = pl.pallas_call(
        functools.partial(own_kernel, plan),
        out_shape=results + [out_shape, turned_shape],
        in_specs=[vmem] * 3 + [hbm] + [vmem] * 3,
        out_specs=[vmem] * 3 + [hbm, vmem],
        scratch_shapes=[beta_scratch, pltpu.SemaphoreType.DMA] + store_scratch,
        input_output_aliases={4: 0, 5: 1, 6: 2},
        compiler_params=params,
        cost_estimate=estimate(1.0),
    )(queries, gain, own, beta, summed, stats, gains)
    read = pl.pallas_call(
        functools.partial(read_kernel, plan),
        out_shape=gains_shape,
        in_specs=[vmem] * 4,
        out_specs=vmem,
        compiler_params=params,
    )(turned, own, three, gains)
    read, state, out = pl.pallas_call(
        functools.partial(early_kernel, plan),
        out_shape=[gains_shape, state_shape, out_shape],
        in_specs=[vmem] * 8 + [hbm],
        out_specs=[vmem] * 2 + [hbm],
        scratch_shapes=store_scratch,
        input_output_aliases={7: 0, 8: 2},
        compiler_params=params,
    )(turned, own, one, three, stats, gains, summed, read, out)
    return pl.pallas_call(
        functools.partial(late_kernel, plan),
        out_shape=out_shape,
        in_specs=[vmem] * 8 + [hbm],
        out_specs=hbm,
        scratch_shapes=store_scratch,
        input_output_aliases={8: 0},
        compiler_params=params,
    )(turned, own, two, state, summed, stats, gains, read, out)


def carried_in(part, axis, combine, identity):
    place = lax.axis_index(axis)
    gathered = jax.tree.map(lambda a: lax.all_gather(a, axis), part)
    state = jax.tree.map(lambda a, e: jnp.zeros_like(a) + jnp.asarray(e, a.dtype), part, identity)

    def one(step, state):
        return combine(
            state, jax.tree.map(lambda a: lax.dynamic_index_in_dim(a, step, 0, False), gathered)
        )

    return lax.fori_loop(0, place, one, state)


def join_states(earlier, later):
    state_early, first_early, last_early = earlier
    state_late, first_late, last_late = later
    empty_late = first_late < 0
    joined = (first_late == last_late) & (last_early == first_late)
    merged = state_late + jnp.where(joined, state_early, jnp.zeros_like(state_early))
    combined = jnp.where(empty_late, state_early, merged)
    first_doc = jnp.where(first_early < 0, first_late, first_early)
    last_doc = jnp.where(empty_late, last_early, last_late)
    return (combined, first_doc, last_doc)


def tail_merge(one_side, other_side):
    state_one, first_one, last_one = one_side
    state_other, first_other, last_other = other_side
    top_doc = jnp.maximum(last_one, last_other)
    state_sum = jnp.where(last_one == top_doc, state_one, jnp.zeros_like(state_one))
    state_sum = state_sum + jnp.where(
        last_other == top_doc, state_other, jnp.zeros_like(state_other)
    )
    return (state_sum, jnp.minimum(first_one, first_other), top_doc)


def tail_state(key_rows, value_rows, doc_rows, target_doc):
    count = key_rows.shape[0]
    key_heads = key_rows.reshape(count, KV_HEADS, HEAD_DIM)
    value_heads = value_rows.reshape(count, KV_HEADS, HEAD_DIM)
    live = doc_rows == target_doc
    masked = jnp.where(live[:, None, None], key_heads, jnp.zeros_like(key_heads))
    return jnp.einsum("rgd,rge->gde", masked, value_heads, preferred_element_type=jnp.float32)


def attend_block(
    carry, query_heads, query_pos, query_doc, key_rows, value_rows, key_doc, key_start
):
    running_max, running_sum, accumulated = carry
    key_count = key_rows.shape[0]
    key_heads = key_rows.reshape(key_count, KV_HEADS, HEAD_DIM)
    value_heads = value_rows.reshape(key_count, KV_HEADS, HEAD_DIM)
    scores = jnp.einsum(
        "rgqd,kgd->gqrk", query_heads, key_heads, preferred_element_type=jnp.float32
    )
    scores = scores / jnp.sqrt(jnp.float32(HEAD_DIM))
    key_pos = key_start + jnp.arange(key_count, dtype=jnp.int32)
    allowed = (key_pos[None, :] <= query_pos[:, None]) & (key_doc[None, :] == query_doc[:, None])
    masked = jnp.where(allowed, scores, jnp.float32(-1e30))
    new_max = jnp.maximum(running_max, jnp.max(masked, axis=-1))
    factor = jnp.exp(running_max - new_max)
    weights = jnp.where(allowed, jnp.exp(masked - new_max[..., None]), jnp.float32(0.0))
    new_sum = running_sum * factor + jnp.sum(weights, axis=-1)
    product = jnp.einsum(
        "gqrk,kge->gqre",
        weights.astype(jnp.bfloat16),
        value_heads,
        preferred_element_type=jnp.float32,
    )
    new_accum = accumulated * factor[..., None] + product
    return (new_max, new_sum, new_accum)


def far_device(queries, keys, values, doc_ids, beta, lin_gain):
    row_count = queries.shape[0]
    groups = HEADS // KV_HEADS
    query_heads = queries.reshape(row_count, KV_HEADS, groups, HEAD_DIM)
    position = lax.axis_index("kv") * row_count
    query_pos = position + jnp.arange(row_count, dtype=jnp.int32)
    last_query = position + row_count - 1
    initial = (
        jnp.full((KV_HEADS, groups, row_count), -1e30, jnp.float32),
        jnp.zeros((KV_HEADS, groups, row_count), jnp.float32),
        jnp.zeros((KV_HEADS, groups, row_count, HEAD_DIM), jnp.float32),
    )
    empty_tail = (
        jnp.zeros((KV_HEADS, HEAD_DIM, HEAD_DIM), jnp.float32),
        jnp.array(2**30, jnp.int32),
        jnp.array(-1, jnp.int32),
    )
    key_piece = lax.all_gather(keys, "kv", axis=0, tiled=True)
    value_piece = lax.all_gather(values, "kv", axis=0, tiled=True)
    doc_piece = lax.all_gather(doc_ids, "kv", axis=0, tiled=True)
    blocks = key_piece.shape[0] // row_count

    def one_block(state, item):
        soft_state, tail_now = state
        key_block, value_block, doc_block, number = item
        block_start = number * row_count
        soft_next = lax.cond(
            block_start <= last_query,
            lambda inner: attend_block(
                inner,
                query_heads,
                query_pos,
                doc_ids,
                key_block,
                value_block,
                doc_block,
                block_start,
            ),
            lambda inner: inner,
            soft_state,
        )
        block_tail = (
            tail_state(key_block, value_block, doc_block, doc_block[-1]),
            doc_block[0],
            doc_block[-1],
        )
        tail_now = tail_merge(tail_now, block_tail)
        return ((soft_next, tail_now), None)

    stacked = (
        key_piece.reshape(blocks, row_count, -1),
        value_piece.reshape(blocks, row_count, -1),
        doc_piece.reshape(blocks, row_count),
        jnp.arange(blocks, dtype=jnp.int32),
    )
    result, _ = lax.scan(one_block, (initial, empty_tail), stacked)
    running, segment_tail = result
    running_max, running_sum, accumulated = running
    soft_out = jnp.transpose(accumulated / running_sum[..., None], (2, 0, 1, 3))
    identity = (
        jnp.zeros((KV_HEADS, HEAD_DIM, HEAD_DIM), jnp.float32),
        jnp.array(-1, jnp.int32),
        jnp.array(-1, jnp.int32),
    )
    memory = carried_in(segment_tail, "seq", join_states, identity)
    memory_state, memory_first, memory_last = memory
    query_float = query_heads.astype(jnp.float32)
    recalled = jnp.einsum(
        "rgqd,gde->rgqe", query_float, memory_state, precision=lax.Precision.HIGHEST
    )
    recalled = jnp.where((doc_ids == memory_last)[:, None, None, None], recalled, jnp.float32(0.0))
    mean_square = jnp.mean(recalled * recalled, axis=-1, keepdims=True)
    normed = (
        recalled * lax.rsqrt(mean_square + 1e-06) * lin_gain.reshape(KV_HEADS, groups, HEAD_DIM)
    )
    mixing = jax.nn.sigmoid(beta).reshape(KV_HEADS, groups)[None, :, :, None]
    mixed = mixing * normed + (1.0 - mixing) * soft_out
    return mixed.reshape(row_count, HEADS * HEAD_DIM).astype(jnp.float32)


def solution(mesh):
    n_seq, n_kv = mesh.shape["seq"], mesh.shape["kv"]
    in_specs = (
        P(("dp", "seq", "kv"), None),
        P(("dp", "seq", "kv"), None),
        P(("dp", "seq", "kv"), None),
        P(("dp", "seq", "kv")),
        P(),
        P(),
    )
    out_specs = P(("dp", "seq", "kv"), None)
    if n_kv == 2 and n_seq * n_kv <= 2 * LONGEST:
        on_device = functools.partial(near_device, n_seq)
    else:
        on_device = far_device
    return jax.shard_map(
        on_device, mesh=mesh, in_specs=in_specs, out_specs=out_specs, check_vma=False
    )
```

```python
import functools
import math

import jax
import jax.numpy as jnp
from jax import lax
from jax.experimental import pallas as pl
from jax.experimental.pallas import tpu as pltpu
from jax.sharding import PartitionSpec as P

HEADS = 16
KV_HEADS = 4
HEAD_DIM = 128
GROUPS = HEADS // KV_HEADS
LONGEST = 4
SCALE = math.log2(math.e) / math.sqrt(HEAD_DIM)
LOWEST = -1e30
EXTRA = 16

NT = (((1,), (1,)), ((), ()))
TN = (((0,), (0,)), ((), ()))
NN = (((1,), (0,)), ((), ()))


def dot(a, b, dims):
    return lax.dot_general(a, b, dims, preferred_element_type=jnp.float32)


def column(row):
    return jnp.transpose(jnp.broadcast_to(row, (HEAD_DIM, row.shape[1])))


def part_of(i, size):
    return slice(i * size, (i + 1) * size)


def group_queries(q_ref, g):
    heads = [q_ref[:, part_of(g * GROUPS + i, HEAD_DIM)] for i in range(GROUPS)]
    return jnp.concatenate(heads, axis=0)


def share_of(beta_ref, h):
    return 1.0 / (1.0 + jnp.exp(-jnp.full((1, HEAD_DIM), beta_ref[h], jnp.float32)))


def scaled_gains(beta_ref, gain_ref, out_ref):
    for h in range(HEADS):
        scaled = gain_ref[h : h + 1, :] * share_of(beta_ref, h)
        out_ref[part_of(h, HEAD_DIM), :] = column(scaled)


def suffix(others, least=0.0):
    count = jnp.maximum(jnp.sum(others, axis=1, keepdims=True), least)
    shape = (others.shape[1], HEAD_DIM)
    return lax.broadcasted_iota(jnp.int32, shape, 0).astype(jnp.float32) >= count


def first_document(docs):
    first = jnp.broadcast_to(docs[:, 0:1], docs.shape)
    return first, docs == first


def load_block(key_ref, value_ref, doc_ref, out_ref, doc_scratch, sems):
    rows = key_ref.shape[0]
    doc_copy = pltpu.make_async_copy(doc_ref, doc_scratch, sems.at[0])
    doc_copy.start()
    copies = []
    for g in range(2 * KV_HEADS):
        source = key_ref if g < KV_HEADS else value_ref
        copy = pltpu.make_async_copy(
            source.at[:, part_of(g % KV_HEADS, HEAD_DIM)],
            out_ref.at[part_of(g, rows), :],
            sems.at[1 + g],
        )
        copy.start()
        copies.append(copy)
    doc_copy.wait()
    start = 2 * KV_HEADS * rows
    docs = doc_scratch[...].astype(jnp.float32)
    docs = jnp.broadcast_to(docs, (out_ref.shape[0] - start, rows))
    out_ref[start:, :] = docs.astype(jnp.bfloat16)
    for copy in copies:
        copy.wait()


def block_keys(ref, g):
    return ref[part_of(g, HEAD_DIM), :]


def block_values(ref, g):
    return ref[part_of(KV_HEADS + g, HEAD_DIM), :]


def block_docs(ref):
    start = 2 * KV_HEADS * HEAD_DIM
    return ref[start : start + EXTRA, :].astype(jnp.float32)[0:1, :]


class Plan:
    def __init__(self, n_seq):
        devices = 2 * n_seq
        near = [(b, b + 1) for b in range(devices - 1)]
        far = [(b, b + 2) for b in range(devices - 2)]
        crossing = [p for p in far if p[0] // 2 % 2 == 1]
        touched = {b for p in crossing for b in p}
        targets = {p[1] for p in crossing}
        first = crossing + [p for p in near if p[0] not in touched and p[1] not in targets]
        second = [p for p in near if p not in first]
        last = [p for p in far if p not in first]
        self.pairs = [first, second, last]
        self.senders = sorted({p[0] for p in first})
        busy = {b for p in first for b in p} & {b for p in second for b in p}
        self.early = [b for b in range(devices) if b not in busy]
        self.late = sorted({p[1] for p in second})
        received = {p[1] for pairs in self.pairs for p in pairs}
        self.alone = [b for b in range(devices) if b not in received]
        self.memory_first = [p[1] for p in crossing if p[1] % 2 == 1]


def among(members):
    block = 2 * lax.axis_index("seq") + lax.axis_index("kv")
    return functools.reduce(jnp.logical_or, [block == b for b in members])


def pack_kernel(plan, key_ref, value_ref, doc_ref, out_ref, doc_scratch, sems):
    @pl.when(among(plan.senders))
    def _():
        load_block(key_ref, value_ref, doc_ref, out_ref, doc_scratch, sems)


def attend_own(q_ref, block_ref, g, bias):
    rows = q_ref.shape[0]
    scores = dot(block_keys(block_ref, g), group_queries(q_ref, g), NT)
    tops, totals, weights = [], [], []
    for i in range(GROUPS):
        masked = scores[:, part_of(i, rows)] * SCALE + bias
        top = jnp.max(masked, axis=0, keepdims=True)
        weight = jnp.exp2(masked - top)
        tops.append(top)
        totals.append(jnp.sum(weight, axis=0, keepdims=True))
        weights.append(weight.astype(jnp.bfloat16))
    summed = dot(block_values(block_ref, g), jnp.concatenate(weights, axis=1), TN)
    return summed, jnp.concatenate(tops, axis=1), jnp.concatenate(totals, axis=1)


def own_bias(docs):
    rows = docs.shape[1]
    place = lax.broadcasted_iota(jnp.int32, (rows, rows), 0)
    row = lax.broadcasted_iota(jnp.int32, (rows, rows), 1)
    return jnp.where((place <= row) & (column(docs) == docs), 0.0, LOWEST)


def attend_itself(
    q_ref, block_ref, gain_ref, beta_ref, beta_copy, summed_ref, stats_ref, gains_ref
):
    bias = own_bias(block_docs(block_ref))
    results = [attend_own(q_ref, block_ref, g, bias) for g in range(KV_HEADS)]
    beta_copy.wait()
    scaled_gains(beta_ref, gain_ref, gains_ref)
    done = lax.axis_index("kv") == 0
    for g, (summed, top, total) in enumerate(results):
        rest = [1.0 - share_of(beta_ref, g * GROUPS + i) for i in range(GROUPS)]
        rest = jnp.concatenate(rest, axis=1)
        summed_ref[part_of(g, HEAD_DIM), :] = summed * jnp.where(done, rest / total, 1.0)
        stats_ref[g : g + 1, :] = top
        stats_ref[KV_HEADS + g : KV_HEADS + g + 1, :] = total
        stats_ref[2 * KV_HEADS + g : 2 * KV_HEADS + g + 1, :] = rest


def settle_kernel(
    plan, gain_ref, packed_ref, key_ref, value_ref, doc_ref, query_ref, beta_ref,
    own_ref, short_ref, summed_ref, stats_ref, gains_ref,
    q_scratch, beta_scratch, early_sems,
):
    sender, early = among(plan.senders), among(plan.early)
    query_copy = pltpu.make_async_copy(query_ref, q_scratch, early_sems.at[0])
    beta_copy = pltpu.make_async_copy(beta_ref, beta_scratch, early_sems.at[1])

    @pl.when(early)
    def _():
        query_copy.start()
        beta_copy.start()

    @pl.when(sender)
    def _():
        own_ref[...] = packed_ref[...]

    @pl.when(jnp.logical_not(sender))
    def _():
        for g in range(KV_HEADS):
            cols = part_of(g, HEAD_DIM)
            own_ref[part_of(g, HEAD_DIM), :] = key_ref[:, cols]
            own_ref[part_of(KV_HEADS + g, HEAD_DIM), :] = value_ref[:, cols]
        start = 2 * KV_HEADS * HEAD_DIM
        docs = jnp.broadcast_to(doc_ref[...].astype(jnp.float32), (EXTRA, HEAD_DIM))
        own_ref[start:, :] = docs.astype(jnp.bfloat16)

    short_ref[...] = own_ref[0 : short_ref.shape[0], :]
    line = lax.broadcasted_iota(jnp.int32, (EXTRA, HEAD_DIM), 0)
    keys = own_ref[0:EXTRA, :].astype(jnp.float32)
    keys = jnp.where(line == 0, block_docs(own_ref), keys)
    short_ref[0:EXTRA, :] = keys.astype(jnp.bfloat16)

    @pl.when(early)
    def _():
        query_copy.wait()
        attend_itself(
            q_scratch, own_ref, gain_ref, beta_scratch, beta_copy,
            summed_ref, stats_ref, gains_ref,
        )


def own_kernel(
    plan, q_ref, gain_ref, own_ref, beta_ref, summed_in, stats_in, gains_in,
    summed_ref, stats_ref, gains_ref, out_ref, turned_ref, beta_scratch, sem, held, sems,
):
    rows = q_ref.shape[0]
    for g in range(KV_HEADS):
        for i in range(GROUPS):
            head = q_ref[:, part_of(g * GROUPS + i, HEAD_DIM)]
            turned_ref[part_of(g, HEAD_DIM), part_of(i, rows)] = jnp.transpose(head)

    @pl.when(among(plan.alone))
    def _():
        _, same = first_document(block_docs(own_ref))
        states = [jnp.zeros((HEAD_DIM, HEAD_DIM), jnp.float32)] * KV_HEADS
        read_and_store(states, turned_ref, gains_ref, same, summed_ref, out_ref, held, sems)

    @pl.when(jnp.logical_not(among(plan.early)))
    def _():
        beta_copy = pltpu.make_async_copy(beta_ref, beta_scratch, sem)
        beta_copy.start()
        attend_itself(
            q_ref, own_ref, gain_ref, beta_scratch, beta_copy, summed_ref, stats_ref, gains_ref
        )


def memory_states(refs, first):
    lives = []
    for ref in refs:
        short = ref.shape[0] == 2 * KV_HEADS * HEAD_DIM
        docs = ref[0:EXTRA, :].astype(jnp.float32)[0:1, :] if short else block_docs(ref)
        live = suffix(jnp.where(docs == first, 0.0, 1.0), 1.0 if short else 0.0)
        lives.append(jnp.where(live, 1.0, 0.0).astype(jnp.bfloat16))
    return [
        functools.reduce(
            jnp.add,
            [
                dot(block_values(ref, g), block_keys(ref, g) * live, TN)
                for ref, live in zip(refs, lives)
            ],
        )
        for g in range(KV_HEADS)
    ]


def read_memory(states, turned_ref, gains_ref, reads):
    rows = turned_ref.shape[1] // GROUPS
    pieces = []
    for state in states:
        high = state.astype(jnp.bfloat16)
        state = state - high.astype(jnp.float32)
        middle = state.astype(jnp.bfloat16)
        low = (state - middle.astype(jnp.float32)).astype(jnp.bfloat16)
        pieces.append(jnp.concatenate([high, middle, low], axis=0))
    products = [
        dot(pieces[g], turned_ref[part_of(g, HEAD_DIM), :], NN) for g in range(KV_HEADS)
    ]

    def read(g):
        recalled = products[g][part_of(0, HEAD_DIM), :] + (
            products[g][part_of(1, HEAD_DIM), :] + products[g][part_of(2, HEAD_DIM), :]
        )
        heads = []
        for i in range(GROUPS):
            head = recalled[:, part_of(i, rows)]
            square = jnp.sum(head * head, axis=0, keepdims=True) * (1.0 / HEAD_DIM)
            head = head * (lax.rsqrt(square + 1e-06) * reads)
            heads.append(head * gains_ref[part_of(g * GROUPS + i, HEAD_DIM), :])
        return heads

    return read


def attend_before(turned_ref, one_ref, stats_ref, summed_ref, first, same):
    rows = (turned_ref.shape[1] // GROUPS)
    live = suffix(jnp.where(block_docs(one_ref) == first, 0.0, 1.0))
    bias = jnp.where(live & same, 0.0, LOWEST)
    ahead = {}

    def score(g):
        if g < KV_HEADS and g not in ahead:
            ahead[g] = dot(block_keys(one_ref, g), turned_ref[part_of(g, HEAD_DIM), :], NN)

    def attend(g):
        for later in range(KV_HEADS):
            score(g + later)
        weights, factors, scales = [], [], []
        for i in range(GROUPS):
            cut = part_of(i, rows)
            masked = ahead[g][:, cut] * SCALE + bias
            top_own = stats_ref[g : g + 1, cut]
            top = jnp.maximum(jnp.max(masked, axis=0, keepdims=True), top_own)
            weight = jnp.exp2(masked - top)
            factor = jnp.exp2(top_own - top)
            total = stats_ref[KV_HEADS + g : KV_HEADS + g + 1, cut] * factor
            total = total + jnp.sum(weight, axis=0, keepdims=True)
            factors.append(factor)
            scales.append(stats_ref[2 * KV_HEADS + g : 2 * KV_HEADS + g + 1, cut] / total)
            weights.append(weight.astype(jnp.bfloat16))
        added = dot(block_values(one_ref, g), jnp.concatenate(weights, axis=1), TN)
        summed = summed_ref[part_of(g, HEAD_DIM), :] * jnp.concatenate(factors, axis=1) + added
        return summed * jnp.concatenate(scales, axis=1)

    return attend


def store_heads(mixed, out_ref, held, sems):
    copies = []
    ahead = mixed(0)
    for g in range(KV_HEADS):
        heads, ahead = ahead, mixed(g + 1) if g + 1 < KV_HEADS else None
        for i, head in enumerate(heads):
            held[:, part_of(g * GROUPS + i, HEAD_DIM)] = jnp.transpose(head)
        wide = part_of(g, GROUPS * HEAD_DIM)
        copies.append(pltpu.make_async_copy(held.at[:, wide], out_ref.at[:, wide], sems.at[g]))
        copies[g].start()
    for copy in copies:
        copy.wait()


def read_into(read_ref, refs, turned_ref, own_ref, gains_ref):
    first, same = first_document(block_docs(own_ref))
    read = read_memory(
        memory_states(refs, first), turned_ref, gains_ref, jnp.where(same, 1.0, 0.0)
    )
    for g in range(KV_HEADS):
        for i, head in enumerate(read(g)):
            read_ref[part_of(g * GROUPS + i, HEAD_DIM), :] = head


def read_kernel(plan, turned_ref, own_ref, three_ref, gains_ref, read_ref):
    @pl.when((lax.axis_index("kv") == 1) & jnp.logical_not(among(plan.memory_first)))
    def _():
        read_into(read_ref, [three_ref], turned_ref, own_ref, gains_ref)


def attend_and_store(
    turned_ref, own_ref, earlier_ref, stats_ref, summed_ref, read_ref, out_ref, held, sems
):
    first, same = first_document(block_docs(own_ref))
    attend = attend_before(turned_ref, earlier_ref, stats_ref, summed_ref, first, same)
    rows = (turned_ref.shape[1] // GROUPS)

    def mixed(g):
        attended = attend(g)
        return [
            read_ref[part_of(g * GROUPS + i, HEAD_DIM), :] + attended[:, part_of(i, rows)]
            for i in range(GROUPS)
        ]

    store_heads(mixed, out_ref, held, sems)


def read_and_store(states, turned_ref, gains_ref, same, summed_ref, out_ref, held, sems):
    rows = (turned_ref.shape[1] // GROUPS)
    read = read_memory(states, turned_ref, gains_ref, jnp.where(same, 1.0, 0.0))

    def mixed(g):
        return [
            head + summed_ref[part_of(g, HEAD_DIM), part_of(i, rows)]
            for i, head in enumerate(read(g))
        ]

    store_heads(mixed, out_ref, held, sems)


def early_kernel(
    plan, turned_ref, own_ref, one_ref, three_ref, stats_ref, gains_ref, summed_ref, read_in, out_in,
    read_ref, state_ref, out_ref, held, sems,
):
    kv = lax.axis_index("kv")
    late = among(plan.late)

    @pl.when((kv == 0) & jnp.logical_not(late | among(plan.alone)))
    def _():
        first, same = first_document(block_docs(own_ref))
        states = memory_states([one_ref, three_ref], first)
        read_and_store(states, turned_ref, gains_ref, same, summed_ref, out_ref, held, sems)

    @pl.when((kv == 1) & jnp.logical_not(late))
    def _():
        attend_and_store(
            turned_ref, own_ref, one_ref, stats_ref, summed_ref, read_ref, out_ref, held, sems
        )

    @pl.when((kv == 0) & late)
    def _():
        first, _ = first_document(block_docs(own_ref))
        for g, state in enumerate(memory_states([one_ref, three_ref], first)):
            state_ref[part_of(g, HEAD_DIM), :] = state

    @pl.when((kv == 1) & among(plan.memory_first))
    def _():
        read_into(read_ref, [one_ref, three_ref], turned_ref, own_ref, gains_ref)


def late_kernel(
    plan, turned_ref, own_ref, two_ref, state_ref, summed_ref, stats_ref, gains_ref, read_ref, out_in,
    out_ref, held, sems,
):
    kv = lax.axis_index("kv")
    late = among(plan.late)

    @pl.when((kv == 1) & late)
    def _():
        attend_and_store(
            turned_ref, own_ref, two_ref, stats_ref, summed_ref, read_ref, out_ref, held, sems
        )

    @pl.when((kv == 0) & late)
    def _():
        first, same = first_document(block_docs(own_ref))
        states = [
            state_ref[part_of(g, HEAD_DIM), :] + state
            for g, state in enumerate(memory_states([two_ref], first))
        ]
        read_and_store(states, turned_ref, gains_ref, same, summed_ref, out_ref, held, sems)


def near_device(n_seq, queries, keys, values, doc_ids, beta, lin_gain):
    rows = queries.shape[0]
    vmem = pl.BlockSpec(memory_space=pltpu.VMEM)
    hbm = pl.BlockSpec(memory_space=pltpu.HBM)
    in_hbm = functools.partial(pltpu.with_memory_space_constraint, memory_space=pltpu.HBM)
    params = pltpu.CompilerParams(vmem_limit_bytes=32 * 1024 * 1024)
    wide = GROUPS * rows
    group_shape = jax.ShapeDtypeStruct((KV_HEADS * HEAD_DIM, wide), jnp.float32)
    gains_shape = jax.ShapeDtypeStruct((HEADS * HEAD_DIM, HEAD_DIM), jnp.float32)
    docs = doc_ids.reshape(1, rows)
    gain = lin_gain.reshape(HEADS, HEAD_DIM)
    deep = 2 * KV_HEADS * rows + EXTRA

    def estimate(share):
        return pl.CostEstimate(
            flops=int(share * 4 * HEADS * HEAD_DIM * rows * rows),
            bytes_accessed=int(share * 4 * 1024 * 1024),
            transcendentals=int(share * HEADS * rows * rows),
        )

    def send(payload, pairs):
        return lax.ppermute(payload, ("seq", "kv"), pairs)

    plan = Plan(n_seq)
    block_shape = jax.ShapeDtypeStruct((deep, HEAD_DIM), jnp.bfloat16)
    short_shape = jax.ShapeDtypeStruct((deep - EXTRA, HEAD_DIM), jnp.bfloat16)
    stats_shape = jax.ShapeDtypeStruct((4 * KV_HEADS, wide), jnp.float32)
    state_shape = jax.ShapeDtypeStruct((KV_HEADS * HEAD_DIM, HEAD_DIM), jnp.float32)
    results = [group_shape, stats_shape, gains_shape]
    doc_scratch = pltpu.VMEM((1, rows), jnp.int32)
    beta_scratch = pltpu.SMEM((HEADS,), jnp.float32)
    sems = pltpu.SemaphoreType.DMA((2 * KV_HEADS + 1,))
    block = (in_hbm(keys), in_hbm(values), in_hbm(docs))
    beta = in_hbm(beta)
    packed = pl.pallas_call(
        functools.partial(pack_kernel, plan),
        out_shape=block_shape,
        in_specs=[hbm] * 3,
        out_specs=vmem,
        scratch_shapes=[doc_scratch, sems],
        compiler_params=params,
        cost_estimate=estimate(0.1),
    )(*block)
    one = send(packed, plan.pairs[0])
    own, short, summed, stats, gains = pl.pallas_call(
        functools.partial(settle_kernel, plan),
        out_shape=[block_shape, short_shape] + results,
        in_specs=[vmem] * 5 + [hbm] * 2,
        out_specs=[vmem] * 5,
        scratch_shapes=[
            pltpu.VMEM(queries.shape, queries.dtype),
            beta_scratch,
            pltpu.SemaphoreType.DMA((2,)),
        ],
        compiler_params=params,
        cost_estimate=estimate(1.0),
    )(gain, packed, keys, values, docs, in_hbm(queries), beta)
    two = send(own, plan.pairs[1])
    three = send(short, plan.pairs[2])
    out_shape = jax.ShapeDtypeStruct((rows, HEADS * HEAD_DIM), jnp.float32)
    store_scratch = [
        pltpu.VMEM((rows, HEADS * HEAD_DIM), jnp.float32),
        pltpu.SemaphoreType.DMA((KV_HEADS,)),
    ]
    turned_shape = jax.ShapeDtypeStruct((KV_HEADS * HEAD_DIM, wide), queries.dtype)
    summed, stats, gains, out, turned = pl.pallas_call(
        functools.partial(own_kernel, plan),
        out_shape=results + [out_shape, turned_shape],
        in_specs=[vmem] * 3 + [hbm] + [vmem] * 3,
        out_specs=[vmem] * 3 + [hbm, vmem],
        scratch_shapes=[beta_scratch, pltpu.SemaphoreType.DMA] + store_scratch,
        input_output_aliases={4: 0, 5: 1, 6: 2},
        compiler_params=params,
        cost_estimate=estimate(1.0),
    )(queries, gain, own, beta, summed, stats, gains)
    read = pl.pallas_call(
        functools.partial(read_kernel, plan),
        out_shape=gains_shape,
        in_specs=[vmem] * 4,
        out_specs=vmem,
        compiler_params=params,
    )(turned, own, three, gains)
    read, state, out = pl.pallas_call(
        functools.partial(early_kernel, plan),
        out_shape=[gains_shape, state_shape, out_shape],
        in_specs=[vmem] * 8 + [hbm],
        out_specs=[vmem] * 2 + [hbm],
        scratch_shapes=store_scratch,
        input_output_aliases={7: 0, 8: 2},
        compiler_params=params,
    )(turned, own, one, three, stats, gains, summed, read, out)
    return pl.pallas_call(
        functools.partial(late_kernel, plan),
        out_shape=out_shape,
        in_specs=[vmem] * 8 + [hbm],
        out_specs=hbm,
        scratch_shapes=store_scratch,
        input_output_aliases={8: 0},
        compiler_params=params,
    )(turned, own, two, state, summed, stats, gains, read, out)


def carried_in(part, axis, combine, identity):
    place = lax.axis_index(axis)
    gathered = jax.tree.map(lambda a: lax.all_gather(a, axis), part)
    state = jax.tree.map(lambda a, e: jnp.zeros_like(a) + jnp.asarray(e, a.dtype), part, identity)

    def one(step, state):
        return combine(
            state, jax.tree.map(lambda a: lax.dynamic_index_in_dim(a, step, 0, False), gathered)
        )

    return lax.fori_loop(0, place, one, state)


def join_states(earlier, later):
    state_early, first_early, last_early = earlier
    state_late, first_late, last_late = later
    empty_late = first_late < 0
    joined = (first_late == last_late) & (last_early == first_late)
    merged = state_late + jnp.where(joined, state_early, jnp.zeros_like(state_early))
    combined = jnp.where(empty_late, state_early, merged)
    first_doc = jnp.where(first_early < 0, first_late, first_early)
    last_doc = jnp.where(empty_late, last_early, last_late)
    return (combined, first_doc, last_doc)


def tail_merge(one_side, other_side):
    state_one, first_one, last_one = one_side
    state_other, first_other, last_other = other_side
    top_doc = jnp.maximum(last_one, last_other)
    state_sum = jnp.where(last_one == top_doc, state_one, jnp.zeros_like(state_one))
    state_sum = state_sum + jnp.where(
        last_other == top_doc, state_other, jnp.zeros_like(state_other)
    )
    return (state_sum, jnp.minimum(first_one, first_other), top_doc)


def tail_state(key_rows, value_rows, doc_rows, target_doc):
    count = key_rows.shape[0]
    key_heads = key_rows.reshape(count, KV_HEADS, HEAD_DIM)
    value_heads = value_rows.reshape(count, KV_HEADS, HEAD_DIM)
    live = doc_rows == target_doc
    masked = jnp.where(live[:, None, None], key_heads, jnp.zeros_like(key_heads))
    return jnp.einsum("rgd,rge->gde", masked, value_heads, preferred_element_type=jnp.float32)


def attend_block(
    carry, query_heads, query_pos, query_doc, key_rows, value_rows, key_doc, key_start
):
    running_max, running_sum, accumulated = carry
    key_count = key_rows.shape[0]
    key_heads = key_rows.reshape(key_count, KV_HEADS, HEAD_DIM)
    value_heads = value_rows.reshape(key_count, KV_HEADS, HEAD_DIM)
    scores = jnp.einsum(
        "rgqd,kgd->gqrk", query_heads, key_heads, preferred_element_type=jnp.float32
    )
    scores = scores / jnp.sqrt(jnp.float32(HEAD_DIM))
    key_pos = key_start + jnp.arange(key_count, dtype=jnp.int32)
    allowed = (key_pos[None, :] <= query_pos[:, None]) & (key_doc[None, :] == query_doc[:, None])
    masked = jnp.where(allowed, scores, jnp.float32(-1e30))
    new_max = jnp.maximum(running_max, jnp.max(masked, axis=-1))
    factor = jnp.exp(running_max - new_max)
    weights = jnp.where(allowed, jnp.exp(masked - new_max[..., None]), jnp.float32(0.0))
    new_sum = running_sum * factor + jnp.sum(weights, axis=-1)
    product = jnp.einsum(
        "gqrk,kge->gqre",
        weights.astype(jnp.bfloat16),
        value_heads,
        preferred_element_type=jnp.float32,
    )
    new_accum = accumulated * factor[..., None] + product
    return (new_max, new_sum, new_accum)


def far_device(queries, keys, values, doc_ids, beta, lin_gain):
    row_count = queries.shape[0]
    groups = HEADS // KV_HEADS
    query_heads = queries.reshape(row_count, KV_HEADS, groups, HEAD_DIM)
    position = lax.axis_index("kv") * row_count
    query_pos = position + jnp.arange(row_count, dtype=jnp.int32)
    last_query = position + row_count - 1
    initial = (
        jnp.full((KV_HEADS, groups, row_count), -1e30, jnp.float32),
        jnp.zeros((KV_HEADS, groups, row_count), jnp.float32),
        jnp.zeros((KV_HEADS, groups, row_count, HEAD_DIM), jnp.float32),
    )
    empty_tail = (
        jnp.zeros((KV_HEADS, HEAD_DIM, HEAD_DIM), jnp.float32),
        jnp.array(2**30, jnp.int32),
        jnp.array(-1, jnp.int32),
    )
    key_piece = lax.all_gather(keys, "kv", axis=0, tiled=True)
    value_piece = lax.all_gather(values, "kv", axis=0, tiled=True)
    doc_piece = lax.all_gather(doc_ids, "kv", axis=0, tiled=True)
    blocks = key_piece.shape[0] // row_count

    def one_block(state, item):
        soft_state, tail_now = state
        key_block, value_block, doc_block, number = item
        block_start = number * row_count
        soft_next = lax.cond(
            block_start <= last_query,
            lambda inner: attend_block(
                inner,
                query_heads,
                query_pos,
                doc_ids,
                key_block,
                value_block,
                doc_block,
                block_start,
            ),
            lambda inner: inner,
            soft_state,
        )
        block_tail = (
            tail_state(key_block, value_block, doc_block, doc_block[-1]),
            doc_block[0],
            doc_block[-1],
        )
        tail_now = tail_merge(tail_now, block_tail)
        return ((soft_next, tail_now), None)

    stacked = (
        key_piece.reshape(blocks, row_count, -1),
        value_piece.reshape(blocks, row_count, -1),
        doc_piece.reshape(blocks, row_count),
        jnp.arange(blocks, dtype=jnp.int32),
    )
    result, _ = lax.scan(one_block, (initial, empty_tail), stacked)
    running, segment_tail = result
    running_max, running_sum, accumulated = running
    soft_out = jnp.transpose(accumulated / running_sum[..., None], (2, 0, 1, 3))
    identity = (
        jnp.zeros((KV_HEADS, HEAD_DIM, HEAD_DIM), jnp.float32),
        jnp.array(-1, jnp.int32),
        jnp.array(-1, jnp.int32),
    )
    memory = carried_in(segment_tail, "seq", join_states, identity)
    memory_state, memory_first, memory_last = memory
    query_float = query_heads.astype(jnp.float32)
    recalled = jnp.einsum(
        "rgqd,gde->rgqe", query_float, memory_state, precision=lax.Precision.HIGHEST
    )
    recalled = jnp.where((doc_ids == memory_last)[:, None, None, None], recalled, jnp.float32(0.0))
    mean_square = jnp.mean(recalled * recalled, axis=-1, keepdims=True)
    normed = (
        recalled * lax.rsqrt(mean_square + 1e-06) * lin_gain.reshape(KV_HEADS, groups, HEAD_DIM)
    )
    mixing = jax.nn.sigmoid(beta).reshape(KV_HEADS, groups)[None, :, :, None]
    mixed = mixing * normed + (1.0 - mixing) * soft_out
    return mixed.reshape(row_count, HEADS * HEAD_DIM).astype(jnp.float32)


def solution(mesh):
    n_seq, n_kv = mesh.shape["seq"], mesh.shape["kv"]
    in_specs = (
        P(("dp", "seq", "kv"), None),
        P(("dp", "seq", "kv"), None),
        P(("dp", "seq", "kv"), None),
        P(("dp", "seq", "kv")),
        P(),
        P(),
    )
    out_specs = P(("dp", "seq", "kv"), None)
    if n_kv == 2 and n_seq * n_kv <= 2 * LONGEST:
        on_device = functools.partial(near_device, n_seq)
    else:
        on_device = far_device
    return jax.shard_map(
        on_device, mesh=mesh, in_specs=in_specs, out_specs=out_specs, check_vma=False
    )
```

```python
import functools
import math

import jax
import jax.numpy as jnp
from jax import lax
from jax.experimental import pallas as pl
from jax.experimental.pallas import tpu as pltpu
from jax.sharding import PartitionSpec as P

HEADS = 16
KV_HEADS = 4
HEAD_DIM = 128
GROUPS = HEADS // KV_HEADS
LONGEST = 4
SCALE = math.log2(math.e) / math.sqrt(HEAD_DIM)
LOWEST = -1e30
EXTRA = 16

NT = (((1,), (1,)), ((), ()))
TN = (((0,), (0,)), ((), ()))
NN = (((1,), (0,)), ((), ()))


def dot(a, b, dims):
    return lax.dot_general(a, b, dims, preferred_element_type=jnp.float32)


def column(row):
    return jnp.transpose(jnp.broadcast_to(row, (HEAD_DIM, row.shape[1])))


def part_of(i, size):
    return slice(i * size, (i + 1) * size)


def group_queries(q_ref, g):
    heads = [q_ref[:, part_of(g * GROUPS + i, HEAD_DIM)] for i in range(GROUPS)]
    return jnp.concatenate(heads, axis=0)


def share_of(beta_ref, h):
    return 1.0 / (1.0 + jnp.exp(-jnp.full((1, HEAD_DIM), beta_ref[h], jnp.float32)))


def scaled_gains(beta_ref, gain_ref, out_ref):
    for h in range(HEADS):
        scaled = gain_ref[h : h + 1, :] * share_of(beta_ref, h)
        out_ref[part_of(h, HEAD_DIM), :] = column(scaled)


def suffix(others, least=0.0):
    count = jnp.maximum(jnp.sum(others, axis=1, keepdims=True), least)
    shape = (others.shape[1], HEAD_DIM)
    return lax.broadcasted_iota(jnp.int32, shape, 0).astype(jnp.float32) >= count


def first_document(docs):
    first = jnp.broadcast_to(docs[:, 0:1], docs.shape)
    return first, docs == first


def load_block(key_ref, value_ref, doc_ref, out_ref, doc_scratch, sems):
    rows = key_ref.shape[0]
    doc_copy = pltpu.make_async_copy(doc_ref, doc_scratch, sems.at[0])
    doc_copy.start()
    copies = []
    for g in range(2 * KV_HEADS):
        source = key_ref if g < KV_HEADS else value_ref
        copy = pltpu.make_async_copy(
            source.at[:, part_of(g % KV_HEADS, HEAD_DIM)],
            out_ref.at[part_of(g, rows), :],
            sems.at[1 + g],
        )
        copy.start()
        copies.append(copy)
    doc_copy.wait()
    start = 2 * KV_HEADS * rows
    docs = doc_scratch[...].astype(jnp.float32)
    docs = jnp.broadcast_to(docs, (out_ref.shape[0] - start, rows))
    out_ref[start:, :] = docs.astype(jnp.bfloat16)
    for copy in copies:
        copy.wait()


def block_keys(ref, g):
    return ref[part_of(g, HEAD_DIM), :]


def block_values(ref, g):
    return ref[part_of(KV_HEADS + g, HEAD_DIM), :]


def block_docs(ref):
    start = 2 * KV_HEADS * HEAD_DIM
    return ref[start : start + EXTRA, :].astype(jnp.float32)[0:1, :]


class Plan:
    def __init__(self, n_seq):
        devices = 2 * n_seq
        near = [(b, b + 1) for b in range(devices - 1)]
        far = [(b, b + 2) for b in range(devices - 2)]
        crossing = [p for p in far if p[0] // 2 % 2 == 1]
        touched = {b for p in crossing for b in p}
        targets = {p[1] for p in crossing}
        first = crossing + [p for p in near if p[0] not in touched and p[1] not in targets]
        second = [p for p in near if p not in first]
        last = [p for p in far if p not in first]
        self.pairs = [first, second, last]
        self.senders = sorted({p[0] for p in first})
        busy = {b for p in first for b in p} & {b for p in second for b in p}
        self.early = [b for b in range(devices) if b not in busy]
        self.late = sorted({p[1] for p in second})
        received = {p[1] for pairs in self.pairs for p in pairs}
        self.alone = [b for b in range(devices) if b not in received]
        self.memory_first = [p[1] for p in crossing if p[1] % 2 == 1]


def among(members):
    block = 2 * lax.axis_index("seq") + lax.axis_index("kv")
    return functools.reduce(jnp.logical_or, [block == b for b in members])


def pack_kernel(plan, key_ref, value_ref, doc_ref, out_ref, doc_scratch, sems):
    @pl.when(among(plan.senders))
    def _():
        load_block(key_ref, value_ref, doc_ref, out_ref, doc_scratch, sems)


def attend_own(q_ref, block_ref, g, bias):
    rows = q_ref.shape[0]
    scores = dot(block_keys(block_ref, g), group_queries(q_ref, g), NT)
    tops, totals, weights = [], [], []
    for i in range(GROUPS):
        masked = scores[:, part_of(i, rows)] * SCALE + bias
        top = jnp.max(masked, axis=0, keepdims=True)
        weight = jnp.exp2(masked - top)
        tops.append(top)
        totals.append(jnp.sum(weight, axis=0, keepdims=True))
        weights.append(weight.astype(jnp.bfloat16))
    summed = dot(block_values(block_ref, g), jnp.concatenate(weights, axis=1), TN)
    return summed, jnp.concatenate(tops, axis=1), jnp.concatenate(totals, axis=1)


def own_bias(docs):
    rows = docs.shape[1]
    place = lax.broadcasted_iota(jnp.int32, (rows, rows), 0)
    row = lax.broadcasted_iota(jnp.int32, (rows, rows), 1)
    return jnp.where((place <= row) & (column(docs) == docs), 0.0, LOWEST)


def attend_itself(
    q_ref, block_ref, gain_ref, beta_ref, beta_copy, summed_ref, stats_ref, gains_ref
):
    bias = own_bias(block_docs(block_ref))
    results = [attend_own(q_ref, block_ref, g, bias) for g in range(KV_HEADS)]
    beta_copy.wait()
    scaled_gains(beta_ref, gain_ref, gains_ref)
    done = lax.axis_index("kv") == 0
    for g, (summed, top, total) in enumerate(results):
        rest = [1.0 - share_of(beta_ref, g * GROUPS + i) for i in range(GROUPS)]
        rest = jnp.concatenate(rest, axis=1)
        summed_ref[part_of(g, HEAD_DIM), :] = summed * jnp.where(done, rest / total, 1.0)
        stats_ref[g : g + 1, :] = top
        stats_ref[KV_HEADS + g : KV_HEADS + g + 1, :] = total
        stats_ref[2 * KV_HEADS + g : 2 * KV_HEADS + g + 1, :] = rest


def settle_kernel(
    plan, gain_ref, packed_ref, q_ref, key_ref, value_ref, doc_ref, beta_ref,
    own_ref, short_ref, summed_ref, stats_ref, gains_ref,
    beta_scratch, doc_scratch, sems, early_sem,
):
    sender, early = among(plan.senders), among(plan.early)
    beta_copy = pltpu.make_async_copy(beta_ref, beta_scratch, early_sem)

    @pl.when(early)
    def _():
        beta_copy.start()

    @pl.when(sender)
    def _():
        own_ref[...] = packed_ref[...]

    @pl.when(jnp.logical_not(sender))
    def _():
        load_block(key_ref, value_ref, doc_ref, own_ref, doc_scratch, sems)

    short_ref[...] = own_ref[0 : short_ref.shape[0], :]
    line = lax.broadcasted_iota(jnp.int32, (EXTRA, HEAD_DIM), 0)
    keys = own_ref[0:EXTRA, :].astype(jnp.float32)
    keys = jnp.where(line == 0, block_docs(own_ref), keys)
    short_ref[0:EXTRA, :] = keys.astype(jnp.bfloat16)

    @pl.when(early)
    def _():
        attend_itself(
            q_ref, own_ref, gain_ref, beta_scratch, beta_copy,
            summed_ref, stats_ref, gains_ref,
        )


def own_kernel(
    plan, q_ref, gain_ref, own_ref, beta_ref, summed_in, stats_in, gains_in,
    summed_ref, stats_ref, gains_ref, out_ref, turned_ref, beta_scratch, sem, held, sems,
):
    rows = q_ref.shape[0]
    for g in range(KV_HEADS):
        for i in range(GROUPS):
            head = q_ref[:, part_of(g * GROUPS + i, HEAD_DIM)]
            turned_ref[part_of(g, HEAD_DIM), part_of(i, rows)] = jnp.transpose(head)

    @pl.when(among(plan.alone))
    def _():
        _, same = first_document(block_docs(own_ref))
        states = [jnp.zeros((HEAD_DIM, HEAD_DIM), jnp.float32)] * KV_HEADS
        read_and_store(states, turned_ref, gains_ref, same, summed_ref, out_ref, held, sems)

    @pl.when(jnp.logical_not(among(plan.early)))
    def _():
        beta_copy = pltpu.make_async_copy(beta_ref, beta_scratch, sem)
        beta_copy.start()
        attend_itself(
            q_ref, own_ref, gain_ref, beta_scratch, beta_copy, summed_ref, stats_ref, gains_ref
        )


def memory_states(refs, first):
    lives = []
    for ref in refs:
        short = ref.shape[0] == 2 * KV_HEADS * HEAD_DIM
        docs = ref[0:EXTRA, :].astype(jnp.float32)[0:1, :] if short else block_docs(ref)
        live = suffix(jnp.where(docs == first, 0.0, 1.0), 1.0 if short else 0.0)
        lives.append(jnp.where(live, 1.0, 0.0).astype(jnp.bfloat16))
    return [
        functools.reduce(
            jnp.add,
            [
                dot(block_values(ref, g), block_keys(ref, g) * live, TN)
                for ref, live in zip(refs, lives)
            ],
        )
        for g in range(KV_HEADS)
    ]


def read_memory(states, turned_ref, gains_ref, reads):
    rows = turned_ref.shape[1] // GROUPS
    pieces = []
    for state in states:
        high = state.astype(jnp.bfloat16)
        state = state - high.astype(jnp.float32)
        middle = state.astype(jnp.bfloat16)
        low = (state - middle.astype(jnp.float32)).astype(jnp.bfloat16)
        pieces.append(jnp.concatenate([high, middle, low], axis=0))
    products = [
        dot(pieces[g], turned_ref[part_of(g, HEAD_DIM), :], NN) for g in range(KV_HEADS)
    ]

    def read(g):
        recalled = products[g][part_of(0, HEAD_DIM), :] + (
            products[g][part_of(1, HEAD_DIM), :] + products[g][part_of(2, HEAD_DIM), :]
        )
        heads = []
        for i in range(GROUPS):
            head = recalled[:, part_of(i, rows)]
            square = jnp.sum(head * head, axis=0, keepdims=True) * (1.0 / HEAD_DIM)
            head = head * (lax.rsqrt(square + 1e-06) * reads)
            heads.append(head * gains_ref[part_of(g * GROUPS + i, HEAD_DIM), :])
        return heads

    return read


def attend_before(turned_ref, one_ref, stats_ref, summed_ref, first, same):
    rows = (turned_ref.shape[1] // GROUPS)
    live = suffix(jnp.where(block_docs(one_ref) == first, 0.0, 1.0))
    bias = jnp.where(live & same, 0.0, LOWEST)
    ahead = {}

    def score(g):
        if g < KV_HEADS and g not in ahead:
            ahead[g] = dot(block_keys(one_ref, g), turned_ref[part_of(g, HEAD_DIM), :], NN)

    def attend(g):
        for later in range(3):
            score(g + later)
        weights, factors, scales = [], [], []
        for i in range(GROUPS):
            cut = part_of(i, rows)
            masked = ahead[g][:, cut] * SCALE + bias
            top_own = stats_ref[g : g + 1, cut]
            top = jnp.maximum(jnp.max(masked, axis=0, keepdims=True), top_own)
            weight = jnp.exp2(masked - top)
            factor = jnp.exp2(top_own - top)
            total = stats_ref[KV_HEADS + g : KV_HEADS + g + 1, cut] * factor
            total = total + jnp.sum(weight, axis=0, keepdims=True)
            factors.append(factor)
            scales.append(stats_ref[2 * KV_HEADS + g : 2 * KV_HEADS + g + 1, cut] / total)
            weights.append(weight.astype(jnp.bfloat16))
        added = dot(block_values(one_ref, g), jnp.concatenate(weights, axis=1), TN)
        summed = summed_ref[part_of(g, HEAD_DIM), :] * jnp.concatenate(factors, axis=1) + added
        return summed * jnp.concatenate(scales, axis=1)

    return attend


def store_heads(mixed, out_ref, held, sems):
    copies = []
    ahead = mixed(0)
    for g in range(KV_HEADS):
        heads, ahead = ahead, mixed(g + 1) if g + 1 < KV_HEADS else None
        for i, head in enumerate(heads):
            held[:, part_of(g * GROUPS + i, HEAD_DIM)] = jnp.transpose(head)
        wide = part_of(g, GROUPS * HEAD_DIM)
        copies.append(pltpu.make_async_copy(held.at[:, wide], out_ref.at[:, wide], sems.at[g]))
        copies[g].start()
    for copy in copies:
        copy.wait()


def read_into(read_ref, refs, turned_ref, own_ref, gains_ref):
    first, same = first_document(block_docs(own_ref))
    read = read_memory(
        memory_states(refs, first), turned_ref, gains_ref, jnp.where(same, 1.0, 0.0)
    )
    for g in range(KV_HEADS):
        for i, head in enumerate(read(g)):
            read_ref[part_of(g * GROUPS + i, HEAD_DIM), :] = head


def read_kernel(plan, turned_ref, own_ref, three_ref, gains_ref, read_ref):
    @pl.when((lax.axis_index("kv") == 1) & jnp.logical_not(among(plan.memory_first)))
    def _():
        read_into(read_ref, [three_ref], turned_ref, own_ref, gains_ref)


def attend_and_store(
    turned_ref, own_ref, earlier_ref, stats_ref, summed_ref, read_ref, out_ref, held, sems
):
    first, same = first_document(block_docs(own_ref))
    attend = attend_before(turned_ref, earlier_ref, stats_ref, summed_ref, first, same)
    rows = (turned_ref.shape[1] // GROUPS)

    def mixed(g):
        attended = attend(g)
        return [
            read_ref[part_of(g * GROUPS + i, HEAD_DIM), :] + attended[:, part_of(i, rows)]
            for i in range(GROUPS)
        ]

    store_heads(mixed, out_ref, held, sems)


def read_and_store(states, turned_ref, gains_ref, same, summed_ref, out_ref, held, sems):
    rows = (turned_ref.shape[1] // GROUPS)
    read = read_memory(states, turned_ref, gains_ref, jnp.where(same, 1.0, 0.0))

    def mixed(g):
        return [
            head + summed_ref[part_of(g, HEAD_DIM), part_of(i, rows)]
            for i, head in enumerate(read(g))
        ]

    store_heads(mixed, out_ref, held, sems)


def early_kernel(
    plan, turned_ref, own_ref, one_ref, three_ref, stats_ref, gains_ref, summed_ref, read_in, out_in,
    read_ref, state_ref, out_ref, held, sems,
):
    kv = lax.axis_index("kv")
    late = among(plan.late)

    @pl.when((kv == 0) & jnp.logical_not(late | among(plan.alone)))
    def _():
        first, same = first_document(block_docs(own_ref))
        states = memory_states([one_ref, three_ref], first)
        read_and_store(states, turned_ref, gains_ref, same, summed_ref, out_ref, held, sems)

    @pl.when((kv == 1) & jnp.logical_not(late))
    def _():
        attend_and_store(
            turned_ref, own_ref, one_ref, stats_ref, summed_ref, read_ref, out_ref, held, sems
        )

    @pl.when((kv == 0) & late)
    def _():
        first, _ = first_document(block_docs(own_ref))
        for g, state in enumerate(memory_states([one_ref, three_ref], first)):
            state_ref[part_of(g, HEAD_DIM), :] = state

    @pl.when((kv == 1) & among(plan.memory_first))
    def _():
        read_into(read_ref, [one_ref, three_ref], turned_ref, own_ref, gains_ref)


def late_kernel(
    plan, turned_ref, own_ref, two_ref, state_ref, summed_ref, stats_ref, gains_ref, read_ref, out_in,
    out_ref, held, sems,
):
    kv = lax.axis_index("kv")
    late = among(plan.late)

    @pl.when((kv == 1) & late)
    def _():
        attend_and_store(
            turned_ref, own_ref, two_ref, stats_ref, summed_ref, read_ref, out_ref, held, sems
        )

    @pl.when((kv == 0) & late)
    def _():
        first, same = first_document(block_docs(own_ref))
        states = [
            state_ref[part_of(g, HEAD_DIM), :] + state
            for g, state in enumerate(memory_states([two_ref], first))
        ]
        read_and_store(states, turned_ref, gains_ref, same, summed_ref, out_ref, held, sems)


def near_device(n_seq, queries, keys, values, doc_ids, beta, lin_gain):
    rows = queries.shape[0]
    vmem = pl.BlockSpec(memory_space=pltpu.VMEM)
    hbm = pl.BlockSpec(memory_space=pltpu.HBM)
    in_hbm = functools.partial(pltpu.with_memory_space_constraint, memory_space=pltpu.HBM)
    params = pltpu.CompilerParams(vmem_limit_bytes=32 * 1024 * 1024)
    wide = GROUPS * rows
    group_shape = jax.ShapeDtypeStruct((KV_HEADS * HEAD_DIM, wide), jnp.float32)
    gains_shape = jax.ShapeDtypeStruct((HEADS * HEAD_DIM, HEAD_DIM), jnp.float32)
    docs = doc_ids.reshape(1, rows)
    gain = lin_gain.reshape(HEADS, HEAD_DIM)
    deep = 2 * KV_HEADS * rows + EXTRA

    def estimate(share):
        return pl.CostEstimate(
            flops=int(share * 4 * HEADS * HEAD_DIM * rows * rows),
            bytes_accessed=int(share * 4 * 1024 * 1024),
            transcendentals=int(share * HEADS * rows * rows),
        )

    def send(payload, pairs):
        return lax.ppermute(payload, ("seq", "kv"), pairs)

    plan = Plan(n_seq)
    block_shape = jax.ShapeDtypeStruct((deep, HEAD_DIM), jnp.bfloat16)
    short_shape = jax.ShapeDtypeStruct((deep - EXTRA, HEAD_DIM), jnp.bfloat16)
    stats_shape = jax.ShapeDtypeStruct((4 * KV_HEADS, wide), jnp.float32)
    state_shape = jax.ShapeDtypeStruct((KV_HEADS * HEAD_DIM, HEAD_DIM), jnp.float32)
    results = [group_shape, stats_shape, gains_shape]
    doc_scratch = pltpu.VMEM((1, rows), jnp.int32)
    beta_scratch = pltpu.SMEM((HEADS,), jnp.float32)
    sems = pltpu.SemaphoreType.DMA((2 * KV_HEADS + 1,))
    block = (in_hbm(keys), in_hbm(values), in_hbm(docs))
    beta = in_hbm(beta)
    packed = pl.pallas_call(
        functools.partial(pack_kernel, plan),
        out_shape=block_shape,
        in_specs=[hbm] * 3,
        out_specs=vmem,
        scratch_shapes=[doc_scratch, sems],
        compiler_params=params,
        cost_estimate=estimate(0.1),
    )(*block)
    one = send(packed, plan.pairs[0])
    own, short, summed, stats, gains = pl.pallas_call(
        functools.partial(settle_kernel, plan),
        out_shape=[block_shape, short_shape] + results,
        in_specs=[vmem] * 3 + [hbm] * 4,
        out_specs=[vmem] * 5,
        scratch_shapes=[beta_scratch, doc_scratch, sems, pltpu.SemaphoreType.DMA],
        compiler_params=params,
        cost_estimate=estimate(1.0),
    )(gain, packed, queries, *block, beta)
    two = send(own, plan.pairs[1])
    three = send(short, plan.pairs[2])
    out_shape = jax.ShapeDtypeStruct((rows, HEADS * HEAD_DIM), jnp.float32)
    store_scratch = [
        pltpu.VMEM((rows, HEADS * HEAD_DIM), jnp.float32),
        pltpu.SemaphoreType.DMA((KV_HEADS,)),
    ]
    turned_shape = jax.ShapeDtypeStruct((KV_HEADS * HEAD_DIM, wide), queries.dtype)
    summed, stats, gains, out, turned = pl.pallas_call(
        functools.partial(own_kernel, plan),
        out_shape=results + [out_shape, turned_shape],
        in_specs=[vmem] * 3 + [hbm] + [vmem] * 3,
        out_specs=[vmem] * 3 + [hbm, vmem],
        scratch_shapes=[beta_scratch, pltpu.SemaphoreType.DMA] + store_scratch,
        input_output_aliases={4: 0, 5: 1, 6: 2},
        compiler_params=params,
        cost_estimate=estimate(1.0),
    )(queries, gain, own, beta, summed, stats, gains)
    read = pl.pallas_call(
        functools.partial(read_kernel, plan),
        out_shape=gains_shape,
        in_specs=[vmem] * 4,
        out_specs=vmem,
        compiler_params=params,
    )(turned, own, three, gains)
    read, state, out = pl.pallas_call(
        functools.partial(early_kernel, plan),
        out_shape=[gains_shape, state_shape, out_shape],
        in_specs=[vmem] * 8 + [hbm],
        out_specs=[vmem] * 2 + [hbm],
        scratch_shapes=store_scratch,
        input_output_aliases={7: 0, 8: 2},
        compiler_params=params,
    )(turned, own, one, three, stats, gains, summed, read, out)
    return pl.pallas_call(
        functools.partial(late_kernel, plan),
        out_shape=out_shape,
        in_specs=[vmem] * 8 + [hbm],
        out_specs=hbm,
        scratch_shapes=store_scratch,
        input_output_aliases={8: 0},
        compiler_params=params,
    )(turned, own, two, state, summed, stats, gains, read, out)


def carried_in(part, axis, combine, identity):
    place = lax.axis_index(axis)
    gathered = jax.tree.map(lambda a: lax.all_gather(a, axis), part)
    state = jax.tree.map(lambda a, e: jnp.zeros_like(a) + jnp.asarray(e, a.dtype), part, identity)

    def one(step, state):
        return combine(
            state, jax.tree.map(lambda a: lax.dynamic_index_in_dim(a, step, 0, False), gathered)
        )

    return lax.fori_loop(0, place, one, state)


def join_states(earlier, later):
    state_early, first_early, last_early = earlier
    state_late, first_late, last_late = later
    empty_late = first_late < 0
    joined = (first_late == last_late) & (last_early == first_late)
    merged = state_late + jnp.where(joined, state_early, jnp.zeros_like(state_early))
    combined = jnp.where(empty_late, state_early, merged)
    first_doc = jnp.where(first_early < 0, first_late, first_early)
    last_doc = jnp.where(empty_late, last_early, last_late)
    return (combined, first_doc, last_doc)


def tail_merge(one_side, other_side):
    state_one, first_one, last_one = one_side
    state_other, first_other, last_other = other_side
    top_doc = jnp.maximum(last_one, last_other)
    state_sum = jnp.where(last_one == top_doc, state_one, jnp.zeros_like(state_one))
    state_sum = state_sum + jnp.where(
        last_other == top_doc, state_other, jnp.zeros_like(state_other)
    )
    return (state_sum, jnp.minimum(first_one, first_other), top_doc)


def tail_state(key_rows, value_rows, doc_rows, target_doc):
    count = key_rows.shape[0]
    key_heads = key_rows.reshape(count, KV_HEADS, HEAD_DIM)
    value_heads = value_rows.reshape(count, KV_HEADS, HEAD_DIM)
    live = doc_rows == target_doc
    masked = jnp.where(live[:, None, None], key_heads, jnp.zeros_like(key_heads))
    return jnp.einsum("rgd,rge->gde", masked, value_heads, preferred_element_type=jnp.float32)


def attend_block(
    carry, query_heads, query_pos, query_doc, key_rows, value_rows, key_doc, key_start
):
    running_max, running_sum, accumulated = carry
    key_count = key_rows.shape[0]
    key_heads = key_rows.reshape(key_count, KV_HEADS, HEAD_DIM)
    value_heads = value_rows.reshape(key_count, KV_HEADS, HEAD_DIM)
    scores = jnp.einsum(
        "rgqd,kgd->gqrk", query_heads, key_heads, preferred_element_type=jnp.float32
    )
    scores = scores / jnp.sqrt(jnp.float32(HEAD_DIM))
    key_pos = key_start + jnp.arange(key_count, dtype=jnp.int32)
    allowed = (key_pos[None, :] <= query_pos[:, None]) & (key_doc[None, :] == query_doc[:, None])
    masked = jnp.where(allowed, scores, jnp.float32(-1e30))
    new_max = jnp.maximum(running_max, jnp.max(masked, axis=-1))
    factor = jnp.exp(running_max - new_max)
    weights = jnp.where(allowed, jnp.exp(masked - new_max[..., None]), jnp.float32(0.0))
    new_sum = running_sum * factor + jnp.sum(weights, axis=-1)
    product = jnp.einsum(
        "gqrk,kge->gqre",
        weights.astype(jnp.bfloat16),
        value_heads,
        preferred_element_type=jnp.float32,
    )
    new_accum = accumulated * factor[..., None] + product
    return (new_max, new_sum, new_accum)


def far_device(queries, keys, values, doc_ids, beta, lin_gain):
    row_count = queries.shape[0]
    groups = HEADS // KV_HEADS
    query_heads = queries.reshape(row_count, KV_HEADS, groups, HEAD_DIM)
    position = lax.axis_index("kv") * row_count
    query_pos = position + jnp.arange(row_count, dtype=jnp.int32)
    last_query = position + row_count - 1
    initial = (
        jnp.full((KV_HEADS, groups, row_count), -1e30, jnp.float32),
        jnp.zeros((KV_HEADS, groups, row_count), jnp.float32),
        jnp.zeros((KV_HEADS, groups, row_count, HEAD_DIM), jnp.float32),
    )
    empty_tail = (
        jnp.zeros((KV_HEADS, HEAD_DIM, HEAD_DIM), jnp.float32),
        jnp.array(2**30, jnp.int32),
        jnp.array(-1, jnp.int32),
    )
    key_piece = lax.all_gather(keys, "kv", axis=0, tiled=True)
    value_piece = lax.all_gather(values, "kv", axis=0, tiled=True)
    doc_piece = lax.all_gather(doc_ids, "kv", axis=0, tiled=True)
    blocks = key_piece.shape[0] // row_count

    def one_block(state, item):
        soft_state, tail_now = state
        key_block, value_block, doc_block, number = item
        block_start = number * row_count
        soft_next = lax.cond(
            block_start <= last_query,
            lambda inner: attend_block(
                inner,
                query_heads,
                query_pos,
                doc_ids,
                key_block,
                value_block,
                doc_block,
                block_start,
            ),
            lambda inner: inner,
            soft_state,
        )
        block_tail = (
            tail_state(key_block, value_block, doc_block, doc_block[-1]),
            doc_block[0],
            doc_block[-1],
        )
        tail_now = tail_merge(tail_now, block_tail)
        return ((soft_next, tail_now), None)

    stacked = (
        key_piece.reshape(blocks, row_count, -1),
        value_piece.reshape(blocks, row_count, -1),
        doc_piece.reshape(blocks, row_count),
        jnp.arange(blocks, dtype=jnp.int32),
    )
    result, _ = lax.scan(one_block, (initial, empty_tail), stacked)
    running, segment_tail = result
    running_max, running_sum, accumulated = running
    soft_out = jnp.transpose(accumulated / running_sum[..., None], (2, 0, 1, 3))
    identity = (
        jnp.zeros((KV_HEADS, HEAD_DIM, HEAD_DIM), jnp.float32),
        jnp.array(-1, jnp.int32),
        jnp.array(-1, jnp.int32),
    )
    memory = carried_in(segment_tail, "seq", join_states, identity)
    memory_state, memory_first, memory_last = memory
    query_float = query_heads.astype(jnp.float32)
    recalled = jnp.einsum(
        "rgqd,gde->rgqe", query_float, memory_state, precision=lax.Precision.HIGHEST
    )
    recalled = jnp.where((doc_ids == memory_last)[:, None, None, None], recalled, jnp.float32(0.0))
    mean_square = jnp.mean(recalled * recalled, axis=-1, keepdims=True)
    normed = (
        recalled * lax.rsqrt(mean_square + 1e-06) * lin_gain.reshape(KV_HEADS, groups, HEAD_DIM)
    )
    mixing = jax.nn.sigmoid(beta).reshape(KV_HEADS, groups)[None, :, :, None]
    mixed = mixing * normed + (1.0 - mixing) * soft_out
    return mixed.reshape(row_count, HEADS * HEAD_DIM).astype(jnp.float32)


def solution(mesh):
    n_seq, n_kv = mesh.shape["seq"], mesh.shape["kv"]
    in_specs = (
        P(("dp", "seq", "kv"), None),
        P(("dp", "seq", "kv"), None),
        P(("dp", "seq", "kv"), None),
        P(("dp", "seq", "kv")),
        P(),
        P(),
    )
    out_specs = P(("dp", "seq", "kv"), None)
    if n_kv == 2 and n_seq * n_kv <= 2 * LONGEST:
        on_device = functools.partial(near_device, n_seq)
    else:
        on_device = far_device
    return jax.shard_map(
        on_device, mesh=mesh, in_specs=in_specs, out_specs=out_specs, check_vma=False
    )
```

```python
import functools
import math

import jax
import jax.numpy as jnp
from jax import lax
from jax.experimental import pallas as pl
from jax.experimental.pallas import tpu as pltpu
from jax.sharding import PartitionSpec as P

HEADS = 16
KV_HEADS = 4
HEAD_DIM = 128
GROUPS = HEADS // KV_HEADS
LONGEST = 4
SCALE = math.log2(math.e) / math.sqrt(HEAD_DIM)
LOWEST = -1e30
EXTRA = 16

NT = (((1,), (1,)), ((), ()))
TN = (((0,), (0,)), ((), ()))
NN = (((1,), (0,)), ((), ()))


def dot(a, b, dims):
    return lax.dot_general(a, b, dims, preferred_element_type=jnp.float32)


def column(row):
    return jnp.transpose(jnp.broadcast_to(row, (HEAD_DIM, row.shape[1])))


def part_of(i, size):
    return slice(i * size, (i + 1) * size)


def group_queries(q_ref, g):
    heads = [q_ref[:, part_of(g * GROUPS + i, HEAD_DIM)] for i in range(GROUPS)]
    return jnp.concatenate(heads, axis=0)


def share_of(beta_ref, h):
    return 1.0 / (1.0 + jnp.exp(-jnp.full((1, HEAD_DIM), beta_ref[h], jnp.float32)))


def scaled_gains(beta_ref, gain_ref, out_ref):
    for h in range(HEADS):
        scaled = gain_ref[h : h + 1, :] * share_of(beta_ref, h)
        out_ref[part_of(h, HEAD_DIM), :] = column(scaled)


def suffix(others, least=0.0):
    count = jnp.maximum(jnp.sum(others, axis=1, keepdims=True), least)
    shape = (others.shape[1], HEAD_DIM)
    return lax.broadcasted_iota(jnp.int32, shape, 0).astype(jnp.float32) >= count


def first_document(docs):
    first = jnp.broadcast_to(docs[:, 0:1], docs.shape)
    return first, docs == first


def load_block(key_ref, value_ref, doc_ref, out_ref, doc_scratch, sems):
    rows = key_ref.shape[0]
    doc_copy = pltpu.make_async_copy(doc_ref, doc_scratch, sems.at[0])
    doc_copy.start()
    copies = []
    for g in range(2 * KV_HEADS):
        source = key_ref if g < KV_HEADS else value_ref
        copy = pltpu.make_async_copy(
            source.at[:, part_of(g % KV_HEADS, HEAD_DIM)],
            out_ref.at[part_of(g, rows), :],
            sems.at[1 + g],
        )
        copy.start()
        copies.append(copy)
    doc_copy.wait()
    start = 2 * KV_HEADS * rows
    docs = doc_scratch[...].astype(jnp.float32)
    docs = jnp.broadcast_to(docs, (out_ref.shape[0] - start, rows))
    out_ref[start:, :] = docs.astype(jnp.bfloat16)
    for copy in copies:
        copy.wait()


def block_keys(ref, g):
    return ref[part_of(g, HEAD_DIM), :]


def block_values(ref, g):
    return ref[part_of(KV_HEADS + g, HEAD_DIM), :]


def block_docs(ref):
    start = 2 * KV_HEADS * HEAD_DIM
    return ref[start : start + EXTRA, :].astype(jnp.float32)[0:1, :]


class Plan:
    def __init__(self, n_seq):
        devices = 2 * n_seq
        near = [(b, b + 1) for b in range(devices - 1)]
        far = [(b, b + 2) for b in range(devices - 2)]
        crossing = [p for p in far if p[0] // 2 % 2 == 1]
        touched = {b for p in crossing for b in p}
        targets = {p[1] for p in crossing}
        first = crossing + [p for p in near if p[0] not in touched and p[1] not in targets]
        second = [p for p in near if p not in first]
        last = [p for p in far if p not in first]
        self.pairs = [first, second, last]
        self.senders = sorted({p[0] for p in first})
        busy = {b for p in first for b in p} & {b for p in second for b in p}
        self.early = [b for b in range(devices) if b not in busy]
        self.late = sorted({p[1] for p in second})
        received = {p[1] for pairs in self.pairs for p in pairs}
        self.alone = [b for b in range(devices) if b not in received]
        self.memory_first = [p[1] for p in crossing if p[1] % 2 == 1]


def among(members):
    block = 2 * lax.axis_index("seq") + lax.axis_index("kv")
    return functools.reduce(jnp.logical_or, [block == b for b in members])


def pack_kernel(plan, key_ref, value_ref, doc_ref, out_ref, doc_scratch, sems):
    @pl.when(among(plan.senders))
    def _():
        load_block(key_ref, value_ref, doc_ref, out_ref, doc_scratch, sems)


def attend_own(q_ref, block_ref, g, bias):
    rows = q_ref.shape[0]
    scores = dot(block_keys(block_ref, g), group_queries(q_ref, g), NT)
    tops, totals, weights = [], [], []
    for i in range(GROUPS):
        masked = scores[:, part_of(i, rows)] * SCALE + bias
        top = jnp.max(masked, axis=0, keepdims=True)
        weight = jnp.exp2(masked - top)
        tops.append(top)
        totals.append(jnp.sum(weight, axis=0, keepdims=True))
        weights.append(weight.astype(jnp.bfloat16))
    summed = dot(block_values(block_ref, g), jnp.concatenate(weights, axis=1), TN)
    return summed, jnp.concatenate(tops, axis=1), jnp.concatenate(totals, axis=1)


def own_bias(docs):
    rows = docs.shape[1]
    place = lax.broadcasted_iota(jnp.int32, (rows, rows), 0)
    row = lax.broadcasted_iota(jnp.int32, (rows, rows), 1)
    return jnp.where((place <= row) & (column(docs) == docs), 0.0, LOWEST)


def attend_itself(
    q_ref, block_ref, gain_ref, beta_ref, beta_copy, summed_ref, stats_ref, gains_ref
):
    bias = own_bias(block_docs(block_ref))
    results = [attend_own(q_ref, block_ref, g, bias) for g in range(KV_HEADS)]
    beta_copy.wait()
    scaled_gains(beta_ref, gain_ref, gains_ref)
    done = lax.axis_index("kv") == 0
    for g, (summed, top, total) in enumerate(results):
        rest = [1.0 - share_of(beta_ref, g * GROUPS + i) for i in range(GROUPS)]
        rest = jnp.concatenate(rest, axis=1)
        summed_ref[part_of(g, HEAD_DIM), :] = summed * jnp.where(done, rest / total, 1.0)
        stats_ref[g : g + 1, :] = top
        stats_ref[KV_HEADS + g : KV_HEADS + g + 1, :] = total
        stats_ref[2 * KV_HEADS + g : 2 * KV_HEADS + g + 1, :] = rest


def settle_kernel(
    plan, gain_ref, packed_ref, q_ref, key_ref, value_ref, doc_ref, beta_ref,
    own_ref, short_ref, summed_ref, stats_ref, gains_ref,
    beta_scratch, doc_scratch, sems, early_sem,
):
    sender, early = among(plan.senders), among(plan.early)
    beta_copy = pltpu.make_async_copy(beta_ref, beta_scratch, early_sem)

    @pl.when(early)
    def _():
        beta_copy.start()

    @pl.when(sender)
    def _():
        own_ref[...] = packed_ref[...]

    @pl.when(jnp.logical_not(sender))
    def _():
        load_block(key_ref, value_ref, doc_ref, own_ref, doc_scratch, sems)

    short_ref[...] = own_ref[0 : short_ref.shape[0], :]
    line = lax.broadcasted_iota(jnp.int32, (EXTRA, HEAD_DIM), 0)
    keys = own_ref[0:EXTRA, :].astype(jnp.float32)
    keys = jnp.where(line == 0, block_docs(own_ref), keys)
    short_ref[0:EXTRA, :] = keys.astype(jnp.bfloat16)

    @pl.when(early)
    def _():
        attend_itself(
            q_ref, own_ref, gain_ref, beta_scratch, beta_copy,
            summed_ref, stats_ref, gains_ref,
        )


def own_kernel(
    plan, q_ref, gain_ref, own_ref, beta_ref, summed_in, stats_in, gains_in,
    summed_ref, stats_ref, gains_ref, out_ref, turned_ref, beta_scratch, sem, held, sems,
):
    rows = q_ref.shape[0]
    for g in range(KV_HEADS):
        for i in range(GROUPS):
            head = q_ref[:, part_of(g * GROUPS + i, HEAD_DIM)]
            turned_ref[part_of(g, HEAD_DIM), part_of(i, rows)] = jnp.transpose(head)

    @pl.when(among(plan.alone))
    def _():
        _, same = first_document(block_docs(own_ref))
        states = [jnp.zeros((HEAD_DIM, HEAD_DIM), jnp.float32)] * KV_HEADS
        read_and_store(states, turned_ref, gains_ref, same, summed_ref, out_ref, held, sems)

    @pl.when(jnp.logical_not(among(plan.early)))
    def _():
        beta_copy = pltpu.make_async_copy(beta_ref, beta_scratch, sem)
        beta_copy.start()
        attend_itself(
            q_ref, own_ref, gain_ref, beta_scratch, beta_copy, summed_ref, stats_ref, gains_ref
        )


def memory_states(refs, first):
    lives = []
    for ref in refs:
        short = ref.shape[0] == 2 * KV_HEADS * HEAD_DIM
        docs = ref[0:EXTRA, :].astype(jnp.float32)[0:1, :] if short else block_docs(ref)
        live = suffix(jnp.where(docs == first, 0.0, 1.0), 1.0 if short else 0.0)
        lives.append(jnp.where(live, 1.0, 0.0).astype(jnp.bfloat16))
    return [
        functools.reduce(
            jnp.add,
            [
                dot(block_values(ref, g), block_keys(ref, g) * live, TN)
                for ref, live in zip(refs, lives)
            ],
        )
        for g in range(KV_HEADS)
    ]


def read_memory(states, turned_ref, gains_ref, reads):
    rows = turned_ref.shape[1] // GROUPS
    pieces = []
    for state in states:
        high = state.astype(jnp.bfloat16)
        state = state - high.astype(jnp.float32)
        middle = state.astype(jnp.bfloat16)
        low = (state - middle.astype(jnp.float32)).astype(jnp.bfloat16)
        pieces.append(jnp.concatenate([high, middle, low], axis=0))
    products = [
        dot(pieces[g], turned_ref[part_of(g, HEAD_DIM), :], NN) for g in range(KV_HEADS)
    ]

    def read(g):
        recalled = products[g][part_of(0, HEAD_DIM), :] + (
            products[g][part_of(1, HEAD_DIM), :] + products[g][part_of(2, HEAD_DIM), :]
        )
        heads = []
        for i in range(GROUPS):
            head = recalled[:, part_of(i, rows)]
            square = jnp.sum(head * head, axis=0, keepdims=True) * (1.0 / HEAD_DIM)
            head = head * (lax.rsqrt(square + 1e-06) * reads)
            heads.append(head * gains_ref[part_of(g * GROUPS + i, HEAD_DIM), :])
        return heads

    return read


def attend_before(turned_ref, one_ref, stats_ref, summed_ref, first, same):
    rows = (turned_ref.shape[1] // GROUPS)
    live = suffix(jnp.where(block_docs(one_ref) == first, 0.0, 1.0))
    bias = jnp.where(live & same, 0.0, LOWEST)
    ahead = {}

    def score(g):
        if g < KV_HEADS and g not in ahead:
            ahead[g] = dot(block_keys(one_ref, g), turned_ref[part_of(g, HEAD_DIM), :], NN)

    def attend(g):
        for later in range(2):
            score(g + later)
        weights, factors, scales = [], [], []
        for i in range(GROUPS):
            cut = part_of(i, rows)
            masked = ahead[g][:, cut] * SCALE + bias
            top_own = stats_ref[g : g + 1, cut]
            top = jnp.maximum(jnp.max(masked, axis=0, keepdims=True), top_own)
            weight = jnp.exp2(masked - top)
            factor = jnp.exp2(top_own - top)
            total = stats_ref[KV_HEADS + g : KV_HEADS + g + 1, cut] * factor
            total = total + jnp.sum(weight, axis=0, keepdims=True)
            factors.append(factor)
            scales.append(stats_ref[2 * KV_HEADS + g : 2 * KV_HEADS + g + 1, cut] / total)
            weights.append(weight.astype(jnp.bfloat16))
        added = dot(block_values(one_ref, g), jnp.concatenate(weights, axis=1), TN)
        summed = summed_ref[part_of(g, HEAD_DIM), :] * jnp.concatenate(factors, axis=1) + added
        return summed * jnp.concatenate(scales, axis=1)

    return attend


def store_heads(mixed, out_ref, held, sems):
    copies = []
    ahead = mixed(0)
    for g in range(KV_HEADS):
        heads, ahead = ahead, mixed(g + 1) if g + 1 < KV_HEADS else None
        for i, head in enumerate(heads):
            held[:, part_of(g * GROUPS + i, HEAD_DIM)] = jnp.transpose(head)
        wide = part_of(g, GROUPS * HEAD_DIM)
        copies.append(pltpu.make_async_copy(held.at[:, wide], out_ref.at[:, wide], sems.at[g]))
        copies[g].start()
    for copy in copies:
        copy.wait()


def read_into(read_ref, refs, turned_ref, own_ref, gains_ref):
    first, same = first_document(block_docs(own_ref))
    read = read_memory(
        memory_states(refs, first), turned_ref, gains_ref, jnp.where(same, 1.0, 0.0)
    )
    for g in range(KV_HEADS):
        for i, head in enumerate(read(g)):
            read_ref[part_of(g * GROUPS + i, HEAD_DIM), :] = head


def read_kernel(plan, turned_ref, own_ref, three_ref, gains_ref, read_ref):
    @pl.when((lax.axis_index("kv") == 1) & jnp.logical_not(among(plan.memory_first)))
    def _():
        read_into(read_ref, [three_ref], turned_ref, own_ref, gains_ref)


def attend_and_store(
    turned_ref, own_ref, earlier_ref, stats_ref, summed_ref, read_ref, out_ref, held, sems
):
    first, same = first_document(block_docs(own_ref))
    attend = attend_before(turned_ref, earlier_ref, stats_ref, summed_ref, first, same)
    rows = (turned_ref.shape[1] // GROUPS)

    def mixed(g):
        attended = attend(g)
        return [
            read_ref[part_of(g * GROUPS + i, HEAD_DIM), :] + attended[:, part_of(i, rows)]
            for i in range(GROUPS)
        ]

    store_heads(mixed, out_ref, held, sems)


def read_and_store(states, turned_ref, gains_ref, same, summed_ref, out_ref, held, sems):
    rows = (turned_ref.shape[1] // GROUPS)
    read = read_memory(states, turned_ref, gains_ref, jnp.where(same, 1.0, 0.0))

    def mixed(g):
        return [
            head + summed_ref[part_of(g, HEAD_DIM), part_of(i, rows)]
            for i, head in enumerate(read(g))
        ]

    store_heads(mixed, out_ref, held, sems)


def early_kernel(
    plan, turned_ref, own_ref, one_ref, three_ref, stats_ref, gains_ref, summed_ref, read_in, out_in,
    read_ref, state_ref, out_ref, held, sems,
):
    kv = lax.axis_index("kv")
    late = among(plan.late)

    @pl.when((kv == 0) & jnp.logical_not(late | among(plan.alone)))
    def _():
        first, same = first_document(block_docs(own_ref))
        states = memory_states([one_ref, three_ref], first)
        read_and_store(states, turned_ref, gains_ref, same, summed_ref, out_ref, held, sems)

    @pl.when((kv == 1) & jnp.logical_not(late))
    def _():
        attend_and_store(
            turned_ref, own_ref, one_ref, stats_ref, summed_ref, read_ref, out_ref, held, sems
        )

    @pl.when((kv == 0) & late)
    def _():
        first, _ = first_document(block_docs(own_ref))
        for g, state in enumerate(memory_states([one_ref, three_ref], first)):
            state_ref[part_of(g, HEAD_DIM), :] = state

    @pl.when((kv == 1) & among(plan.memory_first))
    def _():
        read_into(read_ref, [one_ref, three_ref], turned_ref, own_ref, gains_ref)


def late_kernel(
    plan, turned_ref, own_ref, two_ref, state_ref, summed_ref, stats_ref, gains_ref, read_ref, out_in,
    out_ref, held, sems,
):
    kv = lax.axis_index("kv")
    late = among(plan.late)

    @pl.when((kv == 1) & late)
    def _():
        attend_and_store(
            turned_ref, own_ref, two_ref, stats_ref, summed_ref, read_ref, out_ref, held, sems
        )

    @pl.when((kv == 0) & late)
    def _():
        first, same = first_document(block_docs(own_ref))
        states = [
            state_ref[part_of(g, HEAD_DIM), :] + state
            for g, state in enumerate(memory_states([two_ref], first))
        ]
        read_and_store(states, turned_ref, gains_ref, same, summed_ref, out_ref, held, sems)


def near_device(n_seq, queries, keys, values, doc_ids, beta, lin_gain):
    rows = queries.shape[0]
    vmem = pl.BlockSpec(memory_space=pltpu.VMEM)
    hbm = pl.BlockSpec(memory_space=pltpu.HBM)
    in_hbm = functools.partial(pltpu.with_memory_space_constraint, memory_space=pltpu.HBM)
    params = pltpu.CompilerParams(vmem_limit_bytes=32 * 1024 * 1024)
    wide = GROUPS * rows
    group_shape = jax.ShapeDtypeStruct((KV_HEADS * HEAD_DIM, wide), jnp.float32)
    gains_shape = jax.ShapeDtypeStruct((HEADS * HEAD_DIM, HEAD_DIM), jnp.float32)
    docs = doc_ids.reshape(1, rows)
    gain = lin_gain.reshape(HEADS, HEAD_DIM)
    deep = 2 * KV_HEADS * rows + EXTRA

    def estimate(share):
        return pl.CostEstimate(
            flops=int(share * 4 * HEADS * HEAD_DIM * rows * rows),
            bytes_accessed=int(share * 4 * 1024 * 1024),
            transcendentals=int(share * HEADS * rows * rows),
        )

    def send(payload, pairs):
        return lax.ppermute(payload, ("seq", "kv"), pairs)

    plan = Plan(n_seq)
    block_shape = jax.ShapeDtypeStruct((deep, HEAD_DIM), jnp.bfloat16)
    short_shape = jax.ShapeDtypeStruct((deep - EXTRA, HEAD_DIM), jnp.bfloat16)
    stats_shape = jax.ShapeDtypeStruct((4 * KV_HEADS, wide), jnp.float32)
    state_shape = jax.ShapeDtypeStruct((KV_HEADS * HEAD_DIM, HEAD_DIM), jnp.float32)
    results = [group_shape, stats_shape, gains_shape]
    doc_scratch = pltpu.VMEM((1, rows), jnp.int32)
    beta_scratch = pltpu.SMEM((HEADS,), jnp.float32)
    sems = pltpu.SemaphoreType.DMA((2 * KV_HEADS + 1,))
    block = (in_hbm(keys), in_hbm(values), in_hbm(docs))
    beta = in_hbm(beta)
    packed = pl.pallas_call(
        functools.partial(pack_kernel, plan),
        out_shape=block_shape,
        in_specs=[hbm] * 3,
        out_specs=vmem,
        scratch_shapes=[doc_scratch, sems],
        compiler_params=params,
        cost_estimate=estimate(0.1),
    )(*block)
    one = send(packed, plan.pairs[0])
    own, short, summed, stats, gains = pl.pallas_call(
        functools.partial(settle_kernel, plan),
        out_shape=[block_shape, short_shape] + results,
        in_specs=[vmem] * 3 + [hbm] * 4,
        out_specs=[vmem] * 5,
        scratch_shapes=[beta_scratch, doc_scratch, sems, pltpu.SemaphoreType.DMA],
        compiler_params=params,
        cost_estimate=estimate(1.0),
    )(gain, packed, queries, *block, beta)
    two = send(own, plan.pairs[1])
    three = send(short, plan.pairs[2])
    out_shape = jax.ShapeDtypeStruct((rows, HEADS * HEAD_DIM), jnp.float32)
    store_scratch = [
        pltpu.VMEM((rows, HEADS * HEAD_DIM), jnp.float32),
        pltpu.SemaphoreType.DMA((KV_HEADS,)),
    ]
    turned_shape = jax.ShapeDtypeStruct((KV_HEADS * HEAD_DIM, wide), queries.dtype)
    summed, stats, gains, out, turned = pl.pallas_call(
        functools.partial(own_kernel, plan),
        out_shape=results + [out_shape, turned_shape],
        in_specs=[vmem] * 3 + [hbm] + [vmem] * 3,
        out_specs=[vmem] * 3 + [hbm, vmem],
        scratch_shapes=[beta_scratch, pltpu.SemaphoreType.DMA] + store_scratch,
        input_output_aliases={4: 0, 5: 1, 6: 2},
        compiler_params=params,
        cost_estimate=estimate(1.0),
    )(queries, gain, own, beta, summed, stats, gains)
    read = pl.pallas_call(
        functools.partial(read_kernel, plan),
        out_shape=gains_shape,
        in_specs=[vmem] * 4,
        out_specs=vmem,
        compiler_params=params,
    )(turned, own, three, gains)
    read, state, out = pl.pallas_call(
        functools.partial(early_kernel, plan),
        out_shape=[gains_shape, state_shape, out_shape],
        in_specs=[vmem] * 8 + [hbm],
        out_specs=[vmem] * 2 + [hbm],
        scratch_shapes=store_scratch,
        input_output_aliases={7: 0, 8: 2},
        compiler_params=params,
    )(turned, own, one, three, stats, gains, summed, read, out)
    return pl.pallas_call(
        functools.partial(late_kernel, plan),
        out_shape=out_shape,
        in_specs=[vmem] * 8 + [hbm],
        out_specs=hbm,
        scratch_shapes=store_scratch,
        input_output_aliases={8: 0},
        compiler_params=params,
    )(turned, own, two, state, summed, stats, gains, read, out)


def carried_in(part, axis, combine, identity):
    place = lax.axis_index(axis)
    gathered = jax.tree.map(lambda a: lax.all_gather(a, axis), part)
    state = jax.tree.map(lambda a, e: jnp.zeros_like(a) + jnp.asarray(e, a.dtype), part, identity)

    def one(step, state):
        return combine(
            state, jax.tree.map(lambda a: lax.dynamic_index_in_dim(a, step, 0, False), gathered)
        )

    return lax.fori_loop(0, place, one, state)


def join_states(earlier, later):
    state_early, first_early, last_early = earlier
    state_late, first_late, last_late = later
    empty_late = first_late < 0
    joined = (first_late == last_late) & (last_early == first_late)
    merged = state_late + jnp.where(joined, state_early, jnp.zeros_like(state_early))
    combined = jnp.where(empty_late, state_early, merged)
    first_doc = jnp.where(first_early < 0, first_late, first_early)
    last_doc = jnp.where(empty_late, last_early, last_late)
    return (combined, first_doc, last_doc)


def tail_merge(one_side, other_side):
    state_one, first_one, last_one = one_side
    state_other, first_other, last_other = other_side
    top_doc = jnp.maximum(last_one, last_other)
    state_sum = jnp.where(last_one == top_doc, state_one, jnp.zeros_like(state_one))
    state_sum = state_sum + jnp.where(
        last_other == top_doc, state_other, jnp.zeros_like(state_other)
    )
    return (state_sum, jnp.minimum(first_one, first_other), top_doc)


def tail_state(key_rows, value_rows, doc_rows, target_doc):
    count = key_rows.shape[0]
    key_heads = key_rows.reshape(count, KV_HEADS, HEAD_DIM)
    value_heads = value_rows.reshape(count, KV_HEADS, HEAD_DIM)
    live = doc_rows == target_doc
    masked = jnp.where(live[:, None, None], key_heads, jnp.zeros_like(key_heads))
    return jnp.einsum("rgd,rge->gde", masked, value_heads, preferred_element_type=jnp.float32)


def attend_block(
    carry, query_heads, query_pos, query_doc, key_rows, value_rows, key_doc, key_start
):
    running_max, running_sum, accumulated = carry
    key_count = key_rows.shape[0]
    key_heads = key_rows.reshape(key_count, KV_HEADS, HEAD_DIM)
    value_heads = value_rows.reshape(key_count, KV_HEADS, HEAD_DIM)
    scores = jnp.einsum(
        "rgqd,kgd->gqrk", query_heads, key_heads, preferred_element_type=jnp.float32
    )
    scores = scores / jnp.sqrt(jnp.float32(HEAD_DIM))
    key_pos = key_start + jnp.arange(key_count, dtype=jnp.int32)
    allowed = (key_pos[None, :] <= query_pos[:, None]) & (key_doc[None, :] == query_doc[:, None])
    masked = jnp.where(allowed, scores, jnp.float32(-1e30))
    new_max = jnp.maximum(running_max, jnp.max(masked, axis=-1))
    factor = jnp.exp(running_max - new_max)
    weights = jnp.where(allowed, jnp.exp(masked - new_max[..., None]), jnp.float32(0.0))
    new_sum = running_sum * factor + jnp.sum(weights, axis=-1)
    product = jnp.einsum(
        "gqrk,kge->gqre",
        weights.astype(jnp.bfloat16),
        value_heads,
        preferred_element_type=jnp.float32,
    )
    new_accum = accumulated * factor[..., None] + product
    return (new_max, new_sum, new_accum)


def far_device(queries, keys, values, doc_ids, beta, lin_gain):
    row_count = queries.shape[0]
    groups = HEADS // KV_HEADS
    query_heads = queries.reshape(row_count, KV_HEADS, groups, HEAD_DIM)
    position = lax.axis_index("kv") * row_count
    query_pos = position + jnp.arange(row_count, dtype=jnp.int32)
    last_query = position + row_count - 1
    initial = (
        jnp.full((KV_HEADS, groups, row_count), -1e30, jnp.float32),
        jnp.zeros((KV_HEADS, groups, row_count), jnp.float32),
        jnp.zeros((KV_HEADS, groups, row_count, HEAD_DIM), jnp.float32),
    )
    empty_tail = (
        jnp.zeros((KV_HEADS, HEAD_DIM, HEAD_DIM), jnp.float32),
        jnp.array(2**30, jnp.int32),
        jnp.array(-1, jnp.int32),
    )
    key_piece = lax.all_gather(keys, "kv", axis=0, tiled=True)
    value_piece = lax.all_gather(values, "kv", axis=0, tiled=True)
    doc_piece = lax.all_gather(doc_ids, "kv", axis=0, tiled=True)
    blocks = key_piece.shape[0] // row_count

    def one_block(state, item):
        soft_state, tail_now = state
        key_block, value_block, doc_block, number = item
        block_start = number * row_count
        soft_next = lax.cond(
            block_start <= last_query,
            lambda inner: attend_block(
                inner,
                query_heads,
                query_pos,
                doc_ids,
                key_block,
                value_block,
                doc_block,
                block_start,
            ),
            lambda inner: inner,
            soft_state,
        )
        block_tail = (
            tail_state(key_block, value_block, doc_block, doc_block[-1]),
            doc_block[0],
            doc_block[-1],
        )
        tail_now = tail_merge(tail_now, block_tail)
        return ((soft_next, tail_now), None)

    stacked = (
        key_piece.reshape(blocks, row_count, -1),
        value_piece.reshape(blocks, row_count, -1),
        doc_piece.reshape(blocks, row_count),
        jnp.arange(blocks, dtype=jnp.int32),
    )
    result, _ = lax.scan(one_block, (initial, empty_tail), stacked)
    running, segment_tail = result
    running_max, running_sum, accumulated = running
    soft_out = jnp.transpose(accumulated / running_sum[..., None], (2, 0, 1, 3))
    identity = (
        jnp.zeros((KV_HEADS, HEAD_DIM, HEAD_DIM), jnp.float32),
        jnp.array(-1, jnp.int32),
        jnp.array(-1, jnp.int32),
    )
    memory = carried_in(segment_tail, "seq", join_states, identity)
    memory_state, memory_first, memory_last = memory
    query_float = query_heads.astype(jnp.float32)
    recalled = jnp.einsum(
        "rgqd,gde->rgqe", query_float, memory_state, precision=lax.Precision.HIGHEST
    )
    recalled = jnp.where((doc_ids == memory_last)[:, None, None, None], recalled, jnp.float32(0.0))
    mean_square = jnp.mean(recalled * recalled, axis=-1, keepdims=True)
    normed = (
        recalled * lax.rsqrt(mean_square + 1e-06) * lin_gain.reshape(KV_HEADS, groups, HEAD_DIM)
    )
    mixing = jax.nn.sigmoid(beta).reshape(KV_HEADS, groups)[None, :, :, None]
    mixed = mixing * normed + (1.0 - mixing) * soft_out
    return mixed.reshape(row_count, HEADS * HEAD_DIM).astype(jnp.float32)


def solution(mesh):
    n_seq, n_kv = mesh.shape["seq"], mesh.shape["kv"]
    in_specs = (
        P(("dp", "seq", "kv"), None),
        P(("dp", "seq", "kv"), None),
        P(("dp", "seq", "kv"), None),
        P(("dp", "seq", "kv")),
        P(),
        P(),
    )
    out_specs = P(("dp", "seq", "kv"), None)
    if n_kv == 2 and n_seq * n_kv <= 2 * LONGEST:
        on_device = functools.partial(near_device, n_seq)
    else:
        on_device = far_device
    return jax.shard_map(
        on_device, mesh=mesh, in_specs=in_specs, out_specs=out_specs, check_vma=False
    )
```
